256 devices in a mesh: slide: 64 (over z, y, core), seq: 4 (over x).
Axes of the slice: x: 4, y: 4, z: 8, core: 2. Of those that a mesh axis runs over, the one named last changes fastest.
Arguments:
- embeddings: bfloat16 [64, 512, 1536], P('slide', 'seq'), may hold values from -30 to 30
- tile_counts: int32 [64], P('slide'), may hold values from 256 to 512, as said below
- masked_tiles: int32 [64, 128], P('slide'), may hold values from 0 to 511, as said below
- w_in: bfloat16 [1536, 768], replicated, may hold values from -0.15625 to 0.15625
- norm_gain: float32 [768], replicated, may hold values from 0.25 to 1.75
- w_qkv: bfloat16 [768, 2304], replicated, may hold values from -1 to 1
- w_out: bfloat16 [768, 768], replicated, may hold values from -0.21875 to 0.21875
Outputs:
- grad_weights: float32 [3072, 768], P(('slide', 'seq'))
- loss_sum: float32 [], replicated
The draws below stay inside these ranges and needn't reach their ends.
Inputs may be any that keep to these rules, and one draw needn't show every extreme that they name: `tile_counts`: number of real tiles of each slide; positions at or past it are padding. `masked_tiles`: each slide's 128 positions are distinct and below that slide's tile count.
All inputs are finite; a program needn't handle non-finite values.
Results may differ from the reference program's by a relative error of at most 0.02.
Values may be sent and summed in bfloat16 or wider, within the bound.
No kernel may reach another device: no remote copies, remote signals or barrier semaphores. Data moves between devices by JAX's collectives and lax.ppermute only.
A program may use at most 128 MiB of HBM per device.

```python
import math
import jax
import jax.numpy as jnp
from jax import lax

D = 768
HEADS = 16
E = 1536
HD = 48
RATE = 4
TOK_DEV = 128
SLIDES = 64
SEQ = 512
MASK = 128
N_SEQ = 4


def shared_counts(key):
    raw_counts = jax.random.randint(jax.random.fold_in(key, 11), (SLIDES,), SEQ // 2, SEQ + 1)
    slide_ids = jnp.arange(SLIDES)
    raw_counts = jnp.where(slide_ids == 0, SEQ, raw_counts)
    raw_counts = jnp.where(slide_ids == 1, SEQ // 2, raw_counts)
    return raw_counts.astype(jnp.int32)


def draw_tile_counts(key, part):
    counts_drawn = shared_counts(key)
    return counts_drawn


def draw_masked_tiles(key, part):
    counts_drawn = shared_counts(key)
    key = jax.random.fold_in(key, 5)
    ranks = jax.vmap(lambda slide_key: jax.random.permutation(slide_key, SEQ))(jax.random.split(key, SLIDES))
    positions = jnp.arange(SEQ, dtype=jnp.int32)
    ordering = jnp.where(positions[None, :] < counts_drawn[:, None], ranks, ranks + SEQ)
    _, chosen = lax.top_k(-ordering, MASK)
    return chosen.astype(jnp.int32)


def slide_scaled(key, top_scale):
    values = jnp.clip(jax.random.normal(jax.random.fold_in(key, 1), (SLIDES, SEQ, E), jnp.float32), -6.0, 6.0)
    rising = 1.0 + (top_scale - 1.0) * jnp.arange(SLIDES, dtype=jnp.float32) / max(SLIDES - 1, 1)
    return values * rising[:, None, None]


def draw_embeddings(key, part):
    key = jax.random.fold_in(key, 9)
    values = slide_scaled(key, 3.0)
    return values.astype(jnp.bfloat16)


def draw_w_qkv(key, part):
    key = jax.random.fold_in(key, 7)
    scale_in = D ** (-0.5)
    weights = jax.random.normal(jax.random.fold_in(key, 1), (D, 3 * D), jnp.float32) * scale_in
    weights = jnp.clip(weights, -6.0 * scale_in, 6.0 * scale_in)
    return weights.astype(jnp.bfloat16)


def scatter_about(stream_key, shape, scale, limit, held_as=jnp.bfloat16):
    drawn = scale * jax.random.normal(stream_key, shape, jnp.float32)
    return jnp.clip(drawn, min=-limit, max=limit).astype(held_as)


def setup_inputs(seed: int = 0) -> dict:
    key_list = jax.random.split(jax.random.key(seed), 8)
    return {
        "embeddings": draw_embeddings(jax.random.fold_in(key_list[7], 71), 0),
        "tile_counts": draw_tile_counts(jax.random.fold_in(key_list[7], 71), 0),
        "masked_tiles": draw_masked_tiles(jax.random.fold_in(key_list[7], 71), 0),
        "w_in": scatter_about(key_list[3], (E, D), E ** -0.5, 0.15625),
        "norm_gain": jnp.clip(1.0 + 0.15 * jax.random.normal(key_list[4], (D,), jnp.float32), 0.25, 1.75),
        "w_qkv": draw_w_qkv(jax.random.fold_in(key_list[7], 71), 0),
        "w_out": scatter_about(key_list[6], (D, D), D ** -0.5, 0.21875),
    }


NORM_EPS = 1e-06
NEG_FILL = -1e+30

def dilate(array):
    row_count = array.shape[0] // RATE
    head_size = array.shape[-1]
    grouped = array.reshape(row_count, RATE, HEADS // RATE, RATE, head_size)
    picked = jnp.diagonal(grouped, axis1=1, axis2=3)
    return jnp.transpose(picked, (0, 1, 3, 2)).reshape(row_count, HEADS, head_size)

def spread(far_grads):
    row_count = far_grads.shape[0]
    head_size = far_grads.shape[-1]
    grouped = far_grads.reshape(row_count, HEADS // RATE, RATE, head_size)
    identity = jnp.arange(RATE)[:, None] == jnp.arange(RATE)[None, :]
    placed = jnp.where(identity[None, :, None, :, None], grouped[:, None], jnp.zeros((), far_grads.dtype))
    return placed.reshape(row_count * RATE, HEADS, head_size)

def key_mask(head_index, query_pos, key_pos, real_count, far_count):
    near_mask = (key_pos[None, :] < real_count) | (key_pos[None, :] == query_pos[:, None])
    offset = head_index % RATE
    far_pos = jnp.arange(far_count, dtype=jnp.int32) * RATE + offset
    far_mask = (query_pos % RATE == offset)[:, None] & (far_pos < real_count)[None, :]
    return jnp.concatenate([near_mask, far_mask], axis=1)

def softmax_rows(query_head, key_head, allowed):
    scores = jnp.dot(query_head, key_head.T, preferred_element_type=jnp.float32) / math.sqrt(query_head.shape[-1])
    scores = jnp.where(allowed, scores, NEG_FILL)
    row_max = lax.optimization_barrier(jnp.max(scores, axis=1, keepdims=True))
    numerators = jnp.where(allowed, jnp.exp(scores - row_max), 0.0)
    return numerators / lax.optimization_barrier(jnp.sum(numerators, axis=1, keepdims=True))

def by_head(array):
    return jnp.transpose(array, (1, 0, 2))

def attend(queries, keys_all, values_all, query_pos, real_count):
    far_count = keys_all.shape[0] - queries.shape[0]

    def per_head(pieces):
        query_head, key_head, value_head, head_index = pieces
        weights_f = softmax_rows(query_head, key_head, key_mask(head_index, query_pos, query_pos, real_count, far_count))
        return jnp.dot(weights_f.astype(jnp.bfloat16), value_head, preferred_element_type=jnp.float32)
    outputs = lax.map(per_head, (by_head(queries), by_head(keys_all), by_head(values_all), jnp.arange(HEADS, dtype=jnp.int32)))
    return by_head(outputs).reshape(queries.shape[0], -1).astype(jnp.bfloat16)

def attend_back(queries, keys_all, values_all, grad_attended, query_pos, real_count):
    far_count = keys_all.shape[0] - queries.shape[0]
    grad_heads = by_head(grad_attended.reshape(queries.shape))

    def per_head(pieces):
        query_head, key_head, value_head, grad_head, head_index = pieces
        weights_f = softmax_rows(query_head, key_head, key_mask(head_index, query_pos, query_pos, real_count, far_count))
        grad_values = jnp.dot(weights_f.astype(jnp.bfloat16).T, grad_head, preferred_element_type=jnp.float32)
        grad_probs = jnp.dot(grad_head, value_head.T, preferred_element_type=jnp.float32)
        row_dots = lax.optimization_barrier(jnp.sum(weights_f * grad_probs, axis=1, keepdims=True))
        grad_scores = (weights_f * (grad_probs - row_dots) / math.sqrt(query_head.shape[-1])).astype(jnp.bfloat16)
        grad_query = jnp.dot(grad_scores, key_head, preferred_element_type=jnp.float32)
        grad_keys = jnp.dot(grad_scores.T, query_head, preferred_element_type=jnp.float32)
        return (grad_query, grad_keys, grad_values)
    grad_query, grad_keys, grad_values = lax.map(per_head, (by_head(queries), by_head(keys_all), by_head(values_all), grad_heads, jnp.arange(HEADS, dtype=jnp.int32)))
    return (by_head(grad_query), by_head(grad_keys), by_head(grad_values))

def project(inputs, w_in, norm_gain, w_qkv):
    hidden = jnp.dot(inputs, w_in, preferred_element_type=jnp.float32).astype(jnp.bfloat16)
    hidden_f = hidden.astype(jnp.float32)
    scale_rows = lax.rsqrt(lax.optimization_barrier(jnp.mean(hidden_f * hidden_f, axis=-1, keepdims=True)) + NORM_EPS)
    normed = (hidden_f * scale_rows * norm_gain.astype(jnp.float32)).astype(jnp.bfloat16)
    projected = jnp.dot(normed, w_qkv, preferred_element_type=jnp.float32).astype(jnp.bfloat16)
    return (hidden, normed, projected)

def split_blocks(array):
    return array.reshape((N_SEQ, TOK_DEV) + array.shape[1:])

def make_slide_step(w_in, norm_gain, w_qkv, w_out):

    def slide_step(running, pieces):
        gradients, loss_acc = running
        tiles, real_count, masked = pieces
        positions = jnp.arange(SEQ, dtype=jnp.int32)
        masked_flag = jnp.any(positions[:, None] == masked[None, :], axis=1)
        inputs = jnp.where(masked_flag[:, None], jnp.zeros((), jnp.bfloat16), tiles)
        hidden, normed, projected = project(inputs, w_in, norm_gain, w_qkv)
        queries = projected[:, :D].reshape(SEQ, HEADS, HD)
        keys_near = projected[:, D:2 * D].reshape(SEQ, HEADS, HD)
        values_near = projected[:, 2 * D:].reshape(SEQ, HEADS, HD)
        far_keys = dilate(keys_near)
        far_values = dilate(values_near)

        def forward_block(block_parts):
            query_block, key_block, value_block, pos_block = block_parts
            return attend(query_block, jnp.concatenate([key_block, far_keys], 0), jnp.concatenate([value_block, far_values], 0), pos_block, real_count)
        attended = lax.map(forward_block, (split_blocks(queries), split_blocks(keys_near), split_blocks(values_near), split_blocks(positions))).reshape(SEQ, D)
        mixed = (hidden.astype(jnp.float32) + jnp.dot(attended, w_out, preferred_element_type=jnp.float32)).astype(jnp.bfloat16)
        predicted = jnp.dot(mixed, w_in.T, preferred_element_type=jnp.float32)
        error_rows = jnp.where(masked_flag[:, None], predicted - tiles.astype(jnp.float32), 0.0)
        inv_count = 1.0 / (SLIDES * MASK)
        loss_part = jnp.sum(error_rows * error_rows) * inv_count
        grad_pred = (2.0 * inv_count * error_rows).astype(jnp.bfloat16)
        grad_mixed = jnp.dot(grad_pred, w_in, preferred_element_type=jnp.float32).astype(jnp.bfloat16)
        grad_attended = jnp.dot(grad_mixed, w_out.T, preferred_element_type=jnp.float32).astype(jnp.bfloat16)

        def backward_block(block_parts):
            query_block, key_block, value_block, grad_block, pos_block = block_parts
            return attend_back(query_block, jnp.concatenate([key_block, far_keys], 0), jnp.concatenate([value_block, far_values], 0), grad_block, pos_block, real_count)
        grad_query, grad_keys_all, grad_values_all = lax.map(backward_block, (split_blocks(queries), split_blocks(keys_near), split_blocks(values_near), split_blocks(grad_attended), split_blocks(positions)))
        grad_keys = grad_keys_all[:, :TOK_DEV].reshape(SEQ, HEADS, HD) + spread(lax.optimization_barrier(jnp.sum(grad_keys_all[:, TOK_DEV:], axis=0)))
        grad_values = grad_values_all[:, :TOK_DEV].reshape(SEQ, HEADS, HD) + spread(lax.optimization_barrier(jnp.sum(grad_values_all[:, TOK_DEV:], axis=0)))
        grad_projected = jnp.concatenate([grad_query.reshape(SEQ, D), grad_keys.reshape(SEQ, D), grad_values.reshape(SEQ, D)], axis=1).astype(jnp.bfloat16)
        weight_terms = jnp.concatenate([jnp.dot(grad_projected.T, normed, preferred_element_type=jnp.float32), jnp.dot(grad_mixed.T, attended, preferred_element_type=jnp.float32)], axis=0)
        return ((gradients + weight_terms, loss_acc + loss_part), None)
    return slide_step

def reference(embeddings, tile_counts, masked_tiles, w_in, norm_gain, w_qkv, w_out):
    start_state = (jnp.zeros((4 * D, D), jnp.float32), jnp.zeros((), jnp.float32))
    (gradients, loss_acc), _ = lax.scan(make_slide_step(w_in, norm_gain, w_qkv, w_out), start_state, (embeddings, tile_counts, masked_tiles))
    return (gradients, loss_acc)
```

```python
import math

import numpy as np
import jax
import jax.numpy as jnp
from jax import lax
from jax.experimental import pallas as pl
from jax.experimental.pallas import tpu as pltpu
from jax.sharding import PartitionSpec as P

HEADS = 16
RATE = 4
HD = 48
D = 768
TOK = 128
N_SEQ = 4
GROUPS = HEADS // RATE
FAR = TOK // RATE
NORM_EPS = 1e-06
NEG_FILL = -1e30
SCALE = 1.0 / math.sqrt(HD)
BF = jnp.bfloat16
F32 = jnp.float32
HALF = 384
SUB = 96
SECTIONS = 12
XROWS = SECTIONS * SUB + 16
NZ, NY, NC = 8, 4, 2


def dot(a, b, dims):
    return lax.dot_general(a, b, (dims, ((), ())), preferred_element_type=F32)


def nn(a, b):
    return dot(a, b, ((1,), (0,)))


def nt(a, b):
    return dot(a, b, ((1,), (1,)))


def tn(a, b):
    return dot(a, b, ((0,), (0,)))


def iota(shape, dim):
    return lax.broadcasted_iota(jnp.int32, shape, dim)


def class_major(index):
    return (index & (FAR - 1)) * RATE + (index >> 5)


def split_rows(value, shape, first):
    high = value.astype(BF).astype(F32)
    rest = value - high
    mid = rest.astype(BF).astype(F32)
    low = rest - mid
    row = iota(shape, 0)
    return jnp.where(
        row == first,
        high,
        jnp.where(row == first + 1, mid, jnp.where(row == first + 2, low, 0.0)),
    )


def masked_rows(pos0, masked):
    positions = pos0 + class_major(iota((TOK, TOK), 0))
    hits = jnp.where(positions == masked, 1.0, 0.0)
    return jnp.max(hits, axis=1, keepdims=True) > 0.5


def prep_kernel(s_ref, tiles_ref, masked_ref, w_in_ref, gain_ref, tiles_out, hidden_out, normed_out):
    pos0 = s_ref[0] * TOK
    shape = (TOK, TOK)
    order = (iota(shape, 1) == class_major(iota(shape, 0))).astype(F32).astype(BF)
    tiles = nn(order, tiles_ref[...]).astype(BF)
    tiles_out[...] = tiles
    flag = masked_rows(pos0, masked_ref[...])
    inputs = jnp.where(flag, 0.0, tiles.astype(F32)).astype(BF)
    hidden = nn(inputs, w_in_ref[...]).astype(BF)
    hidden_out[...] = hidden
    hidden_f = hidden.astype(F32)
    scale_rows = lax.rsqrt(jnp.mean(hidden_f * hidden_f, axis=1, keepdims=True) + NORM_EPS)
    normed_out[...] = (hidden_f * scale_rows * gain_ref[...]).astype(BF)


def window(group):
    return (group * RATE * HD) // 128 * 128


def head_masks(group):
    lane = iota((TOK, 256), 1) + window(group)
    row_class = iota((TOK, 256), 0) >> 5
    masks = []
    for r in range(RATE):
        first = (group * RATE + r) * HD
        masks.append((lane >= first) & (lane < first + HD))
    picked = masks[0] & (row_class == 0)
    for r in range(1, RATE):
        picked = picked | (masks[r] & (row_class == r))
    return masks, picked


def keep(mask, value):
    return jnp.where(mask, value, jnp.zeros((), value.dtype))


def by_class(own_class, pieces):
    out = pieces[0]
    for r in range(1, RATE):
        out = jnp.where(own_class == r, pieces[r], out)
    return out


def forward_kernel(
    s_ref, proj_ref, hidden_ref, tiles_ref, masked_ref, n0, n1, n2, n3, w_in_ref, w_qkv_ref, w_out_ref,
    pn_ref, fk_ref, fv_ref, pnear_ref, pfar_ref, att_ref, gm_ref, ga_ref, loss_ref,
    att_acc,
):
    seq = s_ref[0]
    count = s_ref[1]
    pos0 = seq * TOK
    for shift, ref in enumerate((n0, n1, n2, n3)):
        pn_ref[(seq - shift) & 3] = ref[...]
    pn_all = pn_ref[...].reshape(N_SEQ * TOK, D)
    for part, far_ref in enumerate((fk_ref, fv_ref)):
        for block in range(D // 256):
            first = (1 + part) * D + block * 256
            every = nn(pn_all, w_qkv_ref[:, first : first + 256])
            lane_head = iota((FAR, 256), 1) + block * 256
            lane_class = (lane_head // HD) & 3
            for src in range(N_SEQ):
                base = src * TOK
                pieces = [every[base + FAR * r : base + FAR * (r + 1)] for r in range(RATE)]
                far_ref[src * FAR : (src + 1) * FAR, block * 256 : (block + 1) * 256] = by_class(
                    lane_class, pieces
                ).astype(BF)

    square = (TOK, TOK)
    key_pos = pos0 + class_major(iota(square, 0))
    query_pos = pos0 + class_major(iota(square, 1))
    near_ok = (key_pos < count) | (key_pos == query_pos)
    far_row = iota(square, 0)
    far_ok = (far_row >> 5) * TOK + (far_row & (FAR - 1)) * RATE + (iota(square, 1) >> 5) < count
    own_class = iota((1, TOK), 1) >> 5

    att_acc[...] = jnp.zeros_like(att_acc)
    for g in range(GROUPS):
        lo = window(g)
        win = slice(lo, lo + 256)
        masks, picked = head_masks(g)
        q = proj_ref[:, lo : lo + 256]
        k = proj_ref[:, D + lo : D + lo + 256]
        v = proj_ref[:, 2 * D + lo : 2 * D + lo + 256]
        q_stack = jnp.concatenate([keep(m, q) for m in masks], 0)
        near = nt(k, q_stack)
        far = jnp.where(far_ok, nt(fk_ref[:, win], keep(picked, q)) * SCALE, NEG_FILL)
        far_max = jnp.max(far, axis=0, keepdims=True)
        scores = [
            jnp.where(near_ok, near[:, TOK * r : TOK * (r + 1)] * SCALE, NEG_FILL) for r in range(RATE)
        ]
        tops = []
        for r in range(RATE):
            top = jnp.max(scores[r], axis=0, keepdims=True)
            tops.append(jnp.where(own_class == r, jnp.maximum(top, far_max), top))
        exps = [jnp.exp(scores[r] - tops[r]) for r in range(RATE)]
        far_exp = jnp.exp(far - by_class(own_class, tops))
        far_sum = jnp.sum(far_exp, axis=0, keepdims=True)
        inverse = []
        for r in range(RATE):
            total = jnp.sum(exps[r], axis=0, keepdims=True)
            inverse.append(1.0 / jnp.where(own_class == r, total + far_sum, total))
        probs = [exps[r] * inverse[r] for r in range(RATE)]
        far_probs = far_exp * by_class(own_class, inverse)
        for r in range(RATE):
            pnear_ref[g, :, TOK * r : TOK * (r + 1)] = probs[r]
        pfar_ref[g] = far_probs
        att = tn(
            jnp.concatenate([p.astype(BF) for p in probs], 0),
            jnp.concatenate([keep(m, v) for m in masks], 0),
        )
        att_acc[:, win] += att + keep(picked, tn(far_probs.astype(BF), fv_ref[:, win]))

    attended = att_acc[...].astype(BF)
    att_ref[...] = attended
    mixed = (hidden_ref[...].astype(F32) + nn(attended, w_out_ref[...])).astype(BF)
    flag = masked_rows(pos0, masked_ref[...])
    error = jnp.where(flag, nt(mixed, w_in_ref[...]) - tiles_ref[...].astype(F32), 0.0)
    inv_count = s_ref[3].astype(F32)
    inv_count = 1.0 / inv_count
    loss = jnp.sum(jnp.sum(error * error, axis=1, keepdims=True), axis=0, keepdims=True) * inv_count
    loss_ref[...] = split_rows(jnp.broadcast_to(loss, (16, 128)), (16, 128), 0).astype(BF)
    grad_pred = (2.0 * inv_count * error).astype(BF)
    grad_mixed = nn(grad_pred, w_in_ref[...]).astype(BF)
    gm_ref[...] = grad_mixed
    ga_ref[...] = nt(grad_mixed, w_out_ref[...]).astype(BF)


def backward_kernel(
    proj_ref, fk_ref, fv_ref, pnear_ref, pfar_ref, gm_ref, ga_ref, loss_ref, spread_ref,
    x_ref,
    gq, gk, gv, gkf, gvf,
):
    own_class = iota((1, TOK), 1) >> 5
    for ref in (gq, gk, gv, gkf, gvf):
        ref[...] = jnp.zeros_like(ref)
    for g in range(GROUPS):
        lo = window(g)
        win = slice(lo, lo + 256)
        masks, picked = head_masks(g)
        q = proj_ref[:, lo : lo + 256]
        k = proj_ref[:, D + lo : D + lo + 256]
        v = proj_ref[:, 2 * D + lo : 2 * D + lo + 256]
        ga = ga_ref[:, win]
        fk = fk_ref[:, win]
        fv = fv_ref[:, win]
        ga_stack = jnp.concatenate([keep(m, ga) for m in masks], 0)
        ga_picked = keep(picked, ga)
        near = nt(v, ga_stack)
        far = nt(fv, ga_picked)
        probs = [pnear_ref[g, :, TOK * r : TOK * (r + 1)] for r in range(RATE)]
        far_probs = pfar_ref[g]
        far_dot = jnp.sum(far_probs * far, axis=0, keepdims=True)
        grads = [near[:, TOK * r : TOK * (r + 1)] for r in range(RATE)]
        dots = []
        for r in range(RATE):
            own = jnp.sum(probs[r] * grads[r], axis=0, keepdims=True)
            dots.append(jnp.where(own_class == r, own + far_dot, own))
        scores = [(probs[r] * (grads[r] - dots[r]) * SCALE).astype(BF) for r in range(RATE)]
        far_scores = (far_probs * (far - by_class(own_class, dots)) * SCALE).astype(BF)
        gq[:, win] += tn(
            jnp.concatenate(scores, 0), jnp.concatenate([keep(m, k) for m in masks], 0)
        ) + keep(picked, tn(far_scores, fk))
        gk[:, win] += nn(
            jnp.concatenate(scores, 1), jnp.concatenate([keep(m, q) for m in masks], 0)
        )
        gv[:, win] += nn(jnp.concatenate([p.astype(BF) for p in probs], 1), ga_stack)
        gkf[:, win] += nn(far_scores, keep(picked, q))
        gvf[:, win] += nn(far_probs.astype(BF), ga_picked)
    place = spread_ref[...]
    section = 0
    for ref in (gq, gk, gv, gkf, gvf, gm_ref):
        for half in range(2):
            turned = nt(place, ref[:, half * HALF : (half + 1) * HALF].astype(BF)).astype(BF)
            for j in range(N_SEQ):
                x_ref[j, section * SUB : (section + 1) * SUB] = turned[j * SUB : (j + 1) * SUB]
            section += 1
    for j in range(N_SEQ):
        x_ref[j, SECTIONS * SUB :] = loss_ref[...]


def product_kernel(s_ref, x_ref, pn_ref, a0, a1, a2, a3, order_ref, out_ref, left, att, res):
    seq = s_ref[0]
    core = s_ref[2]
    for shift, ref in enumerate((a0, a1, a2, a3)):
        att[pl.ds(((seq - shift) & 3) * TOK, TOK)] = ref[...]
    for src in range(N_SEQ):
        left[0 : 2 * SUB, src * TOK : (src + 1) * TOK] = x_ref[src, 0 : 2 * SUB]
        left[6 * SUB : 8 * SUB, src * TOK : (src + 1) * TOK] = x_ref[src, 10 * SUB : 12 * SUB]
    shape = (SUB, TOK)
    row = iota(shape, 0)
    lane_class = iota(shape, 1) >> 5
    core_row = jnp.where(row >= 48, 1, 0)
    row_y = (row - 48 * core_row) // 12
    row_class = ((row_y & 1) << 1) + core_row
    spots = [(row_class == r) & (lane_class == r) for r in range(RATE)]
    for part in range(2):
        for half in range(2):
            near_at = (2 + 2 * part + half) * SUB
            far_at = (6 + 2 * part + half) * SUB
            far = x_ref[0, far_at : far_at + SUB].astype(F32)
            for src in range(1, N_SEQ):
                far = far + x_ref[src, far_at : far_at + SUB].astype(F32)
            turns = [far] + [pltpu.roll(far, FAR * t, 1) for t in range(1, RATE)]
            for src in range(N_SEQ):
                total = x_ref[src, near_at : near_at + SUB].astype(F32)
                for r in range(RATE):
                    total = total + jnp.where(spots[r], turns[(r - src) & 3], 0.0)
                left[near_at : near_at + SUB, src * TOK : (src + 1) * TOK] = total.astype(BF)
    right = pn_ref[...].reshape(N_SEQ * TOK, D)
    res[0 : 6 * SUB] = nn(left[0 : 6 * SUB], right).astype(BF)
    res[6 * SUB :] = nn(left[6 * SUB :], att[...]).astype(BF)
    loss = x_ref[0, SECTIONS * SUB :].astype(F32)
    for src in range(1, N_SEQ):
        loss = loss + x_ref[src, SECTIONS * SUB :].astype(F32)
    loss = jnp.sum(jnp.sum(loss, axis=0, keepdims=True)[:, 0:1], axis=0, keepdims=True)
    tail = split_rows(jnp.broadcast_to(loss, (16, D)), (16, D), 0).astype(BF)
    whole = res[...]
    for c in range(NC):
        spot = (core + c) & 1
        out_ref[spot, 0:HALF] = nn(order_ref[c * HALF : (c + 1) * HALF], whole).astype(BF)
        out_ref[spot, HALF : HALF + 16] = tail


def core_kernel(mine_ref, other_ref, out_ref):
    for y in range(NY):
        rows = slice(y * SUB, (y + 1) * SUB)
        out_ref[y, 0:SUB] = (mine_ref[0, rows].astype(F32) + other_ref[rows].astype(F32)).astype(BF)
    tail = mine_ref[0, HALF:].astype(F32) + other_ref[HALF:].astype(F32)
    loss = jnp.sum(tail, axis=0, keepdims=True)
    rows = split_rows(jnp.broadcast_to(loss, (16, D)), (16, D), 0).astype(BF)
    for y in range(NY):
        out_ref[y, SUB:] = rows


def y_kernel(in_ref, order_ref, out_ref):
    total = in_ref[0].astype(F32)
    for src in range(1, NY):
        total = total + in_ref[src].astype(F32)
    loss = jnp.sum(total[SUB:], axis=0, keepdims=True)
    rows = split_rows(jnp.broadcast_to(loss, (16, D)), (16, D), 0)
    total = jnp.concatenate([total[:SUB], rows], 0).astype(BF)
    out_ref[...] = nn(order_ref[...], total).astype(BF).reshape(NZ, 16, D)


def z_kernel(in_ref, out_ref, loss_ref):
    total = in_ref[0].astype(F32)
    for src in range(1, NZ):
        total = total + in_ref[src].astype(F32)
    out_ref[...] = total[0:12]
    loss_ref[...] = jnp.sum(total[12:15, 0:1], axis=0, keepdims=True)


def spread_order():
    place = np.zeros((HALF, HALF), np.float32)
    for row in range(HALF):
        j, rest = divmod(row, SUB)
        c, rest = divmod(rest, 48)
        y, r = divmod(rest, 12)
        place[row, (y * NC + c) * HD + j * 12 + r] = 1.0
    return jnp.asarray(place, BF)


def product_order():
    place = np.zeros((D, D), np.float32)
    for row in range(D):
        c, rest = divmod(row, HALF)
        y, rest = divmod(rest, SUB)
        z, r = divmod(rest, 12)
        place[row, z * SUB + c * 48 + y * 12 + r] = 1.0
    return jnp.asarray(place, BF)


def pad_order():
    place = np.zeros((NZ * 16, SUB + 16), np.float32)
    for z in range(NZ):
        for r in range(12):
            place[z * 16 + r, z * 12 + r] = 1.0
        for r in range(3):
            place[z * 16 + 12 + r, SUB + r] = 1.0
    return jnp.asarray(place, BF)


SMEM = pl.BlockSpec(memory_space=pltpu.SMEM)
VMEM = pl.BlockSpec(memory_space=pltpu.VMEM)


def call(kernel, out_shapes, args, scratch=(), flops=1_000_000):
    specs = [SMEM if a.dtype == jnp.int32 and a.ndim == 1 else VMEM for a in args]
    single = not isinstance(out_shapes, (list, tuple))
    return pl.pallas_call(
        kernel,
        out_shape=out_shapes,
        in_specs=specs,
        out_specs=VMEM if single else [VMEM] * len(out_shapes),
        scratch_shapes=list(scratch),
        compiler_params=pltpu.CompilerParams(vmem_limit_bytes=48 * 1024 * 1024),
        cost_estimate=pl.CostEstimate(flops=flops, bytes_accessed=1_000_000, transcendentals=0),
    )(*args)


def shape(*dims, dtype=BF):
    return jax.ShapeDtypeStruct(dims, dtype)


def slide_at(z, y, c):
    return (z * NY + y) * NC + c


CORE_PAIRS = [(i, i ^ 1) for i in range(NZ * NY * NC)]
Y_GROUPS = [[slide_at(z, y, c) for y in range(NY)] for z in range(NZ) for c in range(NC)]
Z_GROUPS = [[slide_at(z, y, c) for z in range(NZ)] for y in range(NY) for c in range(NC)]


def gather_seq(array):
    return [array] + [
        lax.ppermute(array, "seq", [(k, (k + t) % N_SEQ) for k in range(N_SEQ)]) for t in range(1, N_SEQ)
    ]


def per_device(embeddings, tile_counts, masked_tiles, w_in, norm_gain, w_qkv, w_out):
    seq = lax.axis_index("seq")
    core = lax.axis_index("slide") % NC
    scale = lax.axis_size("slide") * masked_tiles.shape[1]
    scalars = jnp.stack(
        [seq.astype(jnp.int32), tile_counts[0], core.astype(jnp.int32), jnp.int32(scale)]
    )
    tiles, hidden, normed = call(
        prep_kernel,
        [shape(TOK, 2 * D), shape(TOK, D), shape(TOK, D)],
        (scalars, embeddings[0], masked_tiles, w_in, norm_gain.reshape(1, D)),
    )
    spread_norms = gather_seq(normed)
    projected = jnp.dot(normed, w_qkv, preferred_element_type=F32).astype(BF)
    pn, fk, fv, pnear, pfar, attended, grad_mixed, grad_attended, loss = call(
        forward_kernel,
        [
            shape(N_SEQ, TOK, D),
            shape(TOK, D),
            shape(TOK, D),
            shape(GROUPS, TOK, RATE * TOK, dtype=F32),
            shape(GROUPS, TOK, TOK, dtype=F32),
            shape(TOK, D),
            shape(TOK, D),
            shape(TOK, D),
            shape(16, 128),
        ],
        (scalars, projected, hidden, tiles, masked_tiles, *spread_norms, w_in, w_qkv, w_out),
        [pltpu.VMEM((TOK, D), F32)],
    )
    spread_att = gather_seq(attended)
    sent = call(
        backward_kernel,
        shape(N_SEQ, XROWS, TOK),
        (projected, fk, fv, pnear, pfar, grad_mixed, grad_attended, loss, spread_order()),
        [pltpu.VMEM((TOK, D), F32)] * 5,
    )
    got = lax.all_to_all(sent, "seq", 0, 0, tiled=True)
    halves = call(
        product_kernel,
        shape(NC, HALF + 16, D),
        (scalars, got, pn, *spread_att, product_order()),
        [pltpu.VMEM((D, N_SEQ * TOK), BF), pltpu.VMEM((N_SEQ * TOK, D), BF), pltpu.VMEM((D, D), BF)],
    )
    other = lax.ppermute(halves[1], "slide", CORE_PAIRS)
    by_y = call(core_kernel, shape(NY, SUB + 16, D), (halves, other))
    by_y = lax.all_to_all(by_y, "slide", 0, 0, tiled=True, axis_index_groups=Y_GROUPS)
    by_z = call(y_kernel, shape(NZ, 16, D), (by_y, pad_order()))
    by_z = lax.all_to_all(by_z, "slide", 0, 0, tiled=True, axis_index_groups=Z_GROUPS)
    gradients, loss_total = call(z_kernel, [shape(12, D, dtype=F32), shape(1, 1, dtype=F32)], (by_z,))
    return (gradients, loss_total[0, 0])


def solution(mesh):
    in_specs = (P("slide", "seq", None), P("slide"), P("slide", None), P(), P(), P(), P())
    out_specs = (P(("slide", "seq"), None), P())
    return jax.shard_map(
        per_device, mesh=mesh, in_specs=in_specs, out_specs=out_specs, check_vma=False
    )
```

```python
import functools
import math

import numpy as np
import jax
import jax.numpy as jnp
from jax import lax
from jax.experimental import pallas as pl
from jax.experimental.pallas import tpu as pltpu
from jax.sharding import PartitionSpec as P

HEADS = 16
RATE = 4
HD = 48
D = 768
TOK = 128
N_SEQ = 4
GROUPS = HEADS // RATE
FAR = TOK // RATE
NORM_EPS = 1e-06
NEG_FILL = -1e30
SCALE = 1.0 / math.sqrt(HD)
BF = jnp.bfloat16
F32 = jnp.float32
HALF = 384
SUB = 96
SECTIONS = 12
XROWS = SECTIONS * SUB + 16
NZ, NY, NC = 8, 4, 2


def dot(a, b, dims):
    return lax.dot_general(a, b, (dims, ((), ())), preferred_element_type=F32)


def nn(a, b):
    return dot(a, b, ((1,), (0,)))


def nt(a, b):
    return dot(a, b, ((1,), (1,)))


def tn(a, b):
    return dot(a, b, ((0,), (0,)))


def iota(shape, dim):
    return lax.broadcasted_iota(jnp.int32, shape, dim)


def class_major(index):
    return (index & (FAR - 1)) * RATE + (index >> 5)


def split_rows(value, shape, first):
    high = value.astype(BF).astype(F32)
    rest = value - high
    mid = rest.astype(BF).astype(F32)
    low = rest - mid
    row = iota(shape, 0)
    return jnp.where(
        row == first,
        high,
        jnp.where(row == first + 1, mid, jnp.where(row == first + 2, low, 0.0)),
    )


def prep_kernel(
    tiles_hbm, masked_hbm, gain_hbm, w_in_hbm, tiles_out, hidden_out, normed_out, flag_out,
    raw, masked, gain, w_in, sems,
):
    blocks = w_in_hbm.shape[0] // 256
    loads = [
        pltpu.make_async_copy(tiles_hbm.at[0], raw, sems.at[0]),
        pltpu.make_async_copy(masked_hbm, masked, sems.at[1]),
        pltpu.make_async_copy(gain_hbm, gain, sems.at[2]),
    ]
    chunks = [
        pltpu.make_async_copy(
            w_in_hbm.at[256 * i : 256 * (i + 1)], w_in.at[256 * i : 256 * (i + 1)], sems.at[3 + i]
        )
        for i in range(blocks)
    ]
    for copy in loads + chunks:
        copy.start()
    pos0 = lax.axis_index("seq") * TOK
    shape = (TOK, TOK)
    order = (iota(shape, 1) == class_major(iota(shape, 0))).astype(F32).astype(BF)
    loads[1].wait()
    positions = pos0 + class_major(iota(shape, 0))
    hits = jnp.where(positions == masked[...], 1.0, 0.0)
    hit = jnp.max(hits, axis=1, keepdims=True)
    flag_out[...] = jnp.broadcast_to(hit, shape)
    flag = hit > 0.5
    loads[0].wait()
    hidden = jnp.zeros((TOK, D), F32)
    for i in range(blocks):
        cols = slice(256 * i, 256 * (i + 1))
        tiles = nn(order, raw[:, cols])
        tiles_out[:, cols] = tiles.astype(BF)
        chunks[i].wait()
        hidden += nn(jnp.where(flag, 0.0, tiles).astype(BF), w_in[cols])
    hidden = hidden.astype(BF)
    hidden_out[...] = hidden
    hidden_f = hidden.astype(F32)
    scale_rows = lax.rsqrt(jnp.mean(hidden_f * hidden_f, axis=1, keepdims=True) + NORM_EPS)
    loads[2].wait()
    normed_out[...] = (hidden_f * scale_rows * gain[...].reshape(1, D)).astype(BF)


def window(group):
    return (group * RATE * HD) // 128 * 128


def head_masks(group):
    lane = iota((TOK, 256), 1) + window(group)
    row_class = iota((TOK, 256), 0) >> 5
    masks = []
    for r in range(RATE):
        first = (group * RATE + r) * HD
        masks.append((lane >= first) & (lane < first + HD))
    picked = masks[0] & (row_class == 0)
    for r in range(1, RATE):
        picked = picked | (masks[r] & (row_class == r))
    return masks, picked


def keep(mask, value):
    return jnp.where(mask, value, jnp.zeros((), value.dtype))


def by_class(own_class, pieces):
    out = pieces[0]
    for r in range(1, RATE):
        out = jnp.where(own_class == r, pieces[r], out)
    return out


def near_kernel(count_ref, normed_ref, w_qkv_ref, proj_ref, exp_ref, top_ref, sum_ref):
    count = count_ref[0]
    pos0 = lax.axis_index("seq") * TOK
    normed = normed_ref[...]
    for block in range(3 * D // 256):
        cols = slice(block * 256, (block + 1) * 256)
        proj_ref[:, cols] = nn(normed, w_qkv_ref[:, cols]).astype(BF)
    square = (TOK, TOK)
    key_pos = pos0 + class_major(iota(square, 0))
    query_pos = pos0 + class_major(iota(square, 1))
    near_ok = (key_pos < count) | (key_pos == query_pos)
    for g in range(GROUPS):
        lo = window(g)
        masks, _ = head_masks(g)
        q = proj_ref[:, lo : lo + 256]
        k = proj_ref[:, D + lo : D + lo + 256]
        near = nt(k, jnp.concatenate([keep(m, q) for m in masks], 0))
        for r in range(RATE):
            head = g * RATE + r
            scores = jnp.where(near_ok, near[:, TOK * r : TOK * (r + 1)] * SCALE, NEG_FILL)
            top = jnp.max(scores, axis=0, keepdims=True)
            exps = jnp.exp(scores - top)
            exp_ref[g, :, TOK * r : TOK * (r + 1)] = exps
            top_ref[head : head + 1] = top
            sum_ref[head : head + 1] = jnp.sum(exps, axis=0, keepdims=True)


def far_kernel(
    count_ref, n0, n1, n2, n3, proj_ref, exp_ref, top_ref, sum_ref, w_qkv_ref,
    pn_ref, fk_ref, fv_ref, pnear_ref, pfar_ref, att_ref,
    att_acc,
):
    count = count_ref[0]
    seq = lax.axis_index("seq")
    for turn, ref in enumerate((n0, n1, n2, n3)):
        pn_ref[(seq - turn) & 3] = ref[...]
    pn_all = pn_ref[...].reshape(N_SEQ * TOK, D)
    for part, far_ref in enumerate((fk_ref, fv_ref)):
        for block in range(D // 256):
            first = (1 + part) * D + block * 256
            every = nn(pn_all, w_qkv_ref[:, first : first + 256])
            lane_class = ((iota((FAR, 256), 1) + block * 256) // HD) & 3
            for src in range(N_SEQ):
                base = src * TOK
                pieces = [every[base + FAR * r : base + FAR * (r + 1)] for r in range(RATE)]
                far_ref[src * FAR : (src + 1) * FAR, block * 256 : (block + 1) * 256] = by_class(
                    lane_class, pieces
                ).astype(BF)

    square = (TOK, TOK)
    far_row = iota(square, 0)
    far_ok = (far_row >> 5) * TOK + (far_row & (FAR - 1)) * RATE + (iota(square, 1) >> 5) < count
    own_class = iota((1, TOK), 1) >> 5

    att_acc[...] = jnp.zeros_like(att_acc)
    for g in range(GROUPS):
        lo = window(g)
        win = slice(lo, lo + 256)
        masks, picked = head_masks(g)
        q = proj_ref[:, lo : lo + 256]
        v = proj_ref[:, 2 * D + lo : 2 * D + lo + 256]
        far = jnp.where(far_ok, nt(fk_ref[:, win], keep(picked, q)) * SCALE, NEG_FILL)
        heads = range(g * RATE, (g + 1) * RATE)
        near_tops = [top_ref[h : h + 1] for h in heads]
        near_sums = [sum_ref[h : h + 1] for h in heads]
        top = jnp.maximum(jnp.max(far, axis=0, keepdims=True), by_class(own_class, near_tops))
        shrink = jnp.exp(by_class(own_class, near_tops) - top)
        far_exp = jnp.exp(far - top)
        total = by_class(own_class, near_sums) * shrink + jnp.sum(far_exp, axis=0, keepdims=True)
        far_probs = far_exp / total
        probs = []
        for r in range(RATE):
            factor = jnp.where(own_class == r, shrink / total, 1.0 / near_sums[r])
            probs.append(exp_ref[g, :, TOK * r : TOK * (r + 1)] * factor)
            pnear_ref[g, :, TOK * r : TOK * (r + 1)] = probs[r]
        pfar_ref[g] = far_probs
        att = tn(
            jnp.concatenate([p.astype(BF) for p in probs], 0),
            jnp.concatenate([keep(m, v) for m in masks], 0),
        )
        att_acc[:, win] += att + keep(picked, tn(far_probs.astype(BF), fv_ref[:, win]))
    att_ref[...] = att_acc[...].astype(BF)


def backward_kernel(
    inv_count,
    proj_ref, fk_ref, fv_ref, pnear_ref, pfar_ref, att_ref, hidden_ref, tiles_ref, flag_ref, spread_ref,
    w_in_ref, w_out_ref,
    x0, x1, x2, x3,
    gq, gk, gv, gkf, gvf, ga_ref, turned,
):
    seq = lax.axis_index("seq")
    mixed = (hidden_ref[...].astype(F32) + nn(att_ref[...], w_out_ref[...])).astype(BF)
    flag = flag_ref[:, 0:1] > 0.5
    error = jnp.where(flag, nt(mixed, w_in_ref[...]) - tiles_ref[...].astype(F32), 0.0)
    loss = jnp.sum(jnp.sum(error * error, axis=1, keepdims=True), axis=0, keepdims=True) * inv_count
    tail = split_rows(jnp.broadcast_to(loss, (16, 128)), (16, 128), 0).astype(BF)
    grad_pred = (2.0 * inv_count * error).astype(BF)
    grad_mixed = nn(grad_pred, w_in_ref[...]).astype(BF)
    ga_ref[...] = nt(grad_mixed, w_out_ref[...]).astype(BF)

    own_class = iota((1, TOK), 1) >> 5
    for ref in (gq, gk, gv, gkf, gvf):
        ref[...] = jnp.zeros_like(ref)
    for g in range(GROUPS):
        lo = window(g)
        win = slice(lo, lo + 256)
        masks, picked = head_masks(g)
        q = proj_ref[:, lo : lo + 256]
        k = proj_ref[:, D + lo : D + lo + 256]
        v = proj_ref[:, 2 * D + lo : 2 * D + lo + 256]
        ga = ga_ref[:, win]
        fk = fk_ref[:, win]
        fv = fv_ref[:, win]
        ga_stack = jnp.concatenate([keep(m, ga) for m in masks], 0)
        ga_picked = keep(picked, ga)
        near = nt(v, ga_stack)
        far = nt(fv, ga_picked)
        probs = [pnear_ref[g, :, TOK * r : TOK * (r + 1)] for r in range(RATE)]
        far_probs = pfar_ref[g]
        far_dot = jnp.sum(far_probs * far, axis=0, keepdims=True)
        grads = [near[:, TOK * r : TOK * (r + 1)] for r in range(RATE)]
        dots = []
        for r in range(RATE):
            own = jnp.sum(probs[r] * grads[r], axis=0, keepdims=True)
            dots.append(jnp.where(own_class == r, own + far_dot, own))
        scores = [(probs[r] * (grads[r] - dots[r]) * SCALE).astype(BF) for r in range(RATE)]
        far_scores = (far_probs * (far - by_class(own_class, dots)) * SCALE).astype(BF)
        gq[:, win] += tn(
            jnp.concatenate(scores, 0), jnp.concatenate([keep(m, k) for m in masks], 0)
        ) + keep(picked, tn(far_scores, fk))
        gk[:, win] += nn(
            jnp.concatenate(scores, 1), jnp.concatenate([keep(m, q) for m in masks], 0)
        )
        gv[:, win] += nn(jnp.concatenate([p.astype(BF) for p in probs], 1), ga_stack)
        gkf[:, win] += nn(far_scores, keep(picked, q))
        gvf[:, win] += nn(far_probs.astype(BF), ga_picked)
    place = spread_ref[...]
    section = 0
    for value in (gq, gk, gv, gkf, gvf, grad_mixed):
        for half in range(2):
            piece = value[:, half * HALF : (half + 1) * HALF].astype(BF)
            turned[section] = nt(place, piece).astype(BF)
            section += 1
    for turn, ref in enumerate((x0, x1, x2, x3)):
        first = pl.multiple_of(((seq + turn) & 3) * SUB, 16)
        for section in range(SECTIONS):
            ref[section * SUB : (section + 1) * SUB] = turned[section, pl.ds(first, SUB)]
        ref[SECTIONS * SUB :] = tail


def product_kernel(
    x0, x1, x2, x3, pn_ref, a0, a1, a2, a3, order_ref, mine_ref, other_ref, got, left, att, res
):
    seq = lax.axis_index("seq")
    core = lax.axis_index("slide") & 1
    for turn, (ref, x_ref) in enumerate(zip((a0, a1, a2, a3), (x0, x1, x2, x3))):
        src = (seq - turn) & 3
        att[pl.ds(pl.multiple_of(src * TOK, TOK), TOK)] = ref[...]
        got[src] = x_ref[...]
    for src in range(N_SEQ):
        left[0 : 2 * SUB, src * TOK : (src + 1) * TOK] = got[src, 0 : 2 * SUB]
        left[6 * SUB : 8 * SUB, src * TOK : (src + 1) * TOK] = got[src, 10 * SUB : 12 * SUB]
    shape = (SUB, TOK)
    row = iota(shape, 0)
    lane_class = iota(shape, 1) >> 5
    core_row = jnp.where(row >= 48, 1, 0)
    row_y = (row - 48 * core_row) // 12
    row_class = ((row_y & 1) << 1) + core_row
    spots = [(row_class == r) & (lane_class == r) for r in range(RATE)]
    for part in range(2):
        for half in range(2):
            near_at = (2 + 2 * part + half) * SUB
            far_at = (6 + 2 * part + half) * SUB
            far = got[0, far_at : far_at + SUB].astype(F32)
            for src in range(1, N_SEQ):
                far = far + got[src, far_at : far_at + SUB].astype(F32)
            turns = [far] + [pltpu.roll(far, FAR * t, 1) for t in range(1, RATE)]
            for src in range(N_SEQ):
                total = got[src, near_at : near_at + SUB].astype(F32)
                for r in range(RATE):
                    total = total + jnp.where(spots[r], turns[(r - src) & 3], 0.0)
                left[near_at : near_at + SUB, src * TOK : (src + 1) * TOK] = total.astype(BF)
    right = pn_ref[...].reshape(N_SEQ * TOK, D)
    res[0 : 6 * SUB] = nn(left[0 : 6 * SUB], right).astype(BF)
    res[6 * SUB :] = nn(left[6 * SUB :], att[...]).astype(BF)
    loss = got[0, SECTIONS * SUB :].astype(F32)
    for src in range(1, N_SEQ):
        loss = loss + got[src, SECTIONS * SUB :].astype(F32)
    loss = jnp.sum(loss, axis=0, keepdims=True)[:, 0:1]
    tail = split_rows(jnp.broadcast_to(loss, (16, D)), (16, D), 0).astype(BF)
    whole = res[...]
    for turn, ref in enumerate((mine_ref, other_ref)):
        first = pl.multiple_of(((core + turn) & 1) * HALF, HALF)
        ref[0:HALF] = nn(order_ref[pl.ds(first, HALF)], whole).astype(BF)
        ref[HALF:] = tail


def core_kernel(mine_ref, other_ref, y0, y1, y2, y3):
    y = (lax.axis_index("slide") >> 1) & 3
    loss = jnp.sum(mine_ref[HALF:].astype(F32) + other_ref[HALF:].astype(F32), axis=0, keepdims=True)
    tail = split_rows(jnp.broadcast_to(loss, (16, D)), (16, D), 0).astype(BF)
    for turn, ref in enumerate((y0, y1, y2, y3)):
        rows = pl.ds(pl.multiple_of(((y + turn) & 3) * SUB, 16), SUB)
        ref[0:SUB] = (mine_ref[rows].astype(F32) + other_ref[rows].astype(F32)).astype(BF)
        ref[SUB:] = tail


def y_kernel(y0, y1, y2, y3, order_ref, out_ref):
    total = y0[...].astype(F32) + y1[...].astype(F32) + y2[...].astype(F32) + y3[...].astype(F32)
    loss = jnp.sum(total[SUB:], axis=0, keepdims=True)
    rows = split_rows(jnp.broadcast_to(loss, (16, D)), (16, D), 0)
    total = jnp.concatenate([total[:SUB], rows], 0).astype(BF)
    out_ref[...] = nn(order_ref[...], total).astype(BF).reshape(NZ, 16, D)


def z_kernel(in_ref, out_ref, loss_ref):
    total = in_ref[0].astype(F32)
    for src in range(1, NZ):
        total = total + in_ref[src].astype(F32)
    out_ref[...] = total[0:12]
    loss_ref[...] = jnp.sum(total[12:15, 0:1], axis=0, keepdims=True)


def spread_order():
    place = np.zeros((HALF, HALF), np.float32)
    for row in range(HALF):
        j, rest = divmod(row, SUB)
        c, rest = divmod(rest, 48)
        y, r = divmod(rest, 12)
        place[row, (y * NC + c) * HD + j * 12 + r] = 1.0
    return jnp.asarray(place, BF)


def product_order():
    place = np.zeros((D, D), np.float32)
    for row in range(D):
        c, rest = divmod(row, HALF)
        y, rest = divmod(rest, SUB)
        z, r = divmod(rest, 12)
        place[row, z * SUB + c * 48 + y * 12 + r] = 1.0
    return jnp.asarray(place, BF)


def pad_order():
    place = np.zeros((NZ * 16, SUB + 16), np.float32)
    for z in range(NZ):
        for r in range(12):
            place[z * 16 + r, z * 12 + r] = 1.0
        for r in range(3):
            place[z * 16 + 12 + r, SUB + r] = 1.0
    return jnp.asarray(place, BF)


SMEM = pl.BlockSpec(memory_space=pltpu.SMEM)
VMEM = pl.BlockSpec(memory_space=pltpu.VMEM)
HBM = pl.BlockSpec(memory_space=pltpu.HBM)


def call(kernel, out_shapes, args, scratch=(), micros=1.0, specs=None):
    if specs is None:
        specs = [SMEM if a.dtype == jnp.int32 else VMEM for a in args]
    return pl.pallas_call(
        kernel,
        out_shape=out_shapes,
        in_specs=specs,
        out_specs=[VMEM] * len(out_shapes),
        scratch_shapes=list(scratch),
        compiler_params=pltpu.CompilerParams(vmem_limit_bytes=24 * 1024 * 1024),
        cost_estimate=pl.CostEstimate(
            flops=int(micros * 1.0e9), bytes_accessed=int(micros * 1.0e6), transcendentals=0
        ),
    )(*args)


def shape(*dims, dtype=BF):
    return jax.ShapeDtypeStruct(dims, dtype)


def slide_at(z, y, c):
    return (z * NY + y) * NC + c


CORE_PAIRS = [(i, i ^ 1) for i in range(NZ * NY * NC)]
Z_GROUPS = [[slide_at(z, y, c) for z in range(NZ)] for y in range(NY) for c in range(NC)]
SEQ_TURNS = [[(k, (k + t) % N_SEQ) for k in range(N_SEQ)] for t in range(N_SEQ)]
Y_TURNS = [
    [
        (slide_at(z, y, c), slide_at(z, (y + t) % NY, c))
        for z in range(NZ)
        for y in range(NY)
        for c in range(NC)
    ]
    for t in range(NY)
]


def swap(arrays, axis, turns):
    return [arrays[0]] + [lax.ppermute(arrays[t], axis, turns[t]) for t in range(1, len(arrays))]


def per_device(embeddings, tile_counts, masked_tiles, w_in, norm_gain, w_qkv, w_out):
    inv_count = 1.0 / (lax.axis_size("slide") * masked_tiles.shape[1])
    tiles, hidden, normed, flag = call(
        prep_kernel,
        [shape(TOK, 2 * D), shape(TOK, D), shape(TOK, D), shape(TOK, TOK, dtype=F32)],
        (embeddings, masked_tiles, norm_gain, w_in),
        [
            pltpu.VMEM((TOK, 2 * D), BF),
            pltpu.VMEM((1, TOK), jnp.int32),
            pltpu.VMEM((D,), F32),
            pltpu.VMEM((2 * D, D), BF),
            pltpu.SemaphoreType.DMA((3 + 2 * D // 256,)),
        ],
        2.0,
        [HBM] * 4,
    )
    norms = swap([normed] * N_SEQ, "seq", SEQ_TURNS)
    scores = shape(GROUPS, TOK, RATE * TOK, dtype=F32)
    rows = shape(HEADS, TOK, dtype=F32)
    projected, exps, tops, sums = call(
        near_kernel, [shape(TOK, 3 * D), scores, rows, rows], (tile_counts, normed, w_qkv), (), 5.0
    )
    pn, fk, fv, pnear, pfar, attended = call(
        far_kernel,
        [
            shape(N_SEQ, TOK, D),
            shape(TOK, D),
            shape(TOK, D),
            scores,
            shape(GROUPS, TOK, TOK, dtype=F32),
            shape(TOK, D),
        ],
        (tile_counts, *norms, projected, exps, tops, sums, w_qkv),
        [pltpu.VMEM((TOK, D), F32)],
        4.0,
    )
    atts = swap([attended] * N_SEQ, "seq", SEQ_TURNS)
    sent = call(
        functools.partial(backward_kernel, inv_count),
        [shape(XROWS, TOK)] * N_SEQ,
        (projected, fk, fv, pnear, pfar, attended, hidden, tiles, flag, spread_order(), w_in, w_out),
        [pltpu.VMEM((TOK, D), F32)] * 5
        + [pltpu.VMEM((TOK, D), BF), pltpu.VMEM((SECTIONS, HALF, TOK), BF)],
        8.0,
    )
    got = swap(sent, "seq", SEQ_TURNS)
    mine, other = call(
        product_kernel,
        [shape(HALF + 16, D)] * 2,
        (*got, pn, *atts, product_order()),
        [
            pltpu.VMEM((N_SEQ, XROWS, TOK), BF),
            pltpu.VMEM((D, N_SEQ * TOK), BF),
            pltpu.VMEM((N_SEQ * TOK, D), BF),
            pltpu.VMEM((D, D), BF),
        ],
        3.0,
    )
    other = lax.ppermute(other, "slide", CORE_PAIRS)
    by_y = call(core_kernel, [shape(SUB + 16, D)] * NY, (mine, other))
    by_y = swap(by_y, "slide", Y_TURNS)
    (by_z,) = call(y_kernel, [shape(NZ, 16, D)], (*by_y, pad_order()))
    by_z = lax.all_to_all(by_z, "slide", 0, 0, tiled=True, axis_index_groups=Z_GROUPS)
    gradients, loss = call(z_kernel, [shape(12, D, dtype=F32), shape(1, 1, dtype=F32)], (by_z,))
    return (gradients, loss[0, 0])


def solution(mesh):
    in_specs = (P("slide", "seq", None), P("slide"), P("slide", None), P(), P(), P(), P())
    out_specs = (P(("slide", "seq"), None), P())
    return jax.shard_map(
        per_device, mesh=mesh, in_specs=in_specs, out_specs=out_specs, check_vma=False
    )
```

```python
import functools
import math

import numpy as np
import jax
import jax.numpy as jnp
from jax import lax
from jax.experimental import pallas as pl
from jax.experimental.pallas import tpu as pltpu
from jax.sharding import PartitionSpec as P

HEADS = 16
RATE = 4
HD = 48
D = 768
TOK = 128
N_SEQ = 4
GROUPS = HEADS // RATE
FAR = TOK // RATE
NORM_EPS = 1e-06
NEG_FILL = -1e30
SCALE = 1.0 / math.sqrt(HD)
BF = jnp.bfloat16
F32 = jnp.float32
HALF = 384
SUB = 96
SECTIONS = 10
YROWS = 80
XROWS = SECTIONS * SUB + 16
NZ, NY, NC = 8, 4, 2


def dot(a, b, dims):
    return lax.dot_general(a, b, (dims, ((), ())), preferred_element_type=F32)


def nn(a, b):
    return dot(a, b, ((1,), (0,)))


def nt(a, b):
    return dot(a, b, ((1,), (1,)))


def tn(a, b):
    return dot(a, b, ((0,), (0,)))


def iota(shape, dim):
    return lax.broadcasted_iota(jnp.int32, shape, dim)


def class_major(index):
    return (index & (FAR - 1)) * RATE + (index >> 5)


def split_rows(value, shape, first):
    high = value.astype(BF).astype(F32)
    rest = value - high
    mid = rest.astype(BF).astype(F32)
    low = rest - mid
    row = iota(shape, 0)
    return jnp.where(
        row == first,
        high,
        jnp.where(row == first + 1, mid, jnp.where(row == first + 2, low, 0.0)),
    )


def prep_kernel(
    tiles_hbm, masked_hbm, gain_hbm, w_in_hbm, tiles_out, hidden_out, normed_out, flag_out,
    raw, masked, gain, w_in, sems,
):
    blocks = w_in_hbm.shape[0] // 256
    loads = [
        pltpu.make_async_copy(tiles_hbm.at[0], raw, sems.at[0]),
        pltpu.make_async_copy(masked_hbm, masked, sems.at[1]),
        pltpu.make_async_copy(gain_hbm, gain, sems.at[2]),
    ]
    chunks = [
        pltpu.make_async_copy(
            w_in_hbm.at[256 * i : 256 * (i + 1)], w_in.at[256 * i : 256 * (i + 1)], sems.at[3 + i]
        )
        for i in range(blocks)
    ]
    for copy in loads + chunks:
        copy.start()
    pos0 = lax.axis_index("seq") * TOK
    shape = (TOK, TOK)
    order = (iota(shape, 1) == class_major(iota(shape, 0))).astype(F32).astype(BF)
    loads[1].wait()
    positions = pos0 + class_major(iota(shape, 0))
    hits = jnp.where(positions == masked[...], 1.0, 0.0)
    hit = jnp.max(hits, axis=1, keepdims=True)
    flag_out[...] = jnp.broadcast_to(hit, shape)
    flag = hit > 0.5
    loads[0].wait()
    hidden = jnp.zeros((TOK, D), F32)
    for i in range(blocks):
        cols = slice(256 * i, 256 * (i + 1))
        tiles = nn(order, raw[:, cols])
        tiles_out[:, cols] = tiles.astype(BF)
        chunks[i].wait()
        hidden += nn(jnp.where(flag, 0.0, tiles).astype(BF), w_in[cols])
    hidden = hidden.astype(BF)
    hidden_out[...] = hidden
    hidden_f = hidden.astype(F32)
    scale_rows = lax.rsqrt(jnp.mean(hidden_f * hidden_f, axis=1, keepdims=True) + NORM_EPS)
    loads[2].wait()
    normed_out[...] = (hidden_f * scale_rows * gain[...].reshape(1, D)).astype(BF)


def window(group):
    return (group * RATE * HD) // 128 * 128


def head_masks(group):
    lane = iota((TOK, 256), 1) + window(group)
    row_class = iota((TOK, 256), 0) >> 5
    masks = []
    for r in range(RATE):
        first = (group * RATE + r) * HD
        masks.append((lane >= first) & (lane < first + HD))
    picked = masks[0] & (row_class == 0)
    for r in range(1, RATE):
        picked = picked | (masks[r] & (row_class == r))
    return masks, picked


def keep(mask, value):
    return jnp.where(mask, value, jnp.zeros((), value.dtype))


def by_class(own_class, pieces):
    out = pieces[0]
    for r in range(1, RATE):
        out = jnp.where(own_class == r, pieces[r], out)
    return out


def near_kernel(count_ref, normed_ref, w_qkv_ref, proj_ref, exp_ref, top_ref, sum_ref):
    count = count_ref[0]
    pos0 = lax.axis_index("seq") * TOK
    normed = normed_ref[...]
    for block in range(3 * D // 256):
        cols = slice(block * 256, (block + 1) * 256)
        proj_ref[:, cols] = nn(normed, w_qkv_ref[:, cols]).astype(BF)
    square = (TOK, TOK)
    key_pos = pos0 + class_major(iota(square, 0))
    query_pos = pos0 + class_major(iota(square, 1))
    near_ok = (key_pos < count) | (key_pos == query_pos)
    for g in range(GROUPS):
        lo = window(g)
        masks, _ = head_masks(g)
        q = proj_ref[:, lo : lo + 256]
        k = proj_ref[:, D + lo : D + lo + 256]
        near = nt(k, jnp.concatenate([keep(m, q) for m in masks], 0))
        for r in range(RATE):
            head = g * RATE + r
            scores = jnp.where(near_ok, near[:, TOK * r : TOK * (r + 1)] * SCALE, NEG_FILL)
            top = jnp.max(scores, axis=0, keepdims=True)
            exps = jnp.exp(scores - top)
            exp_ref[g, :, TOK * r : TOK * (r + 1)] = exps
            top_ref[head : head + 1] = top
            sum_ref[head : head + 1] = jnp.sum(exps, axis=0, keepdims=True)


def far_kernel(
    count_ref, n0, n1, n2, n3, proj_ref, exp_ref, top_ref, sum_ref, w_qkv_ref,
    pn_ref, fk_ref, fv_ref, pnear_ref, pfar_ref, att_ref,
    att_acc,
):
    count = count_ref[0]
    seq = lax.axis_index("seq")
    for turn, ref in enumerate((n0, n1, n2, n3)):
        pn_ref[(seq - turn) & 3] = ref[...]
    pn_all = pn_ref[...].reshape(N_SEQ * TOK, D)
    for part, far_ref in enumerate((fk_ref, fv_ref)):
        for block in range(D // 256):
            first = (1 + part) * D + block * 256
            every = nn(pn_all, w_qkv_ref[:, first : first + 256])
            lane_class = ((iota((FAR, 256), 1) + block * 256) // HD) & 3
            for src in range(N_SEQ):
                base = src * TOK
                pieces = [every[base + FAR * r : base + FAR * (r + 1)] for r in range(RATE)]
                far_ref[src * FAR : (src + 1) * FAR, block * 256 : (block + 1) * 256] = by_class(
                    lane_class, pieces
                ).astype(BF)

    square = (TOK, TOK)
    far_row = iota(square, 0)
    far_ok = (far_row >> 5) * TOK + (far_row & (FAR - 1)) * RATE + (iota(square, 1) >> 5) < count
    own_class = iota((1, TOK), 1) >> 5

    att_acc[...] = jnp.zeros_like(att_acc)
    for g in range(GROUPS):
        lo = window(g)
        win = slice(lo, lo + 256)
        masks, picked = head_masks(g)
        q = proj_ref[:, lo : lo + 256]
        v = proj_ref[:, 2 * D + lo : 2 * D + lo + 256]
        far = jnp.where(far_ok, nt(fk_ref[:, win], keep(picked, q)) * SCALE, NEG_FILL)
        heads = range(g * RATE, (g + 1) * RATE)
        near_tops = [top_ref[h : h + 1] for h in heads]
        near_sums = [sum_ref[h : h + 1] for h in heads]
        top = jnp.maximum(jnp.max(far, axis=0, keepdims=True), by_class(own_class, near_tops))
        shrink = jnp.exp(by_class(own_class, near_tops) - top)
        far_exp = jnp.exp(far - top)
        total = by_class(own_class, near_sums) * shrink + jnp.sum(far_exp, axis=0, keepdims=True)
        far_probs = far_exp / total
        probs = []
        for r in range(RATE):
            factor = jnp.where(own_class == r, shrink / total, 1.0 / near_sums[r])
            probs.append(exp_ref[g, :, TOK * r : TOK * (r + 1)] * factor)
            pnear_ref[g, :, TOK * r : TOK * (r + 1)] = probs[r]
        pfar_ref[g] = far_probs
        att = tn(
            jnp.concatenate([p.astype(BF) for p in probs], 0),
            jnp.concatenate([keep(m, v) for m in masks], 0),
        )
        att_acc[:, win] += att + keep(picked, tn(far_probs.astype(BF), fv_ref[:, win]))
    att_ref[...] = att_acc[...].astype(BF)


def chain_kernel(
    inv_count,
    att_ref, hidden_ref, tiles_ref, flag_ref, w_in_ref, w_out_ref, order_ref,
    ga_ref, loss_ref, mine_ref, other_ref,
):
    core = lax.axis_index("slide") & 1
    attended = att_ref[...]
    mixed = (hidden_ref[...].astype(F32) + nn(attended, w_out_ref[...])).astype(BF)
    flag = flag_ref[:, 0:1] > 0.5
    error = jnp.where(flag, nt(mixed, w_in_ref[...]) - tiles_ref[...].astype(F32), 0.0)
    loss = jnp.sum(jnp.sum(error * error, axis=1, keepdims=True), axis=0, keepdims=True) * inv_count
    loss_ref[...] = split_rows(jnp.broadcast_to(loss, (16, 128)), (16, 128), 0).astype(BF)
    grad_pred = (2.0 * inv_count * error).astype(BF)
    grad_mixed = nn(grad_pred, w_in_ref[...]).astype(BF)
    ga_ref[...] = nt(grad_mixed, w_out_ref[...]).astype(BF)
    for turn, ref in enumerate((mine_ref, other_ref)):
        first = pl.multiple_of(((core + turn) & 1) * HALF, HALF)
        left = nt(order_ref[pl.ds(first, HALF)], grad_mixed).astype(BF)
        ref[...] = nn(left, attended).astype(BF)


def backward_kernel(
    proj_ref, fk_ref, fv_ref, pnear_ref, pfar_ref, ga_ref, loss_ref, spread_ref,
    x0, x1, x2, x3,
    gq, gk, gv, gkf, gvf, turned,
):
    seq = lax.axis_index("seq")
    own_class = iota((1, TOK), 1) >> 5
    for ref in (gq, gk, gv, gkf, gvf):
        ref[...] = jnp.zeros_like(ref)
    for g in range(GROUPS):
        lo = window(g)
        win = slice(lo, lo + 256)
        masks, picked = head_masks(g)
        q = proj_ref[:, lo : lo + 256]
        k = proj_ref[:, D + lo : D + lo + 256]
        v = proj_ref[:, 2 * D + lo : 2 * D + lo + 256]
        ga = ga_ref[:, win]
        fk = fk_ref[:, win]
        fv = fv_ref[:, win]
        ga_stack = jnp.concatenate([keep(m, ga) for m in masks], 0)
        ga_picked = keep(picked, ga)
        near = nt(v, ga_stack)
        far = nt(fv, ga_picked)
        probs = [pnear_ref[g, :, TOK * r : TOK * (r + 1)] for r in range(RATE)]
        far_probs = pfar_ref[g]
        far_dot = jnp.sum(far_probs * far, axis=0, keepdims=True)
        grads = [near[:, TOK * r : TOK * (r + 1)] for r in range(RATE)]
        dots = []
        for r in range(RATE):
            own = jnp.sum(probs[r] * grads[r], axis=0, keepdims=True)
            dots.append(jnp.where(own_class == r, own + far_dot, own))
        scores = [(probs[r] * (grads[r] - dots[r]) * SCALE).astype(BF) for r in range(RATE)]
        far_scores = (far_probs * (far - by_class(own_class, dots)) * SCALE).astype(BF)
        gq[:, win] += tn(
            jnp.concatenate(scores, 0), jnp.concatenate([keep(m, k) for m in masks], 0)
        ) + keep(picked, tn(far_scores, fk))
        gk[:, win] += nn(
            jnp.concatenate(scores, 1), jnp.concatenate([keep(m, q) for m in masks], 0)
        )
        gv[:, win] += nn(jnp.concatenate([p.astype(BF) for p in probs], 1), ga_stack)
        gkf[:, win] += nn(far_scores, keep(picked, q))
        gvf[:, win] += nn(far_probs.astype(BF), ga_picked)
    place = spread_ref[...]
    section = 0
    for value in (gq, gk, gv, gkf, gvf):
        for half in range(2):
            piece = value[:, half * HALF : (half + 1) * HALF].astype(BF)
            turned[section] = nt(place, piece).astype(BF)
            section += 1
    for turn, ref in enumerate((x0, x1, x2, x3)):
        first = pl.multiple_of(((seq + turn) & 3) * SUB, 16)
        for section in range(SECTIONS):
            ref[section * SUB : (section + 1) * SUB] = turned[section, pl.ds(first, SUB)]
        ref[SECTIONS * SUB :] = loss_ref[...]


def product_kernel(x0, x1, x2, x3, pn_ref, order_ref, mine_ref, other_ref, got, left):
    seq = lax.axis_index("seq")
    core = lax.axis_index("slide") & 1
    for turn, x_ref in enumerate((x0, x1, x2, x3)):
        got[(seq - turn) & 3] = x_ref[...]
    for src in range(N_SEQ):
        left[0 : 2 * SUB, src * TOK : (src + 1) * TOK] = got[src, 0 : 2 * SUB]
    shape = (SUB, TOK)
    row = iota(shape, 0)
    lane_class = iota(shape, 1) >> 5
    core_row = jnp.where(row >= 48, 1, 0)
    row_y = (row - 48 * core_row) // 12
    row_class = ((row_y & 1) << 1) + core_row
    spots = [(row_class == r) & (lane_class == r) for r in range(RATE)]
    for part in range(2):
        for half in range(2):
            near_at = (2 + 2 * part + half) * SUB
            far_at = (6 + 2 * part + half) * SUB
            far = got[0, far_at : far_at + SUB].astype(F32)
            for src in range(1, N_SEQ):
                far = far + got[src, far_at : far_at + SUB].astype(F32)
            turns = [far] + [pltpu.roll(far, FAR * t, 1) for t in range(1, RATE)]
            for src in range(N_SEQ):
                total = got[src, near_at : near_at + SUB].astype(F32)
                for r in range(RATE):
                    total = total + jnp.where(spots[r], turns[(r - src) & 3], 0.0)
                left[near_at : near_at + SUB, src * TOK : (src + 1) * TOK] = total.astype(BF)
    whole = nn(left[...], pn_ref[...].reshape(N_SEQ * TOK, D)).astype(BF)
    loss = got[0, SECTIONS * SUB :].astype(F32)
    for src in range(1, N_SEQ):
        loss = loss + got[src, SECTIONS * SUB :].astype(F32)
    loss = jnp.sum(loss, axis=0, keepdims=True)[:, 0:1]
    tail = split_rows(jnp.broadcast_to(loss, (YROWS, D)), (YROWS, D), 72)
    for turn, ref in enumerate((mine_ref, other_ref)):
        first = pl.multiple_of(((core + turn) & 1) * NY * YROWS, NY * YROWS)
        half = nn(order_ref[pl.ds(first, NY * YROWS)], whole)
        for y in range(NY):
            rows = slice(y * YROWS, (y + 1) * YROWS)
            ref[rows] = (half[rows] + tail).astype(BF)


def resplit(total):
    row = iota(total.shape, 0)
    loss = jnp.sum(jnp.where(row >= 72, total, 0.0), axis=0, keepdims=True)
    pieces = split_rows(jnp.broadcast_to(loss, total.shape), total.shape, 72)
    return jnp.where(row >= 72, pieces, total), loss


def core_kernel(mine_ref, other_ref, y0, y1, y2, y3):
    y = (lax.axis_index("slide") >> 1) & 3
    for turn, ref in enumerate((y0, y1, y2, y3)):
        rows = pl.ds(pl.multiple_of(((y + turn) & 3) * YROWS, 16), YROWS)
        ref[...] = resplit(mine_ref[rows].astype(F32) + other_ref[rows].astype(F32))[0].astype(BF)


def y_kernel(y0, y1, y2, y3, o0, o1, o2, o3, order_ref, out_ref):
    total = y0[...].astype(F32) + y1[...].astype(F32) + y2[...].astype(F32) + y3[...].astype(F32)
    total, loss = resplit(total)
    out_ref[0:6] = nn(order_ref[...], total.astype(BF)).astype(BF).reshape(6, 16, D)
    out = o0[...].astype(F32) + o1[...].astype(F32) + o2[...].astype(F32) + o3[...].astype(F32)
    tail = split_rows(jnp.broadcast_to(loss, (16, D)), (16, D), 12)
    for half in range(2):
        out_ref[6 + half] = (out[16 * half : 16 * (half + 1)] + tail).astype(BF)


def out_core_kernel(mine_ref, other_ref, y0, y1, y2, y3):
    y = (lax.axis_index("slide") >> 1) & 3
    for turn, ref in enumerate((y0, y1, y2, y3)):
        rows = pl.ds(pl.multiple_of(((y + turn) & 3) * SUB, 16), SUB)
        ref[...] = (mine_ref[rows].astype(F32) + other_ref[rows].astype(F32)).astype(BF)


def out_y_kernel(y0, y1, y2, y3, order_ref, x0, x1, x2, x3):
    seq = lax.axis_index("seq")
    total = y0[...].astype(F32) + y1[...].astype(F32) + y2[...].astype(F32) + y3[...].astype(F32)
    total = total.astype(BF)
    for turn, ref in enumerate((x0, x1, x2, x3)):
        rows = pl.ds(pl.multiple_of(((seq + turn) & 3) * 32, 32), 32)
        ref[...] = nn(order_ref[rows], total).astype(BF)


def z_kernel(in_ref, out_ref, loss_ref):
    total = in_ref[0].astype(F32)
    for src in range(1, NZ):
        total = total + in_ref[src].astype(F32)
    out_ref[...] = total[0:12]
    loss_ref[...] = jnp.sum(total[12:15, 0:1], axis=0, keepdims=True)


def spread_order():
    place = np.zeros((HALF, HALF), np.float32)
    for row in range(HALF):
        j, rest = divmod(row, SUB)
        c, rest = divmod(rest, 48)
        y, r = divmod(rest, 12)
        place[row, (y * NC + c) * HD + j * 12 + r] = 1.0
    return jnp.asarray(place, BF)


def product_order():
    place = np.zeros((NC * NY * YROWS, 6 * SUB), np.float32)
    for c in range(NC):
        for y in range(NY):
            for z in range(6):
                for r in range(12):
                    place[(c * NY + y) * YROWS + z * 12 + r, z * SUB + c * 48 + y * 12 + r] = 1.0
    return jnp.asarray(place, BF)


def out_order():
    place = np.zeros((D, D), np.float32)
    row = 0
    for c in range(NC):
        for y in range(NY):
            for j in range(N_SEQ):
                for half in range(2):
                    for r in range(12):
                        place[row, (half * 8 + y * NC + c) * HD + j * 12 + r] = 1.0
                        row += 1
    return jnp.asarray(place, BF)


def out_pad_order():
    place = np.zeros((N_SEQ * 32, SUB), np.float32)
    for j in range(N_SEQ):
        for half in range(2):
            for r in range(12):
                place[j * 32 + half * 16 + r, j * 24 + half * 12 + r] = 1.0
    return jnp.asarray(place, BF)


def pad_order():
    place = np.zeros((SUB, YROWS), np.float32)
    for z in range(6):
        for r in range(12):
            place[z * 16 + r, z * 12 + r] = 1.0
        for r in range(3):
            place[z * 16 + 12 + r, 72 + r] = 1.0
    return jnp.asarray(place, BF)


SMEM = pl.BlockSpec(memory_space=pltpu.SMEM)
VMEM = pl.BlockSpec(memory_space=pltpu.VMEM)
HBM = pl.BlockSpec(memory_space=pltpu.HBM)


def call(kernel, out_shapes, args, scratch=(), micros=1.0, specs=None, grant=24):
    if specs is None:
        specs = [SMEM if a.dtype == jnp.int32 else VMEM for a in args]
    return pl.pallas_call(
        kernel,
        out_shape=out_shapes,
        in_specs=specs,
        out_specs=[VMEM] * len(out_shapes),
        scratch_shapes=list(scratch),
        compiler_params=pltpu.CompilerParams(vmem_limit_bytes=grant * 1024 * 1024),
        cost_estimate=pl.CostEstimate(
            flops=int(micros * 1.0e9), bytes_accessed=int(micros * 1.0e6), transcendentals=0
        ),
    )(*args)


def shape(*dims, dtype=BF):
    return jax.ShapeDtypeStruct(dims, dtype)


def slide_at(z, y, c):
    return (z * NY + y) * NC + c


CORE_PAIRS = [(i, i ^ 1) for i in range(NZ * NY * NC)]
Z_GROUPS = [[slide_at(z, y, c) for z in range(NZ)] for y in range(NY) for c in range(NC)]
SEQ_TURNS = [[(k, (k + t) % N_SEQ) for k in range(N_SEQ)] for t in range(N_SEQ)]
Y_TURNS = [
    [
        (slide_at(z, y, c), slide_at(z, (y + t) % NY, c))
        for z in range(NZ)
        for y in range(NY)
        for c in range(NC)
    ]
    for t in range(NY)
]


def swap(arrays, axis, turns):
    return [arrays[0]] + [lax.ppermute(arrays[t], axis, turns[t]) for t in range(1, len(arrays))]


def per_device(embeddings, tile_counts, masked_tiles, w_in, norm_gain, w_qkv, w_out):
    inv_count = 1.0 / (lax.axis_size("slide") * masked_tiles.shape[1])
    tiles, hidden, normed, flag = call(
        prep_kernel,
        [shape(TOK, 2 * D), shape(TOK, D), shape(TOK, D), shape(TOK, TOK, dtype=F32)],
        (embeddings, masked_tiles, norm_gain, w_in),
        [
            pltpu.VMEM((TOK, 2 * D), BF),
            pltpu.VMEM((1, TOK), jnp.int32),
            pltpu.VMEM((D,), F32),
            pltpu.VMEM((2 * D, D), BF),
            pltpu.SemaphoreType.DMA((3 + 2 * D // 256,)),
        ],
        2.0,
        [HBM] * 4,
        60,
    )
    norms = swap([normed] * N_SEQ, "seq", SEQ_TURNS)
    scores = shape(GROUPS, TOK, RATE * TOK, dtype=F32)
    rows = shape(HEADS, TOK, dtype=F32)
    projected, exps, tops, sums = call(
        near_kernel, [shape(TOK, 3 * D), scores, rows, rows], (tile_counts, normed, w_qkv), (), 5.0
    )
    pn, fk, fv, pnear, pfar, attended = call(
        far_kernel,
        [
            shape(N_SEQ, TOK, D),
            shape(TOK, D),
            shape(TOK, D),
            scores,
            shape(GROUPS, TOK, TOK, dtype=F32),
            shape(TOK, D),
        ],
        (tile_counts, *norms, projected, exps, tops, sums, w_qkv),
        [pltpu.VMEM((TOK, D), F32)],
        4.0,
    )
    grad_attended, loss, out_mine, out_other = call(
        functools.partial(chain_kernel, inv_count),
        [shape(TOK, D), shape(16, 128), shape(HALF, D), shape(HALF, D)],
        (attended, hidden, tiles, flag, w_in, w_out, out_order()),
        (),
        3.0,
    )
    out_other = lax.ppermute(out_other, "slide", CORE_PAIRS)
    sent = call(
        backward_kernel,
        [shape(XROWS, TOK)] * N_SEQ,
        (projected, fk, fv, pnear, pfar, grad_attended, loss, spread_order()),
        [pltpu.VMEM((TOK, D), F32)] * 5 + [pltpu.VMEM((SECTIONS, HALF, TOK), BF)],
        4.0,
    )
    got = swap(sent, "seq", SEQ_TURNS)
    out = call(out_core_kernel, [shape(SUB, D)] * NY, (out_mine, out_other))
    out = swap(out, "slide", Y_TURNS)
    out = call(out_y_kernel, [shape(32, D)] * N_SEQ, (*out, out_pad_order()))
    out = swap(out, "seq", SEQ_TURNS)
    mine, other = call(
        product_kernel,
        [shape(NY * YROWS, D)] * 2,
        (*got, pn, product_order()),
        [pltpu.VMEM((N_SEQ, XROWS, TOK), BF), pltpu.VMEM((6 * SUB, N_SEQ * TOK), BF)],
        3.0,
    )
    other = lax.ppermute(other, "slide", CORE_PAIRS)
    by_y = call(core_kernel, [shape(YROWS, D)] * NY, (mine, other))
    by_y = swap(by_y, "slide", Y_TURNS)
    (by_z,) = call(y_kernel, [shape(NZ, 16, D)], (*by_y, *out, pad_order()))
    by_z = lax.all_to_all(by_z, "slide", 0, 0, tiled=True, axis_index_groups=Z_GROUPS)
    gradients, loss = call(z_kernel, [shape(12, D, dtype=F32), shape(1, 1, dtype=F32)], (by_z,))
    return (gradients, loss[0, 0])


def solution(mesh):
    in_specs = (P("slide", "seq", None), P("slide"), P("slide", None), P(), P(), P(), P())
    out_specs = (P(("slide", "seq"), None), P())
    return jax.shard_map(
        per_device, mesh=mesh, in_specs=in_specs, out_specs=out_specs, check_vma=False
    )
```

```python
import functools
import math

import numpy as np
import jax
import jax.numpy as jnp
from jax import lax
from jax.experimental import pallas as pl
from jax.experimental.pallas import tpu as pltpu
from jax.sharding import PartitionSpec as P

HEADS = 16
RATE = 4
HD = 48
D = 768
TOK = 128
N_SEQ = 4
GROUPS = HEADS // RATE
FAR = TOK // RATE
NORM_EPS = 1e-06
NEG_FILL = -1e30
SCALE = 1.0 / math.sqrt(HD)
BF = jnp.bfloat16
F32 = jnp.float32
HALF = 384
SUB = 96
SECTIONS = 10
YROWS = 80
XROWS = SECTIONS * SUB + 16
NZ, NY, NC = 8, 4, 2


def dot(a, b, dims):
    return lax.dot_general(a, b, (dims, ((), ())), preferred_element_type=F32)


def nn(a, b):
    return dot(a, b, ((1,), (0,)))


def nt(a, b):
    return dot(a, b, ((1,), (1,)))


def tn(a, b):
    return dot(a, b, ((0,), (0,)))


def iota(shape, dim):
    return lax.broadcasted_iota(jnp.int32, shape, dim)


def class_major(index):
    return (index & (FAR - 1)) * RATE + (index >> 5)


def split_rows(value, shape, first):
    high = value.astype(BF).astype(F32)
    rest = value - high
    mid = rest.astype(BF).astype(F32)
    low = rest - mid
    row = iota(shape, 0)
    return jnp.where(
        row == first,
        high,
        jnp.where(row == first + 1, mid, jnp.where(row == first + 2, low, 0.0)),
    )


def class_order():
    shape = (TOK, TOK)
    return (iota(shape, 1) == class_major(iota(shape, 0))).astype(F32).astype(BF)


def masked_rows(positions, masked):
    hits = jnp.where(positions == masked, 1.0, 0.0)
    return jnp.broadcast_to(jnp.max(hits, axis=1, keepdims=True), (TOK, TOK))


def prep_kernel(
    tiles_hbm, masked_hbm, gain_hbm, w_in_hbm, hidden_out, normed_out, tiles, masked, gain, w_in, sems
):
    blocks = w_in_hbm.shape[0] // 256
    loads = [
        pltpu.make_async_copy(masked_hbm, masked, sems.at[0]),
        pltpu.make_async_copy(tiles_hbm.at[0], tiles, sems.at[1]),
        pltpu.make_async_copy(gain_hbm, gain, sems.at[2]),
    ]
    chunks = [
        pltpu.make_async_copy(
            w_in_hbm.at[256 * i : 256 * (i + 1)], w_in.at[256 * i : 256 * (i + 1)], sems.at[3 + i]
        )
        for i in range(blocks)
    ]
    for copy in loads + chunks:
        copy.start()
    order = class_order()
    positions = lax.axis_index("seq") * TOK + iota((TOK, TOK), 0)
    loads[0].wait()
    flag = masked_rows(positions, masked[...])[:, 0:1] > 0.5
    loads[1].wait()
    hidden = jnp.zeros((TOK, D), F32)
    for i in range(blocks):
        cols = slice(256 * i, 256 * (i + 1))
        inputs = jnp.where(flag, jnp.zeros((), BF), tiles[:, cols])
        chunks[i].wait()
        hidden += nn(inputs, w_in[cols])
    hidden_f = nn(order, hidden.astype(BF))
    hidden_out[...] = hidden_f.astype(BF)
    scale_rows = lax.rsqrt(jnp.mean(hidden_f * hidden_f, axis=1, keepdims=True) + NORM_EPS)
    loads[2].wait()
    normed_out[...] = (hidden_f * scale_rows * gain[...].reshape(1, D)).astype(BF)


def window(group):
    return (group * RATE * HD) // 128 * 128


def head_masks(group):
    lane = iota((TOK, 256), 1) + window(group)
    row_class = iota((TOK, 256), 0) >> 5
    masks = []
    for r in range(RATE):
        first = (group * RATE + r) * HD
        masks.append((lane >= first) & (lane < first + HD))
    picked = masks[0] & (row_class == 0)
    for r in range(1, RATE):
        picked = picked | (masks[r] & (row_class == r))
    return masks, picked


def keep(mask, value):
    return jnp.where(mask, value, jnp.zeros((), value.dtype))


def by_class(own_class, pieces):
    out = pieces[0]
    for r in range(1, RATE):
        out = jnp.where(own_class == r, pieces[r], out)
    return out


def near_kernel(
    count_ref, normed_ref, w_qkv_ref, tiles_ref, masked_ref,
    proj_ref, exp_ref, top_ref, sum_ref, tiles_out, flag_ref,
):
    count = count_ref[0]
    pos0 = lax.axis_index("seq") * TOK
    flag_ref[...] = masked_rows(pos0 + class_major(iota((TOK, TOK), 0)), masked_ref[...])
    tiles_out[...] = nn(class_order(), tiles_ref[0]).astype(BF)
    normed = normed_ref[...]
    for block in range(3 * D // 256):
        cols = slice(block * 256, (block + 1) * 256)
        proj_ref[:, cols] = nn(normed, w_qkv_ref[:, cols]).astype(BF)
    square = (TOK, TOK)
    key_pos = pos0 + class_major(iota(square, 0))
    query_pos = pos0 + class_major(iota(square, 1))
    near_ok = (key_pos < count) | (key_pos == query_pos)
    for g in range(GROUPS):
        lo = window(g)
        masks, _ = head_masks(g)
        q = proj_ref[:, lo : lo + 256]
        k = proj_ref[:, D + lo : D + lo + 256]
        near = nt(k, jnp.concatenate([keep(m, q) for m in masks], 0))
        for r in range(RATE):
            head = g * RATE + r
            scores = jnp.where(near_ok, near[:, TOK * r : TOK * (r + 1)] * SCALE, NEG_FILL)
            top = jnp.max(scores, axis=0, keepdims=True)
            exps = jnp.exp(scores - top)
            exp_ref[g, :, TOK * r : TOK * (r + 1)] = exps
            top_ref[head : head + 1] = top
            sum_ref[head : head + 1] = jnp.sum(exps, axis=0, keepdims=True)


def far_kernel(
    count_ref, n0, n1, n2, n3, proj_ref, exp_ref, top_ref, sum_ref, w_qkv_ref,
    pn_ref, fk_ref, fv_ref, pnear_ref, pfar_ref, att_ref,
    att_acc,
):
    count = count_ref[0]
    seq = lax.axis_index("seq")
    for turn, ref in enumerate((n0, n1, n2, n3)):
        pn_ref[(seq - turn) & 3] = ref[...]
    pn_all = pn_ref[...].reshape(N_SEQ * TOK, D)
    for part, far_ref in enumerate((fk_ref, fv_ref)):
        for block in range(D // 256):
            first = (1 + part) * D + block * 256
            every = nn(pn_all, w_qkv_ref[:, first : first + 256])
            lane_class = ((iota((FAR, 256), 1) + block * 256) // HD) & 3
            for src in range(N_SEQ):
                base = src * TOK
                pieces = [every[base + FAR * r : base + FAR * (r + 1)] for r in range(RATE)]
                far_ref[src * FAR : (src + 1) * FAR, block * 256 : (block + 1) * 256] = by_class(
                    lane_class, pieces
                ).astype(BF)

    square = (TOK, TOK)
    far_row = iota(square, 0)
    far_ok = (far_row >> 5) * TOK + (far_row & (FAR - 1)) * RATE + (iota(square, 1) >> 5) < count
    own_class = iota((1, TOK), 1) >> 5

    att_acc[...] = jnp.zeros_like(att_acc)
    for g in range(GROUPS):
        lo = window(g)
        win = slice(lo, lo + 256)
        masks, picked = head_masks(g)
        q = proj_ref[:, lo : lo + 256]
        v = proj_ref[:, 2 * D + lo : 2 * D + lo + 256]
        far = jnp.where(far_ok, nt(fk_ref[:, win], keep(picked, q)) * SCALE, NEG_FILL)
        heads = range(g * RATE, (g + 1) * RATE)
        near_tops = [top_ref[h : h + 1] for h in heads]
        near_sums = [sum_ref[h : h + 1] for h in heads]
        top = jnp.maximum(jnp.max(far, axis=0, keepdims=True), by_class(own_class, near_tops))
        shrink = jnp.exp(by_class(own_class, near_tops) - top)
        far_exp = jnp.exp(far - top)
        total = by_class(own_class, near_sums) * shrink + jnp.sum(far_exp, axis=0, keepdims=True)
        far_probs = far_exp / total
        probs = []
        for r in range(RATE):
            factor = jnp.where(own_class == r, shrink / total, 1.0 / near_sums[r])
            probs.append(exp_ref[g, :, TOK * r : TOK * (r + 1)] * factor)
            pnear_ref[g, :, TOK * r : TOK * (r + 1)] = probs[r]
        pfar_ref[g] = far_probs
        att = tn(
            jnp.concatenate([p.astype(BF) for p in probs], 0),
            jnp.concatenate([keep(m, v) for m in masks], 0),
        )
        att_acc[:, win] += att + keep(picked, tn(far_probs.astype(BF), fv_ref[:, win]))
    att_ref[...] = att_acc[...].astype(BF)


def chain_kernel(
    inv_count,
    att_ref, hidden_ref, tiles_ref, flag_ref, w_in_ref, w_out_ref, order_ref,
    ga_ref, loss_ref, mine_ref, other_ref,
):
    core = lax.axis_index("slide") & 1
    attended = att_ref[...]
    mixed = (hidden_ref[...].astype(F32) + nn(attended, w_out_ref[...])).astype(BF)
    flag = flag_ref[:, 0:1] > 0.5
    error = jnp.where(flag, nt(mixed, w_in_ref[...]) - tiles_ref[...].astype(F32), 0.0)
    loss = jnp.sum(jnp.sum(error * error, axis=1, keepdims=True), axis=0, keepdims=True) * inv_count
    loss_ref[...] = split_rows(jnp.broadcast_to(loss, (16, 128)), (16, 128), 0).astype(BF)
    grad_pred = (2.0 * inv_count * error).astype(BF)
    grad_mixed = nn(grad_pred, w_in_ref[...]).astype(BF)
    ga_ref[...] = nt(grad_mixed, w_out_ref[...]).astype(BF)
    for turn, ref in enumerate((mine_ref, other_ref)):
        first = pl.multiple_of(((core + turn) & 1) * HALF, HALF)
        left = nt(order_ref[pl.ds(first, HALF)], grad_mixed).astype(BF)
        ref[...] = nn(left, attended).astype(BF)


def backward_kernel(
    proj_ref, fk_ref, fv_ref, pnear_ref, pfar_ref, ga_ref, loss_ref, spread_ref,
    x0, x1, x2, x3,
    gq, gk, gv, gkf, gvf, turned,
):
    seq = lax.axis_index("seq")
    own_class = iota((1, TOK), 1) >> 5
    for ref in (gq, gk, gv, gkf, gvf):
        ref[...] = jnp.zeros_like(ref)
    for g in range(GROUPS):
        lo = window(g)
        win = slice(lo, lo + 256)
        masks, picked = head_masks(g)
        q = proj_ref[:, lo : lo + 256]
        k = proj_ref[:, D + lo : D + lo + 256]
        v = proj_ref[:, 2 * D + lo : 2 * D + lo + 256]
        ga = ga_ref[:, win]
        fk = fk_ref[:, win]
        fv = fv_ref[:, win]
        ga_stack = jnp.concatenate([keep(m, ga) for m in masks], 0)
        ga_picked = keep(picked, ga)
        near = nt(v, ga_stack)
        far = nt(fv, ga_picked)
        probs = [pnear_ref[g, :, TOK * r : TOK * (r + 1)] for r in range(RATE)]
        far_probs = pfar_ref[g]
        far_dot = jnp.sum(far_probs * far, axis=0, keepdims=True)
        grads = [near[:, TOK * r : TOK * (r + 1)] for r in range(RATE)]
        dots = []
        for r in range(RATE):
            own = jnp.sum(probs[r] * grads[r], axis=0, keepdims=True)
            dots.append(jnp.where(own_class == r, own + far_dot, own))
        scores = [(probs[r] * (grads[r] - dots[r]) * SCALE).astype(BF) for r in range(RATE)]
        far_scores = (far_probs * (far - by_class(own_class, dots)) * SCALE).astype(BF)
        gq[:, win] += tn(
            jnp.concatenate(scores, 0), jnp.concatenate([keep(m, k) for m in masks], 0)
        ) + keep(picked, tn(far_scores, fk))
        gk[:, win] += nn(
            jnp.concatenate(scores, 1), jnp.concatenate([keep(m, q) for m in masks], 0)
        )
        gv[:, win] += nn(jnp.concatenate([p.astype(BF) for p in probs], 1), ga_stack)
        gkf[:, win] += nn(far_scores, keep(picked, q))
        gvf[:, win] += nn(far_probs.astype(BF), ga_picked)
    place = spread_ref[...]
    section = 0
    for value in (gq, gk, gv, gkf, gvf):
        for half in range(2):
            piece = value[:, half * HALF : (half + 1) * HALF].astype(BF)
            turned[section] = nt(place, piece).astype(BF)
            section += 1
    for turn, ref in enumerate((x0, x1, x2, x3)):
        first = pl.multiple_of(((seq + turn) & 3) * SUB, 16)
        for section in range(SECTIONS):
            ref[section * SUB : (section + 1) * SUB] = turned[section, pl.ds(first, SUB)]
        ref[SECTIONS * SUB :] = loss_ref[...]


def product_kernel(x0, x1, x2, x3, pn_ref, order_ref, wait_ref, mine_ref, other_ref, got, left):
    seq = lax.axis_index("seq")
    core = lax.axis_index("slide") & 1
    for turn, x_ref in enumerate((x0, x1, x2, x3)):
        got[(seq - turn) & 3] = x_ref[...]
    for src in range(N_SEQ):
        left[0 : 2 * SUB, src * TOK : (src + 1) * TOK] = got[src, 0 : 2 * SUB]
    shape = (SUB, TOK)
    row = iota(shape, 0)
    lane_class = iota(shape, 1) >> 5
    core_row = jnp.where(row >= 48, 1, 0)
    row_y = (row - 48 * core_row) // 12
    row_class = ((row_y & 1) << 1) + core_row
    spots = [(row_class == r) & (lane_class == r) for r in range(RATE)]
    for part in range(2):
        for half in range(2):
            near_at = (2 + 2 * part + half) * SUB
            far_at = (6 + 2 * part + half) * SUB
            far = got[0, far_at : far_at + SUB].astype(F32)
            for src in range(1, N_SEQ):
                far = far + got[src, far_at : far_at + SUB].astype(F32)
            turns = [far] + [pltpu.roll(far, FAR * t, 1) for t in range(1, RATE)]
            for src in range(N_SEQ):
                total = got[src, near_at : near_at + SUB].astype(F32)
                for r in range(RATE):
                    total = total + jnp.where(spots[r], turns[(r - src) & 3], 0.0)
                left[near_at : near_at + SUB, src * TOK : (src + 1) * TOK] = total.astype(BF)
    whole = nn(left[...], pn_ref[...].reshape(N_SEQ * TOK, D)).astype(BF)
    loss = got[0, SECTIONS * SUB :].astype(F32)
    for src in range(1, N_SEQ):
        loss = loss + got[src, SECTIONS * SUB :].astype(F32)
    loss = jnp.sum(loss, axis=0, keepdims=True)[:, 0:1]
    tail = split_rows(jnp.broadcast_to(loss, (YROWS, D)), (YROWS, D), 72)
    for turn, ref in enumerate((mine_ref, other_ref)):
        first = pl.multiple_of(((core + turn) & 1) * NY * YROWS, NY * YROWS)
        half = nn(order_ref[pl.ds(first, NY * YROWS)], whole)
        for y in range(NY):
            rows = slice(y * YROWS, (y + 1) * YROWS)
            ref[rows] = (half[rows] + tail).astype(BF)


def resplit(total):
    row = iota(total.shape, 0)
    loss = jnp.sum(jnp.where(row >= 72, total, 0.0), axis=0, keepdims=True)
    pieces = split_rows(jnp.broadcast_to(loss, total.shape), total.shape, 72)
    return jnp.where(row >= 72, pieces, total), loss


def core_kernel(mine_ref, other_ref, wait1, wait2, wait3, y0, y1, y2, y3):
    y = (lax.axis_index("slide") >> 1) & 3
    for turn, ref in enumerate((y0, y1, y2, y3)):
        rows = pl.ds(pl.multiple_of(((y + turn) & 3) * YROWS, 16), YROWS)
        ref[...] = resplit(mine_ref[rows].astype(F32) + other_ref[rows].astype(F32))[0].astype(BF)


def y_kernel(y0, y1, y2, y3, o0, o1, o2, o3, order_ref, out_ref):
    total = y0[...].astype(F32) + y1[...].astype(F32) + y2[...].astype(F32) + y3[...].astype(F32)
    total, loss = resplit(total)
    out_ref[0:6] = nn(order_ref[...], total.astype(BF)).astype(BF).reshape(6, 16, D)
    out = o0[...].astype(F32) + o1[...].astype(F32) + o2[...].astype(F32) + o3[...].astype(F32)
    tail = split_rows(jnp.broadcast_to(loss, (16, D)), (16, D), 12)
    for half in range(2):
        out_ref[6 + half] = (out[16 * half : 16 * (half + 1)] + tail).astype(BF)


def out_core_kernel(mine_ref, other_ref, wait_ref, y0, y1, y2, y3):
    y = (lax.axis_index("slide") >> 1) & 3
    for turn, ref in enumerate((y0, y1, y2, y3)):
        rows = pl.ds(pl.multiple_of(((y + turn) & 3) * SUB, 16), SUB)
        ref[...] = (mine_ref[rows].astype(F32) + other_ref[rows].astype(F32)).astype(BF)


def out_y_kernel(y0, y1, y2, y3, order_ref, x0, x1, x2, x3):
    seq = lax.axis_index("seq")
    total = y0[...].astype(F32) + y1[...].astype(F32) + y2[...].astype(F32) + y3[...].astype(F32)
    total = total.astype(BF)
    for turn, ref in enumerate((x0, x1, x2, x3)):
        rows = pl.ds(pl.multiple_of(((seq + turn) & 3) * 32, 32), 32)
        ref[...] = nn(order_ref[rows], total).astype(BF)


def z_kernel(in_ref, out_ref, loss_ref):
    total = in_ref[0].astype(F32)
    for src in range(1, NZ):
        total = total + in_ref[src].astype(F32)
    out_ref[...] = total[0:12]
    loss_ref[...] = jnp.sum(total[12:15, 0:1], axis=0, keepdims=True)


def spread_order():
    place = np.zeros((HALF, HALF), np.float32)
    for row in range(HALF):
        j, rest = divmod(row, SUB)
        c, rest = divmod(rest, 48)
        y, r = divmod(rest, 12)
        place[row, (y * NC + c) * HD + j * 12 + r] = 1.0
    return jnp.asarray(place, BF)


def product_order():
    place = np.zeros((NC * NY * YROWS, 6 * SUB), np.float32)
    for c in range(NC):
        for y in range(NY):
            for z in range(6):
                for r in range(12):
                    place[(c * NY + y) * YROWS + z * 12 + r, z * SUB + c * 48 + y * 12 + r] = 1.0
    return jnp.asarray(place, BF)


def out_order():
    place = np.zeros((D, D), np.float32)
    row = 0
    for c in range(NC):
        for y in range(NY):
            for j in range(N_SEQ):
                for half in range(2):
                    for r in range(12):
                        place[row, (half * 8 + y * NC + c) * HD + j * 12 + r] = 1.0
                        row += 1
    return jnp.asarray(place, BF)


def out_pad_order():
    place = np.zeros((N_SEQ * 32, SUB), np.float32)
    for j in range(N_SEQ):
        for half in range(2):
            for r in range(12):
                place[j * 32 + half * 16 + r, j * 24 + half * 12 + r] = 1.0
    return jnp.asarray(place, BF)


def pad_order():
    place = np.zeros((SUB, YROWS), np.float32)
    for z in range(6):
        for r in range(12):
            place[z * 16 + r, z * 12 + r] = 1.0
        for r in range(3):
            place[z * 16 + 12 + r, 72 + r] = 1.0
    return jnp.asarray(place, BF)


SMEM = pl.BlockSpec(memory_space=pltpu.SMEM)
VMEM = pl.BlockSpec(memory_space=pltpu.VMEM)
HBM = pl.BlockSpec(memory_space=pltpu.HBM)
ANY = pl.BlockSpec(memory_space=pl.ANY)


def call(kernel, out_shapes, args, scratch=(), micros=1.0, specs=None, grant=24, unread=0):
    if specs is None:
        specs = [SMEM if a.dtype == jnp.int32 else VMEM for a in args]
        specs = specs[: len(specs) - unread] + [ANY] * unread
    return pl.pallas_call(
        kernel,
        out_shape=out_shapes,
        in_specs=specs,
        out_specs=[VMEM] * len(out_shapes),
        scratch_shapes=list(scratch),
        compiler_params=pltpu.CompilerParams(vmem_limit_bytes=grant * 1024 * 1024),
        cost_estimate=pl.CostEstimate(
            flops=int(micros * 1.0e9), bytes_accessed=int(micros * 1.0e6), transcendentals=0
        ),
    )(*args)


def shape(*dims, dtype=BF):
    return jax.ShapeDtypeStruct(dims, dtype)


def slide_at(z, y, c):
    return (z * NY + y) * NC + c


CORE_PAIRS = [(i, i ^ 1) for i in range(NZ * NY * NC)]
Z_GROUPS = [[slide_at(z, y, c) for z in range(NZ)] for y in range(NY) for c in range(NC)]
SEQ_TURNS = [[(k, (k + t) % N_SEQ) for k in range(N_SEQ)] for t in range(N_SEQ)]
Y_TURNS = [
    [
        (slide_at(z, y, c), slide_at(z, (y + t) % NY, c))
        for z in range(NZ)
        for y in range(NY)
        for c in range(NC)
    ]
    for t in range(NY)
]


def swap(arrays, axis, turns):
    return [arrays[0]] + [lax.ppermute(arrays[t], axis, turns[t]) for t in range(1, len(arrays))]


def per_device(embeddings, tile_counts, masked_tiles, w_in, norm_gain, w_qkv, w_out):
    inv_count = 1.0 / (lax.axis_size("slide") * masked_tiles.shape[1])
    hidden, normed = call(
        prep_kernel,
        [shape(TOK, D), shape(TOK, D)],
        (embeddings, masked_tiles, norm_gain, w_in),
        [
            pltpu.VMEM((TOK, 2 * D), BF),
            pltpu.VMEM((1, TOK), jnp.int32),
            pltpu.VMEM((D,), F32),
            pltpu.VMEM((2 * D, D), BF),
            pltpu.SemaphoreType.DMA((3 + 2 * D // 256,)),
        ],
        2.0,
        [HBM] * 4,
        60,
    )
    norms = swap([normed] * N_SEQ, "seq", SEQ_TURNS)
    scores = shape(GROUPS, TOK, RATE * TOK, dtype=F32)
    rows = shape(HEADS, TOK, dtype=F32)
    projected, exps, tops, sums, tiles, flag = call(
        near_kernel,
        [shape(TOK, 3 * D), scores, rows, rows, shape(TOK, 2 * D), shape(TOK, TOK, dtype=F32)],
        (tile_counts, normed, w_qkv, embeddings, masked_tiles),
        (),
        5.0,
        [SMEM] + [VMEM] * 4,
    )
    pn, fk, fv, pnear, pfar, attended = call(
        far_kernel,
        [
            shape(N_SEQ, TOK, D),
            shape(TOK, D),
            shape(TOK, D),
            scores,
            shape(GROUPS, TOK, TOK, dtype=F32),
            shape(TOK, D),
        ],
        (tile_counts, *norms, projected, exps, tops, sums, w_qkv),
        [pltpu.VMEM((TOK, D), F32)],
        4.0,
    )
    grad_attended, loss, out_mine, out_other = call(
        functools.partial(chain_kernel, inv_count),
        [shape(TOK, D), shape(16, 128), shape(HALF, D), shape(HALF, D)],
        (attended, hidden, tiles, flag, w_in, w_out, out_order()),
        (),
        3.0,
    )
    out_other = lax.ppermute(out_other, "slide", CORE_PAIRS)
    sent = call(
        backward_kernel,
        [shape(XROWS, TOK)] * N_SEQ,
        (projected, fk, fv, pnear, pfar, grad_attended, loss, spread_order()),
        [pltpu.VMEM((TOK, D), F32)] * 5 + [pltpu.VMEM((SECTIONS, HALF, TOK), BF)],
        4.0,
    )
    got = swap(sent, "seq", SEQ_TURNS)
    out = call(out_core_kernel, [shape(SUB, D)] * NY, (out_mine, out_other, sent[0]), unread=1)
    out = swap(out, "slide", Y_TURNS)
    out_sums = call(out_y_kernel, [shape(32, D)] * N_SEQ, (*out, out_pad_order()))
    out = swap(out_sums, "seq", SEQ_TURNS)
    mine, other = call(
        product_kernel,
        [shape(NY * YROWS, D)] * 2,
        (*got, pn, product_order(), out_sums[0]),
        [pltpu.VMEM((N_SEQ, XROWS, TOK), BF), pltpu.VMEM((6 * SUB, N_SEQ * TOK), BF)],
        3.0,
        unread=1,
    )
    other = lax.ppermute(other, "slide", CORE_PAIRS)
    by_y = call(core_kernel, [shape(YROWS, D)] * NY, (mine, other, *out[1:]), unread=3)
    by_y = swap(by_y, "slide", Y_TURNS)
    (by_z,) = call(y_kernel, [shape(NZ, 16, D)], (*by_y, *out, pad_order()))
    by_z = lax.all_to_all(by_z, "slide", 0, 0, tiled=True, axis_index_groups=Z_GROUPS)
    gradients, loss = call(z_kernel, [shape(12, D, dtype=F32), shape(1, 1, dtype=F32)], (by_z,))
    return (gradients, loss[0, 0])


def solution(mesh):
    in_specs = (P("slide", "seq", None), P("slide"), P("slide", None), P(), P(), P(), P())
    out_specs = (P(("slide", "seq"), None), P())
    return jax.shard_map(
        per_device, mesh=mesh, in_specs=in_specs, out_specs=out_specs, check_vma=False
    )
```

```python
import functools
import math

import numpy as np
import jax
import jax.numpy as jnp
from jax import lax
from jax.experimental import pallas as pl
from jax.experimental.pallas import tpu as pltpu
from jax.sharding import PartitionSpec as P

HEADS = 16
RATE = 4
HD = 48
D = 768
TOK = 128
N_SEQ = 4
GROUPS = HEADS // RATE
FAR = TOK // RATE
NORM_EPS = 1e-06
NEG_FILL = -1e30
SCALE = 1.0 / math.sqrt(HD)
BF = jnp.bfloat16
F32 = jnp.float32
HALF = 384
SUB = 96
SECTIONS = 10
YROWS = 80
XROWS = SECTIONS * SUB + 16
NZ, NY, NC = 8, 4, 2


def dot(a, b, dims):
    return lax.dot_general(a, b, (dims, ((), ())), preferred_element_type=F32)


def nn(a, b):
    return dot(a, b, ((1,), (0,)))


def nt(a, b):
    return dot(a, b, ((1,), (1,)))


def tn(a, b):
    return dot(a, b, ((0,), (0,)))


def iota(shape, dim):
    return lax.broadcasted_iota(jnp.int32, shape, dim)


def class_major(index):
    return (index & (FAR - 1)) * RATE + (index >> 5)


def split_rows(value, shape, first):
    high = value.astype(BF).astype(F32)
    rest = value - high
    mid = rest.astype(BF).astype(F32)
    low = rest - mid
    row = iota(shape, 0)
    return jnp.where(
        row == first,
        high,
        jnp.where(row == first + 1, mid, jnp.where(row == first + 2, low, 0.0)),
    )


def class_order():
    shape = (TOK, TOK)
    return (iota(shape, 1) == class_major(iota(shape, 0))).astype(F32).astype(BF)


def masked_rows(positions, masked):
    hits = jnp.where(positions == masked, 1.0, 0.0)
    return jnp.broadcast_to(jnp.max(hits, axis=1, keepdims=True), (TOK, TOK))


def prep_kernel(
    tiles_hbm, masked_hbm, gain_hbm, w_in_hbm, hidden_out, normed_out, tiles, masked, gain, w_in, sems
):
    blocks = w_in_hbm.shape[0] // 256
    loads = [
        pltpu.make_async_copy(masked_hbm, masked, sems.at[0]),
        pltpu.make_async_copy(tiles_hbm.at[0], tiles, sems.at[1]),
        pltpu.make_async_copy(gain_hbm, gain, sems.at[2]),
    ]
    chunks = [
        pltpu.make_async_copy(
            w_in_hbm.at[256 * i : 256 * (i + 1)], w_in.at[256 * i : 256 * (i + 1)], sems.at[3 + i]
        )
        for i in range(blocks)
    ]
    for copy in loads + chunks:
        copy.start()
    order = class_order()
    positions = lax.axis_index("seq") * TOK + iota((TOK, TOK), 0)
    loads[0].wait()
    flag = masked_rows(positions, masked[...])[:, 0:1] > 0.5
    loads[1].wait()
    hidden = jnp.zeros((TOK, D), F32)
    for i in range(blocks):
        cols = slice(256 * i, 256 * (i + 1))
        inputs = jnp.where(flag, jnp.zeros((), BF), tiles[:, cols])
        chunks[i].wait()
        hidden += nn(inputs, w_in[cols])
    hidden_f = nn(order, hidden.astype(BF))
    hidden_out[...] = hidden_f.astype(BF)
    scale_rows = lax.rsqrt(jnp.mean(hidden_f * hidden_f, axis=1, keepdims=True) + NORM_EPS)
    loads[2].wait()
    normed_out[...] = (hidden_f * scale_rows * gain[...].reshape(1, D)).astype(BF)


def window(group):
    return (group * RATE * HD) // 128 * 128


def head_masks(group):
    lane = iota((TOK, 256), 1) + window(group)
    row_class = iota((TOK, 256), 0) >> 5
    masks = []
    for r in range(RATE):
        first = (group * RATE + r) * HD
        masks.append((lane >= first) & (lane < first + HD))
    picked = masks[0] & (row_class == 0)
    for r in range(1, RATE):
        picked = picked | (masks[r] & (row_class == r))
    return masks, picked


def keep(mask, value):
    return jnp.where(mask, value, jnp.zeros((), value.dtype))


def by_class(own_class, pieces):
    out = pieces[0]
    for r in range(1, RATE):
        out = jnp.where(own_class == r, pieces[r], out)
    return out


def near_kernel(
    count_ref, normed_ref, w_qkv_ref, tiles_ref, masked_ref,
    proj_ref, exp_ref, top_ref, sum_ref, tiles_out, flag_ref,
):
    count = count_ref[0]
    pos0 = lax.axis_index("seq") * TOK
    flag_ref[...] = masked_rows(pos0 + class_major(iota((TOK, TOK), 0)), masked_ref[...])
    tiles_out[...] = nn(class_order(), tiles_ref[0]).astype(BF)
    normed = normed_ref[...]
    for block in range(3 * D // 256):
        cols = slice(block * 256, (block + 1) * 256)
        proj_ref[:, cols] = nn(normed, w_qkv_ref[:, cols]).astype(BF)
    square = (TOK, TOK)
    key_pos = pos0 + class_major(iota(square, 0))
    query_pos = pos0 + class_major(iota(square, 1))
    near_ok = (key_pos < count) | (key_pos == query_pos)
    for g in range(GROUPS):
        lo = window(g)
        masks, _ = head_masks(g)
        q = proj_ref[:, lo : lo + 256]
        k = proj_ref[:, D + lo : D + lo + 256]
        near = nt(k, jnp.concatenate([keep(m, q) for m in masks], 0))
        for r in range(RATE):
            head = g * RATE + r
            scores = jnp.where(near_ok, near[:, TOK * r : TOK * (r + 1)] * SCALE, NEG_FILL)
            top = jnp.max(scores, axis=0, keepdims=True)
            exps = jnp.exp(scores - top)
            exp_ref[g, :, TOK * r : TOK * (r + 1)] = exps
            top_ref[head : head + 1] = top
            sum_ref[head : head + 1] = jnp.sum(exps, axis=0, keepdims=True)


def far_kernel(
    count_ref, n0, n1, n2, n3, proj_ref, exp_ref, top_ref, sum_ref, w_qkv_ref,
    pn_ref, fk_ref, fv_ref, pnear_ref, pfar_ref, att_ref,
    att_acc,
):
    count = count_ref[0]
    seq = lax.axis_index("seq")
    for turn, ref in enumerate((n0, n1, n2, n3)):
        pn_ref[(seq - turn) & 3] = ref[...]
    others = jnp.concatenate([n1[...], n2[...], n3[...]], 0)
    for part, far_ref in enumerate((fk_ref, fv_ref)):
        for block in range(D // 256):
            cols = slice(block * 256, (block + 1) * 256)
            first = (1 + part) * D + block * 256
            every = nn(others, w_qkv_ref[:, first : first + 256]).astype(BF)
            lane_class = ((iota((FAR, 256), 1) + block * 256) // HD) & 3
            for turn in range(N_SEQ):
                if turn == 0:
                    rows = proj_ref[:, first : first + 256]
                else:
                    rows = every[(turn - 1) * TOK : turn * TOK]
                pieces = [rows[FAR * r : FAR * (r + 1)] for r in range(RATE)]
                place = pl.multiple_of(((seq - turn) & 3) * FAR, FAR)
                far_ref[pl.ds(place, FAR), cols] = by_class(lane_class, pieces)

    square = (TOK, TOK)
    far_row = iota(square, 0)
    far_ok = (far_row >> 5) * TOK + (far_row & (FAR - 1)) * RATE + (iota(square, 1) >> 5) < count
    own_class = iota((1, TOK), 1) >> 5

    att_acc[...] = jnp.zeros_like(att_acc)
    for g in range(GROUPS):
        lo = window(g)
        win = slice(lo, lo + 256)
        masks, picked = head_masks(g)
        q = proj_ref[:, lo : lo + 256]
        v = proj_ref[:, 2 * D + lo : 2 * D + lo + 256]
        far = jnp.where(far_ok, nt(fk_ref[:, win], keep(picked, q)) * SCALE, NEG_FILL)
        heads = range(g * RATE, (g + 1) * RATE)
        near_tops = [top_ref[h : h + 1] for h in heads]
        near_sums = [sum_ref[h : h + 1] for h in heads]
        top = jnp.maximum(jnp.max(far, axis=0, keepdims=True), by_class(own_class, near_tops))
        shrink = jnp.exp(by_class(own_class, near_tops) - top)
        far_exp = jnp.exp(far - top)
        total = by_class(own_class, near_sums) * shrink + jnp.sum(far_exp, axis=0, keepdims=True)
        far_probs = far_exp / total
        probs = []
        for r in range(RATE):
            factor = jnp.where(own_class == r, shrink / total, 1.0 / near_sums[r])
            probs.append(exp_ref[g, :, TOK * r : TOK * (r + 1)] * factor)
            pnear_ref[g, :, TOK * r : TOK * (r + 1)] = probs[r]
        pfar_ref[g] = far_probs
        att = tn(
            jnp.concatenate([p.astype(BF) for p in probs], 0),
            jnp.concatenate([keep(m, v) for m in masks], 0),
        )
        att_acc[:, win] += att + keep(picked, tn(far_probs.astype(BF), fv_ref[:, win]))
    att_ref[...] = att_acc[...].astype(BF)


def chain_kernel(
    inv_count,
    att_ref, hidden_ref, tiles_ref, flag_ref, w_in_ref, w_out_ref,
    ga_ref, loss_ref, gm_ref,
):
    attended = att_ref[...]
    mixed = (hidden_ref[...].astype(F32) + nn(attended, w_out_ref[...])).astype(BF)
    flag = flag_ref[:, 0:1] > 0.5
    error = jnp.where(flag, nt(mixed, w_in_ref[...]) - tiles_ref[...].astype(F32), 0.0)
    loss = jnp.sum(jnp.sum(error * error, axis=1, keepdims=True), axis=0, keepdims=True) * inv_count
    loss_ref[...] = split_rows(jnp.broadcast_to(loss, (16, 128)), (16, 128), 0).astype(BF)
    grad_pred = (2.0 * inv_count * error).astype(BF)
    grad_mixed = nn(grad_pred, w_in_ref[...]).astype(BF)
    ga_ref[...] = nt(grad_mixed, w_out_ref[...]).astype(BF)
    gm_ref[...] = grad_mixed


def out_kernel(gm_ref, att_ref, order_ref, mine_ref, other_ref):
    core = lax.axis_index("slide") & 1
    for turn, ref in enumerate((mine_ref, other_ref)):
        first = pl.multiple_of(((core + turn) & 1) * HALF, HALF)
        left = nt(order_ref[pl.ds(first, HALF)], gm_ref[...]).astype(BF)
        ref[...] = nn(left, att_ref[...]).astype(BF)


def backward_kernel(
    proj_ref, fk_ref, fv_ref, pnear_ref, pfar_ref, ga_ref, loss_ref, spread_ref,
    x0, x1, x2, x3,
    gq, gk, gv, gkf, gvf, turned,
):
    seq = lax.axis_index("seq")
    own_class = iota((1, TOK), 1) >> 5
    for ref in (gq, gk, gv, gkf, gvf):
        ref[...] = jnp.zeros_like(ref)
    for g in range(GROUPS):
        lo = window(g)
        win = slice(lo, lo + 256)
        masks, picked = head_masks(g)
        q = proj_ref[:, lo : lo + 256]
        k = proj_ref[:, D + lo : D + lo + 256]
        v = proj_ref[:, 2 * D + lo : 2 * D + lo + 256]
        ga = ga_ref[:, win]
        fk = fk_ref[:, win]
        fv = fv_ref[:, win]
        ga_stack = jnp.concatenate([keep(m, ga) for m in masks], 0)
        ga_picked = keep(picked, ga)
        near = nt(v, ga_stack)
        far = nt(fv, ga_picked)
        probs = [pnear_ref[g, :, TOK * r : TOK * (r + 1)] for r in range(RATE)]
        far_probs = pfar_ref[g]
        far_dot = jnp.sum(far_probs * far, axis=0, keepdims=True)
        grads = [near[:, TOK * r : TOK * (r + 1)] for r in range(RATE)]
        dots = []
        for r in range(RATE):
            own = jnp.sum(probs[r] * grads[r], axis=0, keepdims=True)
            dots.append(jnp.where(own_class == r, own + far_dot, own))
        scores = [(probs[r] * (grads[r] - dots[r]) * SCALE).astype(BF) for r in range(RATE)]
        far_scores = (far_probs * (far - by_class(own_class, dots)) * SCALE).astype(BF)
        gq[:, win] += tn(
            jnp.concatenate(scores, 0), jnp.concatenate([keep(m, k) for m in masks], 0)
        ) + keep(picked, tn(far_scores, fk))
        gk[:, win] += nn(
            jnp.concatenate(scores, 1), jnp.concatenate([keep(m, q) for m in masks], 0)
        )
        gv[:, win] += nn(jnp.concatenate([p.astype(BF) for p in probs], 1), ga_stack)
        gkf[:, win] += nn(far_scores, keep(picked, q))
        gvf[:, win] += nn(far_probs.astype(BF), ga_picked)
    place = spread_ref[...]
    section = 0
    for value in (gq, gk, gv, gkf, gvf):
        for half in range(2):
            piece = value[:, half * HALF : (half + 1) * HALF].astype(BF)
            turned[section] = nt(place, piece).astype(BF)
            section += 1
    for turn, ref in enumerate((x0, x1, x2, x3)):
        first = pl.multiple_of(((seq + turn) & 3) * SUB, 16)
        for section in range(SECTIONS):
            ref[section * SUB : (section + 1) * SUB] = turned[section, pl.ds(first, SUB)]
        ref[SECTIONS * SUB :] = loss_ref[...]


def product_kernel(x0, x1, x2, x3, pn_ref, order_ref, wait0, wait1, wait2, mine_ref, other_ref, got, left):
    seq = lax.axis_index("seq")
    core = lax.axis_index("slide") & 1
    for turn, x_ref in enumerate((x0, x1, x2, x3)):
        got[(seq - turn) & 3] = x_ref[...]
    for src in range(N_SEQ):
        left[0 : 2 * SUB, src * TOK : (src + 1) * TOK] = got[src, 0 : 2 * SUB]
    shape = (SUB, TOK)
    row = iota(shape, 0)
    lane_class = iota(shape, 1) >> 5
    core_row = jnp.where(row >= 48, 1, 0)
    row_y = (row - 48 * core_row) // 12
    row_class = ((row_y & 1) << 1) + core_row
    spots = [(row_class == r) & (lane_class == r) for r in range(RATE)]
    for part in range(2):
        for half in range(2):
            near_at = (2 + 2 * part + half) * SUB
            far_at = (6 + 2 * part + half) * SUB
            far = got[0, far_at : far_at + SUB].astype(F32)
            for src in range(1, N_SEQ):
                far = far + got[src, far_at : far_at + SUB].astype(F32)
            turns = [far] + [pltpu.roll(far, FAR * t, 1) for t in range(1, RATE)]
            for src in range(N_SEQ):
                total = got[src, near_at : near_at + SUB].astype(F32)
                for r in range(RATE):
                    total = total + jnp.where(spots[r], turns[(r - src) & 3], 0.0)
                left[near_at : near_at + SUB, src * TOK : (src + 1) * TOK] = total.astype(BF)
    whole = nn(left[...], pn_ref[...].reshape(N_SEQ * TOK, D)).astype(BF)
    loss = got[0, SECTIONS * SUB :].astype(F32)
    for src in range(1, N_SEQ):
        loss = loss + got[src, SECTIONS * SUB :].astype(F32)
    loss = jnp.sum(loss, axis=0, keepdims=True)[:, 0:1]
    tail = split_rows(jnp.broadcast_to(loss, (YROWS, D)), (YROWS, D), 72)
    for turn, ref in enumerate((mine_ref, other_ref)):
        first = pl.multiple_of(((core + turn) & 1) * NY * YROWS, NY * YROWS)
        half = nn(order_ref[pl.ds(first, NY * YROWS)], whole)
        for y in range(NY):
            rows = slice(y * YROWS, (y + 1) * YROWS)
            ref[rows] = (half[rows] + tail).astype(BF)


def resplit(total):
    row = iota(total.shape, 0)
    loss = jnp.sum(jnp.where(row >= 72, total, 0.0), axis=0, keepdims=True)
    pieces = split_rows(jnp.broadcast_to(loss, total.shape), total.shape, 72)
    return jnp.where(row >= 72, pieces, total), loss


def core_kernel(mine_ref, other_ref, wait_ref, y0, y1, y2, y3):
    y = (lax.axis_index("slide") >> 1) & 3
    for turn, ref in enumerate((y0, y1, y2, y3)):
        rows = pl.ds(pl.multiple_of(((y + turn) & 3) * YROWS, 16), YROWS)
        ref[...] = resplit(mine_ref[rows].astype(F32) + other_ref[rows].astype(F32))[0].astype(BF)


def y_kernel(y0, y1, y2, y3, o0, o1, o2, o3, order_ref, out_ref):
    total = y0[...].astype(F32) + y1[...].astype(F32) + y2[...].astype(F32) + y3[...].astype(F32)
    total, loss = resplit(total)
    out_ref[0:6] = nn(order_ref[...], total.astype(BF)).astype(BF).reshape(6, 16, D)
    out = o0[...].astype(F32) + o1[...].astype(F32) + o2[...].astype(F32) + o3[...].astype(F32)
    tail = split_rows(jnp.broadcast_to(loss, (16, D)), (16, D), 12)
    for half in range(2):
        out_ref[6 + half] = (out[16 * half : 16 * (half + 1)] + tail).astype(BF)


def out_core_kernel(mine_ref, other_ref, wait_ref, y0, y1, y2, y3):
    y = (lax.axis_index("slide") >> 1) & 3
    for turn, ref in enumerate((y0, y1, y2, y3)):
        rows = pl.ds(pl.multiple_of(((y + turn) & 3) * SUB, 16), SUB)
        ref[...] = (mine_ref[rows].astype(F32) + other_ref[rows].astype(F32)).astype(BF)


def out_y_kernel(y0, y1, y2, y3, order_ref, x0, x1, x2, x3):
    seq = lax.axis_index("seq")
    total = y0[...].astype(F32) + y1[...].astype(F32) + y2[...].astype(F32) + y3[...].astype(F32)
    total = total.astype(BF)
    for turn, ref in enumerate((x0, x1, x2, x3)):
        rows = pl.ds(pl.multiple_of(((seq + turn) & 3) * 32, 32), 32)
        ref[...] = nn(order_ref[rows], total).astype(BF)


def z_kernel(in_ref, out_ref, loss_ref):
    total = in_ref[0].astype(F32)
    for src in range(1, NZ):
        total = total + in_ref[src].astype(F32)
    out_ref[...] = total[0:12]
    loss_ref[...] = jnp.sum(total[12:15, 0:1], axis=0, keepdims=True)


def spread_order():
    place = np.zeros((HALF, HALF), np.float32)
    for row in range(HALF):
        j, rest = divmod(row, SUB)
        c, rest = divmod(rest, 48)
        y, r = divmod(rest, 12)
        place[row, (y * NC + c) * HD + j * 12 + r] = 1.0
    return jnp.asarray(place, BF)


def product_order():
    place = np.zeros((NC * NY * YROWS, 6 * SUB), np.float32)
    for c in range(NC):
        for y in range(NY):
            for z in range(6):
                for r in range(12):
                    place[(c * NY + y) * YROWS + z * 12 + r, z * SUB + c * 48 + y * 12 + r] = 1.0
    return jnp.asarray(place, BF)


def out_order():
    place = np.zeros((D, D), np.float32)
    row = 0
    for c in range(NC):
        for y in range(NY):
            for j in range(N_SEQ):
                for half in range(2):
                    for r in range(12):
                        place[row, (half * 8 + y * NC + c) * HD + j * 12 + r] = 1.0
                        row += 1
    return jnp.asarray(place, BF)


def out_pad_order():
    place = np.zeros((N_SEQ * 32, SUB), np.float32)
    for j in range(N_SEQ):
        for half in range(2):
            for r in range(12):
                place[j * 32 + half * 16 + r, j * 24 + half * 12 + r] = 1.0
    return jnp.asarray(place, BF)


def pad_order():
    place = np.zeros((SUB, YROWS), np.float32)
    for z in range(6):
        for r in range(12):
            place[z * 16 + r, z * 12 + r] = 1.0
        for r in range(3):
            place[z * 16 + 12 + r, 72 + r] = 1.0
    return jnp.asarray(place, BF)


SMEM = pl.BlockSpec(memory_space=pltpu.SMEM)
VMEM = pl.BlockSpec(memory_space=pltpu.VMEM)
HBM = pl.BlockSpec(memory_space=pltpu.HBM)
ANY = pl.BlockSpec(memory_space=pl.ANY)


def call(kernel, out_shapes, args, scratch=(), micros=1.0, specs=None, grant=24, unread=0):
    if specs is None:
        specs = [SMEM if a.dtype == jnp.int32 else VMEM for a in args]
        specs = specs[: len(specs) - unread] + [ANY] * unread
    return pl.pallas_call(
        kernel,
        out_shape=out_shapes,
        in_specs=specs,
        out_specs=[VMEM] * len(out_shapes),
        scratch_shapes=list(scratch),
        compiler_params=pltpu.CompilerParams(vmem_limit_bytes=grant * 1024 * 1024),
        cost_estimate=pl.CostEstimate(
            flops=int(micros * 1.0e9), bytes_accessed=int(micros * 1.0e6), transcendentals=0
        ),
    )(*args)


def shape(*dims, dtype=BF):
    return jax.ShapeDtypeStruct(dims, dtype)


def slide_at(z, y, c):
    return (z * NY + y) * NC + c


CORE_PAIRS = [(i, i ^ 1) for i in range(NZ * NY * NC)]
Z_GROUPS = [[slide_at(z, y, c) for z in range(NZ)] for y in range(NY) for c in range(NC)]
SEQ_TURNS = [[(k, (k + t) % N_SEQ) for k in range(N_SEQ)] for t in range(N_SEQ)]
Y_TURNS = [
    [
        (slide_at(z, y, c), slide_at(z, (y + t) % NY, c))
        for z in range(NZ)
        for y in range(NY)
        for c in range(NC)
    ]
    for t in range(NY)
]


def swap(arrays, axis, turns):
    got = {t: lax.ppermute(arrays[t], axis, turns[t]) for t in (2, 1, 3)}
    return [arrays[0], got[1], got[2], got[3]]


def per_device(embeddings, tile_counts, masked_tiles, w_in, norm_gain, w_qkv, w_out):
    inv_count = 1.0 / (lax.axis_size("slide") * masked_tiles.shape[1])
    hidden, normed = call(
        prep_kernel,
        [shape(TOK, D), shape(TOK, D)],
        (embeddings, masked_tiles, norm_gain, w_in),
        [
            pltpu.VMEM((TOK, 2 * D), BF),
            pltpu.VMEM((1, TOK), jnp.int32),
            pltpu.VMEM((D,), F32),
            pltpu.VMEM((2 * D, D), BF),
            pltpu.SemaphoreType.DMA((3 + 2 * D // 256,)),
        ],
        2.0,
        [HBM] * 4,
        60,
    )
    norms = swap([normed] * N_SEQ, "seq", SEQ_TURNS)
    scores = shape(GROUPS, TOK, RATE * TOK, dtype=F32)
    rows = shape(HEADS, TOK, dtype=F32)
    projected, exps, tops, sums, tiles, flag = call(
        near_kernel,
        [shape(TOK, 3 * D), scores, rows, rows, shape(TOK, 2 * D), shape(TOK, TOK, dtype=F32)],
        (tile_counts, normed, w_qkv, embeddings, masked_tiles),
        (),
        5.0,
        [SMEM] + [VMEM] * 4,
    )
    pn, fk, fv, pnear, pfar, attended = call(
        far_kernel,
        [
            shape(N_SEQ, TOK, D),
            shape(TOK, D),
            shape(TOK, D),
            scores,
            shape(GROUPS, TOK, TOK, dtype=F32),
            shape(TOK, D),
        ],
        (tile_counts, *norms, projected, exps, tops, sums, w_qkv),
        [pltpu.VMEM((TOK, D), F32)],
        4.0,
    )
    grad_attended, loss, grad_mixed = call(
        functools.partial(chain_kernel, inv_count),
        [shape(TOK, D), shape(16, 128), shape(TOK, D)],
        (attended, hidden, tiles, flag, w_in, w_out),
        (),
        3.0,
    )
    sent = call(
        backward_kernel,
        [shape(XROWS, TOK)] * N_SEQ,
        (projected, fk, fv, pnear, pfar, grad_attended, loss, spread_order()),
        [pltpu.VMEM((TOK, D), F32)] * 5 + [pltpu.VMEM((SECTIONS, HALF, TOK), BF)],
        4.0,
    )
    got = swap(sent, "seq", SEQ_TURNS)
    out_mine, out_other = call(
        out_kernel, [shape(HALF, D)] * 2, (grad_mixed, attended, out_order())
    )
    out_other = lax.ppermute(out_other, "slide", CORE_PAIRS)
    out = call(out_core_kernel, [shape(SUB, D)] * NY, (out_mine, out_other, sent[0]), unread=1)
    out = swap(out, "slide", Y_TURNS)
    out_rows = out
    out_sums = call(out_y_kernel, [shape(32, D)] * N_SEQ, (*out, out_pad_order()))
    out = swap(out_sums, "seq", SEQ_TURNS)
    mine, other = call(
        product_kernel,
        [shape(NY * YROWS, D)] * 2,
        (*got, pn, product_order(), *out_rows[1:]),
        [pltpu.VMEM((N_SEQ, XROWS, TOK), BF), pltpu.VMEM((6 * SUB, N_SEQ * TOK), BF)],
        3.0,
        unread=3,
    )
    other = lax.ppermute(other, "slide", CORE_PAIRS)
    by_y = call(core_kernel, [shape(YROWS, D)] * NY, (mine, other, out_sums[0]), unread=1)
    by_y = swap(by_y, "slide", Y_TURNS)
    (by_z,) = call(y_kernel, [shape(NZ, 16, D)], (*by_y, *out, pad_order()))
    by_z = lax.all_to_all(by_z, "slide", 0, 0, tiled=True, axis_index_groups=Z_GROUPS)
    gradients, loss = call(z_kernel, [shape(12, D, dtype=F32), shape(1, 1, dtype=F32)], (by_z,))
    return (gradients, loss[0, 0])


def solution(mesh):
    in_specs = (P("slide", "seq", None), P("slide"), P("slide", None), P(), P(), P(), P())
    out_specs = (P(("slide", "seq"), None), P())
    return jax.shard_map(
        per_device, mesh=mesh, in_specs=in_specs, out_specs=out_specs, check_vma=False
    )
```

```python
import functools
import math

import numpy as np
import jax
import jax.numpy as jnp
from jax import lax
from jax.experimental import pallas as pl
from jax.experimental.pallas import tpu as pltpu
from jax.sharding import PartitionSpec as P

HEADS = 16
RATE = 4
HD = 48
D = 768
TOK = 128
N_SEQ = 4
GROUPS = HEADS // RATE
FAR = TOK // RATE
NORM_EPS = 1e-06
NEG_FILL = -1e30
SCALE = 1.0 / math.sqrt(HD)
BF = jnp.bfloat16
F32 = jnp.float32
HALF = 384
SUB = 96
SECTIONS = 10
YROWS = 80
ALLROWS = 112
MAINROWS = SECTIONS * SUB + 16
XROWS = MAINROWS + 6 * SUB
NZ, NY, NC = 8, 4, 2


def dot(a, b, dims):
    return lax.dot_general(a, b, (dims, ((), ())), preferred_element_type=F32)


def nn(a, b):
    return dot(a, b, ((1,), (0,)))


def nt(a, b):
    return dot(a, b, ((1,), (1,)))


def tn(a, b):
    return dot(a, b, ((0,), (0,)))


def iota(shape, dim):
    return lax.broadcasted_iota(jnp.int32, shape, dim)


def class_major(index):
    return (index & (FAR - 1)) * RATE + (index >> 5)


def split_rows(value, shape, first):
    high = value.astype(BF).astype(F32)
    rest = value - high
    mid = rest.astype(BF).astype(F32)
    low = rest - mid
    row = iota(shape, 0)
    return jnp.where(
        row == first,
        high,
        jnp.where(row == first + 1, mid, jnp.where(row == first + 2, low, 0.0)),
    )


def class_order():
    shape = (TOK, TOK)
    return (iota(shape, 1) == class_major(iota(shape, 0))).astype(F32).astype(BF)


def masked_rows(positions, masked):
    hits = jnp.where(positions == masked, 1.0, 0.0)
    return jnp.broadcast_to(jnp.max(hits, axis=1, keepdims=True), (TOK, TOK))


def prep_kernel(
    tiles_hbm, masked_hbm, gain_hbm, w_in_hbm, hidden_out, normed_out, tiles, masked, gain, w_in, sems
):
    blocks = w_in_hbm.shape[0] // 256
    loads = [
        pltpu.make_async_copy(masked_hbm, masked, sems.at[0]),
        pltpu.make_async_copy(tiles_hbm.at[0], tiles, sems.at[1]),
        pltpu.make_async_copy(gain_hbm, gain, sems.at[2]),
    ]
    chunks = [
        pltpu.make_async_copy(
            w_in_hbm.at[256 * i : 256 * (i + 1)], w_in.at[256 * i : 256 * (i + 1)], sems.at[3 + i]
        )
        for i in range(blocks)
    ]
    for copy in loads + chunks:
        copy.start()
    order = class_order()
    positions = lax.axis_index("seq") * TOK + iota((TOK, TOK), 0)
    loads[0].wait()
    flag = masked_rows(positions, masked[...])[:, 0:1] > 0.5
    loads[1].wait()
    hidden = jnp.zeros((TOK, D), F32)
    for i in range(blocks):
        cols = slice(256 * i, 256 * (i + 1))
        inputs = jnp.where(flag, jnp.zeros((), BF), tiles[:, cols])
        chunks[i].wait()
        hidden += nn(inputs, w_in[cols])
    hidden_f = nn(order, hidden.astype(BF))
    hidden_out[...] = hidden_f.astype(BF)
    scale_rows = lax.rsqrt(jnp.mean(hidden_f * hidden_f, axis=1, keepdims=True) + NORM_EPS)
    loads[2].wait()
    normed_out[...] = (hidden_f * scale_rows * gain[...].reshape(1, D)).astype(BF)


def window(group):
    return (group * RATE * HD) // 128 * 128


def head_masks(group):
    lane = iota((TOK, 256), 1) + window(group)
    row_class = iota((TOK, 256), 0) >> 5
    masks = []
    for r in range(RATE):
        first = (group * RATE + r) * HD
        masks.append((lane >= first) & (lane < first + HD))
    picked = masks[0] & (row_class == 0)
    for r in range(1, RATE):
        picked = picked | (masks[r] & (row_class == r))
    return masks, picked


def keep(mask, value):
    return jnp.where(mask, value, jnp.zeros((), value.dtype))


def by_class(own_class, pieces):
    out = pieces[0]
    for r in range(1, RATE):
        out = jnp.where(own_class == r, pieces[r], out)
    return out


def near_kernel(
    count_ref, normed_ref, w_qkv_ref, tiles_ref, masked_ref,
    proj_ref, exp_ref, top_ref, sum_ref, tiles_out, flag_ref,
):
    count = count_ref[0]
    pos0 = lax.axis_index("seq") * TOK
    flag_ref[...] = masked_rows(pos0 + class_major(iota((TOK, TOK), 0)), masked_ref[...])
    tiles_out[...] = nn(class_order(), tiles_ref[0]).astype(BF)
    normed = normed_ref[...]
    for block in range(3 * D // 256):
        cols = slice(block * 256, (block + 1) * 256)
        proj_ref[:, cols] = nn(normed, w_qkv_ref[:, cols]).astype(BF)
    square = (TOK, TOK)
    key_pos = pos0 + class_major(iota(square, 0))
    query_pos = pos0 + class_major(iota(square, 1))
    near_ok = (key_pos < count) | (key_pos == query_pos)
    for g in range(GROUPS):
        lo = window(g)
        masks, _ = head_masks(g)
        q = proj_ref[:, lo : lo + 256]
        k = proj_ref[:, D + lo : D + lo + 256]
        near = nt(k, jnp.concatenate([keep(m, q) for m in masks], 0))
        for r in range(RATE):
            head = g * RATE + r
            scores = jnp.where(near_ok, near[:, TOK * r : TOK * (r + 1)] * SCALE, NEG_FILL)
            top = jnp.max(scores, axis=0, keepdims=True)
            exps = jnp.exp(scores - top)
            exp_ref[g, :, TOK * r : TOK * (r + 1)] = exps
            top_ref[head : head + 1] = top
            sum_ref[head : head + 1] = jnp.sum(exps, axis=0, keepdims=True)


def far_kernel(
    count_ref, n0, n1, n2, n3, proj_ref, exp_ref, top_ref, sum_ref, w_qkv_ref,
    pn_ref, fk_ref, fv_ref, pnear_ref, pfar_ref, att_ref,
    att_acc,
):
    count = count_ref[0]
    seq = lax.axis_index("seq")
    for turn, ref in enumerate((n0, n1, n2, n3)):
        pn_ref[(seq - turn) & 3] = ref[...]
    others = jnp.concatenate([n1[...], n2[...], n3[...]], 0)
    for part, far_ref in enumerate((fk_ref, fv_ref)):
        for block in range(D // 256):
            cols = slice(block * 256, (block + 1) * 256)
            first = (1 + part) * D + block * 256
            every = nn(others, w_qkv_ref[:, first : first + 256]).astype(BF)
            lane_class = ((iota((FAR, 256), 1) + block * 256) // HD) & 3
            for turn in range(N_SEQ):
                if turn == 0:
                    rows = proj_ref[:, first : first + 256]
                else:
                    rows = every[(turn - 1) * TOK : turn * TOK]
                pieces = [rows[FAR * r : FAR * (r + 1)] for r in range(RATE)]
                place = pl.multiple_of(((seq - turn) & 3) * FAR, FAR)
                far_ref[pl.ds(place, FAR), cols] = by_class(lane_class, pieces)

    square = (TOK, TOK)
    far_row = iota(square, 0)
    far_ok = (far_row >> 5) * TOK + (far_row & (FAR - 1)) * RATE + (iota(square, 1) >> 5) < count
    own_class = iota((1, TOK), 1) >> 5

    att_acc[...] = jnp.zeros_like(att_acc)
    for g in range(GROUPS):
        lo = window(g)
        win = slice(lo, lo + 256)
        masks, picked = head_masks(g)
        q = proj_ref[:, lo : lo + 256]
        v = proj_ref[:, 2 * D + lo : 2 * D + lo + 256]
        far = jnp.where(far_ok, nt(fk_ref[:, win], keep(picked, q)) * SCALE, NEG_FILL)
        heads = range(g * RATE, (g + 1) * RATE)
        near_tops = [top_ref[h : h + 1] for h in heads]
        near_sums = [sum_ref[h : h + 1] for h in heads]
        top = jnp.maximum(jnp.max(far, axis=0, keepdims=True), by_class(own_class, near_tops))
        shrink = jnp.exp(by_class(own_class, near_tops) - top)
        far_exp = jnp.exp(far - top)
        total = by_class(own_class, near_sums) * shrink + jnp.sum(far_exp, axis=0, keepdims=True)
        far_probs = far_exp / total
        probs = []
        for r in range(RATE):
            factor = jnp.where(own_class == r, shrink / total, 1.0 / near_sums[r])
            probs.append(exp_ref[g, :, TOK * r : TOK * (r + 1)] * factor)
            pnear_ref[g, :, TOK * r : TOK * (r + 1)] = probs[r]
        pfar_ref[g] = far_probs
        att = tn(
            jnp.concatenate([p.astype(BF) for p in probs], 0),
            jnp.concatenate([keep(m, v) for m in masks], 0),
        )
        att_acc[:, win] += att + keep(picked, tn(far_probs.astype(BF), fv_ref[:, win]))
    att_ref[...] = att_acc[...].astype(BF)


def chain_kernel(
    inv_count,
    att_ref, hidden_ref, tiles_ref, flag_ref, w_in_ref, w_out_ref,
    ga_ref, loss_ref, gm_ref,
):
    attended = att_ref[...]
    mixed = (hidden_ref[...].astype(F32) + nn(attended, w_out_ref[...])).astype(BF)
    flag = flag_ref[:, 0:1] > 0.5
    error = jnp.where(flag, nt(mixed, w_in_ref[...]) - tiles_ref[...].astype(F32), 0.0)
    loss = jnp.sum(jnp.sum(error * error, axis=1, keepdims=True), axis=0, keepdims=True) * inv_count
    loss_ref[...] = split_rows(jnp.broadcast_to(loss, (16, 128)), (16, 128), 0).astype(BF)
    grad_pred = (2.0 * inv_count * error).astype(BF)
    grad_mixed = nn(grad_pred, w_in_ref[...]).astype(BF)
    ga_ref[...] = nt(grad_mixed, w_out_ref[...]).astype(BF)
    gm_ref[...] = grad_mixed


def out_kernel(gm_ref, att_ref, order_ref, mine_ref, other_ref):
    core = lax.axis_index("slide") & 1
    for turn, ref in enumerate((mine_ref, other_ref)):
        first = pl.multiple_of(((core + turn) & 1) * HALF, HALF)
        left = nt(order_ref[pl.ds(first, HALF)], gm_ref[...]).astype(BF)
        ref[...] = nn(left, att_ref[...]).astype(BF)


def backward_kernel(
    proj_ref, fk_ref, fv_ref, pnear_ref, pfar_ref, ga_ref, spread_ref,
    turned,
    gq, gk, gv, gkf, gvf,
):
    own_class = iota((1, TOK), 1) >> 5
    for ref in (gq, gk, gv, gkf, gvf):
        ref[...] = jnp.zeros_like(ref)
    for g in range(GROUPS):
        lo = window(g)
        win = slice(lo, lo + 256)
        masks, picked = head_masks(g)
        q = proj_ref[:, lo : lo + 256]
        k = proj_ref[:, D + lo : D + lo + 256]
        v = proj_ref[:, 2 * D + lo : 2 * D + lo + 256]
        ga = ga_ref[:, win]
        fk = fk_ref[:, win]
        fv = fv_ref[:, win]
        ga_stack = jnp.concatenate([keep(m, ga) for m in masks], 0)
        ga_picked = keep(picked, ga)
        near = nt(v, ga_stack)
        far = nt(fv, ga_picked)
        probs = [pnear_ref[g, :, TOK * r : TOK * (r + 1)] for r in range(RATE)]
        far_probs = pfar_ref[g]
        far_dot = jnp.sum(far_probs * far, axis=0, keepdims=True)
        grads = [near[:, TOK * r : TOK * (r + 1)] for r in range(RATE)]
        dots = []
        for r in range(RATE):
            own = jnp.sum(probs[r] * grads[r], axis=0, keepdims=True)
            dots.append(jnp.where(own_class == r, own + far_dot, own))
        scores = [(probs[r] * (grads[r] - dots[r]) * SCALE).astype(BF) for r in range(RATE)]
        far_scores = (far_probs * (far - by_class(own_class, dots)) * SCALE).astype(BF)
        gq[:, win] += tn(
            jnp.concatenate(scores, 0), jnp.concatenate([keep(m, k) for m in masks], 0)
        ) + keep(picked, tn(far_scores, fk))
        gk[:, win] += nn(
            jnp.concatenate(scores, 1), jnp.concatenate([keep(m, q) for m in masks], 0)
        )
        gv[:, win] += nn(jnp.concatenate([p.astype(BF) for p in probs], 1), ga_stack)
        gkf[:, win] += nn(far_scores, keep(picked, q))
        gvf[:, win] += nn(far_probs.astype(BF), ga_picked)
    place = spread_ref[...]
    section = 0
    for value in (gq, gk, gv, gkf, gvf):
        for half in range(2):
            piece = value[:, half * HALF : (half + 1) * HALF].astype(BF)
            turned[section] = nt(place, piece).astype(BF)
            section += 1

def pack_kernel(turned_ref, loss_ref, mine_ref, other_ref, x0, x1, x2, x3):
    seq = lax.axis_index("seq")
    for turn, ref in enumerate((x0, x1, x2, x3)):
        rows = pl.ds(pl.multiple_of(((seq + turn) & 3) * SUB, 16), SUB)
        for section in range(SECTIONS):
            ref[section * SUB : (section + 1) * SUB] = turned_ref[section, rows]
        ref[SECTIONS * SUB : MAINROWS] = loss_ref[...]
        for block in range(6):
            cols = slice(128 * block, 128 * (block + 1))
            total = mine_ref[rows, cols].astype(F32) + other_ref[rows, cols].astype(F32)
            ref[MAINROWS + SUB * block : MAINROWS + SUB * (block + 1)] = total.astype(BF)


def product_kernel(x0, x1, x2, x3, pn_ref, order_ref, mine_ref, other_ref, out_ref, got, left):
    seq = lax.axis_index("seq")
    core = lax.axis_index("slide") & 1
    for turn, x_ref in enumerate((x0, x1, x2, x3)):
        got[(seq - turn) & 3] = x_ref[0:MAINROWS]
    for src in range(N_SEQ):
        left[0 : 2 * SUB, src * TOK : (src + 1) * TOK] = got[src, 0 : 2 * SUB]
    shape = (SUB, TOK)
    row = iota(shape, 0)
    lane_class = iota(shape, 1) >> 5
    core_row = jnp.where(row >= 48, 1, 0)
    row_y = (row - 48 * core_row) // 12
    row_class = ((row_y & 1) << 1) + core_row
    spots = [(row_class == r) & (lane_class == r) for r in range(RATE)]
    for part in range(2):
        for half in range(2):
            near_at = (2 + 2 * part + half) * SUB
            far_at = (6 + 2 * part + half) * SUB
            far = got[0, far_at : far_at + SUB].astype(F32)
            for src in range(1, N_SEQ):
                far = far + got[src, far_at : far_at + SUB].astype(F32)
            turns = [far] + [pltpu.roll(far, FAR * t, 1) for t in range(1, RATE)]
            for src in range(N_SEQ):
                total = got[src, near_at : near_at + SUB].astype(F32)
                for r in range(RATE):
                    total = total + jnp.where(spots[r], turns[(r - src) & 3], 0.0)
                left[near_at : near_at + SUB, src * TOK : (src + 1) * TOK] = total.astype(BF)
    for block in range(6):
        rows = slice(MAINROWS + SUB * block, MAINROWS + SUB * (block + 1))
        out = x0[rows].astype(F32) + x1[rows].astype(F32) + x2[rows].astype(F32) + x3[rows].astype(F32)
        out_ref[:, 128 * block : 128 * (block + 1)] = out.astype(BF)
    whole = nn(left[...], pn_ref[...].reshape(N_SEQ * TOK, D)).astype(BF)
    loss = got[0, SECTIONS * SUB : MAINROWS].astype(F32)
    for src in range(1, N_SEQ):
        loss = loss + got[src, SECTIONS * SUB : MAINROWS].astype(F32)
    loss = jnp.sum(loss, axis=0, keepdims=True)[:, 0:1]
    tail = split_rows(jnp.broadcast_to(loss, (YROWS, D)), (YROWS, D), 72)
    for turn, ref in enumerate((mine_ref, other_ref)):
        first = pl.multiple_of(((core + turn) & 1) * NY * YROWS, NY * YROWS)
        half = nn(order_ref[pl.ds(first, NY * YROWS)], whole)
        for y in range(NY):
            rows = slice(y * YROWS, (y + 1) * YROWS)
            ref[rows] = (half[rows] + tail).astype(BF)


def resplit(total):
    row = iota(total.shape, 0)
    loss = jnp.sum(jnp.where(row >= 72, total, 0.0), axis=0, keepdims=True)
    pieces = split_rows(jnp.broadcast_to(loss, total.shape), total.shape, 72)
    return jnp.where(row >= 72, pieces, total)


def core_kernel(mine_ref, other_ref, out_ref, order_ref, y0, y1, y2, y3):
    y = (lax.axis_index("slide") >> 1) & 3
    for turn, ref in enumerate((y0, y1, y2, y3)):
        place = (y + turn) & 3
        rows = pl.ds(pl.multiple_of(place * YROWS, 16), YROWS)
        total = resplit(mine_ref[rows].astype(F32) + other_ref[rows].astype(F32))
        ref[0:YROWS] = total.astype(BF)
        ref[YROWS:] = nn(order_ref[pl.ds(pl.multiple_of(place * 32, 32), 32)], out_ref[...]).astype(BF)


def y_kernel(y0, y1, y2, y3, order_ref, out_ref):
    total = y0[...].astype(F32) + y1[...].astype(F32) + y2[...].astype(F32) + y3[...].astype(F32)
    total = jnp.concatenate([resplit(total[:YROWS]), total[YROWS:]], 0)
    out_ref[...] = nn(order_ref[...], total.astype(BF)).astype(BF).reshape(NZ, 16, D)


def z_kernel(in_ref, out_ref, loss_ref):
    total = in_ref[0].astype(F32)
    for src in range(1, NZ):
        total = total + in_ref[src].astype(F32)
    out_ref[...] = total[0:12]
    loss_ref[...] = jnp.sum(total[12:15, 0:1], axis=0, keepdims=True)


def spread_order():
    place = np.zeros((HALF, HALF), np.float32)
    for row in range(HALF):
        j, rest = divmod(row, SUB)
        c, rest = divmod(rest, 48)
        y, r = divmod(rest, 12)
        place[row, (y * NC + c) * HD + j * 12 + r] = 1.0
    return jnp.asarray(place, BF)


def product_order():
    place = np.zeros((NC * NY * YROWS, 6 * SUB), np.float32)
    for c in range(NC):
        for y in range(NY):
            for z in range(6):
                for r in range(12):
                    place[(c * NY + y) * YROWS + z * 12 + r, z * SUB + c * 48 + y * 12 + r] = 1.0
    return jnp.asarray(place, BF)


def out_order():
    place = np.zeros((D, D), np.float32)
    row = 0
    for c in range(NC):
        for j in range(N_SEQ):
            for y in range(NY):
                for half in range(2):
                    for r in range(12):
                        place[row, (half * 8 + y * NC + c) * HD + j * 12 + r] = 1.0
                        row += 1
    return jnp.asarray(place, BF)


def out_pad_order():
    place = np.zeros((NY * 32, SUB), np.float32)
    for y in range(NY):
        for r in range(24):
            place[y * 32 + r, y * 24 + r] = 1.0
    return jnp.asarray(place, BF)


def pad_order():
    place = np.zeros((NZ * 16, ALLROWS), np.float32)
    for z in range(NZ):
        for r in range(12):
            first = z * 12 if z < 6 else YROWS + (z - 6) * 12
            place[z * 16 + r, first + r] = 1.0
        for r in range(3):
            place[z * 16 + 12 + r, 72 + r] = 1.0
    return jnp.asarray(place, BF)


SMEM = pl.BlockSpec(memory_space=pltpu.SMEM)
VMEM = pl.BlockSpec(memory_space=pltpu.VMEM)
HBM = pl.BlockSpec(memory_space=pltpu.HBM)
ANY = pl.BlockSpec(memory_space=pl.ANY)


def call(kernel, out_shapes, args, scratch=(), micros=1.0, specs=None, grant=24, unread=0):
    if specs is None:
        specs = [SMEM if a.dtype == jnp.int32 else VMEM for a in args]
        specs = specs[: len(specs) - unread] + [ANY] * unread
    return pl.pallas_call(
        kernel,
        out_shape=out_shapes,
        in_specs=specs,
        out_specs=[VMEM] * len(out_shapes),
        scratch_shapes=list(scratch),
        compiler_params=pltpu.CompilerParams(vmem_limit_bytes=grant * 1024 * 1024),
        cost_estimate=pl.CostEstimate(
            flops=int(micros * 1.0e9), bytes_accessed=int(micros * 1.0e6), transcendentals=0
        ),
    )(*args)


def shape(*dims, dtype=BF):
    return jax.ShapeDtypeStruct(dims, dtype)


def slide_at(z, y, c):
    return (z * NY + y) * NC + c


CORE_PAIRS = [(i, i ^ 1) for i in range(NZ * NY * NC)]
Z_GROUPS = [[slide_at(z, y, c) for z in range(NZ)] for y in range(NY) for c in range(NC)]
SEQ_TURNS = [[(k, (k + t) % N_SEQ) for k in range(N_SEQ)] for t in range(N_SEQ)]
Y_TURNS = [
    [
        (slide_at(z, y, c), slide_at(z, (y + t) % NY, c))
        for z in range(NZ)
        for y in range(NY)
        for c in range(NC)
    ]
    for t in range(NY)
]


def swap(arrays, axis, turns):
    got = {t: lax.ppermute(arrays[t], axis, turns[t]) for t in (2, 1, 3)}
    return [arrays[0], got[1], got[2], got[3]]


def per_device(embeddings, tile_counts, masked_tiles, w_in, norm_gain, w_qkv, w_out):
    inv_count = 1.0 / (lax.axis_size("slide") * masked_tiles.shape[1])
    hidden, normed = call(
        prep_kernel,
        [shape(TOK, D), shape(TOK, D)],
        (embeddings, masked_tiles, norm_gain, w_in),
        [
            pltpu.VMEM((TOK, 2 * D), BF),
            pltpu.VMEM((1, TOK), jnp.int32),
            pltpu.VMEM((D,), F32),
            pltpu.VMEM((2 * D, D), BF),
            pltpu.SemaphoreType.DMA((3 + 2 * D // 256,)),
        ],
        2.0,
        [HBM] * 4,
        60,
    )
    norms = swap([normed] * N_SEQ, "seq", SEQ_TURNS)
    scores = shape(GROUPS, TOK, RATE * TOK, dtype=F32)
    rows = shape(HEADS, TOK, dtype=F32)
    projected, exps, tops, sums, tiles, flag = call(
        near_kernel,
        [shape(TOK, 3 * D), scores, rows, rows, shape(TOK, 2 * D), shape(TOK, TOK, dtype=F32)],
        (tile_counts, normed, w_qkv, embeddings, masked_tiles),
        (),
        5.0,
        [SMEM] + [VMEM] * 4,
    )
    pn, fk, fv, pnear, pfar, attended = call(
        far_kernel,
        [
            shape(N_SEQ, TOK, D),
            shape(TOK, D),
            shape(TOK, D),
            scores,
            shape(GROUPS, TOK, TOK, dtype=F32),
            shape(TOK, D),
        ],
        (tile_counts, *norms, projected, exps, tops, sums, w_qkv),
        [pltpu.VMEM((TOK, D), F32)],
        4.0,
    )
    grad_attended, loss, grad_mixed = call(
        functools.partial(chain_kernel, inv_count),
        [shape(TOK, D), shape(16, 128), shape(TOK, D)],
        (attended, hidden, tiles, flag, w_in, w_out),
        (),
        3.0,
    )
    out_mine, out_other = call(
        out_kernel, [shape(HALF, D)] * 2, (grad_mixed, attended, out_order())
    )
    out_other = lax.ppermute(out_other, "slide", CORE_PAIRS)
    (turned,) = call(
        backward_kernel,
        [shape(SECTIONS, HALF, TOK)],
        (projected, fk, fv, pnear, pfar, grad_attended, spread_order()),
        [pltpu.VMEM((TOK, D), F32)] * 5,
        4.0,
    )
    sent = call(pack_kernel, [shape(XROWS, TOK)] * N_SEQ, (turned, loss, out_mine, out_other))
    got = swap(sent, "seq", SEQ_TURNS)
    mine, other, out = call(
        product_kernel,
        [shape(NY * YROWS, D), shape(NY * YROWS, D), shape(SUB, D)],
        (*got, pn, product_order()),
        [pltpu.VMEM((N_SEQ, MAINROWS, TOK), BF), pltpu.VMEM((6 * SUB, N_SEQ * TOK), BF)],
        3.0,
    )
    other = lax.ppermute(other, "slide", CORE_PAIRS)
    by_y = call(core_kernel, [shape(ALLROWS, D)] * NY, (mine, other, out, out_pad_order()))
    by_y = swap(by_y, "slide", Y_TURNS)
    (by_z,) = call(y_kernel, [shape(NZ, 16, D)], (*by_y, pad_order()))
    by_z = lax.all_to_all(by_z, "slide", 0, 0, tiled=True, axis_index_groups=Z_GROUPS)
    gradients, loss = call(z_kernel, [shape(12, D, dtype=F32), shape(1, 1, dtype=F32)], (by_z,))
    return (gradients, loss[0, 0])


def solution(mesh):
    in_specs = (P("slide", "seq", None), P("slide"), P("slide", None), P(), P(), P(), P())
    out_specs = (P(("slide", "seq"), None), P())
    return jax.shard_map(
        per_device, mesh=mesh, in_specs=in_specs, out_specs=out_specs, check_vma=False
    )
```

```python
import functools
import math

import numpy as np
import jax
import jax.numpy as jnp
from jax import lax
from jax.experimental import pallas as pl
from jax.experimental.pallas import tpu as pltpu
from jax.sharding import PartitionSpec as P

HEADS = 16
RATE = 4
HD = 48
D = 768
TOK = 128
N_SEQ = 4
GROUPS = HEADS // RATE
FAR = TOK // RATE
NORM_EPS = 1e-06
NEG_FILL = -1e30
SCALE = 1.0 / math.sqrt(HD)
BF = jnp.bfloat16
F32 = jnp.float32
HALF = 384
SUB = 96
SECTIONS = 10
YROWS = 80
XROWS = SECTIONS * SUB + 16
NZ, NY, NC = 8, 4, 2


def dot(a, b, dims):
    return lax.dot_general(a, b, (dims, ((), ())), preferred_element_type=F32)


def nn(a, b):
    return dot(a, b, ((1,), (0,)))


def nt(a, b):
    return dot(a, b, ((1,), (1,)))


def tn(a, b):
    return dot(a, b, ((0,), (0,)))


def iota(shape, dim):
    return lax.broadcasted_iota(jnp.int32, shape, dim)


def class_major(index):
    return (index & (FAR - 1)) * RATE + (index >> 5)


def split_rows(value, shape, first):
    high = value.astype(BF).astype(F32)
    rest = value - high
    mid = rest.astype(BF).astype(F32)
    low = rest - mid
    row = iota(shape, 0)
    return jnp.where(
        row == first,
        high,
        jnp.where(row == first + 1, mid, jnp.where(row == first + 2, low, 0.0)),
    )


def class_order():
    shape = (TOK, TOK)
    return (iota(shape, 1) == class_major(iota(shape, 0))).astype(F32).astype(BF)


def masked_rows(positions, masked):
    hits = jnp.where(positions == masked, 1.0, 0.0)
    return jnp.broadcast_to(jnp.max(hits, axis=1, keepdims=True), (TOK, TOK))


def prep_kernel(
    tiles_hbm, masked_hbm, gain_hbm, w_in_hbm, w_qkv_hbm,
    hidden_out, normed_out, proj_out, dilated_out,
    tiles, masked, gain, w_in, w_qkv, sems,
):
    blocks = w_in_hbm.shape[0] // 256
    loads = [
        pltpu.make_async_copy(masked_hbm, masked, sems.at[0]),
        pltpu.make_async_copy(tiles_hbm.at[0], tiles, sems.at[1]),
        pltpu.make_async_copy(gain_hbm, gain, sems.at[2]),
    ]
    chunks = [
        pltpu.make_async_copy(
            w_in_hbm.at[256 * i : 256 * (i + 1)], w_in.at[256 * i : 256 * (i + 1)], sems.at[6 + i]
        )
        for i in range(blocks)
    ]
    parts = [
        pltpu.make_async_copy(
            w_qkv_hbm.at[:, D * i : D * (i + 1)], w_qkv.at[:, D * i : D * (i + 1)], sems.at[3 + i]
        )
        for i in range(3)
    ]
    for copy in loads + chunks + parts[1:] + parts[:1]:
        copy.start()
    order = class_order()
    positions = lax.axis_index("seq") * TOK + iota((TOK, TOK), 0)
    loads[0].wait()
    flag = masked_rows(positions, masked[...])[:, 0:1] > 0.5
    loads[1].wait()
    hidden = jnp.zeros((TOK, D), F32)
    for i in range(blocks):
        cols = slice(256 * i, 256 * (i + 1))
        inputs = jnp.where(flag, jnp.zeros((), BF), tiles[:, cols])
        chunks[i].wait()
        hidden += nn(inputs, w_in[cols])
    hidden_f = nn(order, hidden.astype(BF))
    hidden_out[...] = hidden_f.astype(BF)
    scale_rows = lax.rsqrt(jnp.mean(hidden_f * hidden_f, axis=1, keepdims=True) + NORM_EPS)
    loads[2].wait()
    normed = (hidden_f * scale_rows * gain[...].reshape(1, D)).astype(BF)
    normed_out[...] = normed
    for part in (1, 2, 0):
        parts[part].wait()
        for block in range(D // 256):
            first = part * D + block * 256
            rows = nn(normed, w_qkv[:, first : first + 256]).astype(BF)
            proj_out[:, first : first + 256] = rows
            if part > 0:
                lane_class = ((iota((FAR, 256), 1) + block * 256) // HD) & 3
                pieces = [rows[FAR * r : FAR * (r + 1)] for r in range(RATE)]
                dilated_out[:, first - D : first - D + 256] = by_class(lane_class, pieces)


def window(group):
    return (group * RATE * HD) // 128 * 128


def head_masks(group):
    lane = iota((TOK, 256), 1) + window(group)
    row_class = iota((TOK, 256), 0) >> 5
    masks = []
    for r in range(RATE):
        first = (group * RATE + r) * HD
        masks.append((lane >= first) & (lane < first + HD))
    picked = masks[0] & (row_class == 0)
    for r in range(1, RATE):
        picked = picked | (masks[r] & (row_class == r))
    return masks, picked


def keep(mask, value):
    return jnp.where(mask, value, jnp.zeros((), value.dtype))


def by_class(own_class, pieces):
    out = pieces[0]
    for r in range(1, RATE):
        out = jnp.where(own_class == r, pieces[r], out)
    return out


def near_kernel(
    count_ref, normed_ref, proj_ref, tiles_ref, masked_ref,
    exp_ref, top_ref, sum_ref, tiles_out, flag_ref, late_ref,
):
    count = count_ref[0]
    pos0 = lax.axis_index("seq") * TOK
    flag_ref[...] = masked_rows(pos0 + class_major(iota((TOK, TOK), 0)), masked_ref[...])
    tiles_out[...] = nn(class_order(), tiles_ref[0]).astype(BF)
    late_ref[...] = normed_ref[...]
    square = (TOK, TOK)
    key_pos = pos0 + class_major(iota(square, 0))
    query_pos = pos0 + class_major(iota(square, 1))
    near_ok = (key_pos < count) | (key_pos == query_pos)
    for g in range(GROUPS):
        lo = window(g)
        masks, _ = head_masks(g)
        q = proj_ref[:, lo : lo + 256]
        k = proj_ref[:, D + lo : D + lo + 256]
        near = nt(k, jnp.concatenate([keep(m, q) for m in masks], 0))
        for r in range(RATE):
            head = g * RATE + r
            scores = jnp.where(near_ok, near[:, TOK * r : TOK * (r + 1)] * SCALE, NEG_FILL)
            top = jnp.max(scores, axis=0, keepdims=True)
            exps = jnp.exp(scores - top)
            exp_ref[g, :, TOK * r : TOK * (r + 1)] = exps
            top_ref[head : head + 1] = top
            sum_ref[head : head + 1] = jnp.sum(exps, axis=0, keepdims=True)


def far_kernel(
    count_ref, f0, f1, f2, f3, proj_ref, exp_ref, top_ref, sum_ref,
    fk_ref, fv_ref, pnear_ref, pfar_ref, att_ref,
    att_acc,
):
    count = count_ref[0]
    seq = lax.axis_index("seq")
    for turn, ref in enumerate((f0, f1, f2, f3)):
        rows = pl.ds(pl.multiple_of(((seq - turn) & 3) * FAR, FAR), FAR)
        fk_ref[rows] = ref[:, 0:D]
        fv_ref[rows] = ref[:, D:]

    square = (TOK, TOK)
    far_row = iota(square, 0)
    far_ok = (far_row >> 5) * TOK + (far_row & (FAR - 1)) * RATE + (iota(square, 1) >> 5) < count
    own_class = iota((1, TOK), 1) >> 5

    att_acc[...] = jnp.zeros_like(att_acc)
    for g in range(GROUPS):
        lo = window(g)
        win = slice(lo, lo + 256)
        masks, picked = head_masks(g)
        q = proj_ref[:, lo : lo + 256]
        v = proj_ref[:, 2 * D + lo : 2 * D + lo + 256]
        far = jnp.where(far_ok, nt(fk_ref[:, win], keep(picked, q)) * SCALE, NEG_FILL)
        heads = range(g * RATE, (g + 1) * RATE)
        near_tops = [top_ref[h : h + 1] for h in heads]
        near_sums = [sum_ref[h : h + 1] for h in heads]
        top = jnp.maximum(jnp.max(far, axis=0, keepdims=True), by_class(own_class, near_tops))
        shrink = jnp.exp(by_class(own_class, near_tops) - top)
        far_exp = jnp.exp(far - top)
        total = by_class(own_class, near_sums) * shrink + jnp.sum(far_exp, axis=0, keepdims=True)
        far_probs = far_exp / total
        probs = []
        for r in range(RATE):
            factor = jnp.where(own_class == r, shrink / total, 1.0 / near_sums[r])
            probs.append(exp_ref[g, :, TOK * r : TOK * (r + 1)] * factor)
            pnear_ref[g, :, TOK * r : TOK * (r + 1)] = probs[r]
        pfar_ref[g] = far_probs
        att = tn(
            jnp.concatenate([p.astype(BF) for p in probs], 0),
            jnp.concatenate([keep(m, v) for m in masks], 0),
        )
        att_acc[:, win] += att + keep(picked, tn(far_probs.astype(BF), fv_ref[:, win]))
    att_ref[...] = att_acc[...].astype(BF)


def chain_kernel(
    inv_count,
    att_ref, hidden_ref, tiles_ref, flag_ref, w_in_ref, w_out_ref, order_ref,
    ga_ref, loss_ref, mine_ref, other_ref,
):
    core = lax.axis_index("slide") & 1
    attended = att_ref[...]
    mixed = (hidden_ref[...].astype(F32) + nn(attended, w_out_ref[...])).astype(BF)
    flag = flag_ref[:, 0:1] > 0.5
    error = jnp.where(flag, nt(mixed, w_in_ref[...]) - tiles_ref[...].astype(F32), 0.0)
    loss = jnp.sum(jnp.sum(error * error, axis=1, keepdims=True), axis=0, keepdims=True) * inv_count
    loss_ref[...] = split_rows(jnp.broadcast_to(loss, (16, 128)), (16, 128), 0).astype(BF)
    grad_pred = (2.0 * inv_count * error).astype(BF)
    grad_mixed = nn(grad_pred, w_in_ref[...]).astype(BF)
    ga_ref[...] = nt(grad_mixed, w_out_ref[...]).astype(BF)
    for turn, ref in enumerate((mine_ref, other_ref)):
        first = pl.multiple_of(((core + turn) & 1) * HALF, HALF)
        left = nt(order_ref[pl.ds(first, HALF)], grad_mixed).astype(BF)
        ref[...] = nn(left, attended).astype(BF)


def backward_kernel(
    proj_ref, fk_ref, fv_ref, pnear_ref, pfar_ref, ga_ref, loss_ref, spread_ref, wait1, wait2, wait3,
    x0, x1, x2, x3,
    gq, gk, gv, gkf, gvf, turned,
):
    seq = lax.axis_index("seq")
    own_class = iota((1, TOK), 1) >> 5
    for ref in (gq, gk, gv, gkf, gvf):
        ref[...] = jnp.zeros_like(ref)
    for g in range(GROUPS):
        lo = window(g)
        win = slice(lo, lo + 256)
        masks, picked = head_masks(g)
        q = proj_ref[:, lo : lo + 256]
        k = proj_ref[:, D + lo : D + lo + 256]
        v = proj_ref[:, 2 * D + lo : 2 * D + lo + 256]
        ga = ga_ref[:, win]
        fk = fk_ref[:, win]
        fv = fv_ref[:, win]
        ga_stack = jnp.concatenate([keep(m, ga) for m in masks], 0)
        ga_picked = keep(picked, ga)
        near = nt(v, ga_stack)
        far = nt(fv, ga_picked)
        probs = [pnear_ref[g, :, TOK * r : TOK * (r + 1)] for r in range(RATE)]
        far_probs = pfar_ref[g]
        far_dot = jnp.sum(far_probs * far, axis=0, keepdims=True)
        grads = [near[:, TOK * r : TOK * (r + 1)] for r in range(RATE)]
        dots = []
        for r in range(RATE):
            own = jnp.sum(probs[r] * grads[r], axis=0, keepdims=True)
            dots.append(jnp.where(own_class == r, own + far_dot, own))
        scores = [(probs[r] * (grads[r] - dots[r]) * SCALE).astype(BF) for r in range(RATE)]
        far_scores = (far_probs * (far - by_class(own_class, dots)) * SCALE).astype(BF)
        gq[:, win] += tn(
            jnp.concatenate(scores, 0), jnp.concatenate([keep(m, k) for m in masks], 0)
        ) + keep(picked, tn(far_scores, fk))
        gk[:, win] += nn(
            jnp.concatenate(scores, 1), jnp.concatenate([keep(m, q) for m in masks], 0)
        )
        gv[:, win] += nn(jnp.concatenate([p.astype(BF) for p in probs], 1), ga_stack)
        gkf[:, win] += nn(far_scores, keep(picked, q))
        gvf[:, win] += nn(far_probs.astype(BF), ga_picked)
    place = spread_ref[...]
    section = 0
    for value in (gq, gk, gv, gkf, gvf):
        for half in range(2):
            piece = value[:, half * HALF : (half + 1) * HALF].astype(BF)
            turned[section] = nt(place, piece).astype(BF)
            section += 1
    for turn, ref in enumerate((x0, x1, x2, x3)):
        first = pl.multiple_of(((seq + turn) & 3) * SUB, 16)
        for section in range(SECTIONS):
            ref[section * SUB : (section + 1) * SUB] = turned[section, pl.ds(first, SUB)]
        ref[SECTIONS * SUB :] = loss_ref[...]


def product_kernel(
    x0, x1, x2, x3, n0, n1, n2, n3, order_ref, wait_ref, mine_ref, other_ref, got, left, right
):
    seq = lax.axis_index("seq")
    core = lax.axis_index("slide") & 1
    for turn, (x_ref, n_ref) in enumerate(zip((x0, x1, x2, x3), (n0, n1, n2, n3))):
        src = (seq - turn) & 3
        got[src] = x_ref[...]
        right[pl.ds(pl.multiple_of(src * TOK, TOK), TOK)] = n_ref[...]
    for src in range(N_SEQ):
        left[0 : 2 * SUB, src * TOK : (src + 1) * TOK] = got[src, 0 : 2 * SUB]
    shape = (SUB, TOK)
    row = iota(shape, 0)
    lane_class = iota(shape, 1) >> 5
    core_row = jnp.where(row >= 48, 1, 0)
    row_y = (row - 48 * core_row) // 12
    row_class = ((row_y & 1) << 1) + core_row
    spots = [(row_class == r) & (lane_class == r) for r in range(RATE)]
    for part in range(2):
        for half in range(2):
            near_at = (2 + 2 * part + half) * SUB
            far_at = (6 + 2 * part + half) * SUB
            far = got[0, far_at : far_at + SUB].astype(F32)
            for src in range(1, N_SEQ):
                far = far + got[src, far_at : far_at + SUB].astype(F32)
            turns = [far] + [pltpu.roll(far, FAR * t, 1) for t in range(1, RATE)]
            for src in range(N_SEQ):
                total = got[src, near_at : near_at + SUB].astype(F32)
                for r in range(RATE):
                    total = total + jnp.where(spots[r], turns[(r - src) & 3], 0.0)
                left[near_at : near_at + SUB, src * TOK : (src + 1) * TOK] = total.astype(BF)
    whole = nn(left[...], right[...]).astype(BF)
    loss = got[0, SECTIONS * SUB :].astype(F32)
    for src in range(1, N_SEQ):
        loss = loss + got[src, SECTIONS * SUB :].astype(F32)
    loss = jnp.sum(loss, axis=0, keepdims=True)[:, 0:1]
    tail = split_rows(jnp.broadcast_to(loss, (YROWS, D)), (YROWS, D), 72)
    for turn, ref in enumerate((mine_ref, other_ref)):
        first = pl.multiple_of(((core + turn) & 1) * NY * YROWS, NY * YROWS)
        half = nn(order_ref[pl.ds(first, NY * YROWS)], whole)
        for y in range(NY):
            rows = slice(y * YROWS, (y + 1) * YROWS)
            ref[rows] = (half[rows] + tail).astype(BF)


def resplit(total):
    row = iota(total.shape, 0)
    loss = jnp.sum(jnp.where(row >= 72, total, 0.0), axis=0, keepdims=True)
    pieces = split_rows(jnp.broadcast_to(loss, total.shape), total.shape, 72)
    return jnp.where(row >= 72, pieces, total), loss


def core_kernel(mine_ref, other_ref, wait1, wait2, wait3, y0, y1, y2, y3):
    y = (lax.axis_index("slide") >> 1) & 3
    for turn, ref in enumerate((y0, y1, y2, y3)):
        rows = pl.ds(pl.multiple_of(((y + turn) & 3) * YROWS, 16), YROWS)
        ref[...] = resplit(mine_ref[rows].astype(F32) + other_ref[rows].astype(F32))[0].astype(BF)


def y_kernel(y0, y1, y2, y3, o0, o1, o2, o3, order_ref, out_ref):
    total = y0[...].astype(F32) + y1[...].astype(F32) + y2[...].astype(F32) + y3[...].astype(F32)
    total, loss = resplit(total)
    out_ref[0:6] = nn(order_ref[...], total.astype(BF)).astype(BF).reshape(6, 16, D)
    out = o0[...].astype(F32) + o1[...].astype(F32) + o2[...].astype(F32) + o3[...].astype(F32)
    tail = split_rows(jnp.broadcast_to(loss, (16, D)), (16, D), 12)
    for half in range(2):
        out_ref[6 + half] = (out[16 * half : 16 * (half + 1)] + tail).astype(BF)


def out_core_kernel(mine_ref, other_ref, wait_ref, y0, y1, y2, y3):
    y = (lax.axis_index("slide") >> 1) & 3
    for turn, ref in enumerate((y0, y1, y2, y3)):
        rows = pl.ds(pl.multiple_of(((y + turn) & 3) * SUB, 16), SUB)
        ref[...] = (mine_ref[rows].astype(F32) + other_ref[rows].astype(F32)).astype(BF)


def out_y_kernel(y0, y1, y2, y3, order_ref, x0, x1, x2, x3):
    seq = lax.axis_index("seq")
    total = y0[...].astype(F32) + y1[...].astype(F32) + y2[...].astype(F32) + y3[...].astype(F32)
    total = total.astype(BF)
    for turn, ref in enumerate((x0, x1, x2, x3)):
        rows = pl.ds(pl.multiple_of(((seq + turn) & 3) * 32, 32), 32)
        ref[...] = nn(order_ref[rows], total).astype(BF)


def z_kernel(in_ref, out_ref, loss_ref):
    total = in_ref[0].astype(F32)
    for src in range(1, NZ):
        total = total + in_ref[src].astype(F32)
    out_ref[...] = total[0:12]
    loss_ref[...] = jnp.sum(total[12:15, 0:1], axis=0, keepdims=True)


def spread_order():
    place = np.zeros((HALF, HALF), np.float32)
    for row in range(HALF):
        j, rest = divmod(row, SUB)
        c, rest = divmod(rest, 48)
        y, r = divmod(rest, 12)
        place[row, (y * NC + c) * HD + j * 12 + r] = 1.0
    return jnp.asarray(place, BF)


def product_order():
    place = np.zeros((NC * NY * YROWS, 6 * SUB), np.float32)
    for c in range(NC):
        for y in range(NY):
            for z in range(6):
                for r in range(12):
                    place[(c * NY + y) * YROWS + z * 12 + r, z * SUB + c * 48 + y * 12 + r] = 1.0
    return jnp.asarray(place, BF)


def out_order():
    place = np.zeros((D, D), np.float32)
    row = 0
    for c in range(NC):
        for y in range(NY):
            for j in range(N_SEQ):
                for half in range(2):
                    for r in range(12):
                        place[row, (half * 8 + y * NC + c) * HD + j * 12 + r] = 1.0
                        row += 1
    return jnp.asarray(place, BF)


def out_pad_order():
    place = np.zeros((N_SEQ * 32, SUB), np.float32)
    for j in range(N_SEQ):
        for half in range(2):
            for r in range(12):
                place[j * 32 + half * 16 + r, j * 24 + half * 12 + r] = 1.0
    return jnp.asarray(place, BF)


def pad_order():
    place = np.zeros((SUB, YROWS), np.float32)
    for z in range(6):
        for r in range(12):
            place[z * 16 + r, z * 12 + r] = 1.0
        for r in range(3):
            place[z * 16 + 12 + r, 72 + r] = 1.0
    return jnp.asarray(place, BF)


SMEM = pl.BlockSpec(memory_space=pltpu.SMEM)
VMEM = pl.BlockSpec(memory_space=pltpu.VMEM)
HBM = pl.BlockSpec(memory_space=pltpu.HBM)
ANY = pl.BlockSpec(memory_space=pl.ANY)


def call(kernel, out_shapes, args, scratch=(), micros=1.0, specs=None, grant=24, unread=0):
    if specs is None:
        specs = [SMEM if a.dtype == jnp.int32 else VMEM for a in args]
        specs = specs[: len(specs) - unread] + [ANY] * unread
    return pl.pallas_call(
        kernel,
        out_shape=out_shapes,
        in_specs=specs,
        out_specs=[VMEM] * len(out_shapes),
        scratch_shapes=list(scratch),
        compiler_params=pltpu.CompilerParams(vmem_limit_bytes=grant * 1024 * 1024),
        cost_estimate=pl.CostEstimate(
            flops=int(micros * 1.0e9), bytes_accessed=int(micros * 1.0e6), transcendentals=0
        ),
    )(*args)


def shape(*dims, dtype=BF):
    return jax.ShapeDtypeStruct(dims, dtype)


def slide_at(z, y, c):
    return (z * NY + y) * NC + c


CORE_PAIRS = [(i, i ^ 1) for i in range(NZ * NY * NC)]
Z_GROUPS = [[slide_at(z, y, c) for z in range(NZ)] for y in range(NY) for c in range(NC)]
SEQ_TURNS = [[(k, (k + t) % N_SEQ) for k in range(N_SEQ)] for t in range(N_SEQ)]
Y_TURNS = [
    [
        (slide_at(z, y, c), slide_at(z, (y + t) % NY, c))
        for z in range(NZ)
        for y in range(NY)
        for c in range(NC)
    ]
    for t in range(NY)
]


def swap(arrays, axis, turns):
    return [arrays[0]] + [lax.ppermute(arrays[t], axis, turns[t]) for t in range(1, len(arrays))]


def per_device(embeddings, tile_counts, masked_tiles, w_in, norm_gain, w_qkv, w_out):
    inv_count = 1.0 / (lax.axis_size("slide") * masked_tiles.shape[1])
    hidden, normed, projected, dilated = call(
        prep_kernel,
        [shape(TOK, D), shape(TOK, D), shape(TOK, 3 * D), shape(FAR, 2 * D)],
        (embeddings, masked_tiles, norm_gain, w_in, w_qkv),
        [
            pltpu.VMEM((TOK, 2 * D), BF),
            pltpu.VMEM((1, TOK), jnp.int32),
            pltpu.VMEM((D,), F32),
            pltpu.VMEM((2 * D, D), BF),
            pltpu.VMEM((D, 3 * D), BF),
            pltpu.SemaphoreType.DMA((6 + 2 * D // 256,)),
        ],
        4.0,
        [HBM] * 5,
        60,
    )
    fars = swap([dilated] * N_SEQ, "seq", SEQ_TURNS)
    scores = shape(GROUPS, TOK, RATE * TOK, dtype=F32)
    rows = shape(HEADS, TOK, dtype=F32)
    exps, tops, sums, tiles, flag, late = call(
        near_kernel,
        [scores, rows, rows, shape(TOK, 2 * D), shape(TOK, TOK, dtype=F32), shape(TOK, D)],
        (tile_counts, normed, projected, embeddings, masked_tiles),
        (),
        5.0,
        [SMEM] + [VMEM] * 4,
    )
    norms = swap([late] * N_SEQ, "seq", SEQ_TURNS)
    fk, fv, pnear, pfar, attended = call(
        far_kernel,
        [shape(TOK, D), shape(TOK, D), scores, shape(GROUPS, TOK, TOK, dtype=F32), shape(TOK, D)],
        (tile_counts, *fars, projected, exps, tops, sums),
        [pltpu.VMEM((TOK, D), F32)],
        10.0,
    )
    grad_attended, loss, out_mine, out_other = call(
        functools.partial(chain_kernel, inv_count),
        [shape(TOK, D), shape(16, 128), shape(HALF, D), shape(HALF, D)],
        (attended, hidden, tiles, flag, w_in, w_out, out_order()),
        (),
        15.0,
    )
    out_other = lax.ppermute(out_other, "slide", CORE_PAIRS)
    sent = call(
        backward_kernel,
        [shape(XROWS, TOK)] * N_SEQ,
        (projected, fk, fv, pnear, pfar, grad_attended, loss, spread_order(), *norms[1:]),
        [pltpu.VMEM((TOK, D), F32)] * 5 + [pltpu.VMEM((SECTIONS, HALF, TOK), BF)],
        8.0,
        unread=3,
    )
    got = swap(sent, "seq", SEQ_TURNS)
    out = call(out_core_kernel, [shape(SUB, D)] * NY, (out_mine, out_other, sent[0]), unread=1)
    out = swap(out, "slide", Y_TURNS)
    out_sums = call(out_y_kernel, [shape(32, D)] * N_SEQ, (*out, out_pad_order()))
    out = swap(out_sums, "seq", SEQ_TURNS)
    mine, other = call(
        product_kernel,
        [shape(NY * YROWS, D)] * 2,
        (*got, *norms, product_order(), out_sums[0]),
        [
            pltpu.VMEM((N_SEQ, XROWS, TOK), BF),
            pltpu.VMEM((6 * SUB, N_SEQ * TOK), BF),
            pltpu.VMEM((N_SEQ * TOK, D), BF),
        ],
        3.0,
        unread=1,
    )
    other = lax.ppermute(other, "slide", CORE_PAIRS)
    by_y = call(core_kernel, [shape(YROWS, D)] * NY, (mine, other, *out[1:]), unread=3)
    by_y = swap(by_y, "slide", Y_TURNS)
    (by_z,) = call(y_kernel, [shape(NZ, 16, D)], (*by_y, *out, pad_order()))
    by_z = lax.all_to_all(by_z, "slide", 0, 0, tiled=True, axis_index_groups=Z_GROUPS)
    gradients, loss = call(z_kernel, [shape(12, D, dtype=F32), shape(1, 1, dtype=F32)], (by_z,))
    return (gradients, loss[0, 0])


def solution(mesh):
    in_specs = (P("slide", "seq", None), P("slide"), P("slide", None), P(), P(), P(), P())
    out_specs = (P(("slide", "seq"), None), P())
    return jax.shard_map(
        per_device, mesh=mesh, in_specs=in_specs, out_specs=out_specs, check_vma=False
    )
```

```python
import functools
import math

import numpy as np
import jax
import jax.numpy as jnp
from jax import lax
from jax.experimental import pallas as pl
from jax.experimental.pallas import tpu as pltpu
from jax.sharding import PartitionSpec as P

HEADS = 16
RATE = 4
HD = 48
D = 768
TOK = 128
N_SEQ = 4
GROUPS = HEADS // RATE
FAR = TOK // RATE
NORM_EPS = 1e-06
NEG_FILL = -1e30
SCALE = 1.0 / math.sqrt(HD)
BF = jnp.bfloat16
F32 = jnp.float32
HALF = 384
SUB = 96
SECTIONS = 10
YROWS = 80
XROWS = SECTIONS * SUB + 16
NZ, NY, NC = 8, 4, 2


def dot(a, b, dims):
    return lax.dot_general(a, b, (dims, ((), ())), preferred_element_type=F32)


def nn(a, b):
    return dot(a, b, ((1,), (0,)))


def nt(a, b):
    return dot(a, b, ((1,), (1,)))


def tn(a, b):
    return dot(a, b, ((0,), (0,)))


def iota(shape, dim):
    return lax.broadcasted_iota(jnp.int32, shape, dim)


def class_major(index):
    return (index & (FAR - 1)) * RATE + (index >> 5)


def split_rows(value, shape, first):
    high = value.astype(BF).astype(F32)
    rest = value - high
    mid = rest.astype(BF).astype(F32)
    low = rest - mid
    row = iota(shape, 0)
    return jnp.where(
        row == first,
        high,
        jnp.where(row == first + 1, mid, jnp.where(row == first + 2, low, 0.0)),
    )


def class_order():
    shape = (TOK, TOK)
    return (iota(shape, 1) == class_major(iota(shape, 0))).astype(F32).astype(BF)


def masked_rows(positions, masked):
    hits = jnp.where(positions == masked, 1.0, 0.0)
    return jnp.broadcast_to(jnp.max(hits, axis=1, keepdims=True), (TOK, TOK))


def prep_kernel(
    tiles_hbm, masked_hbm, gain_hbm, w_in_hbm, w_qkv_hbm,
    hidden_out, normed_out, proj_out, dilated_out,
    tiles, masked, gain, w_in, w_qkv, sems,
):
    blocks = w_in_hbm.shape[0] // 256
    loads = [
        pltpu.make_async_copy(masked_hbm, masked, sems.at[0]),
        pltpu.make_async_copy(tiles_hbm.at[0], tiles, sems.at[1]),
        pltpu.make_async_copy(gain_hbm, gain, sems.at[2]),
    ]
    chunks = [
        pltpu.make_async_copy(
            w_in_hbm.at[256 * i : 256 * (i + 1)], w_in.at[256 * i : 256 * (i + 1)], sems.at[6 + i]
        )
        for i in range(blocks)
    ]
    parts = [
        pltpu.make_async_copy(
            w_qkv_hbm.at[:, D * i : D * (i + 1)], w_qkv.at[:, D * i : D * (i + 1)], sems.at[3 + i]
        )
        for i in range(3)
    ]
    for copy in loads + chunks + parts[1:] + parts[:1]:
        copy.start()
    order = class_order()
    positions = lax.axis_index("seq") * TOK + iota((TOK, TOK), 0)
    loads[0].wait()
    flag = masked_rows(positions, masked[...])[:, 0:1] > 0.5
    loads[1].wait()
    hidden = jnp.zeros((TOK, D), F32)
    for i in range(blocks):
        cols = slice(256 * i, 256 * (i + 1))
        inputs = jnp.where(flag, jnp.zeros((), BF), tiles[:, cols])
        chunks[i].wait()
        hidden += nn(inputs, w_in[cols])
    hidden_f = nn(order, hidden.astype(BF))
    hidden_out[...] = hidden_f.astype(BF)
    scale_rows = lax.rsqrt(jnp.mean(hidden_f * hidden_f, axis=1, keepdims=True) + NORM_EPS)
    loads[2].wait()
    normed = (hidden_f * scale_rows * gain[...].reshape(1, D)).astype(BF)
    normed_out[...] = normed
    for part in (1, 2, 0):
        parts[part].wait()
        for block in range(D // 256):
            first = part * D + block * 256
            rows = nn(normed, w_qkv[:, first : first + 256]).astype(BF)
            proj_out[:, first : first + 256] = rows
            if part > 0:
                lane_class = ((iota((FAR, 256), 1) + block * 256) // HD) & 3
                pieces = [rows[FAR * r : FAR * (r + 1)] for r in range(RATE)]
                dilated_out[:, first - D : first - D + 256] = by_class(lane_class, pieces)


def window(group):
    return (group * RATE * HD) // 128 * 128


def head_masks(group):
    lane = iota((TOK, 256), 1) + window(group)
    row_class = iota((TOK, 256), 0) >> 5
    masks = []
    for r in range(RATE):
        first = (group * RATE + r) * HD
        masks.append((lane >= first) & (lane < first + HD))
    picked = masks[0] & (row_class == 0)
    for r in range(1, RATE):
        picked = picked | (masks[r] & (row_class == r))
    return masks, picked


def keep(mask, value):
    return jnp.where(mask, value, jnp.zeros((), value.dtype))


def by_class(own_class, pieces):
    out = pieces[0]
    for r in range(1, RATE):
        out = jnp.where(own_class == r, pieces[r], out)
    return out


def near_kernel(
    count_ref, proj_ref, tiles_ref, masked_ref,
    exp_ref, top_ref, sum_ref, tiles_out, flag_ref,
):
    count = count_ref[0]
    pos0 = lax.axis_index("seq") * TOK
    flag_ref[...] = masked_rows(pos0 + class_major(iota((TOK, TOK), 0)), masked_ref[...])
    tiles_out[...] = nn(class_order(), tiles_ref[0]).astype(BF)
    square = (TOK, TOK)
    key_pos = pos0 + class_major(iota(square, 0))
    query_pos = pos0 + class_major(iota(square, 1))
    near_ok = (key_pos < count) | (key_pos == query_pos)
    for g in range(GROUPS):
        lo = window(g)
        masks, _ = head_masks(g)
        q = proj_ref[:, lo : lo + 256]
        k = proj_ref[:, D + lo : D + lo + 256]
        near = nt(k, jnp.concatenate([keep(m, q) for m in masks], 0))
        for r in range(RATE):
            head = g * RATE + r
            scores = jnp.where(near_ok, near[:, TOK * r : TOK * (r + 1)] * SCALE, NEG_FILL)
            top = jnp.max(scores, axis=0, keepdims=True)
            exps = jnp.exp(scores - top)
            exp_ref[g, :, TOK * r : TOK * (r + 1)] = exps
            top_ref[head : head + 1] = top
            sum_ref[head : head + 1] = jnp.sum(exps, axis=0, keepdims=True)


def far_kernel(
    count_ref, f0, f1, f2, f3, proj_ref, exp_ref, top_ref, sum_ref,
    fk_ref, fv_ref, pnear_ref, pfar_ref, att_ref,
    att_acc,
):
    count = count_ref[0]
    seq = lax.axis_index("seq")
    for turn, ref in enumerate((f0, f1, f2, f3)):
        rows = pl.ds(pl.multiple_of(((seq - turn) & 3) * FAR, FAR), FAR)
        fk_ref[rows] = ref[:, 0:D]
        fv_ref[rows] = ref[:, D:]

    square = (TOK, TOK)
    far_row = iota(square, 0)
    far_ok = (far_row >> 5) * TOK + (far_row & (FAR - 1)) * RATE + (iota(square, 1) >> 5) < count
    own_class = iota((1, TOK), 1) >> 5

    att_acc[...] = jnp.zeros_like(att_acc)
    for g in range(GROUPS):
        lo = window(g)
        win = slice(lo, lo + 256)
        masks, picked = head_masks(g)
        q = proj_ref[:, lo : lo + 256]
        v = proj_ref[:, 2 * D + lo : 2 * D + lo + 256]
        far = jnp.where(far_ok, nt(fk_ref[:, win], keep(picked, q)) * SCALE, NEG_FILL)
        heads = range(g * RATE, (g + 1) * RATE)
        near_tops = [top_ref[h : h + 1] for h in heads]
        near_sums = [sum_ref[h : h + 1] for h in heads]
        top = jnp.maximum(jnp.max(far, axis=0, keepdims=True), by_class(own_class, near_tops))
        shrink = jnp.exp(by_class(own_class, near_tops) - top)
        far_exp = jnp.exp(far - top)
        total = by_class(own_class, near_sums) * shrink + jnp.sum(far_exp, axis=0, keepdims=True)
        far_probs = far_exp / total
        probs = []
        for r in range(RATE):
            factor = jnp.where(own_class == r, shrink / total, 1.0 / near_sums[r])
            probs.append(exp_ref[g, :, TOK * r : TOK * (r + 1)] * factor)
            pnear_ref[g, :, TOK * r : TOK * (r + 1)] = probs[r]
        pfar_ref[g] = far_probs
        att = tn(
            jnp.concatenate([p.astype(BF) for p in probs], 0),
            jnp.concatenate([keep(m, v) for m in masks], 0),
        )
        att_acc[:, win] += att + keep(picked, tn(far_probs.astype(BF), fv_ref[:, win]))
    att_ref[...] = att_acc[...].astype(BF)


def chain_kernel(
    inv_count,
    att_ref, hidden_ref, tiles_ref, flag_ref, w_in_ref, w_out_ref, order_ref,
    ga_ref, loss_ref, mine_ref, other_ref,
):
    core = lax.axis_index("slide") & 1
    attended = att_ref[...]
    mixed = (hidden_ref[...].astype(F32) + nn(attended, w_out_ref[...])).astype(BF)
    flag = flag_ref[:, 0:1] > 0.5
    error = jnp.where(flag, nt(mixed, w_in_ref[...]) - tiles_ref[...].astype(F32), 0.0)
    loss = jnp.sum(jnp.sum(error * error, axis=1, keepdims=True), axis=0, keepdims=True) * inv_count
    loss_ref[...] = split_rows(jnp.broadcast_to(loss, (16, 128)), (16, 128), 0).astype(BF)
    grad_pred = (2.0 * inv_count * error).astype(BF)
    grad_mixed = nn(grad_pred, w_in_ref[...]).astype(BF)
    ga_ref[...] = nt(grad_mixed, w_out_ref[...]).astype(BF)
    for turn, ref in enumerate((mine_ref, other_ref)):
        first = pl.multiple_of(((core + turn) & 1) * HALF, HALF)
        left = nt(order_ref[pl.ds(first, HALF)], grad_mixed).astype(BF)
        ref[...] = nn(left, attended).astype(BF)


def backward_kernel(
    proj_ref, fk_ref, fv_ref, pnear_ref, pfar_ref, ga_ref, loss_ref, spread_ref,
    x0, x1, x2, x3,
    gq, gk, gv, gkf, gvf, turned,
):
    seq = lax.axis_index("seq")
    own_class = iota((1, TOK), 1) >> 5
    for ref in (gq, gk, gv, gkf, gvf):
        ref[...] = jnp.zeros_like(ref)
    for g in range(GROUPS):
        lo = window(g)
        win = slice(lo, lo + 256)
        masks, picked = head_masks(g)
        q = proj_ref[:, lo : lo + 256]
        k = proj_ref[:, D + lo : D + lo + 256]
        v = proj_ref[:, 2 * D + lo : 2 * D + lo + 256]
        ga = ga_ref[:, win]
        fk = fk_ref[:, win]
        fv = fv_ref[:, win]
        ga_stack = jnp.concatenate([keep(m, ga) for m in masks], 0)
        ga_picked = keep(picked, ga)
        near = nt(v, ga_stack)
        far = nt(fv, ga_picked)
        probs = [pnear_ref[g, :, TOK * r : TOK * (r + 1)] for r in range(RATE)]
        far_probs = pfar_ref[g]
        far_dot = jnp.sum(far_probs * far, axis=0, keepdims=True)
        grads = [near[:, TOK * r : TOK * (r + 1)] for r in range(RATE)]
        dots = []
        for r in range(RATE):
            own = jnp.sum(probs[r] * grads[r], axis=0, keepdims=True)
            dots.append(jnp.where(own_class == r, own + far_dot, own))
        scores = [(probs[r] * (grads[r] - dots[r]) * SCALE).astype(BF) for r in range(RATE)]
        far_scores = (far_probs * (far - by_class(own_class, dots)) * SCALE).astype(BF)
        gq[:, win] += tn(
            jnp.concatenate(scores, 0), jnp.concatenate([keep(m, k) for m in masks], 0)
        ) + keep(picked, tn(far_scores, fk))
        gk[:, win] += nn(
            jnp.concatenate(scores, 1), jnp.concatenate([keep(m, q) for m in masks], 0)
        )
        gv[:, win] += nn(jnp.concatenate([p.astype(BF) for p in probs], 1), ga_stack)
        gkf[:, win] += nn(far_scores, keep(picked, q))
        gvf[:, win] += nn(far_probs.astype(BF), ga_picked)
    place = spread_ref[...]
    section = 0
    for value in (gq, gk, gv, gkf, gvf):
        for half in range(2):
            piece = value[:, half * HALF : (half + 1) * HALF].astype(BF)
            turned[section] = nt(place, piece).astype(BF)
            section += 1
    for turn, ref in enumerate((x0, x1, x2, x3)):
        first = pl.multiple_of(((seq + turn) & 3) * SUB, 16)
        for section in range(SECTIONS):
            ref[section * SUB : (section + 1) * SUB] = turned[section, pl.ds(first, SUB)]
        ref[SECTIONS * SUB :] = loss_ref[...]


def product_kernel(
    x0, x1, x2, x3, n0, n1, n2, n3, wait_ref, whole_ref, tail_ref, got, left, right
):
    seq = lax.axis_index("seq")
    for turn, (x_ref, n_ref) in enumerate(zip((x0, x1, x2, x3), (n0, n1, n2, n3))):
        src = (seq - turn) & 3
        got[src] = x_ref[...]
        right[pl.ds(pl.multiple_of(src * TOK, TOK), TOK)] = n_ref[...]
    for src in range(N_SEQ):
        left[0 : 2 * SUB, src * TOK : (src + 1) * TOK] = got[src, 0 : 2 * SUB]
    shape = (SUB, TOK)
    row = iota(shape, 0)
    lane_class = iota(shape, 1) >> 5
    core_row = jnp.where(row >= 48, 1, 0)
    row_y = (row - 48 * core_row) // 12
    row_class = ((row_y & 1) << 1) + core_row
    spots = [(row_class == r) & (lane_class == r) for r in range(RATE)]
    for part in range(2):
        for half in range(2):
            near_at = (2 + 2 * part + half) * SUB
            far_at = (6 + 2 * part + half) * SUB
            far = got[0, far_at : far_at + SUB].astype(F32)
            for src in range(1, N_SEQ):
                far = far + got[src, far_at : far_at + SUB].astype(F32)
            turns = [far] + [pltpu.roll(far, FAR * t, 1) for t in range(1, RATE)]
            for src in range(N_SEQ):
                total = got[src, near_at : near_at + SUB].astype(F32)
                for r in range(RATE):
                    total = total + jnp.where(spots[r], turns[(r - src) & 3], 0.0)
                left[near_at : near_at + SUB, src * TOK : (src + 1) * TOK] = total.astype(BF)
    whole_ref[...] = nn(left[...], right[...]).astype(BF)
    loss = got[0, SECTIONS * SUB :].astype(F32)
    for src in range(1, N_SEQ):
        loss = loss + got[src, SECTIONS * SUB :].astype(F32)
    loss = jnp.sum(loss, axis=0, keepdims=True)[:, 0:1]
    tail_ref[...] = split_rows(jnp.broadcast_to(loss, (YROWS, D)), (YROWS, D), 72)


def place_kernel(whole_ref, tail_ref, order_ref, wait1, wait2, wait3, mine_ref, other_ref):
    core = lax.axis_index("slide") & 1
    whole = whole_ref[...]
    for turn, ref in enumerate((mine_ref, other_ref)):
        first = pl.multiple_of(((core + turn) & 1) * NY * YROWS, NY * YROWS)
        half = nn(order_ref[pl.ds(first, NY * YROWS)], whole)
        for y in range(NY):
            rows = slice(y * YROWS, (y + 1) * YROWS)
            ref[rows] = (half[rows] + tail_ref[...]).astype(BF)


def resplit(total):
    row = iota(total.shape, 0)
    loss = jnp.sum(jnp.where(row >= 72, total, 0.0), axis=0, keepdims=True)
    pieces = split_rows(jnp.broadcast_to(loss, total.shape), total.shape, 72)
    return jnp.where(row >= 72, pieces, total), loss


def core_kernel(mine_ref, other_ref, y0, y1, y2, y3):
    y = (lax.axis_index("slide") >> 1) & 3
    for turn, ref in enumerate((y0, y1, y2, y3)):
        rows = pl.ds(pl.multiple_of(((y + turn) & 3) * YROWS, 16), YROWS)
        ref[...] = resplit(mine_ref[rows].astype(F32) + other_ref[rows].astype(F32))[0].astype(BF)


def y_kernel(y0, y1, y2, y3, o0, o1, o2, o3, order_ref, out_ref):
    total = y0[...].astype(F32) + y1[...].astype(F32) + y2[...].astype(F32) + y3[...].astype(F32)
    total, loss = resplit(total)
    out_ref[0:6] = nn(order_ref[...], total.astype(BF)).astype(BF).reshape(6, 16, D)
    out = o0[...].astype(F32) + o1[...].astype(F32) + o2[...].astype(F32) + o3[...].astype(F32)
    tail = split_rows(jnp.broadcast_to(loss, (16, D)), (16, D), 12)
    for half in range(2):
        out_ref[6 + half] = (out[16 * half : 16 * (half + 1)] + tail).astype(BF)


def out_core_kernel(mine_ref, other_ref, wait0, wait1, wait2, wait3, y0, y1, y2, y3):
    y = (lax.axis_index("slide") >> 1) & 3
    for turn, ref in enumerate((y0, y1, y2, y3)):
        rows = pl.ds(pl.multiple_of(((y + turn) & 3) * SUB, 16), SUB)
        ref[...] = (mine_ref[rows].astype(F32) + other_ref[rows].astype(F32)).astype(BF)


def out_y_kernel(y0, y1, y2, y3, order_ref, x0, x1, x2, x3):
    seq = lax.axis_index("seq")
    total = y0[...].astype(F32) + y1[...].astype(F32) + y2[...].astype(F32) + y3[...].astype(F32)
    total = total.astype(BF)
    for turn, ref in enumerate((x0, x1, x2, x3)):
        rows = pl.ds(pl.multiple_of(((seq + turn) & 3) * 32, 32), 32)
        ref[...] = nn(order_ref[rows], total).astype(BF)


def z_kernel(in_ref, out_ref, loss_ref):
    total = in_ref[0].astype(F32)
    for src in range(1, NZ):
        total = total + in_ref[src].astype(F32)
    out_ref[...] = total[0:12]
    loss_ref[...] = jnp.sum(total[12:15, 0:1], axis=0, keepdims=True)


def spread_order():
    place = np.zeros((HALF, HALF), np.float32)
    for row in range(HALF):
        j, rest = divmod(row, SUB)
        c, rest = divmod(rest, 48)
        y, r = divmod(rest, 12)
        place[row, (y * NC + c) * HD + j * 12 + r] = 1.0
    return jnp.asarray(place, BF)


def product_order():
    place = np.zeros((NC * NY * YROWS, 6 * SUB), np.float32)
    for c in range(NC):
        for y in range(NY):
            for z in range(6):
                for r in range(12):
                    place[(c * NY + y) * YROWS + z * 12 + r, z * SUB + c * 48 + y * 12 + r] = 1.0
    return jnp.asarray(place, BF)


def out_order():
    place = np.zeros((D, D), np.float32)
    row = 0
    for c in range(NC):
        for y in range(NY):
            for j in range(N_SEQ):
                for half in range(2):
                    for r in range(12):
                        place[row, (half * 8 + y * NC + c) * HD + j * 12 + r] = 1.0
                        row += 1
    return jnp.asarray(place, BF)


def out_pad_order():
    place = np.zeros((N_SEQ * 32, SUB), np.float32)
    for j in range(N_SEQ):
        for half in range(2):
            for r in range(12):
                place[j * 32 + half * 16 + r, j * 24 + half * 12 + r] = 1.0
    return jnp.asarray(place, BF)


def pad_order():
    place = np.zeros((SUB, YROWS), np.float32)
    for z in range(6):
        for r in range(12):
            place[z * 16 + r, z * 12 + r] = 1.0
        for r in range(3):
            place[z * 16 + 12 + r, 72 + r] = 1.0
    return jnp.asarray(place, BF)


SMEM = pl.BlockSpec(memory_space=pltpu.SMEM)
VMEM = pl.BlockSpec(memory_space=pltpu.VMEM)
HBM = pl.BlockSpec(memory_space=pltpu.HBM)
ANY = pl.BlockSpec(memory_space=pl.ANY)


def call(kernel, out_shapes, args, scratch=(), micros=1.0, specs=None, grant=24, unread=0):
    if specs is None:
        specs = [SMEM if a.dtype == jnp.int32 else VMEM for a in args]
        specs = specs[: len(specs) - unread] + [ANY] * unread
    return pl.pallas_call(
        kernel,
        out_shape=out_shapes,
        in_specs=specs,
        out_specs=[VMEM] * len(out_shapes),
        scratch_shapes=list(scratch),
        compiler_params=pltpu.CompilerParams(vmem_limit_bytes=grant * 1024 * 1024),
        cost_estimate=pl.CostEstimate(
            flops=int(micros * 1.0e9), bytes_accessed=int(micros * 1.0e6), transcendentals=0
        ),
    )(*args)


def shape(*dims, dtype=BF):
    return jax.ShapeDtypeStruct(dims, dtype)


def slide_at(z, y, c):
    return (z * NY + y) * NC + c


CORE_PAIRS = [(i, i ^ 1) for i in range(NZ * NY * NC)]
Z_GROUPS = [[slide_at(z, y, c) for z in range(NZ)] for y in range(NY) for c in range(NC)]
SEQ_TURNS = [[(k, (k + t) % N_SEQ) for k in range(N_SEQ)] for t in range(N_SEQ)]
Y_TURNS = [
    [
        (slide_at(z, y, c), slide_at(z, (y + t) % NY, c))
        for z in range(NZ)
        for y in range(NY)
        for c in range(NC)
    ]
    for t in range(NY)
]


def swap(arrays, axis, turns):
    return [arrays[0]] + [lax.ppermute(arrays[t], axis, turns[t]) for t in range(1, len(arrays))]


def per_device(embeddings, tile_counts, masked_tiles, w_in, norm_gain, w_qkv, w_out):
    inv_count = 1.0 / (lax.axis_size("slide") * masked_tiles.shape[1])
    hidden, normed, projected, dilated = call(
        prep_kernel,
        [shape(TOK, D), shape(TOK, D), shape(TOK, 3 * D), shape(FAR, 2 * D)],
        (embeddings, masked_tiles, norm_gain, w_in, w_qkv),
        [
            pltpu.VMEM((TOK, 2 * D), BF),
            pltpu.VMEM((1, TOK), jnp.int32),
            pltpu.VMEM((D,), F32),
            pltpu.VMEM((2 * D, D), BF),
            pltpu.VMEM((D, 3 * D), BF),
            pltpu.SemaphoreType.DMA((6 + 2 * D // 256,)),
        ],
        4.0,
        [HBM] * 5,
        60,
    )
    fars = swap([dilated] * N_SEQ, "seq", SEQ_TURNS)
    scores = shape(GROUPS, TOK, RATE * TOK, dtype=F32)
    rows = shape(HEADS, TOK, dtype=F32)
    exps, tops, sums, tiles, flag = call(
        near_kernel,
        [scores, rows, rows, shape(TOK, 2 * D), shape(TOK, TOK, dtype=F32)],
        (tile_counts, projected, embeddings, masked_tiles),
        (),
        1.0,
        [SMEM] + [VMEM] * 3,
    )
    norms = swap([normed] * N_SEQ, "seq", SEQ_TURNS)
    fk, fv, pnear, pfar, attended = call(
        far_kernel,
        [shape(TOK, D), shape(TOK, D), scores, shape(GROUPS, TOK, TOK, dtype=F32), shape(TOK, D)],
        (tile_counts, *fars, projected, exps, tops, sums),
        [pltpu.VMEM((TOK, D), F32)],
        2.0,
    )
    grad_attended, loss, out_mine, out_other = call(
        functools.partial(chain_kernel, inv_count),
        [shape(TOK, D), shape(16, 128), shape(HALF, D), shape(HALF, D)],
        (attended, hidden, tiles, flag, w_in, w_out, out_order()),
        (),
        3.0,
    )
    out_other = lax.ppermute(out_other, "slide", CORE_PAIRS)
    sent = call(
        backward_kernel,
        [shape(XROWS, TOK)] * N_SEQ,
        (projected, fk, fv, pnear, pfar, grad_attended, loss, spread_order()),
        [pltpu.VMEM((TOK, D), F32)] * 5 + [pltpu.VMEM((SECTIONS, HALF, TOK), BF)],
        8.0,
    )
    got = swap(sent, "seq", SEQ_TURNS)
    out = call(out_core_kernel, [shape(SUB, D)] * NY, (out_mine, out_other, sent[0], *norms[1:]), unread=4)
    out = swap(out, "slide", Y_TURNS)
    out_sums = call(out_y_kernel, [shape(32, D)] * N_SEQ, (*out, out_pad_order()))
    out = swap(out_sums, "seq", SEQ_TURNS)
    whole, tail = call(
        product_kernel,
        [shape(6 * SUB, D), shape(YROWS, D, dtype=F32)],
        (*got, *norms, out_sums[0]),
        [
            pltpu.VMEM((N_SEQ, XROWS, TOK), BF),
            pltpu.VMEM((6 * SUB, N_SEQ * TOK), BF),
            pltpu.VMEM((N_SEQ * TOK, D), BF),
        ],
        15.0,
        unread=1,
    )
    mine, other = call(
        place_kernel,
        [shape(NY * YROWS, D)] * 2,
        (whole, tail, product_order(), *out[1:]),
        unread=3,
    )
    other = lax.ppermute(other, "slide", CORE_PAIRS)
    by_y = call(core_kernel, [shape(YROWS, D)] * NY, (mine, other))
    by_y = swap(by_y, "slide", Y_TURNS)
    (by_z,) = call(y_kernel, [shape(NZ, 16, D)], (*by_y, *out, pad_order()))
    by_z = lax.all_to_all(by_z, "slide", 0, 0, tiled=True, axis_index_groups=Z_GROUPS)
    gradients, loss = call(z_kernel, [shape(12, D, dtype=F32), shape(1, 1, dtype=F32)], (by_z,))
    return (gradients, loss[0, 0])


def solution(mesh):
    in_specs = (P("slide", "seq", None), P("slide"), P("slide", None), P(), P(), P(), P())
    out_specs = (P(("slide", "seq"), None), P())
    return jax.shard_map(
        per_device, mesh=mesh, in_specs=in_specs, out_specs=out_specs, check_vma=False
    )
```

```python
import functools
import math

import numpy as np
import jax
import jax.numpy as jnp
from jax import lax
from jax.experimental import pallas as pl
from jax.experimental.pallas import tpu as pltpu
from jax.sharding import PartitionSpec as P

HEADS = 16
RATE = 4
HD = 48
D = 768
TOK = 128
N_SEQ = 4
GROUPS = HEADS // RATE
FAR = TOK // RATE
NORM_EPS = 1e-06
NEG_FILL = -1e30
SCALE = 1.0 / math.sqrt(HD)
BF = jnp.bfloat16
F32 = jnp.float32
HALF = 384
SUB = 96
SECTIONS = 10
YROWS = 80
XROWS = SECTIONS * SUB + 16
NZ, NY, NC = 8, 4, 2


def dot(a, b, dims):
    return lax.dot_general(a, b, (dims, ((), ())), preferred_element_type=F32)


def nn(a, b):
    return dot(a, b, ((1,), (0,)))


def nt(a, b):
    return dot(a, b, ((1,), (1,)))


def tn(a, b):
    return dot(a, b, ((0,), (0,)))


def iota(shape, dim):
    return lax.broadcasted_iota(jnp.int32, shape, dim)


def class_major(index):
    return (index & (FAR - 1)) * RATE + (index >> 5)


def split_rows(value, shape, first):
    high = value.astype(BF).astype(F32)
    rest = value - high
    mid = rest.astype(BF).astype(F32)
    low = rest - mid
    row = iota(shape, 0)
    return jnp.where(
        row == first,
        high,
        jnp.where(row == first + 1, mid, jnp.where(row == first + 2, low, 0.0)),
    )


def class_order():
    shape = (TOK, TOK)
    return (iota(shape, 1) == class_major(iota(shape, 0))).astype(F32).astype(BF)


def masked_rows(positions, masked):
    hits = jnp.where(positions == masked, 1.0, 0.0)
    return jnp.broadcast_to(jnp.max(hits, axis=1, keepdims=True), (TOK, TOK))


def prep_kernel(
    tiles_hbm, masked_hbm, gain_hbm, w_in_hbm, w_qkv_hbm,
    hidden_out, normed_out, proj_out, dilated_out,
    tiles, masked, gain, w_in, w_qkv, sems,
):
    blocks = w_in_hbm.shape[0] // 256
    loads = [
        pltpu.make_async_copy(masked_hbm, masked, sems.at[0]),
        pltpu.make_async_copy(tiles_hbm.at[0], tiles, sems.at[1]),
        pltpu.make_async_copy(gain_hbm, gain, sems.at[2]),
    ]
    chunks = [
        pltpu.make_async_copy(
            w_in_hbm.at[256 * i : 256 * (i + 1)], w_in.at[256 * i : 256 * (i + 1)], sems.at[6 + i]
        )
        for i in range(blocks)
    ]
    parts = [
        pltpu.make_async_copy(
            w_qkv_hbm.at[:, D * i : D * (i + 1)], w_qkv.at[:, D * i : D * (i + 1)], sems.at[3 + i]
        )
        for i in range(3)
    ]
    for copy in loads + chunks + parts[1:] + parts[:1]:
        copy.start()
    order = class_order()
    positions = lax.axis_index("seq") * TOK + iota((TOK, TOK), 0)
    loads[0].wait()
    flag = masked_rows(positions, masked[...])[:, 0:1] > 0.5
    loads[1].wait()
    hidden = jnp.zeros((TOK, D), F32)
    for i in range(blocks):
        cols = slice(256 * i, 256 * (i + 1))
        inputs = jnp.where(flag, jnp.zeros((), BF), tiles[:, cols])
        chunks[i].wait()
        hidden += nn(inputs, w_in[cols])
    hidden_f = nn(order, hidden.astype(BF))
    hidden_out[...] = hidden_f.astype(BF)
    scale_rows = lax.rsqrt(jnp.mean(hidden_f * hidden_f, axis=1, keepdims=True) + NORM_EPS)
    loads[2].wait()
    normed = (hidden_f * scale_rows * gain[...].reshape(1, D)).astype(BF)
    normed_out[...] = normed
    for part in (1, 2, 0):
        parts[part].wait()
        for block in range(D // 256):
            first = part * D + block * 256
            rows = nn(normed, w_qkv[:, first : first + 256]).astype(BF)
            proj_out[:, first : first + 256] = rows
            if part > 0:
                lane_class = ((iota((FAR, 256), 1) + block * 256) // HD) & 3
                pieces = [rows[FAR * r : FAR * (r + 1)] for r in range(RATE)]
                dilated_out[:, first - D : first - D + 256] = by_class(lane_class, pieces)


def window(group):
    return (group * RATE * HD) // 128 * 128


def head_masks(group):
    lane = iota((TOK, 256), 1) + window(group)
    row_class = iota((TOK, 256), 0) >> 5
    masks = []
    for r in range(RATE):
        first = (group * RATE + r) * HD
        masks.append((lane >= first) & (lane < first + HD))
    picked = masks[0] & (row_class == 0)
    for r in range(1, RATE):
        picked = picked | (masks[r] & (row_class == r))
    return masks, picked


def keep(mask, value):
    return jnp.where(mask, value, jnp.zeros((), value.dtype))


def by_class(own_class, pieces):
    out = pieces[0]
    for r in range(1, RATE):
        out = jnp.where(own_class == r, pieces[r], out)
    return out


def forward_kernel(
    count_ref, f0, f1, f2, f3, proj_ref, tiles_ref, masked_ref,
    fk_ref, fv_ref, pnear_ref, pfar_ref, att_ref, tiles_out, flag_ref,
    att_acc,
):
    count = count_ref[...]
    seq = lax.axis_index("seq")
    pos0 = seq * TOK
    for turn, ref in enumerate((f0, f1, f2, f3)):
        rows = pl.ds(pl.multiple_of(((seq - turn) & 3) * FAR, FAR), FAR)
        fk_ref[rows] = ref[:, 0:D]
        fv_ref[rows] = ref[:, D:]
    flag_ref[...] = masked_rows(pos0 + class_major(iota((TOK, TOK), 0)), masked_ref[...])
    tiles_out[...] = nn(class_order(), tiles_ref[0]).astype(BF)

    square = (TOK, TOK)
    key_pos = pos0 + class_major(iota(square, 0))
    query_pos = pos0 + class_major(iota(square, 1))
    near_ok = (key_pos < count) | (key_pos == query_pos)
    far_row = iota(square, 0)
    far_ok = (far_row >> 5) * TOK + (far_row & (FAR - 1)) * RATE + (iota(square, 1) >> 5) < count
    own_class = iota((1, TOK), 1) >> 5

    att_acc[...] = jnp.zeros_like(att_acc)
    for g in range(GROUPS):
        lo = window(g)
        win = slice(lo, lo + 256)
        masks, picked = head_masks(g)
        q = proj_ref[:, lo : lo + 256]
        k = proj_ref[:, D + lo : D + lo + 256]
        v = proj_ref[:, 2 * D + lo : 2 * D + lo + 256]
        near = nt(k, jnp.concatenate([keep(m, q) for m in masks], 0))
        far = jnp.where(far_ok, nt(fk_ref[:, win], keep(picked, q)) * SCALE, NEG_FILL)
        far_max = jnp.max(far, axis=0, keepdims=True)
        scores = [
            jnp.where(near_ok, near[:, TOK * r : TOK * (r + 1)] * SCALE, NEG_FILL) for r in range(RATE)
        ]
        tops = []
        for r in range(RATE):
            top = jnp.max(scores[r], axis=0, keepdims=True)
            tops.append(jnp.where(own_class == r, jnp.maximum(top, far_max), top))
        exps = [jnp.exp(scores[r] - tops[r]) for r in range(RATE)]
        far_exp = jnp.exp(far - by_class(own_class, tops))
        far_sum = jnp.sum(far_exp, axis=0, keepdims=True)
        inverse = []
        for r in range(RATE):
            total = jnp.sum(exps[r], axis=0, keepdims=True)
            inverse.append(1.0 / jnp.where(own_class == r, total + far_sum, total))
        probs = [exps[r] * inverse[r] for r in range(RATE)]
        far_probs = far_exp * by_class(own_class, inverse)
        for r in range(RATE):
            pnear_ref[g, :, TOK * r : TOK * (r + 1)] = probs[r]
        pfar_ref[g] = far_probs
        att = tn(
            jnp.concatenate([p.astype(BF) for p in probs], 0),
            jnp.concatenate([keep(m, v) for m in masks], 0),
        )
        att_acc[:, win] += att + keep(picked, tn(far_probs.astype(BF), fv_ref[:, win]))
    att_ref[...] = att_acc[...].astype(BF)


def chain_kernel(
    inv_count,
    att_ref, hidden_ref, tiles_ref, flag_ref, w_in_ref, w_out_ref, order_ref,
    ga_ref, loss_ref, mine_ref, other_ref,
):
    core = lax.axis_index("slide") & 1
    attended = att_ref[...]
    mixed = (hidden_ref[...].astype(F32) + nn(attended, w_out_ref[...])).astype(BF)
    flag = flag_ref[:, 0:1] > 0.5
    error = jnp.where(flag, nt(mixed, w_in_ref[...]) - tiles_ref[...].astype(F32), 0.0)
    loss = jnp.sum(jnp.sum(error * error, axis=1, keepdims=True), axis=0, keepdims=True) * inv_count
    loss_ref[...] = split_rows(jnp.broadcast_to(loss, (16, 128)), (16, 128), 0).astype(BF)
    grad_pred = (2.0 * inv_count * error).astype(BF)
    grad_mixed = nn(grad_pred, w_in_ref[...]).astype(BF)
    ga_ref[...] = nt(grad_mixed, w_out_ref[...]).astype(BF)
    for turn, ref in enumerate((mine_ref, other_ref)):
        first = pl.multiple_of(((core + turn) & 1) * HALF, HALF)
        left = nt(order_ref[pl.ds(first, HALF)], grad_mixed).astype(BF)
        ref[...] = nn(left, attended).astype(BF)


def backward_kernel(
    proj_ref, fk_ref, fv_ref, pnear_ref, pfar_ref, ga_ref, loss_ref, spread_ref,
    x0, x1, x2, x3,
    gq, gk, gv, gkf, gvf, turned,
):
    seq = lax.axis_index("seq")
    own_class = iota((1, TOK), 1) >> 5
    for ref in (gq, gk, gv, gkf, gvf):
        ref[...] = jnp.zeros_like(ref)
    for g in range(GROUPS):
        lo = window(g)
        win = slice(lo, lo + 256)
        masks, picked = head_masks(g)
        q = proj_ref[:, lo : lo + 256]
        k = proj_ref[:, D + lo : D + lo + 256]
        v = proj_ref[:, 2 * D + lo : 2 * D + lo + 256]
        ga = ga_ref[:, win]
        fk = fk_ref[:, win]
        fv = fv_ref[:, win]
        ga_stack = jnp.concatenate([keep(m, ga) for m in masks], 0)
        ga_picked = keep(picked, ga)
        near = nt(v, ga_stack)
        far = nt(fv, ga_picked)
        probs = [pnear_ref[g, :, TOK * r : TOK * (r + 1)] for r in range(RATE)]
        far_probs = pfar_ref[g]
        far_dot = jnp.sum(far_probs * far, axis=0, keepdims=True)
        grads = [near[:, TOK * r : TOK * (r + 1)] for r in range(RATE)]
        dots = []
        for r in range(RATE):
            own = jnp.sum(probs[r] * grads[r], axis=0, keepdims=True)
            dots.append(jnp.where(own_class == r, own + far_dot, own))
        scores = [(probs[r] * (grads[r] - dots[r]) * SCALE).astype(BF) for r in range(RATE)]
        far_scores = (far_probs * (far - by_class(own_class, dots)) * SCALE).astype(BF)
        gq[:, win] += tn(
            jnp.concatenate(scores, 0), jnp.concatenate([keep(m, k) for m in masks], 0)
        ) + keep(picked, tn(far_scores, fk))
        gk[:, win] += nn(
            jnp.concatenate(scores, 1), jnp.concatenate([keep(m, q) for m in masks], 0)
        )
        gv[:, win] += nn(jnp.concatenate([p.astype(BF) for p in probs], 1), ga_stack)
        gkf[:, win] += nn(far_scores, keep(picked, q))
        gvf[:, win] += nn(far_probs.astype(BF), ga_picked)
    place = spread_ref[...]
    section = 0
    for value in (gq, gk, gv, gkf, gvf):
        for half in range(2):
            piece = value[:, half * HALF : (half + 1) * HALF].astype(BF)
            turned[section] = nt(place, piece).astype(BF)
            section += 1
    for turn, ref in enumerate((x0, x1, x2, x3)):
        first = pl.multiple_of(((seq + turn) & 3) * SUB, 16)
        for section in range(SECTIONS):
            ref[section * SUB : (section + 1) * SUB] = turned[section, pl.ds(first, SUB)]
        ref[SECTIONS * SUB :] = loss_ref[...]


def product_kernel(
    x0, x1, x2, x3, n0, n1, n2, n3, wait_ref, whole_ref, tail_ref, got, left, right
):
    seq = lax.axis_index("seq")
    for turn, (x_ref, n_ref) in enumerate(zip((x0, x1, x2, x3), (n0, n1, n2, n3))):
        src = (seq - turn) & 3
        got[src] = x_ref[...]
        right[pl.ds(pl.multiple_of(src * TOK, TOK), TOK)] = n_ref[...]
    for src in range(N_SEQ):
        left[0 : 2 * SUB, src * TOK : (src + 1) * TOK] = got[src, 0 : 2 * SUB]
    shape = (SUB, TOK)
    row = iota(shape, 0)
    lane_class = iota(shape, 1) >> 5
    core_row = jnp.where(row >= 48, 1, 0)
    row_y = (row - 48 * core_row) // 12
    row_class = ((row_y & 1) << 1) + core_row
    spots = [(row_class == r) & (lane_class == r) for r in range(RATE)]
    for part in range(2):
        for half in range(2):
            near_at = (2 + 2 * part + half) * SUB
            far_at = (6 + 2 * part + half) * SUB
            far = got[0, far_at : far_at + SUB].astype(F32)
            for src in range(1, N_SEQ):
                far = far + got[src, far_at : far_at + SUB].astype(F32)
            turns = [far] + [pltpu.roll(far, FAR * t, 1) for t in range(1, RATE)]
            for src in range(N_SEQ):
                total = got[src, near_at : near_at + SUB].astype(F32)
                for r in range(RATE):
                    total = total + jnp.where(spots[r], turns[(r - src) & 3], 0.0)
                left[near_at : near_at + SUB, src * TOK : (src + 1) * TOK] = total.astype(BF)
    whole_ref[...] = nn(left[...], right[...]).astype(BF)
    loss = got[0, SECTIONS * SUB :].astype(F32)
    for src in range(1, N_SEQ):
        loss = loss + got[src, SECTIONS * SUB :].astype(F32)
    loss = jnp.sum(loss, axis=0, keepdims=True)[:, 0:1]
    tail_ref[...] = split_rows(jnp.broadcast_to(loss, (YROWS, D)), (YROWS, D), 72)


def place_kernel(whole_ref, tail_ref, order_ref, wait1, wait2, wait3, mine_ref, other_ref):
    core = lax.axis_index("slide") & 1
    whole = whole_ref[...]
    for turn, ref in enumerate((mine_ref, other_ref)):
        first = pl.multiple_of(((core + turn) & 1) * NY * YROWS, NY * YROWS)
        half = nn(order_ref[pl.ds(first, NY * YROWS)], whole)
        for y in range(NY):
            rows = slice(y * YROWS, (y + 1) * YROWS)
            ref[rows] = (half[rows] + tail_ref[...]).astype(BF)


def resplit(total):
    row = iota(total.shape, 0)
    loss = jnp.sum(jnp.where(row >= 72, total, 0.0), axis=0, keepdims=True)
    pieces = split_rows(jnp.broadcast_to(loss, total.shape), total.shape, 72)
    return jnp.where(row >= 72, pieces, total), loss


def core_kernel(mine_ref, other_ref, y0, y1, y2, y3):
    y = (lax.axis_index("slide") >> 1) & 3
    for turn, ref in enumerate((y0, y1, y2, y3)):
        rows = pl.ds(pl.multiple_of(((y + turn) & 3) * YROWS, 16), YROWS)
        ref[...] = resplit(mine_ref[rows].astype(F32) + other_ref[rows].astype(F32))[0].astype(BF)


def y_kernel(y0, y1, y2, y3, o0, o1, o2, o3, order_ref, out_ref):
    total = y0[...].astype(F32) + y1[...].astype(F32) + y2[...].astype(F32) + y3[...].astype(F32)
    total, loss = resplit(total)
    out_ref[0:6] = nn(order_ref[...], total.astype(BF)).astype(BF).reshape(6, 16, D)
    out = o0[...].astype(F32) + o1[...].astype(F32) + o2[...].astype(F32) + o3[...].astype(F32)
    tail = split_rows(jnp.broadcast_to(loss, (16, D)), (16, D), 12)
    for half in range(2):
        out_ref[6 + half] = (out[16 * half : 16 * (half + 1)] + tail).astype(BF)


def out_core_kernel(mine_ref, other_ref, wait0, wait1, wait2, wait3, y0, y1, y2, y3):
    y = (lax.axis_index("slide") >> 1) & 3
    for turn, ref in enumerate((y0, y1, y2, y3)):
        rows = pl.ds(pl.multiple_of(((y + turn) & 3) * SUB, 16), SUB)
        ref[...] = (mine_ref[rows].astype(F32) + other_ref[rows].astype(F32)).astype(BF)


def out_y_kernel(y0, y1, y2, y3, order_ref, x0, x1, x2, x3):
    seq = lax.axis_index("seq")
    total = y0[...].astype(F32) + y1[...].astype(F32) + y2[...].astype(F32) + y3[...].astype(F32)
    total = total.astype(BF)
    for turn, ref in enumerate((x0, x1, x2, x3)):
        rows = pl.ds(pl.multiple_of(((seq + turn) & 3) * 32, 32), 32)
        ref[...] = nn(order_ref[rows], total).astype(BF)


def z_kernel(in_ref, out_ref, loss_ref):
    total = in_ref[0].astype(F32)
    for src in range(1, NZ):
        total = total + in_ref[src].astype(F32)
    out_ref[...] = total[0:12]
    loss_ref[...] = jnp.sum(total[12:15, 0:1], axis=0, keepdims=True)


def spread_order():
    place = np.zeros((HALF, HALF), np.float32)
    for row in range(HALF):
        j, rest = divmod(row, SUB)
        c, rest = divmod(rest, 48)
        y, r = divmod(rest, 12)
        place[row, (y * NC + c) * HD + j * 12 + r] = 1.0
    return jnp.asarray(place, BF)


def product_order():
    place = np.zeros((NC * NY * YROWS, 6 * SUB), np.float32)
    for c in range(NC):
        for y in range(NY):
            for z in range(6):
                for r in range(12):
                    place[(c * NY + y) * YROWS + z * 12 + r, z * SUB + c * 48 + y * 12 + r] = 1.0
    return jnp.asarray(place, BF)


def out_order():
    place = np.zeros((D, D), np.float32)
    row = 0
    for c in range(NC):
        for y in range(NY):
            for j in range(N_SEQ):
                for half in range(2):
                    for r in range(12):
                        place[row, (half * 8 + y * NC + c) * HD + j * 12 + r] = 1.0
                        row += 1
    return jnp.asarray(place, BF)


def out_pad_order():
    place = np.zeros((N_SEQ * 32, SUB), np.float32)
    for j in range(N_SEQ):
        for half in range(2):
            for r in range(12):
                place[j * 32 + half * 16 + r, j * 24 + half * 12 + r] = 1.0
    return jnp.asarray(place, BF)


def pad_order():
    place = np.zeros((SUB, YROWS), np.float32)
    for z in range(6):
        for r in range(12):
            place[z * 16 + r, z * 12 + r] = 1.0
        for r in range(3):
            place[z * 16 + 12 + r, 72 + r] = 1.0
    return jnp.asarray(place, BF)


SMEM = pl.BlockSpec(memory_space=pltpu.SMEM)
VMEM = pl.BlockSpec(memory_space=pltpu.VMEM)
HBM = pl.BlockSpec(memory_space=pltpu.HBM)
ANY = pl.BlockSpec(memory_space=pl.ANY)


def call(kernel, out_shapes, args, scratch=(), micros=1.0, specs=None, grant=24, unread=0):
    if specs is None:
        specs = [SMEM if a.dtype == jnp.int32 else VMEM for a in args]
        specs = specs[: len(specs) - unread] + [ANY] * unread
    return pl.pallas_call(
        kernel,
        out_shape=out_shapes,
        in_specs=specs,
        out_specs=[VMEM] * len(out_shapes),
        scratch_shapes=list(scratch),
        compiler_params=pltpu.CompilerParams(vmem_limit_bytes=grant * 1024 * 1024),
        cost_estimate=pl.CostEstimate(
            flops=int(micros * 1.0e9), bytes_accessed=int(micros * 1.0e6), transcendentals=0
        ),
    )(*args)


def shape(*dims, dtype=BF):
    return jax.ShapeDtypeStruct(dims, dtype)


def slide_at(z, y, c):
    return (z * NY + y) * NC + c


CORE_PAIRS = [(i, i ^ 1) for i in range(NZ * NY * NC)]
Z_GROUPS = [[slide_at(z, y, c) for z in range(NZ)] for y in range(NY) for c in range(NC)]
SEQ_TURNS = [[(k, (k + t) % N_SEQ) for k in range(N_SEQ)] for t in range(N_SEQ)]
Y_TURNS = [
    [
        (slide_at(z, y, c), slide_at(z, (y + t) % NY, c))
        for z in range(NZ)
        for y in range(NY)
        for c in range(NC)
    ]
    for t in range(NY)
]


def swap(arrays, axis, turns):
    return [arrays[0]] + [lax.ppermute(arrays[t], axis, turns[t]) for t in range(1, len(arrays))]


def per_device(embeddings, tile_counts, masked_tiles, w_in, norm_gain, w_qkv, w_out):
    inv_count = 1.0 / (lax.axis_size("slide") * masked_tiles.shape[1])
    hidden, normed, projected, dilated = call(
        prep_kernel,
        [shape(TOK, D), shape(TOK, D), shape(TOK, 3 * D), shape(FAR, 2 * D)],
        (embeddings, masked_tiles, norm_gain, w_in, w_qkv),
        [
            pltpu.VMEM((TOK, 2 * D), BF),
            pltpu.VMEM((1, TOK), jnp.int32),
            pltpu.VMEM((D,), F32),
            pltpu.VMEM((2 * D, D), BF),
            pltpu.VMEM((D, 3 * D), BF),
            pltpu.SemaphoreType.DMA((6 + 2 * D // 256,)),
        ],
        4.0,
        [HBM] * 5,
        60,
    )
    fars = swap([dilated] * N_SEQ, "seq", SEQ_TURNS)
    norms = swap([normed] * N_SEQ, "seq", SEQ_TURNS)
    fk, fv, pnear, pfar, attended, tiles, flag = call(
        forward_kernel,
        [
            shape(TOK, D),
            shape(TOK, D),
            shape(GROUPS, TOK, RATE * TOK, dtype=F32),
            shape(GROUPS, TOK, TOK, dtype=F32),
            shape(TOK, D),
            shape(TOK, 2 * D),
            shape(TOK, TOK, dtype=F32),
        ],
        (tile_counts.reshape(1, 1), *fars, projected, embeddings, masked_tiles),
        [pltpu.VMEM((TOK, D), F32)],
        2.0,
        [VMEM] * 8,
    )
    grad_attended, loss, out_mine, out_other = call(
        functools.partial(chain_kernel, inv_count),
        [shape(TOK, D), shape(16, 128), shape(HALF, D), shape(HALF, D)],
        (attended, hidden, tiles, flag, w_in, w_out, out_order()),
        (),
        3.0,
    )
    out_other = lax.ppermute(out_other, "slide", CORE_PAIRS)
    sent = call(
        backward_kernel,
        [shape(XROWS, TOK)] * N_SEQ,
        (projected, fk, fv, pnear, pfar, grad_attended, loss, spread_order()),
        [pltpu.VMEM((TOK, D), F32)] * 5 + [pltpu.VMEM((SECTIONS, HALF, TOK), BF)],
        8.0,
    )
    got = swap(sent, "seq", SEQ_TURNS)
    out = call(out_core_kernel, [shape(SUB, D)] * NY, (out_mine, out_other, sent[0], *norms[1:]), unread=4)
    out = swap(out, "slide", Y_TURNS)
    out_sums = call(out_y_kernel, [shape(32, D)] * N_SEQ, (*out, out_pad_order()))
    out = swap(out_sums, "seq", SEQ_TURNS)
    whole, tail = call(
        product_kernel,
        [shape(6 * SUB, D), shape(YROWS, D, dtype=F32)],
        (*got, *norms, out_sums[0]),
        [
            pltpu.VMEM((N_SEQ, XROWS, TOK), BF),
            pltpu.VMEM((6 * SUB, N_SEQ * TOK), BF),
            pltpu.VMEM((N_SEQ * TOK, D), BF),
        ],
        15.0,
        unread=1,
    )
    mine, other = call(
        place_kernel,
        [shape(NY * YROWS, D)] * 2,
        (whole, tail, product_order(), *out[1:]),
        unread=3,
    )
    other = lax.ppermute(other, "slide", CORE_PAIRS)
    by_y = call(core_kernel, [shape(YROWS, D)] * NY, (mine, other))
    by_y = swap(by_y, "slide", Y_TURNS)
    (by_z,) = call(y_kernel, [shape(NZ, 16, D)], (*by_y, *out, pad_order()))
    by_z = lax.all_to_all(by_z, "slide", 0, 0, tiled=True, axis_index_groups=Z_GROUPS)
    gradients, loss = call(z_kernel, [shape(12, D, dtype=F32), shape(1, 1, dtype=F32)], (by_z,))
    return (gradients, loss[0, 0])


def solution(mesh):
    in_specs = (P("slide", "seq", None), P("slide"), P("slide", None), P(), P(), P(), P())
    out_specs = (P(("slide", "seq"), None), P())
    return jax.shard_map(
        per_device, mesh=mesh, in_specs=in_specs, out_specs=out_specs, check_vma=False
    )
```

```python
import functools
import math

import numpy as np
import jax
import jax.numpy as jnp
from jax import lax
from jax.experimental import pallas as pl
from jax.experimental.pallas import tpu as pltpu
from jax.sharding import PartitionSpec as P

HEADS = 16
RATE = 4
HD = 48
D = 768
TOK = 128
N_SEQ = 4
GROUPS = HEADS // RATE
FAR = TOK // RATE
NORM_EPS = 1e-06
NEG_FILL = -1e30
SCALE = 1.0 / math.sqrt(HD)
BF = jnp.bfloat16
F32 = jnp.float32
HALF = 384
SUB = 96
SECTIONS = 10
YROWS = 80
XROWS = SECTIONS * SUB + 16
NZ, NY, NC = 8, 4, 2


def dot(a, b, dims):
    return lax.dot_general(a, b, (dims, ((), ())), preferred_element_type=F32)


def nn(a, b):
    return dot(a, b, ((1,), (0,)))


def nt(a, b):
    return dot(a, b, ((1,), (1,)))


def tn(a, b):
    return dot(a, b, ((0,), (0,)))


def iota(shape, dim):
    return lax.broadcasted_iota(jnp.int32, shape, dim)


def class_major(index):
    return (index & (FAR - 1)) * RATE + (index >> 5)


def split_rows(value, shape, first):
    high = value.astype(BF).astype(F32)
    rest = value - high
    mid = rest.astype(BF).astype(F32)
    low = rest - mid
    row = iota(shape, 0)
    return jnp.where(
        row == first,
        high,
        jnp.where(row == first + 1, mid, jnp.where(row == first + 2, low, 0.0)),
    )


def class_order():
    shape = (TOK, TOK)
    return (iota(shape, 1) == class_major(iota(shape, 0))).astype(F32).astype(BF)


def masked_rows(positions, masked):
    hits = jnp.where(positions == masked, 1.0, 0.0)
    return jnp.broadcast_to(jnp.max(hits, axis=1, keepdims=True), (TOK, TOK))


def prep_kernel(
    tiles_hbm, masked_hbm, gain_hbm, w_in_hbm, w_qkv_hbm,
    hidden_out, normed_out, proj_out, dilated_out,
    tiles, masked, gain, w_in, w_qkv, sems,
):
    blocks = w_in_hbm.shape[0] // 256
    loads = [
        pltpu.make_async_copy(masked_hbm, masked, sems.at[0]),
        pltpu.make_async_copy(tiles_hbm.at[0], tiles, sems.at[1]),
        pltpu.make_async_copy(gain_hbm, gain, sems.at[2]),
    ]
    chunks = [
        pltpu.make_async_copy(
            w_in_hbm.at[256 * i : 256 * (i + 1)], w_in.at[256 * i : 256 * (i + 1)], sems.at[6 + i]
        )
        for i in range(blocks)
    ]
    parts = [
        pltpu.make_async_copy(
            w_qkv_hbm.at[:, D * i : D * (i + 1)], w_qkv.at[:, D * i : D * (i + 1)], sems.at[3 + i]
        )
        for i in range(3)
    ]
    for copy in loads + chunks + parts[1:] + parts[:1]:
        copy.start()
    order = class_order()
    positions = lax.axis_index("seq") * TOK + iota((TOK, TOK), 0)
    loads[0].wait()
    flag = masked_rows(positions, masked[...])[:, 0:1] > 0.5
    loads[1].wait()
    hidden = jnp.zeros((TOK, D), F32)
    for i in range(blocks):
        cols = slice(256 * i, 256 * (i + 1))
        inputs = jnp.where(flag, jnp.zeros((), BF), tiles[:, cols])
        chunks[i].wait()
        hidden += nn(inputs, w_in[cols])
    hidden_f = nn(order, hidden.astype(BF))
    hidden_out[...] = hidden_f.astype(BF)
    scale_rows = lax.rsqrt(jnp.mean(hidden_f * hidden_f, axis=1, keepdims=True) + NORM_EPS)
    loads[2].wait()
    normed = (hidden_f * scale_rows * gain[...].reshape(1, D)).astype(BF)
    normed_out[...] = normed
    for part in (1, 2, 0):
        parts[part].wait()
        for block in range(D // 256):
            first = part * D + block * 256
            rows = nn(normed, w_qkv[:, first : first + 256]).astype(BF)
            proj_out[:, first : first + 256] = rows
            if part > 0:
                dilated_out[:, first - D : first - D + 256] = dilate(rows, block * 256)


def dilate(rows, lane0):
    lane_class = ((iota((FAR, 256), 1) + lane0) // HD) & 3
    return by_class(lane_class, [rows[FAR * r : FAR * (r + 1)] for r in range(RATE)])


def window(group):
    return (group * RATE * HD) // 128 * 128


def head_masks(group):
    lane = iota((TOK, 256), 1) + window(group)
    row_class = iota((TOK, 256), 0) >> 5
    masks = []
    for r in range(RATE):
        first = (group * RATE + r) * HD
        masks.append((lane >= first) & (lane < first + HD))
    picked = masks[0] & (row_class == 0)
    for r in range(1, RATE):
        picked = picked | (masks[r] & (row_class == r))
    return masks, picked


def keep(mask, value):
    return jnp.where(mask, value, jnp.zeros((), value.dtype))


def by_class(own_class, pieces):
    out = pieces[0]
    for r in range(1, RATE):
        out = jnp.where(own_class == r, pieces[r], out)
    return out


def forward_kernel(
    count_ref, f2, f1, f3, proj_ref, tiles_ref, masked_ref,
    fk_ref, fv_ref, pnear_ref, pfar_ref, att_ref, tiles_out, flag_ref,
    att_acc,
):
    count = count_ref[...]
    seq = lax.axis_index("seq")
    pos0 = seq * TOK
    for turn, ref in enumerate((f1, f2, f3)):
        rows = pl.ds(pl.multiple_of(((seq - turn - 1) & 3) * FAR, FAR), FAR)
        fk_ref[rows] = ref[:, 0:D]
        fv_ref[rows] = ref[:, D:]
    own_rows = pl.ds(pl.multiple_of(seq * FAR, FAR), FAR)
    for part, far_ref in enumerate((fk_ref, fv_ref)):
        for block in range(D // 256):
            first = (1 + part) * D + block * 256
            far_ref[own_rows, block * 256 : (block + 1) * 256] = dilate(
                proj_ref[:, first : first + 256], block * 256
            )
    flag_ref[...] = masked_rows(pos0 + class_major(iota((TOK, TOK), 0)), masked_ref[...])
    tiles_out[...] = nn(class_order(), tiles_ref[0]).astype(BF)

    square = (TOK, TOK)
    key_pos = pos0 + class_major(iota(square, 0))
    query_pos = pos0 + class_major(iota(square, 1))
    near_ok = (key_pos < count) | (key_pos == query_pos)
    far_row = iota(square, 0)
    far_ok = (far_row >> 5) * TOK + (far_row & (FAR - 1)) * RATE + (iota(square, 1) >> 5) < count
    own_class = iota((1, TOK), 1) >> 5

    att_acc[...] = jnp.zeros_like(att_acc)
    for g in range(GROUPS):
        lo = window(g)
        win = slice(lo, lo + 256)
        masks, picked = head_masks(g)
        q = proj_ref[:, lo : lo + 256]
        k = proj_ref[:, D + lo : D + lo + 256]
        v = proj_ref[:, 2 * D + lo : 2 * D + lo + 256]
        near = nt(k, jnp.concatenate([keep(m, q) for m in masks], 0))
        far = jnp.where(far_ok, nt(fk_ref[:, win], keep(picked, q)) * SCALE, NEG_FILL)
        far_max = jnp.max(far, axis=0, keepdims=True)
        scores = [
            jnp.where(near_ok, near[:, TOK * r : TOK * (r + 1)] * SCALE, NEG_FILL) for r in range(RATE)
        ]
        tops = []
        for r in range(RATE):
            top = jnp.max(scores[r], axis=0, keepdims=True)
            tops.append(jnp.where(own_class == r, jnp.maximum(top, far_max), top))
        exps = [jnp.exp(scores[r] - tops[r]) for r in range(RATE)]
        far_exp = jnp.exp(far - by_class(own_class, tops))
        far_sum = jnp.sum(far_exp, axis=0, keepdims=True)
        inverse = []
        for r in range(RATE):
            total = jnp.sum(exps[r], axis=0, keepdims=True)
            inverse.append(1.0 / jnp.where(own_class == r, total + far_sum, total))
        probs = [exps[r] * inverse[r] for r in range(RATE)]
        far_probs = far_exp * by_class(own_class, inverse)
        for r in range(RATE):
            pnear_ref[g, :, TOK * r : TOK * (r + 1)] = probs[r]
        pfar_ref[g] = far_probs
        att = tn(
            jnp.concatenate([p.astype(BF) for p in probs], 0),
            jnp.concatenate([keep(m, v) for m in masks], 0),
        )
        att_acc[:, win] += att + keep(picked, tn(far_probs.astype(BF), fv_ref[:, win]))
    att_ref[...] = att_acc[...].astype(BF)


def chain_kernel(
    inv_count,
    att_ref, hidden_ref, tiles_ref, flag_ref, w_in_ref, w_out_ref, order_ref,
    ga_ref, loss_ref, mine_ref, other_ref,
):
    core = lax.axis_index("slide") & 1
    attended = att_ref[...]
    mixed = (hidden_ref[...].astype(F32) + nn(attended, w_out_ref[...])).astype(BF)
    flag = flag_ref[:, 0:1] > 0.5
    error = jnp.where(flag, nt(mixed, w_in_ref[...]) - tiles_ref[...].astype(F32), 0.0)
    loss = jnp.sum(jnp.sum(error * error, axis=1, keepdims=True), axis=0, keepdims=True) * inv_count
    loss_ref[...] = split_rows(jnp.broadcast_to(loss, (16, 128)), (16, 128), 0).astype(BF)
    grad_pred = (2.0 * inv_count * error).astype(BF)
    grad_mixed = nn(grad_pred, w_in_ref[...]).astype(BF)
    ga_ref[...] = nt(grad_mixed, w_out_ref[...]).astype(BF)
    for turn, ref in enumerate((mine_ref, other_ref)):
        first = pl.multiple_of(((core + turn) & 1) * HALF, HALF)
        left = nt(order_ref[pl.ds(first, HALF)], grad_mixed).astype(BF)
        ref[...] = nn(left, attended).astype(BF)


def backward_kernel(
    proj_ref, fk_ref, fv_ref, pnear_ref, pfar_ref, ga_ref, loss_ref, spread_ref,
    x0, x1, x2, x3,
    gq, gk, gv, gkf, gvf, turned,
):
    seq = lax.axis_index("seq")
    own_class = iota((1, TOK), 1) >> 5
    for ref in (gq, gk, gv, gkf, gvf):
        ref[...] = jnp.zeros_like(ref)
    for g in range(GROUPS):
        lo = window(g)
        win = slice(lo, lo + 256)
        masks, picked = head_masks(g)
        q = proj_ref[:, lo : lo + 256]
        k = proj_ref[:, D + lo : D + lo + 256]
        v = proj_ref[:, 2 * D + lo : 2 * D + lo + 256]
        ga = ga_ref[:, win]
        fk = fk_ref[:, win]
        fv = fv_ref[:, win]
        ga_stack = jnp.concatenate([keep(m, ga) for m in masks], 0)
        ga_picked = keep(picked, ga)
        near = nt(v, ga_stack)
        far = nt(fv, ga_picked)
        probs = [pnear_ref[g, :, TOK * r : TOK * (r + 1)] for r in range(RATE)]
        far_probs = pfar_ref[g]
        far_dot = jnp.sum(far_probs * far, axis=0, keepdims=True)
        grads = [near[:, TOK * r : TOK * (r + 1)] for r in range(RATE)]
        dots = []
        for r in range(RATE):
            own = jnp.sum(probs[r] * grads[r], axis=0, keepdims=True)
            dots.append(jnp.where(own_class == r, own + far_dot, own))
        scores = [(probs[r] * (grads[r] - dots[r]) * SCALE).astype(BF) for r in range(RATE)]
        far_scores = (far_probs * (far - by_class(own_class, dots)) * SCALE).astype(BF)
        gq[:, win] += tn(
            jnp.concatenate(scores, 0), jnp.concatenate([keep(m, k) for m in masks], 0)
        ) + keep(picked, tn(far_scores, fk))
        gk[:, win] += nn(
            jnp.concatenate(scores, 1), jnp.concatenate([keep(m, q) for m in masks], 0)
        )
        gv[:, win] += nn(jnp.concatenate([p.astype(BF) for p in probs], 1), ga_stack)
        gkf[:, win] += nn(far_scores, keep(picked, q))
        gvf[:, win] += nn(far_probs.astype(BF), ga_picked)
    place = spread_ref[...]
    for section, value in enumerate((gq, gk, gv, gkf, gvf)):
        halves = jnp.concatenate([value[:, 0:HALF], value[:, HALF:]], 0).astype(BF)
        both = nt(place, halves).astype(BF)
        turned[2 * section] = both[:, 0:TOK]
        turned[2 * section + 1] = both[:, TOK:]
    for turn, ref in enumerate((x0, x1, x2, x3)):
        first = pl.multiple_of(((seq + turn) & 3) * SUB, 16)
        for section in range(SECTIONS):
            ref[section * SUB : (section + 1) * SUB] = turned[section, pl.ds(first, SUB)]
        ref[SECTIONS * SUB :] = loss_ref[...]


def product_kernel(
    x0, x2, x1, x3, n0, n1, n3, n2, wait_ref, whole_ref, tail_ref, got, left, right
):
    seq = lax.axis_index("seq")
    for turn, (x_ref, n_ref) in enumerate(zip((x0, x1, x2, x3), (n0, n1, n2, n3))):
        src = (seq - turn) & 3
        got[src] = x_ref[...]
        right[pl.ds(pl.multiple_of(src * TOK, TOK), TOK)] = n_ref[...]
    for src in range(N_SEQ):
        left[0 : 2 * SUB, src * TOK : (src + 1) * TOK] = got[src, 0 : 2 * SUB]
    shape = (SUB, TOK)
    row = iota(shape, 0)
    lane_class = iota(shape, 1) >> 5
    core_row = jnp.where(row >= 48, 1, 0)
    row_y = (row - 48 * core_row) // 12
    row_class = ((row_y & 1) << 1) + core_row
    spots = [(row_class == r) & (lane_class == r) for r in range(RATE)]
    for part in range(2):
        for half in range(2):
            near_at = (2 + 2 * part + half) * SUB
            far_at = (6 + 2 * part + half) * SUB
            far = got[0, far_at : far_at + SUB].astype(F32)
            for src in range(1, N_SEQ):
                far = far + got[src, far_at : far_at + SUB].astype(F32)
            turns = [far] + [pltpu.roll(far, FAR * t, 1) for t in range(1, RATE)]
            for src in range(N_SEQ):
                total = got[src, near_at : near_at + SUB].astype(F32)
                for r in range(RATE):
                    total = total + jnp.where(spots[r], turns[(r - src) & 3], 0.0)
                left[near_at : near_at + SUB, src * TOK : (src + 1) * TOK] = total.astype(BF)
    whole_ref[...] = nn(left[...], right[...]).astype(BF)
    loss = got[0, SECTIONS * SUB :].astype(F32)
    for src in range(1, N_SEQ):
        loss = loss + got[src, SECTIONS * SUB :].astype(F32)
    loss = jnp.sum(loss, axis=0, keepdims=True)[:, 0:1]
    tail_ref[...] = split_rows(jnp.broadcast_to(loss, (YROWS, D)), (YROWS, D), 72)


def place_kernel(whole_ref, tail_ref, order_ref, wait1, wait2, wait3, mine_ref, other_ref):
    core = lax.axis_index("slide") & 1
    whole = whole_ref[...]
    for turn, ref in enumerate((mine_ref, other_ref)):
        first = pl.multiple_of(((core + turn) & 1) * NY * YROWS, NY * YROWS)
        half = nn(order_ref[pl.ds(first, NY * YROWS)], whole)
        for y in range(NY):
            rows = slice(y * YROWS, (y + 1) * YROWS)
            ref[rows] = (half[rows] + tail_ref[...]).astype(BF)


def resplit(total):
    row = iota(total.shape, 0)
    loss = jnp.sum(jnp.where(row >= 72, total, 0.0), axis=0, keepdims=True)
    pieces = split_rows(jnp.broadcast_to(loss, total.shape), total.shape, 72)
    return jnp.where(row >= 72, pieces, total), loss


def core_kernel(mine_ref, other_ref, y0, y1, y2, y3):
    y = (lax.axis_index("slide") >> 1) & 3
    for turn, ref in enumerate((y0, y1, y2, y3)):
        rows = pl.ds(pl.multiple_of(((y + turn) & 3) * YROWS, 16), YROWS)
        ref[...] = resplit(mine_ref[rows].astype(F32) + other_ref[rows].astype(F32))[0].astype(BF)


def y_kernel(y0, y1, y2, y3, o0, o1, o2, o3, order_ref, out_ref):
    total = y0[...].astype(F32) + y1[...].astype(F32) + y2[...].astype(F32) + y3[...].astype(F32)
    total, loss = resplit(total)
    out_ref[0:6] = nn(order_ref[...], total.astype(BF)).astype(BF).reshape(6, 16, D)
    out = o0[...].astype(F32) + o1[...].astype(F32) + o2[...].astype(F32) + o3[...].astype(F32)
    tail = split_rows(jnp.broadcast_to(loss, (16, D)), (16, D), 12)
    for half in range(2):
        out_ref[6 + half] = (out[16 * half : 16 * (half + 1)] + tail).astype(BF)


def out_core_kernel(mine_ref, other_ref, wait0, wait1, wait2, wait3, y0, y1, y2, y3):
    y = (lax.axis_index("slide") >> 1) & 3
    for turn, ref in enumerate((y0, y1, y2, y3)):
        rows = pl.ds(pl.multiple_of(((y + turn) & 3) * SUB, 16), SUB)
        ref[...] = (mine_ref[rows].astype(F32) + other_ref[rows].astype(F32)).astype(BF)


def out_y_kernel(y0, y1, y2, y3, order_ref, x0, x1, x2, x3):
    seq = lax.axis_index("seq")
    total = y0[...].astype(F32) + y1[...].astype(F32) + y2[...].astype(F32) + y3[...].astype(F32)
    total = total.astype(BF)
    for turn, ref in enumerate((x0, x1, x2, x3)):
        rows = pl.ds(pl.multiple_of(((seq + turn) & 3) * 32, 32), 32)
        ref[...] = nn(order_ref[rows], total).astype(BF)


def z_kernel(in_ref, out_ref, loss_ref):
    total = in_ref[0].astype(F32)
    for src in range(1, NZ):
        total = total + in_ref[src].astype(F32)
    out_ref[...] = total[0:12]
    loss_ref[...] = jnp.sum(total[12:15, 0:1], axis=0, keepdims=True)


def spread_order():
    place = np.zeros((HALF, HALF), np.float32)
    for row in range(HALF):
        j, rest = divmod(row, SUB)
        c, rest = divmod(rest, 48)
        y, r = divmod(rest, 12)
        place[row, (y * NC + c) * HD + j * 12 + r] = 1.0
    return jnp.asarray(place, BF)


def product_order():
    place = np.zeros((NC * NY * YROWS, 6 * SUB), np.float32)
    for c in range(NC):
        for y in range(NY):
            for z in range(6):
                for r in range(12):
                    place[(c * NY + y) * YROWS + z * 12 + r, z * SUB + c * 48 + y * 12 + r] = 1.0
    return jnp.asarray(place, BF)


def out_order():
    place = np.zeros((D, D), np.float32)
    row = 0
    for c in range(NC):
        for y in range(NY):
            for j in range(N_SEQ):
                for half in range(2):
                    for r in range(12):
                        place[row, (half * 8 + y * NC + c) * HD + j * 12 + r] = 1.0
                        row += 1
    return jnp.asarray(place, BF)


def out_pad_order():
    place = np.zeros((N_SEQ * 32, SUB), np.float32)
    for j in range(N_SEQ):
        for half in range(2):
            for r in range(12):
                place[j * 32 + half * 16 + r, j * 24 + half * 12 + r] = 1.0
    return jnp.asarray(place, BF)


def pad_order():
    place = np.zeros((SUB, YROWS), np.float32)
    for z in range(6):
        for r in range(12):
            place[z * 16 + r, z * 12 + r] = 1.0
        for r in range(3):
            place[z * 16 + 12 + r, 72 + r] = 1.0
    return jnp.asarray(place, BF)


SMEM = pl.BlockSpec(memory_space=pltpu.SMEM)
VMEM = pl.BlockSpec(memory_space=pltpu.VMEM)
HBM = pl.BlockSpec(memory_space=pltpu.HBM)
ANY = pl.BlockSpec(memory_space=pl.ANY)


def call(kernel, out_shapes, args, scratch=(), micros=1.0, specs=None, grant=24, unread=0):
    if specs is None:
        specs = [SMEM if a.dtype == jnp.int32 else VMEM for a in args]
        specs = specs[: len(specs) - unread] + [ANY] * unread
    return pl.pallas_call(
        kernel,
        out_shape=out_shapes,
        in_specs=specs,
        out_specs=[VMEM] * len(out_shapes),
        scratch_shapes=list(scratch),
        compiler_params=pltpu.CompilerParams(vmem_limit_bytes=grant * 1024 * 1024),
        cost_estimate=pl.CostEstimate(
            flops=int(micros * 1.0e9), bytes_accessed=int(micros * 1.0e6), transcendentals=0
        ),
    )(*args)


def shape(*dims, dtype=BF):
    return jax.ShapeDtypeStruct(dims, dtype)


def slide_at(z, y, c):
    return (z * NY + y) * NC + c


CORE_PAIRS = [(i, i ^ 1) for i in range(NZ * NY * NC)]
Z_GROUPS = [[slide_at(z, y, c) for z in range(NZ)] for y in range(NY) for c in range(NC)]
SEQ_TURNS = [[(k, (k + t) % N_SEQ) for k in range(N_SEQ)] for t in range(N_SEQ)]
Y_TURNS = [
    [
        (slide_at(z, y, c), slide_at(z, (y + t) % NY, c))
        for z in range(NZ)
        for y in range(NY)
        for c in range(NC)
    ]
    for t in range(NY)
]


def swap(arrays, axis, turns, order=(1, 2, 3)):
    got = {t: lax.ppermute(arrays[t], axis, turns[t]) for t in order}
    return [arrays[0], got[1], got[2], got[3]]


def per_device(embeddings, tile_counts, masked_tiles, w_in, norm_gain, w_qkv, w_out):
    inv_count = 1.0 / (lax.axis_size("slide") * masked_tiles.shape[1])
    hidden, normed, projected, dilated = call(
        prep_kernel,
        [shape(TOK, D), shape(TOK, D), shape(TOK, 3 * D), shape(FAR, 2 * D)],
        (embeddings, masked_tiles, norm_gain, w_in, w_qkv),
        [
            pltpu.VMEM((TOK, 2 * D), BF),
            pltpu.VMEM((1, TOK), jnp.int32),
            pltpu.VMEM((D,), F32),
            pltpu.VMEM((2 * D, D), BF),
            pltpu.VMEM((D, 3 * D), BF),
            pltpu.SemaphoreType.DMA((6 + 2 * D // 256,)),
        ],
        4.0,
        [HBM] * 5,
        60,
    )
    fars = swap([dilated] * N_SEQ, "seq", SEQ_TURNS, (2, 1, 3))
    norms = swap([normed] * N_SEQ, "seq", SEQ_TURNS, (1, 3, 2))
    fk, fv, pnear, pfar, attended, tiles, flag = call(
        forward_kernel,
        [
            shape(TOK, D),
            shape(TOK, D),
            shape(GROUPS, TOK, RATE * TOK, dtype=F32),
            shape(GROUPS, TOK, TOK, dtype=F32),
            shape(TOK, D),
            shape(TOK, 2 * D),
            shape(TOK, TOK, dtype=F32),
        ],
        (tile_counts.reshape(1, 1), fars[2], fars[1], fars[3], projected, embeddings, masked_tiles),
        [pltpu.VMEM((TOK, D), F32)],
        2.0,
        [VMEM] * 7,
    )
    grad_attended, loss, out_mine, out_other = call(
        functools.partial(chain_kernel, inv_count),
        [shape(TOK, D), shape(16, 128), shape(HALF, D), shape(HALF, D)],
        (attended, hidden, tiles, flag, w_in, w_out, out_order()),
        (),
        3.0,
    )
    out_other = lax.ppermute(out_other, "slide", CORE_PAIRS)
    sent = call(
        backward_kernel,
        [shape(XROWS, TOK)] * N_SEQ,
        (projected, fk, fv, pnear, pfar, grad_attended, loss, spread_order()),
        [pltpu.VMEM((TOK, D), F32)] * 5 + [pltpu.VMEM((SECTIONS, HALF, TOK), BF)],
        8.0,
    )
    got = swap(sent, "seq", SEQ_TURNS)
    out = call(out_core_kernel, [shape(SUB, D)] * NY, (out_mine, out_other, sent[0], norms[1], norms[3], norms[2]), unread=4)
    out = swap(out, "slide", Y_TURNS)
    out_sums = call(
        out_y_kernel, [shape(32, D)] * N_SEQ, (out[0], out[2], out[1], out[3], out_pad_order())
    )
    out = swap(out_sums, "seq", SEQ_TURNS)
    whole, tail = call(
        product_kernel,
        [shape(6 * SUB, D), shape(YROWS, D, dtype=F32)],
        (got[0], got[2], got[1], got[3], norms[0], norms[1], norms[3], norms[2], out_sums[0]),
        [
            pltpu.VMEM((N_SEQ, XROWS, TOK), BF),
            pltpu.VMEM((6 * SUB, N_SEQ * TOK), BF),
            pltpu.VMEM((N_SEQ * TOK, D), BF),
        ],
        15.0,
        unread=1,
    )
    mine, other = call(
        place_kernel,
        [shape(NY * YROWS, D)] * 2,
        (whole, tail, product_order(), *out[1:]),
        unread=3,
    )
    other = lax.ppermute(other, "slide", CORE_PAIRS)
    by_y = call(core_kernel, [shape(YROWS, D)] * NY, (mine, other))
    by_y = swap(by_y, "slide", Y_TURNS)
    (by_z,) = call(
        y_kernel,
        [shape(NZ, 16, D)],
        (by_y[0], by_y[2], by_y[1], by_y[3], *out, pad_order()),
    )
    by_z = lax.all_to_all(by_z, "slide", 0, 0, tiled=True, axis_index_groups=Z_GROUPS)
    gradients, loss = call(z_kernel, [shape(12, D, dtype=F32), shape(1, 1, dtype=F32)], (by_z,))
    return (gradients, loss[0, 0])


def solution(mesh):
    in_specs = (P("slide", "seq", None), P("slide"), P("slide", None), P(), P(), P(), P())
    out_specs = (P(("slide", "seq"), None), P())
    return jax.shard_map(
        per_device, mesh=mesh, in_specs=in_specs, out_specs=out_specs, check_vma=False
    )
```

```python
import functools
import math

import numpy as np
import jax
import jax.numpy as jnp
from jax import lax
from jax.experimental import pallas as pl
from jax.experimental.pallas import tpu as pltpu
from jax.sharding import PartitionSpec as P

HEADS = 16
RATE = 4
HD = 48
D = 768
TOK = 128
N_SEQ = 4
GROUPS = HEADS // RATE
FAR = TOK // RATE
NORM_EPS = 1e-06
NEG_FILL = -1e30
SCALE = 1.0 / math.sqrt(HD)
BF = jnp.bfloat16
F32 = jnp.float32
HALF = 384
SUB = 96
SECTIONS = 10
YROWS = 80
XROWS = SECTIONS * SUB + 16
NZ, NY, NC = 8, 4, 2


def dot(a, b, dims):
    return lax.dot_general(a, b, (dims, ((), ())), preferred_element_type=F32)


def nn(a, b):
    return dot(a, b, ((1,), (0,)))


def nt(a, b):
    return dot(a, b, ((1,), (1,)))


def tn(a, b):
    return dot(a, b, ((0,), (0,)))


def iota(shape, dim):
    return lax.broadcasted_iota(jnp.int32, shape, dim)


def class_major(index):
    return (index & (FAR - 1)) * RATE + (index >> 5)


def split_rows(value, shape, first):
    high = value.astype(BF).astype(F32)
    rest = value - high
    mid = rest.astype(BF).astype(F32)
    low = rest - mid
    row = iota(shape, 0)
    return jnp.where(
        row == first,
        high,
        jnp.where(row == first + 1, mid, jnp.where(row == first + 2, low, 0.0)),
    )


def class_order():
    shape = (TOK, TOK)
    return (iota(shape, 1) == class_major(iota(shape, 0))).astype(F32).astype(BF)


def masked_rows(positions, masked):
    hits = jnp.where(positions == masked, 1.0, 0.0)
    return jnp.broadcast_to(jnp.max(hits, axis=1, keepdims=True), (TOK, TOK))


def prep_kernel(
    tiles_hbm, masked_hbm, gain_hbm, w_in_hbm, w_qkv_hbm,
    hidden_out, normed_out, proj_out, dilated_out,
    tiles, masked, gain, w_in, w_qkv, sems,
):
    blocks = w_in_hbm.shape[0] // 256
    loads = [
        pltpu.make_async_copy(masked_hbm, masked, sems.at[0]),
        pltpu.make_async_copy(tiles_hbm.at[0], tiles, sems.at[1]),
        pltpu.make_async_copy(gain_hbm, gain, sems.at[2]),
    ]
    chunks = [
        pltpu.make_async_copy(
            w_in_hbm.at[256 * i : 256 * (i + 1)], w_in.at[256 * i : 256 * (i + 1)], sems.at[6 + i]
        )
        for i in range(blocks)
    ]
    parts = [
        pltpu.make_async_copy(
            w_qkv_hbm.at[:, D * i : D * (i + 1)], w_qkv.at[:, D * i : D * (i + 1)], sems.at[3 + i]
        )
        for i in range(3)
    ]
    for copy in loads + chunks + parts[1:] + parts[:1]:
        copy.start()
    order = class_order()
    positions = lax.axis_index("seq") * TOK + iota((TOK, TOK), 0)
    loads[0].wait()
    flag = masked_rows(positions, masked[...])[:, 0:1] > 0.5
    loads[1].wait()
    hidden = jnp.zeros((TOK, D), F32)
    for i in range(blocks):
        cols = slice(256 * i, 256 * (i + 1))
        inputs = jnp.where(flag, jnp.zeros((), BF), tiles[:, cols])
        chunks[i].wait()
        hidden += nn(inputs, w_in[cols])
    hidden_f = nn(order, hidden.astype(BF))
    hidden_out[...] = hidden_f.astype(BF)
    scale_rows = lax.rsqrt(jnp.mean(hidden_f * hidden_f, axis=1, keepdims=True) + NORM_EPS)
    loads[2].wait()
    normed = (hidden_f * scale_rows * gain[...].reshape(1, D)).astype(BF)
    normed_out[...] = normed
    for part in (1, 2, 0):
        parts[part].wait()
        for block in range(D // 256):
            first = part * D + block * 256
            rows = nn(normed, w_qkv[:, first : first + 256]).astype(BF)
            proj_out[:, first : first + 256] = rows
            if part > 0:
                dilated_out[:, first - D : first - D + 256] = dilate(rows, block * 256)


def dilate(rows, lane0):
    lane_class = ((iota((FAR, 256), 1) + lane0) // HD) & 3
    return by_class(lane_class, [rows[FAR * r : FAR * (r + 1)] for r in range(RATE)])


def window(group):
    return (group * RATE * HD) // 128 * 128


def head_masks(group):
    lane = iota((TOK, 256), 1) + window(group)
    row_class = iota((TOK, 256), 0) >> 5
    masks = []
    for r in range(RATE):
        first = (group * RATE + r) * HD
        masks.append((lane >= first) & (lane < first + HD))
    picked = masks[0] & (row_class == 0)
    for r in range(1, RATE):
        picked = picked | (masks[r] & (row_class == r))
    return masks, picked


def keep(mask, value):
    return jnp.where(mask, value, jnp.zeros((), value.dtype))


def by_class(own_class, pieces):
    out = pieces[0]
    for r in range(1, RATE):
        out = jnp.where(own_class == r, pieces[r], out)
    return out


def forward_kernel(
    count_ref, f2, f1, f3, proj_ref, tiles_ref, masked_ref,
    fk_ref, fv_ref, pnear_ref, pfar_ref, att_ref, tiles_out, flag_ref,
    att_acc,
):
    count = count_ref[...]
    seq = lax.axis_index("seq")
    pos0 = seq * TOK
    for turn, ref in enumerate((f1, f2, f3)):
        rows = pl.ds(pl.multiple_of(((seq - turn - 1) & 3) * FAR, FAR), FAR)
        fk_ref[rows] = ref[:, 0:D]
        fv_ref[rows] = ref[:, D:]
    own_rows = pl.ds(pl.multiple_of(seq * FAR, FAR), FAR)
    for part, far_ref in enumerate((fk_ref, fv_ref)):
        for block in range(D // 256):
            first = (1 + part) * D + block * 256
            far_ref[own_rows, block * 256 : (block + 1) * 256] = dilate(
                proj_ref[:, first : first + 256], block * 256
            )
    flag_ref[...] = masked_rows(pos0 + class_major(iota((TOK, TOK), 0)), masked_ref[...])
    tiles_out[...] = nn(class_order(), tiles_ref[0]).astype(BF)

    square = (TOK, TOK)
    key_pos = pos0 + class_major(iota(square, 0))
    query_pos = pos0 + class_major(iota(square, 1))
    near_ok = (key_pos < count) | (key_pos == query_pos)
    far_row = iota(square, 0)
    far_ok = (far_row >> 5) * TOK + (far_row & (FAR - 1)) * RATE + (iota(square, 1) >> 5) < count
    own_class = iota((1, TOK), 1) >> 5

    att_acc[...] = jnp.zeros_like(att_acc)
    for g in range(GROUPS):
        lo = window(g)
        win = slice(lo, lo + 256)
        masks, picked = head_masks(g)
        q = proj_ref[:, lo : lo + 256]
        k = proj_ref[:, D + lo : D + lo + 256]
        v = proj_ref[:, 2 * D + lo : 2 * D + lo + 256]
        near = nt(k, jnp.concatenate([keep(m, q) for m in masks], 0))
        far = jnp.where(far_ok, nt(fk_ref[:, win], keep(picked, q)) * SCALE, NEG_FILL)
        far_max = jnp.max(far, axis=0, keepdims=True)
        scores = [
            jnp.where(near_ok, near[:, TOK * r : TOK * (r + 1)] * SCALE, NEG_FILL) for r in range(RATE)
        ]
        tops = []
        for r in range(RATE):
            top = jnp.max(scores[r], axis=0, keepdims=True)
            tops.append(jnp.where(own_class == r, jnp.maximum(top, far_max), top))
        exps = [jnp.exp(scores[r] - tops[r]) for r in range(RATE)]
        far_exp = jnp.exp(far - by_class(own_class, tops))
        far_sum = jnp.sum(far_exp, axis=0, keepdims=True)
        inverse = []
        for r in range(RATE):
            total = jnp.sum(exps[r], axis=0, keepdims=True)
            inverse.append(1.0 / jnp.where(own_class == r, total + far_sum, total))
        probs = [exps[r] * inverse[r] for r in range(RATE)]
        far_probs = far_exp * by_class(own_class, inverse)
        for r in range(RATE):
            pnear_ref[g, :, TOK * r : TOK * (r + 1)] = probs[r]
        pfar_ref[g] = far_probs
        att = tn(
            jnp.concatenate([p.astype(BF) for p in probs], 0),
            jnp.concatenate([keep(m, v) for m in masks], 0),
        )
        att_acc[:, win] += att + keep(picked, tn(far_probs.astype(BF), fv_ref[:, win]))
    att_ref[...] = att_acc[...].astype(BF)


def chain_kernel(
    inv_count,
    att_ref, hidden_ref, tiles_ref, flag_ref, w_in_ref, w_out_ref, order_ref,
    ga_ref, loss_ref, mine_ref, other_ref,
):
    core = lax.axis_index("slide") & 1
    attended = att_ref[...]
    mixed = (hidden_ref[...].astype(F32) + nn(attended, w_out_ref[...])).astype(BF)
    flag = flag_ref[:, 0:1] > 0.5
    error = jnp.where(flag, nt(mixed, w_in_ref[...]) - tiles_ref[...].astype(F32), 0.0)
    loss = jnp.sum(jnp.sum(error * error, axis=1, keepdims=True), axis=0, keepdims=True) * inv_count
    loss_ref[...] = split_rows(jnp.broadcast_to(loss, (16, 128)), (16, 128), 0).astype(BF)
    grad_pred = (2.0 * inv_count * error).astype(BF)
    grad_mixed = nn(grad_pred, w_in_ref[...]).astype(BF)
    ga_ref[...] = nt(grad_mixed, w_out_ref[...]).astype(BF)
    for turn, ref in enumerate((mine_ref, other_ref)):
        first = pl.multiple_of(((core + turn) & 1) * HALF, HALF)
        left = nt(order_ref[pl.ds(first, HALF)], grad_mixed).astype(BF)
        ref[...] = nn(left, attended).astype(BF)


def backward_kernel(
    proj_ref, fk_ref, fv_ref, pnear_ref, pfar_ref, ga_ref, loss_ref, spread_ref,
    x0, x1, x2, x3,
    gq, gk, gv, gkf, gvf, turned,
):
    seq = lax.axis_index("seq")
    own_class = iota((1, TOK), 1) >> 5
    for ref in (gq, gk, gv, gkf, gvf):
        ref[...] = jnp.zeros_like(ref)
    for g in range(GROUPS):
        lo = window(g)
        win = slice(lo, lo + 256)
        masks, picked = head_masks(g)
        q = proj_ref[:, lo : lo + 256]
        k = proj_ref[:, D + lo : D + lo + 256]
        v = proj_ref[:, 2 * D + lo : 2 * D + lo + 256]
        ga = ga_ref[:, win]
        fk = fk_ref[:, win]
        fv = fv_ref[:, win]
        ga_stack = jnp.concatenate([keep(m, ga) for m in masks], 0)
        ga_picked = keep(picked, ga)
        near = nt(v, ga_stack)
        far = nt(fv, ga_picked)
        probs = [pnear_ref[g, :, TOK * r : TOK * (r + 1)] for r in range(RATE)]
        far_probs = pfar_ref[g]
        far_dot = jnp.sum(far_probs * far, axis=0, keepdims=True)
        grads = [near[:, TOK * r : TOK * (r + 1)] for r in range(RATE)]
        dots = []
        for r in range(RATE):
            own = jnp.sum(probs[r] * grads[r], axis=0, keepdims=True)
            dots.append(jnp.where(own_class == r, own + far_dot, own))
        scores = [(probs[r] * (grads[r] - dots[r]) * SCALE).astype(BF) for r in range(RATE)]
        far_scores = (far_probs * (far - by_class(own_class, dots)) * SCALE).astype(BF)
        gq[:, win] += tn(
            jnp.concatenate(scores, 0), jnp.concatenate([keep(m, k) for m in masks], 0)
        ) + keep(picked, tn(far_scores, fk))
        gk[:, win] += nn(
            jnp.concatenate(scores, 1), jnp.concatenate([keep(m, q) for m in masks], 0)
        )
        gv[:, win] += nn(jnp.concatenate([p.astype(BF) for p in probs], 1), ga_stack)
        gkf[:, win] += nn(far_scores, keep(picked, q))
        gvf[:, win] += nn(far_probs.astype(BF), ga_picked)
    place = spread_ref[...]
    for section, value in enumerate((gq, gk, gv, gkf, gvf)):
        halves = jnp.concatenate([value[:, 0:HALF], value[:, HALF:]], 0).astype(BF)
        both = nt(place, halves).astype(BF)
        turned[2 * section] = both[:, 0:TOK]
        turned[2 * section + 1] = both[:, TOK:]
    for turn, ref in enumerate((x0, x1, x2, x3)):
        first = pl.multiple_of(((seq + turn) & 3) * SUB, 16)
        for section in range(SECTIONS):
            ref[section * SUB : (section + 1) * SUB] = turned[section, pl.ds(first, SUB)]
        ref[SECTIONS * SUB :] = loss_ref[...]


def product_kernel(
    x0, x2, x1, x3, n0, n1, n3, n2, wait_ref, whole_ref, tail_ref, got, left, right
):
    seq = lax.axis_index("seq")
    for turn, (x_ref, n_ref) in enumerate(zip((x0, x1, x2, x3), (n0, n1, n2, n3))):
        src = (seq - turn) & 3
        got[src] = x_ref[...]
        right[pl.ds(pl.multiple_of(src * TOK, TOK), TOK)] = n_ref[...]
    for src in range(N_SEQ):
        left[0 : 2 * SUB, src * TOK : (src + 1) * TOK] = got[src, 0 : 2 * SUB]
    shape = (SUB, TOK)
    row = iota(shape, 0)
    lane_class = iota(shape, 1) >> 5
    core_row = jnp.where(row >= 48, 1, 0)
    row_y = (row - 48 * core_row) // 12
    row_class = ((row_y & 1) << 1) + core_row
    spots = [(row_class == r) & (lane_class == r) for r in range(RATE)]
    for part in range(2):
        for half in range(2):
            near_at = (2 + 2 * part + half) * SUB
            far_at = (6 + 2 * part + half) * SUB
            far = got[0, far_at : far_at + SUB].astype(F32)
            for src in range(1, N_SEQ):
                far = far + got[src, far_at : far_at + SUB].astype(F32)
            turns = [far] + [pltpu.roll(far, FAR * t, 1) for t in range(1, RATE)]
            for src in range(N_SEQ):
                total = got[src, near_at : near_at + SUB].astype(F32)
                for r in range(RATE):
                    total = total + jnp.where(spots[r], turns[(r - src) & 3], 0.0)
                left[near_at : near_at + SUB, src * TOK : (src + 1) * TOK] = total.astype(BF)
    whole_ref[...] = nn(left[...], right[...])
    loss = got[0, SECTIONS * SUB :].astype(F32)
    for src in range(1, N_SEQ):
        loss = loss + got[src, SECTIONS * SUB :].astype(F32)
    loss = jnp.sum(loss, axis=0, keepdims=True)[:, 0:1]
    tail_ref[...] = split_rows(jnp.broadcast_to(loss, (YROWS, D)), (YROWS, D), 72)


def place_kernel(whole_ref, tail_ref, wait1, wait2, wait3, mine_ref, other_ref):
    core = lax.axis_index("slide") & 1
    tail = tail_ref[72:]
    for turn, ref in enumerate((mine_ref, other_ref)):
        side = ((core + turn) & 1) * 48
        blocks = [whole_ref[pl.ds(pl.multiple_of(z * SUB + side, 16), 48)] for z in range(6)]
        for y in range(NY):
            rows = [block[12 * y : 12 * (y + 1)] for block in blocks]
            ref[y * YROWS : (y + 1) * YROWS] = jnp.concatenate(rows + [tail], 0).astype(BF)


def resplit(total):
    row = iota(total.shape, 0)
    loss = jnp.sum(jnp.where(row >= 72, total, 0.0), axis=0, keepdims=True)
    pieces = split_rows(jnp.broadcast_to(loss, total.shape), total.shape, 72)
    return jnp.where(row >= 72, pieces, total), loss


def core_kernel(mine_ref, other_ref, y0, y1, y2, y3):
    y = (lax.axis_index("slide") >> 1) & 3
    for turn, ref in enumerate((y0, y1, y2, y3)):
        rows = pl.ds(pl.multiple_of(((y + turn) & 3) * YROWS, 16), YROWS)
        ref[...] = resplit(mine_ref[rows].astype(F32) + other_ref[rows].astype(F32))[0].astype(BF)


def y_kernel(y0, y1, y2, y3, o0, o1, o2, o3, order_ref, out_ref):
    total = y0[...].astype(F32) + y1[...].astype(F32) + y2[...].astype(F32) + y3[...].astype(F32)
    total, loss = resplit(total)
    out_ref[0:6] = nn(order_ref[...], total.astype(BF)).astype(BF).reshape(6, 16, D)
    out = o0[...].astype(F32) + o1[...].astype(F32) + o2[...].astype(F32) + o3[...].astype(F32)
    tail = split_rows(jnp.broadcast_to(loss, (16, D)), (16, D), 12)
    for half in range(2):
        out_ref[6 + half] = (out[16 * half : 16 * (half + 1)] + tail).astype(BF)


def out_core_kernel(mine_ref, other_ref, wait0, wait1, wait2, wait3, y0, y1, y2, y3):
    y = (lax.axis_index("slide") >> 1) & 3
    for turn, ref in enumerate((y0, y1, y2, y3)):
        rows = pl.ds(pl.multiple_of(((y + turn) & 3) * SUB, 16), SUB)
        ref[...] = (mine_ref[rows].astype(F32) + other_ref[rows].astype(F32)).astype(BF)


def out_y_kernel(y0, y1, y2, y3, order_ref, x0, x1, x2, x3):
    seq = lax.axis_index("seq")
    total = y0[...].astype(F32) + y1[...].astype(F32) + y2[...].astype(F32) + y3[...].astype(F32)
    total = total.astype(BF)
    for turn, ref in enumerate((x0, x1, x2, x3)):
        rows = pl.ds(pl.multiple_of(((seq + turn) & 3) * 32, 32), 32)
        ref[...] = nn(order_ref[rows], total).astype(BF)


def z_kernel(in_ref, out_ref, loss_ref):
    total = in_ref[0].astype(F32)
    for src in range(1, NZ):
        total = total + in_ref[src].astype(F32)
    out_ref[...] = total[0:12]
    loss_ref[...] = jnp.sum(total[12:15, 0:1], axis=0, keepdims=True)


def spread_order():
    place = np.zeros((HALF, HALF), np.float32)
    for row in range(HALF):
        j, rest = divmod(row, SUB)
        c, rest = divmod(rest, 48)
        y, r = divmod(rest, 12)
        place[row, (y * NC + c) * HD + j * 12 + r] = 1.0
    return jnp.asarray(place, BF)


def out_order():
    place = np.zeros((D, D), np.float32)
    row = 0
    for c in range(NC):
        for y in range(NY):
            for j in range(N_SEQ):
                for half in range(2):
                    for r in range(12):
                        place[row, (half * 8 + y * NC + c) * HD + j * 12 + r] = 1.0
                        row += 1
    return jnp.asarray(place, BF)


def out_pad_order():
    place = np.zeros((N_SEQ * 32, SUB), np.float32)
    for j in range(N_SEQ):
        for half in range(2):
            for r in range(12):
                place[j * 32 + half * 16 + r, j * 24 + half * 12 + r] = 1.0
    return jnp.asarray(place, BF)


def pad_order():
    place = np.zeros((SUB, YROWS), np.float32)
    for z in range(6):
        for r in range(12):
            place[z * 16 + r, z * 12 + r] = 1.0
        for r in range(3):
            place[z * 16 + 12 + r, 72 + r] = 1.0
    return jnp.asarray(place, BF)


SMEM = pl.BlockSpec(memory_space=pltpu.SMEM)
VMEM = pl.BlockSpec(memory_space=pltpu.VMEM)
HBM = pl.BlockSpec(memory_space=pltpu.HBM)
ANY = pl.BlockSpec(memory_space=pl.ANY)


def call(kernel, out_shapes, args, scratch=(), micros=1.0, specs=None, grant=24, unread=0):
    if specs is None:
        specs = [SMEM if a.dtype == jnp.int32 else VMEM for a in args]
        specs = specs[: len(specs) - unread] + [ANY] * unread
    return pl.pallas_call(
        kernel,
        out_shape=out_shapes,
        in_specs=specs,
        out_specs=[VMEM] * len(out_shapes),
        scratch_shapes=list(scratch),
        compiler_params=pltpu.CompilerParams(vmem_limit_bytes=grant * 1024 * 1024),
        cost_estimate=pl.CostEstimate(
            flops=int(micros * 1.0e9), bytes_accessed=int(micros * 1.0e6), transcendentals=0
        ),
    )(*args)


def shape(*dims, dtype=BF):
    return jax.ShapeDtypeStruct(dims, dtype)


def slide_at(z, y, c):
    return (z * NY + y) * NC + c


CORE_PAIRS = [(i, i ^ 1) for i in range(NZ * NY * NC)]
Z_GROUPS = [[slide_at(z, y, c) for z in range(NZ)] for y in range(NY) for c in range(NC)]
SEQ_TURNS = [[(k, (k + t) % N_SEQ) for k in range(N_SEQ)] for t in range(N_SEQ)]
Y_TURNS = [
    [
        (slide_at(z, y, c), slide_at(z, (y + t) % NY, c))
        for z in range(NZ)
        for y in range(NY)
        for c in range(NC)
    ]
    for t in range(NY)
]


def swap(arrays, axis, turns, order=(1, 2, 3)):
    got = {t: lax.ppermute(arrays[t], axis, turns[t]) for t in order}
    return [arrays[0], got[1], got[2], got[3]]


def per_device(embeddings, tile_counts, masked_tiles, w_in, norm_gain, w_qkv, w_out):
    inv_count = 1.0 / (lax.axis_size("slide") * masked_tiles.shape[1])
    hidden, normed, projected, dilated = call(
        prep_kernel,
        [shape(TOK, D), shape(TOK, D), shape(TOK, 3 * D), shape(FAR, 2 * D)],
        (embeddings, masked_tiles, norm_gain, w_in, w_qkv),
        [
            pltpu.VMEM((TOK, 2 * D), BF),
            pltpu.VMEM((1, TOK), jnp.int32),
            pltpu.VMEM((D,), F32),
            pltpu.VMEM((2 * D, D), BF),
            pltpu.VMEM((D, 3 * D), BF),
            pltpu.SemaphoreType.DMA((6 + 2 * D // 256,)),
        ],
        4.0,
        [HBM] * 5,
        60,
    )
    fars = swap([dilated] * N_SEQ, "seq", SEQ_TURNS, (2, 1, 3))
    norms = swap([normed] * N_SEQ, "seq", SEQ_TURNS, (1, 3, 2))
    fk, fv, pnear, pfar, attended, tiles, flag = call(
        forward_kernel,
        [
            shape(TOK, D),
            shape(TOK, D),
            shape(GROUPS, TOK, RATE * TOK, dtype=F32),
            shape(GROUPS, TOK, TOK, dtype=F32),
            shape(TOK, D),
            shape(TOK, 2 * D),
            shape(TOK, TOK, dtype=F32),
        ],
        (tile_counts.reshape(1, 1), fars[2], fars[1], fars[3], projected, embeddings, masked_tiles),
        [pltpu.VMEM((TOK, D), F32)],
        2.0,
        [VMEM] * 7,
    )
    grad_attended, loss, out_mine, out_other = call(
        functools.partial(chain_kernel, inv_count),
        [shape(TOK, D), shape(16, 128), shape(HALF, D), shape(HALF, D)],
        (attended, hidden, tiles, flag, w_in, w_out, out_order()),
        (),
        3.0,
    )
    out_other = lax.ppermute(out_other, "slide", CORE_PAIRS)
    sent = call(
        backward_kernel,
        [shape(XROWS, TOK)] * N_SEQ,
        (projected, fk, fv, pnear, pfar, grad_attended, loss, spread_order()),
        [pltpu.VMEM((TOK, D), F32)] * 5 + [pltpu.VMEM((SECTIONS, HALF, TOK), BF)],
        8.0,
    )
    got = swap(sent, "seq", SEQ_TURNS)
    out = call(out_core_kernel, [shape(SUB, D)] * NY, (out_mine, out_other, sent[0], norms[1], norms[3], norms[2]), unread=4)
    out = swap(out, "slide", Y_TURNS)
    out_sums = call(
        out_y_kernel, [shape(32, D)] * N_SEQ, (out[0], out[2], out[1], out[3], out_pad_order()), (), 20.0
    )
    out = swap(out_sums, "seq", SEQ_TURNS)
    whole, tail = call(
        product_kernel,
        [shape(6 * SUB, D, dtype=F32), shape(YROWS, D, dtype=F32)],
        (got[0], got[2], got[1], got[3], norms[0], norms[1], norms[3], norms[2], out_sums[0]),
        [
            pltpu.VMEM((N_SEQ, XROWS, TOK), BF),
            pltpu.VMEM((6 * SUB, N_SEQ * TOK), BF),
            pltpu.VMEM((N_SEQ * TOK, D), BF),
        ],
        15.0,
        unread=1,
    )
    mine, other = call(
        place_kernel,
        [shape(NY * YROWS, D)] * 2,
        (whole, tail, *out[1:]),
        unread=3,
    )
    other = lax.ppermute(other, "slide", CORE_PAIRS)
    by_y = call(core_kernel, [shape(YROWS, D)] * NY, (mine, other))
    by_y = swap(by_y, "slide", Y_TURNS)
    (by_z,) = call(
        y_kernel,
        [shape(NZ, 16, D)],
        (by_y[0], by_y[2], by_y[1], by_y[3], *out, pad_order()),
    )
    by_z = lax.all_to_all(by_z, "slide", 0, 0, tiled=True, axis_index_groups=Z_GROUPS)
    gradients, loss = call(z_kernel, [shape(12, D, dtype=F32), shape(1, 1, dtype=F32)], (by_z,))
    return (gradients, loss[0, 0])


def solution(mesh):
    in_specs = (P("slide", "seq", None), P("slide"), P("slide", None), P(), P(), P(), P())
    out_specs = (P(("slide", "seq"), None), P())
    return jax.shard_map(
        per_device, mesh=mesh, in_specs=in_specs, out_specs=out_specs, check_vma=False
    )
```

```python
import functools
import math

import numpy as np
import jax
import jax.numpy as jnp
from jax import lax
from jax.experimental import pallas as pl
from jax.experimental.pallas import tpu as pltpu
from jax.sharding import PartitionSpec as P

HEADS = 16
RATE = 4
HD = 48
D = 768
TOK = 128
N_SEQ = 4
GROUPS = HEADS // RATE
FAR = TOK // RATE
NORM_EPS = 1e-06
NEG_FILL = -1e30
SCALE = 1.0 / math.sqrt(HD)
BF = jnp.bfloat16
F32 = jnp.float32
HALF = 384
SUB = 96
SECTIONS = 10
YROWS = 80
XROWS = SECTIONS * SUB + 16
NZ, NY, NC = 8, 4, 2


def dot(a, b, dims):
    return lax.dot_general(a, b, (dims, ((), ())), preferred_element_type=F32)


def nn(a, b):
    return dot(a, b, ((1,), (0,)))


def nt(a, b):
    return dot(a, b, ((1,), (1,)))


def tn(a, b):
    return dot(a, b, ((0,), (0,)))


def iota(shape, dim):
    return lax.broadcasted_iota(jnp.int32, shape, dim)


def class_major(index):
    return (index & (FAR - 1)) * RATE + (index >> 5)


def split_rows(value, shape, first):
    high = value.astype(BF).astype(F32)
    rest = value - high
    mid = rest.astype(BF).astype(F32)
    low = rest - mid
    row = iota(shape, 0)
    return jnp.where(
        row == first,
        high,
        jnp.where(row == first + 1, mid, jnp.where(row == first + 2, low, 0.0)),
    )


def class_order():
    shape = (TOK, TOK)
    return (iota(shape, 1) == class_major(iota(shape, 0))).astype(F32).astype(BF)


def masked_rows(positions, masked):
    hits = jnp.where(positions == masked, 1.0, 0.0)
    return jnp.broadcast_to(jnp.max(hits, axis=1, keepdims=True), (TOK, TOK))


def prep_kernel(
    tiles_hbm, masked_hbm, gain_hbm, w_in_hbm, w_qkv_hbm,
    hidden_out, normed_out, proj_out, dilated_out,
    tiles, masked, gain, w_in, w_qkv, sems,
):
    blocks = w_in_hbm.shape[0] // 256
    loads = [
        pltpu.make_async_copy(masked_hbm, masked, sems.at[0]),
        pltpu.make_async_copy(tiles_hbm.at[0], tiles, sems.at[1]),
        pltpu.make_async_copy(gain_hbm, gain, sems.at[2]),
    ]
    chunks = [
        pltpu.make_async_copy(
            w_in_hbm.at[256 * i : 256 * (i + 1)], w_in.at[256 * i : 256 * (i + 1)], sems.at[6 + i]
        )
        for i in range(blocks)
    ]
    parts = [
        pltpu.make_async_copy(
            w_qkv_hbm.at[:, D * i : D * (i + 1)], w_qkv.at[:, D * i : D * (i + 1)], sems.at[3 + i]
        )
        for i in range(3)
    ]
    for copy in loads + chunks + parts[1:] + parts[:1]:
        copy.start()
    order = class_order()
    positions = lax.axis_index("seq") * TOK + iota((TOK, TOK), 0)
    loads[0].wait()
    flag = masked_rows(positions, masked[...])[:, 0:1] > 0.5
    loads[1].wait()
    hidden = jnp.zeros((TOK, D), F32)
    for i in range(blocks):
        cols = slice(256 * i, 256 * (i + 1))
        inputs = jnp.where(flag, jnp.zeros((), BF), tiles[:, cols])
        chunks[i].wait()
        hidden += nn(inputs, w_in[cols])
    hidden_f = nn(order, hidden.astype(BF))
    hidden_out[...] = hidden_f.astype(BF)
    scale_rows = lax.rsqrt(jnp.mean(hidden_f * hidden_f, axis=1, keepdims=True) + NORM_EPS)
    loads[2].wait()
    normed = (hidden_f * scale_rows * gain[...].reshape(1, D)).astype(BF)
    normed_out[...] = normed
    for part in (1, 2, 0):
        parts[part].wait()
        for block in range(D // 256):
            first = part * D + block * 256
            rows = nn(normed, w_qkv[:, first : first + 256]).astype(BF)
            proj_out[:, first : first + 256] = rows
            if part > 0:
                dilated_out[:, first - D : first - D + 256] = dilate(rows, block * 256)


def dilate(rows, lane0):
    lane_class = ((iota((FAR, 256), 1) + lane0) // HD) & 3
    return by_class(lane_class, [rows[FAR * r : FAR * (r + 1)] for r in range(RATE)])


def window(group):
    return (group * RATE * HD) // 128 * 128


def head_masks(group):
    lane = iota((TOK, 256), 1) + window(group)
    row_class = iota((TOK, 256), 0) >> 5
    masks = []
    for r in range(RATE):
        first = (group * RATE + r) * HD
        masks.append((lane >= first) & (lane < first + HD))
    picked = masks[0] & (row_class == 0)
    for r in range(1, RATE):
        picked = picked | (masks[r] & (row_class == r))
    return masks, picked


def keep(mask, value):
    return jnp.where(mask, value, jnp.zeros((), value.dtype))


def by_class(own_class, pieces):
    out = pieces[0]
    for r in range(1, RATE):
        out = jnp.where(own_class == r, pieces[r], out)
    return out


def forward_kernel(
    count_ref, f1, f2, f3, proj_ref, tiles_ref, masked_ref,
    fk_ref, fv_ref, pnear_ref, pfar_ref, att_ref, tiles_out, flag_ref,
    att_acc,
):
    count = count_ref[...]
    seq = lax.axis_index("seq")
    pos0 = seq * TOK
    for turn, ref in enumerate((f1, f2, f3)):
        rows = pl.ds(pl.multiple_of(((seq - turn - 1) & 3) * FAR, FAR), FAR)
        fk_ref[rows] = ref[:, 0:D]
        fv_ref[rows] = ref[:, D:]
    own_rows = pl.ds(pl.multiple_of(seq * FAR, FAR), FAR)
    for part, far_ref in enumerate((fk_ref, fv_ref)):
        for block in range(D // 256):
            first = (1 + part) * D + block * 256
            far_ref[own_rows, block * 256 : (block + 1) * 256] = dilate(
                proj_ref[:, first : first + 256], block * 256
            )
    flag_ref[...] = masked_rows(pos0 + class_major(iota((TOK, TOK), 0)), masked_ref[...])
    tiles_out[...] = nn(class_order(), tiles_ref[0]).astype(BF)

    square = (TOK, TOK)
    key_pos = pos0 + class_major(iota(square, 0))
    query_pos = pos0 + class_major(iota(square, 1))
    near_ok = (key_pos < count) | (key_pos == query_pos)
    far_row = iota(square, 0)
    far_ok = (far_row >> 5) * TOK + (far_row & (FAR - 1)) * RATE + (iota(square, 1) >> 5) < count
    own_class = iota((1, TOK), 1) >> 5

    att_acc[...] = jnp.zeros_like(att_acc)
    for g in range(GROUPS):
        lo = window(g)
        win = slice(lo, lo + 256)
        masks, picked = head_masks(g)
        q = proj_ref[:, lo : lo + 256]
        k = proj_ref[:, D + lo : D + lo + 256]
        v = proj_ref[:, 2 * D + lo : 2 * D + lo + 256]
        near = nt(k, jnp.concatenate([keep(m, q) for m in masks], 0))
        far = jnp.where(far_ok, nt(fk_ref[:, win], keep(picked, q)) * SCALE, NEG_FILL)
        far_max = jnp.max(far, axis=0, keepdims=True)
        scores = [
            jnp.where(near_ok, near[:, TOK * r : TOK * (r + 1)] * SCALE, NEG_FILL) for r in range(RATE)
        ]
        tops = []
        for r in range(RATE):
            top = jnp.max(scores[r], axis=0, keepdims=True)
            tops.append(jnp.where(own_class == r, jnp.maximum(top, far_max), top))
        exps = [jnp.exp(scores[r] - tops[r]) for r in range(RATE)]
        far_exp = jnp.exp(far - by_class(own_class, tops))
        far_sum = jnp.sum(far_exp, axis=0, keepdims=True)
        inverse = []
        for r in range(RATE):
            total = jnp.sum(exps[r], axis=0, keepdims=True)
            inverse.append(1.0 / jnp.where(own_class == r, total + far_sum, total))
        probs = [exps[r] * inverse[r] for r in range(RATE)]
        far_probs = far_exp * by_class(own_class, inverse)
        for r in range(RATE):
            pnear_ref[g, :, TOK * r : TOK * (r + 1)] = probs[r]
        pfar_ref[g] = far_probs
        att = tn(
            jnp.concatenate([p.astype(BF) for p in probs], 0),
            jnp.concatenate([keep(m, v) for m in masks], 0),
        )
        att_acc[:, win] += att + keep(picked, tn(far_probs.astype(BF), fv_ref[:, win]))
    att_ref[...] = att_acc[...].astype(BF)


def chain_kernel(
    inv_count,
    att_ref, hidden_ref, tiles_ref, flag_ref, w_in_ref, w_out_ref, order_ref,
    ga_ref, loss_ref, mine_ref, other_ref,
):
    core = lax.axis_index("slide") & 1
    attended = att_ref[...]
    mixed = (hidden_ref[...].astype(F32) + nn(attended, w_out_ref[...])).astype(BF)
    flag = flag_ref[:, 0:1] > 0.5
    error = jnp.where(flag, nt(mixed, w_in_ref[...]) - tiles_ref[...].astype(F32), 0.0)
    loss = jnp.sum(jnp.sum(error * error, axis=1, keepdims=True), axis=0, keepdims=True) * inv_count
    loss_ref[...] = split_rows(jnp.broadcast_to(loss, (16, 128)), (16, 128), 0).astype(BF)
    grad_pred = (2.0 * inv_count * error).astype(BF)
    grad_mixed = nn(grad_pred, w_in_ref[...]).astype(BF)
    ga_ref[...] = nt(grad_mixed, w_out_ref[...]).astype(BF)
    for turn, ref in enumerate((mine_ref, other_ref)):
        first = pl.multiple_of(((core + turn) & 1) * HALF, HALF)
        left = nt(order_ref[pl.ds(first, HALF)], grad_mixed).astype(BF)
        ref[...] = nn(left, attended).astype(BF)


def backward_kernel(
    proj_ref, fk_ref, fv_ref, pnear_ref, pfar_ref, ga_ref, loss_ref, spread_ref,
    x0, x1, x2, x3,
    gq, gk, gv, gkf, gvf, turned,
):
    seq = lax.axis_index("seq")
    own_class = iota((1, TOK), 1) >> 5
    for ref in (gq, gk, gv, gkf, gvf):
        ref[...] = jnp.zeros_like(ref)
    for g in range(GROUPS):
        lo = window(g)
        win = slice(lo, lo + 256)
        masks, picked = head_masks(g)
        q = proj_ref[:, lo : lo + 256]
        k = proj_ref[:, D + lo : D + lo + 256]
        v = proj_ref[:, 2 * D + lo : 2 * D + lo + 256]
        ga = ga_ref[:, win]
        fk = fk_ref[:, win]
        fv = fv_ref[:, win]
        ga_stack = jnp.concatenate([keep(m, ga) for m in masks], 0)
        ga_picked = keep(picked, ga)
        near = nt(v, ga_stack)
        far = nt(fv, ga_picked)
        probs = [pnear_ref[g, :, TOK * r : TOK * (r + 1)] for r in range(RATE)]
        far_probs = pfar_ref[g]
        far_dot = jnp.sum(far_probs * far, axis=0, keepdims=True)
        grads = [near[:, TOK * r : TOK * (r + 1)] for r in range(RATE)]
        dots = []
        for r in range(RATE):
            own = jnp.sum(probs[r] * grads[r], axis=0, keepdims=True)
            dots.append(jnp.where(own_class == r, own + far_dot, own))
        scores = [(probs[r] * (grads[r] - dots[r]) * SCALE).astype(BF) for r in range(RATE)]
        far_scores = (far_probs * (far - by_class(own_class, dots)) * SCALE).astype(BF)
        gq[:, win] += tn(
            jnp.concatenate(scores, 0), jnp.concatenate([keep(m, k) for m in masks], 0)
        ) + keep(picked, tn(far_scores, fk))
        gk[:, win] += nn(
            jnp.concatenate(scores, 1), jnp.concatenate([keep(m, q) for m in masks], 0)
        )
        gv[:, win] += nn(jnp.concatenate([p.astype(BF) for p in probs], 1), ga_stack)
        gkf[:, win] += nn(far_scores, keep(picked, q))
        gvf[:, win] += nn(far_probs.astype(BF), ga_picked)
    place = spread_ref[...]
    for section, value in enumerate((gq, gk, gv, gkf, gvf)):
        halves = jnp.concatenate([value[:, 0:HALF], value[:, HALF:]], 0).astype(BF)
        both = nt(place, halves).astype(BF)
        turned[2 * section] = both[:, 0:TOK]
        turned[2 * section + 1] = both[:, TOK:]
    for turn, ref in enumerate((x0, x1, x2, x3)):
        first = pl.multiple_of(((seq + turn) & 3) * SUB, 16)
        for section in range(SECTIONS):
            ref[section * SUB : (section + 1) * SUB] = turned[section, pl.ds(first, SUB)]
        ref[SECTIONS * SUB :] = loss_ref[...]


def product_kernel(
    x0, x1, x2, x3, n0, n1, n3, n2, wait_ref, whole_ref, tail_ref, got, left, right
):
    seq = lax.axis_index("seq")
    for turn, (x_ref, n_ref) in enumerate(zip((x0, x1, x2, x3), (n0, n1, n2, n3))):
        src = (seq - turn) & 3
        got[src] = x_ref[...]
        right[pl.ds(pl.multiple_of(src * TOK, TOK), TOK)] = n_ref[...]
    for src in range(N_SEQ):
        left[0 : 2 * SUB, src * TOK : (src + 1) * TOK] = got[src, 0 : 2 * SUB]
    shape = (SUB, TOK)
    row = iota(shape, 0)
    lane_class = iota(shape, 1) >> 5
    core_row = jnp.where(row >= 48, 1, 0)
    row_y = (row - 48 * core_row) // 12
    row_class = ((row_y & 1) << 1) + core_row
    spots = [(row_class == r) & (lane_class == r) for r in range(RATE)]
    for part in range(2):
        for half in range(2):
            near_at = (2 + 2 * part + half) * SUB
            far_at = (6 + 2 * part + half) * SUB
            far = got[0, far_at : far_at + SUB].astype(F32)
            for src in range(1, N_SEQ):
                far = far + got[src, far_at : far_at + SUB].astype(F32)
            turns = [far] + [pltpu.roll(far, FAR * t, 1) for t in range(1, RATE)]
            for src in range(N_SEQ):
                total = got[src, near_at : near_at + SUB].astype(F32)
                for r in range(RATE):
                    total = total + jnp.where(spots[r], turns[(r - src) & 3], 0.0)
                left[near_at : near_at + SUB, src * TOK : (src + 1) * TOK] = total.astype(BF)
    whole_ref[...] = nn(left[...], right[...])
    loss = got[0, SECTIONS * SUB :].astype(F32)
    for src in range(1, N_SEQ):
        loss = loss + got[src, SECTIONS * SUB :].astype(F32)
    loss = jnp.sum(loss, axis=0, keepdims=True)[:, 0:1]
    tail_ref[...] = split_rows(jnp.broadcast_to(loss, (YROWS, D)), (YROWS, D), 72)


def place_kernel(whole_ref, tail_ref, wait1, wait2, wait3, mine_ref, other_ref):
    core = lax.axis_index("slide") & 1
    tail = tail_ref[72:]
    for turn, ref in enumerate((mine_ref, other_ref)):
        side = ((core + turn) & 1) * 48
        blocks = [whole_ref[pl.ds(pl.multiple_of(z * SUB + side, 16), 48)] for z in range(6)]
        for y in range(NY):
            rows = [block[12 * y : 12 * (y + 1)] for block in blocks]
            ref[y * YROWS : (y + 1) * YROWS] = jnp.concatenate(rows + [tail], 0).astype(BF)


def resplit(total):
    row = iota(total.shape, 0)
    loss = jnp.sum(jnp.where(row >= 72, total, 0.0), axis=0, keepdims=True)
    pieces = split_rows(jnp.broadcast_to(loss, total.shape), total.shape, 72)
    return jnp.where(row >= 72, pieces, total), loss


def core_kernel(mine_ref, other_ref, y0, y1, y2, y3):
    y = (lax.axis_index("slide") >> 1) & 3
    for turn, ref in enumerate((y0, y1, y2, y3)):
        rows = pl.ds(pl.multiple_of(((y + turn) & 3) * YROWS, 16), YROWS)
        ref[...] = resplit(mine_ref[rows].astype(F32) + other_ref[rows].astype(F32))[0].astype(BF)


def y_kernel(y0, y1, y2, y3, o0, o1, o2, o3, order_ref, out_ref):
    total = y0[...].astype(F32) + y1[...].astype(F32) + y2[...].astype(F32) + y3[...].astype(F32)
    total, loss = resplit(total)
    out_ref[0:6] = nn(order_ref[...], total.astype(BF)).astype(BF).reshape(6, 16, D)
    out = o0[...].astype(F32) + o1[...].astype(F32) + o2[...].astype(F32) + o3[...].astype(F32)
    tail = split_rows(jnp.broadcast_to(loss, (16, D)), (16, D), 12)
    for half in range(2):
        out_ref[6 + half] = (out[16 * half : 16 * (half + 1)] + tail).astype(BF)


def out_core_kernel(mine_ref, other_ref, wait0, wait1, wait2, wait3, y0, y1, y2, y3):
    y = (lax.axis_index("slide") >> 1) & 3
    for turn, ref in enumerate((y0, y1, y2, y3)):
        rows = pl.ds(pl.multiple_of(((y + turn) & 3) * SUB, 16), SUB)
        ref[...] = (mine_ref[rows].astype(F32) + other_ref[rows].astype(F32)).astype(BF)


def out_y_kernel(y0, y1, y2, y3, order_ref, x0, x1, x2, x3):
    seq = lax.axis_index("seq")
    total = y0[...].astype(F32) + y1[...].astype(F32) + y2[...].astype(F32) + y3[...].astype(F32)
    total = total.astype(BF)
    for turn, ref in enumerate((x0, x1, x2, x3)):
        rows = pl.ds(pl.multiple_of(((seq + turn) & 3) * 32, 32), 32)
        ref[...] = nn(order_ref[rows], total).astype(BF)


def z_kernel(in_ref, out_ref, loss_ref):
    total = in_ref[0].astype(F32)
    for src in range(1, NZ):
        total = total + in_ref[src].astype(F32)
    out_ref[...] = total[0:12]
    loss_ref[...] = jnp.sum(total[12:15, 0:1], axis=0, keepdims=True)


def spread_order():
    place = np.zeros((HALF, HALF), np.float32)
    for row in range(HALF):
        j, rest = divmod(row, SUB)
        c, rest = divmod(rest, 48)
        y, r = divmod(rest, 12)
        place[row, (y * NC + c) * HD + j * 12 + r] = 1.0
    return jnp.asarray(place, BF)


def out_order():
    place = np.zeros((D, D), np.float32)
    row = 0
    for c in range(NC):
        for y in range(NY):
            for j in range(N_SEQ):
                for half in range(2):
                    for r in range(12):
                        place[row, (half * 8 + y * NC + c) * HD + j * 12 + r] = 1.0
                        row += 1
    return jnp.asarray(place, BF)


def out_pad_order():
    place = np.zeros((N_SEQ * 32, SUB), np.float32)
    for j in range(N_SEQ):
        for half in range(2):
            for r in range(12):
                place[j * 32 + half * 16 + r, j * 24 + half * 12 + r] = 1.0
    return jnp.asarray(place, BF)


def pad_order():
    place = np.zeros((SUB, YROWS), np.float32)
    for z in range(6):
        for r in range(12):
            place[z * 16 + r, z * 12 + r] = 1.0
        for r in range(3):
            place[z * 16 + 12 + r, 72 + r] = 1.0
    return jnp.asarray(place, BF)


SMEM = pl.BlockSpec(memory_space=pltpu.SMEM)
VMEM = pl.BlockSpec(memory_space=pltpu.VMEM)
HBM = pl.BlockSpec(memory_space=pltpu.HBM)
ANY = pl.BlockSpec(memory_space=pl.ANY)


def call(kernel, out_shapes, args, scratch=(), micros=1.0, specs=None, grant=24, unread=0):
    if specs is None:
        specs = [SMEM if a.dtype == jnp.int32 else VMEM for a in args]
        specs = specs[: len(specs) - unread] + [ANY] * unread
    return pl.pallas_call(
        kernel,
        out_shape=out_shapes,
        in_specs=specs,
        out_specs=[VMEM] * len(out_shapes),
        scratch_shapes=list(scratch),
        compiler_params=pltpu.CompilerParams(vmem_limit_bytes=grant * 1024 * 1024),
        cost_estimate=pl.CostEstimate(
            flops=int(micros * 1.0e9), bytes_accessed=int(micros * 1.0e6), transcendentals=0
        ),
    )(*args)


def shape(*dims, dtype=BF):
    return jax.ShapeDtypeStruct(dims, dtype)


def slide_at(z, y, c):
    return (z * NY + y) * NC + c


CORE_PAIRS = [(i, i ^ 1) for i in range(NZ * NY * NC)]
Z_GROUPS = [[slide_at(z, y, c) for z in range(NZ)] for y in range(NY) for c in range(NC)]
SEQ_TURNS = [[(k, (k + t) % N_SEQ) for k in range(N_SEQ)] for t in range(N_SEQ)]
Y_TURNS = [
    [
        (slide_at(z, y, c), slide_at(z, (y + t) % NY, c))
        for z in range(NZ)
        for y in range(NY)
        for c in range(NC)
    ]
    for t in range(NY)
]


def swap(arrays, axis, turns, order=(1, 2, 3)):
    got = {t: lax.ppermute(arrays[t], axis, turns[t]) for t in order}
    return [arrays[0], got[1], got[2], got[3]]


def per_device(embeddings, tile_counts, masked_tiles, w_in, norm_gain, w_qkv, w_out):
    inv_count = 1.0 / (lax.axis_size("slide") * masked_tiles.shape[1])
    hidden, normed, projected, dilated = call(
        prep_kernel,
        [shape(TOK, D), shape(TOK, D), shape(TOK, 3 * D), shape(FAR, 2 * D)],
        (embeddings, masked_tiles, norm_gain, w_in, w_qkv),
        [
            pltpu.VMEM((TOK, 2 * D), BF),
            pltpu.VMEM((1, TOK), jnp.int32),
            pltpu.VMEM((D,), F32),
            pltpu.VMEM((2 * D, D), BF),
            pltpu.VMEM((D, 3 * D), BF),
            pltpu.SemaphoreType.DMA((6 + 2 * D // 256,)),
        ],
        4.0,
        [HBM] * 5,
        60,
    )
    fars = swap([dilated] * N_SEQ, "seq", SEQ_TURNS, (2, 1, 3))
    norms = swap([normed] * N_SEQ, "seq", SEQ_TURNS, (1, 3, 2))
    fk, fv, pnear, pfar, attended, tiles, flag = call(
        forward_kernel,
        [
            shape(TOK, D),
            shape(TOK, D),
            shape(GROUPS, TOK, RATE * TOK, dtype=F32),
            shape(GROUPS, TOK, TOK, dtype=F32),
            shape(TOK, D),
            shape(TOK, 2 * D),
            shape(TOK, TOK, dtype=F32),
        ],
        (tile_counts.reshape(1, 1), *fars[1:], projected, embeddings, masked_tiles),
        [pltpu.VMEM((TOK, D), F32)],
        2.0,
        [VMEM] * 7,
    )
    grad_attended, loss, out_mine, out_other = call(
        functools.partial(chain_kernel, inv_count),
        [shape(TOK, D), shape(16, 128), shape(HALF, D), shape(HALF, D)],
        (attended, hidden, tiles, flag, w_in, w_out, out_order()),
        (),
        3.0,
    )
    out_other = lax.ppermute(out_other, "slide", CORE_PAIRS)
    sent = call(
        backward_kernel,
        [shape(XROWS, TOK)] * N_SEQ,
        (projected, fk, fv, pnear, pfar, grad_attended, loss, spread_order()),
        [pltpu.VMEM((TOK, D), F32)] * 5 + [pltpu.VMEM((SECTIONS, HALF, TOK), BF)],
        8.0,
    )
    got = swap(sent, "seq", SEQ_TURNS)
    out = call(out_core_kernel, [shape(SUB, D)] * NY, (out_mine, out_other, sent[0], norms[1], norms[3], norms[2]), unread=4)
    out = swap(out, "slide", Y_TURNS)
    out_sums = call(
        out_y_kernel, [shape(32, D)] * N_SEQ, (*out, out_pad_order()), (), 20.0
    )
    out = swap(out_sums, "seq", SEQ_TURNS)
    whole, tail = call(
        product_kernel,
        [shape(6 * SUB, D, dtype=F32), shape(YROWS, D, dtype=F32)],
        (*got, norms[0], norms[1], norms[3], norms[2], out_sums[0]),
        [
            pltpu.VMEM((N_SEQ, XROWS, TOK), BF),
            pltpu.VMEM((6 * SUB, N_SEQ * TOK), BF),
            pltpu.VMEM((N_SEQ * TOK, D), BF),
        ],
        15.0,
        unread=1,
    )
    mine, other = call(
        place_kernel,
        [shape(NY * YROWS, D)] * 2,
        (whole, tail, *out[1:]),
        unread=3,
    )
    other = lax.ppermute(other, "slide", CORE_PAIRS)
    by_y = call(core_kernel, [shape(YROWS, D)] * NY, (mine, other))
    by_y = swap(by_y, "slide", Y_TURNS)
    (by_z,) = call(
        y_kernel,
        [shape(NZ, 16, D)],
        (by_y[0], by_y[2], by_y[1], by_y[3], *out, pad_order()),
    )
    by_z = lax.all_to_all(by_z, "slide", 0, 0, tiled=True, axis_index_groups=Z_GROUPS)
    gradients, loss = call(z_kernel, [shape(12, D, dtype=F32), shape(1, 1, dtype=F32)], (by_z,))
    return (gradients, loss[0, 0])


def solution(mesh):
    in_specs = (P("slide", "seq", None), P("slide"), P("slide", None), P(), P(), P(), P())
    out_specs = (P(("slide", "seq"), None), P())
    return jax.shard_map(
        per_device, mesh=mesh, in_specs=in_specs, out_specs=out_specs, check_vma=False
    )
```

```python
import functools
import math

import numpy as np
import jax
import jax.numpy as jnp
from jax import lax
from jax.experimental import pallas as pl
from jax.experimental.pallas import tpu as pltpu
from jax.sharding import PartitionSpec as P

HEADS = 16
RATE = 4
HD = 48
D = 768
TOK = 128
N_SEQ = 4
GROUPS = HEADS // RATE
FAR = TOK // RATE
NORM_EPS = 1e-06
NEG_FILL = -1e30
SCALE = 1.0 / math.sqrt(HD)
BF = jnp.bfloat16
F32 = jnp.float32
HALF = 384
SUB = 96
SECTIONS = 9
YROWS = 80
XROWS = SECTIONS * SUB + 16
NZ, NY, NC = 8, 4, 2


def dot(a, b, dims):
    return lax.dot_general(a, b, (dims, ((), ())), preferred_element_type=F32)


def nn(a, b):
    return dot(a, b, ((1,), (0,)))


def nt(a, b):
    return dot(a, b, ((1,), (1,)))


def tn(a, b):
    return dot(a, b, ((0,), (0,)))


def iota(shape, dim):
    return lax.broadcasted_iota(jnp.int32, shape, dim)


def class_major(index):
    return (index & (FAR - 1)) * RATE + (index >> 5)


def split_rows(value, shape, first):
    high = value.astype(BF).astype(F32)
    rest = value - high
    mid = rest.astype(BF).astype(F32)
    low = rest - mid
    row = iota(shape, 0)
    return jnp.where(
        row == first,
        high,
        jnp.where(row == first + 1, mid, jnp.where(row == first + 2, low, 0.0)),
    )


def class_order():
    shape = (TOK, TOK)
    return (iota(shape, 1) == class_major(iota(shape, 0))).astype(F32).astype(BF)


def masked_rows(positions, masked):
    hits = jnp.where(positions == masked, 1.0, 0.0)
    return jnp.broadcast_to(jnp.max(hits, axis=1, keepdims=True), (TOK, TOK))


def prep_kernel(
    tiles_hbm, masked_hbm, gain_hbm, w_in_hbm, w_qkv_hbm,
    hidden_out, normed_out, proj_out, dilated_out,
    tiles, masked, gain, w_in, w_qkv, sems,
):
    blocks = w_in_hbm.shape[0] // 256
    loads = [
        pltpu.make_async_copy(masked_hbm, masked, sems.at[0]),
        pltpu.make_async_copy(tiles_hbm.at[0], tiles, sems.at[1]),
        pltpu.make_async_copy(gain_hbm, gain, sems.at[2]),
    ]
    chunks = [
        pltpu.make_async_copy(
            w_in_hbm.at[256 * i : 256 * (i + 1)], w_in.at[256 * i : 256 * (i + 1)], sems.at[6 + i]
        )
        for i in range(blocks)
    ]
    parts = [
        pltpu.make_async_copy(
            w_qkv_hbm.at[:, D * i : D * (i + 1)], w_qkv.at[:, D * i : D * (i + 1)], sems.at[3 + i]
        )
        for i in range(3)
    ]
    for copy in loads + chunks + parts[1:] + parts[:1]:
        copy.start()
    order = class_order()
    positions = lax.axis_index("seq") * TOK + iota((TOK, TOK), 0)
    loads[0].wait()
    flag = masked_rows(positions, masked[...])[:, 0:1] > 0.5
    loads[1].wait()
    hidden = jnp.zeros((TOK, D), F32)
    for i in range(blocks):
        cols = slice(256 * i, 256 * (i + 1))
        inputs = jnp.where(flag, jnp.zeros((), BF), tiles[:, cols])
        chunks[i].wait()
        hidden += nn(inputs, w_in[cols])
    hidden_f = nn(order, hidden.astype(BF))
    hidden_out[...] = hidden_f.astype(BF)
    scale_rows = lax.rsqrt(jnp.mean(hidden_f * hidden_f, axis=1, keepdims=True) + NORM_EPS)
    loads[2].wait()
    normed = (hidden_f * scale_rows * gain[...].reshape(1, D)).astype(BF)
    normed_out[...] = normed
    for part in (1, 2, 0):
        parts[part].wait()
        for block in range(D // 256):
            first = part * D + block * 256
            rows = nn(normed, w_qkv[:, first : first + 256]).astype(BF)
            proj_out[:, first : first + 256] = rows
            if part > 0:
                dilated_out[:, first - D : first - D + 256] = dilate(rows, block * 256)


def dilate(rows, lane0):
    lane_class = ((iota((FAR, 256), 1) + lane0) // HD) & 3
    return by_class(lane_class, [rows[FAR * r : FAR * (r + 1)] for r in range(RATE)])


def window(group):
    return (group * RATE * HD) // 128 * 128


def head_masks(group):
    lane = iota((TOK, 256), 1) + window(group)
    row_class = iota((TOK, 256), 0) >> 5
    masks = []
    for r in range(RATE):
        first = (group * RATE + r) * HD
        masks.append((lane >= first) & (lane < first + HD))
    picked = masks[0] & (row_class == 0)
    for r in range(1, RATE):
        picked = picked | (masks[r] & (row_class == r))
    return masks, picked


def keep(mask, value):
    return jnp.where(mask, value, jnp.zeros((), value.dtype))


def by_class(own_class, pieces):
    out = pieces[0]
    for r in range(1, RATE):
        out = jnp.where(own_class == r, pieces[r], out)
    return out


def forward_kernel(
    count_ref, f2, f1, f3, proj_ref, tiles_ref, masked_ref,
    fk_ref, fv_ref, pnear_ref, pfar_ref, att_ref, tiles_out, flag_ref,
    att_acc,
):
    count = count_ref[...]
    seq = lax.axis_index("seq")
    pos0 = seq * TOK
    for turn, ref in enumerate((f1, f2, f3)):
        rows = pl.ds(pl.multiple_of(((seq - turn - 1) & 3) * FAR, FAR), FAR)
        fk_ref[rows] = ref[:, 0:D]
        fv_ref[rows] = ref[:, D:]
    own_rows = pl.ds(pl.multiple_of(seq * FAR, FAR), FAR)
    for part, far_ref in enumerate((fk_ref, fv_ref)):
        for block in range(D // 256):
            first = (1 + part) * D + block * 256
            far_ref[own_rows, block * 256 : (block + 1) * 256] = dilate(
                proj_ref[:, first : first + 256], block * 256
            )
    flag_ref[...] = masked_rows(pos0 + class_major(iota((TOK, TOK), 0)), masked_ref[...])
    tiles_out[...] = nn(class_order(), tiles_ref[0]).astype(BF)

    square = (TOK, TOK)
    key_pos = pos0 + class_major(iota(square, 0))
    query_pos = pos0 + class_major(iota(square, 1))
    near_ok = (key_pos < count) | (key_pos == query_pos)
    far_row = iota(square, 0)
    far_ok = (far_row >> 5) * TOK + (far_row & (FAR - 1)) * RATE + (iota(square, 1) >> 5) < count
    own_class = iota((1, TOK), 1) >> 5

    att_acc[...] = jnp.zeros_like(att_acc)
    for g in range(GROUPS):
        lo = window(g)
        win = slice(lo, lo + 256)
        masks, picked = head_masks(g)
        q = proj_ref[:, lo : lo + 256]
        k = proj_ref[:, D + lo : D + lo + 256]
        v = proj_ref[:, 2 * D + lo : 2 * D + lo + 256]
        near = nt(k, jnp.concatenate([keep(m, q) for m in masks], 0))
        far = jnp.where(far_ok, nt(fk_ref[:, win], keep(picked, q)) * SCALE, NEG_FILL)
        far_max = jnp.max(far, axis=0, keepdims=True)
        scores = [
            jnp.where(near_ok, near[:, TOK * r : TOK * (r + 1)] * SCALE, NEG_FILL) for r in range(RATE)
        ]
        tops = []
        for r in range(RATE):
            top = jnp.max(scores[r], axis=0, keepdims=True)
            tops.append(jnp.where(own_class == r, jnp.maximum(top, far_max), top))
        exps = [jnp.exp(scores[r] - tops[r]) for r in range(RATE)]
        far_exp = jnp.exp(far - by_class(own_class, tops))
        far_sum = jnp.sum(far_exp, axis=0, keepdims=True)
        inverse = []
        for r in range(RATE):
            total = jnp.sum(exps[r], axis=0, keepdims=True)
            inverse.append(1.0 / jnp.where(own_class == r, total + far_sum, total))
        probs = [exps[r] * inverse[r] for r in range(RATE)]
        far_probs = far_exp * by_class(own_class, inverse)
        for r in range(RATE):
            pnear_ref[g, :, TOK * r : TOK * (r + 1)] = probs[r]
        pfar_ref[g] = far_probs
        att = tn(
            jnp.concatenate([p.astype(BF) for p in probs], 0),
            jnp.concatenate([keep(m, v) for m in masks], 0),
        )
        att_acc[:, win] += att + keep(picked, tn(far_probs.astype(BF), fv_ref[:, win]))
    att_ref[...] = att_acc[...].astype(BF)


def chain_kernel(
    inv_count,
    att_ref, hidden_ref, tiles_ref, flag_ref, w_in_ref, w_out_ref, order_ref,
    ga_ref, loss_ref, mine_ref, other_ref,
):
    core = lax.axis_index("slide") & 1
    attended = att_ref[...]
    mixed = (hidden_ref[...].astype(F32) + nn(attended, w_out_ref[...])).astype(BF)
    flag = flag_ref[:, 0:1] > 0.5
    error = jnp.where(flag, nt(mixed, w_in_ref[...]) - tiles_ref[...].astype(F32), 0.0)
    loss = jnp.sum(jnp.sum(error * error, axis=1, keepdims=True), axis=0, keepdims=True) * inv_count
    loss_ref[...] = split_rows(jnp.broadcast_to(loss, (16, 128)), (16, 128), 0).astype(BF)
    grad_pred = (2.0 * inv_count * error).astype(BF)
    grad_mixed = nn(grad_pred, w_in_ref[...]).astype(BF)
    ga_ref[...] = nt(grad_mixed, w_out_ref[...]).astype(BF)
    for turn, ref in enumerate((mine_ref, other_ref)):
        first = pl.multiple_of(((core + turn) & 1) * HALF, HALF)
        left = nt(order_ref[pl.ds(first, HALF)], grad_mixed).astype(BF)
        ref[...] = nn(left, attended).astype(BF)


def backward_kernel(
    proj_ref, fk_ref, fv_ref, pnear_ref, pfar_ref, ga_ref, loss_ref, spread_ref,
    x0, x1, x2, x3,
    gq, gk, gv, gkf, gvf, turned,
):
    seq = lax.axis_index("seq")
    own_class = iota((1, TOK), 1) >> 5
    for ref in (gq, gk, gv, gkf, gvf):
        ref[...] = jnp.zeros_like(ref)
    for g in range(GROUPS):
        lo = window(g)
        win = slice(lo, lo + 256)
        masks, picked = head_masks(g)
        q = proj_ref[:, lo : lo + 256]
        k = proj_ref[:, D + lo : D + lo + 256]
        v = proj_ref[:, 2 * D + lo : 2 * D + lo + 256]
        ga = ga_ref[:, win]
        fk = fk_ref[:, win]
        fv = fv_ref[:, win]
        ga_stack = jnp.concatenate([keep(m, ga) for m in masks], 0)
        ga_picked = keep(picked, ga)
        near = nt(v, ga_stack)
        far = nt(fv, ga_picked)
        probs = [pnear_ref[g, :, TOK * r : TOK * (r + 1)] for r in range(RATE)]
        far_probs = pfar_ref[g]
        far_dot = jnp.sum(far_probs * far, axis=0, keepdims=True)
        grads = [near[:, TOK * r : TOK * (r + 1)] for r in range(RATE)]
        dots = []
        for r in range(RATE):
            own = jnp.sum(probs[r] * grads[r], axis=0, keepdims=True)
            dots.append(jnp.where(own_class == r, own + far_dot, own))
        scores = [(probs[r] * (grads[r] - dots[r]) * SCALE).astype(BF) for r in range(RATE)]
        far_scores = (far_probs * (far - by_class(own_class, dots)) * SCALE).astype(BF)
        gq[:, win] += tn(
            jnp.concatenate(scores, 0), jnp.concatenate([keep(m, k) for m in masks], 0)
        ) + keep(picked, tn(far_scores, fk))
        gk[:, win] += nn(
            jnp.concatenate(scores, 1), jnp.concatenate([keep(m, q) for m in masks], 0)
        )
        gv[:, win] += nn(jnp.concatenate([p.astype(BF) for p in probs], 1), ga_stack)
        gkf[:, win] += nn(far_scores, keep(picked, q))
        gvf[:, win] += nn(far_probs.astype(BF), ga_picked)
    own = pl.ds(pl.multiple_of(seq * FAR, FAR), FAR)
    lane_class = (iota((FAR, D), 1) // HD) & 3
    for near_ref, far_ref in ((gk, gkf), (gv, gvf)):
        own_far = far_ref[own]
        for r in range(RATE):
            near_ref[FAR * r : FAR * (r + 1)] += jnp.where(lane_class == r, own_far, 0.0)
    for turn, (ref, cols) in enumerate(
        ((gkf, slice(0, HALF)), (gkf, slice(HALF, D)), (gvf, slice(0, HALF)))
    ):
        other = pl.ds(pl.multiple_of(((seq + turn + 1) & 3) * FAR, FAR), FAR)
        ref[own, cols] = gvf[other, HALF:]
    place = spread_ref[...]
    for section, value in enumerate((gq, gk, gv, gkf)):
        halves = jnp.concatenate([value[:, 0:HALF], value[:, HALF:]], 0).astype(BF)
        both = nt(place, halves).astype(BF)
        turned[2 * section] = both[:, 0:TOK]
        turned[2 * section + 1] = both[:, TOK:]
    turned[SECTIONS - 1] = nt(place, gvf[:, 0:HALF].astype(BF)).astype(BF)
    for turn, ref in enumerate((x0, x1, x2, x3)):
        first = pl.multiple_of(((seq + turn) & 3) * SUB, 16)
        for section in range(SECTIONS):
            ref[section * SUB : (section + 1) * SUB] = turned[section, pl.ds(first, SUB)]
        ref[SECTIONS * SUB :] = loss_ref[...]


def product_kernel(
    x0, x1, x2, x3, n0, n1, n3, n2, wait_ref, whole_ref, tail_ref, got, left, right
):
    seq = lax.axis_index("seq")
    for turn, (x_ref, n_ref) in enumerate(zip((x0, x1, x2, x3), (n0, n1, n2, n3))):
        src = (seq - turn) & 3
        got[src] = x_ref[...]
        right[pl.ds(pl.multiple_of(src * TOK, TOK), TOK)] = n_ref[...]
    for src in range(N_SEQ):
        left[0 : 2 * SUB, src * TOK : (src + 1) * TOK] = got[src, 0 : 2 * SUB]
    shape = (SUB, TOK)
    row = iota(shape, 0)
    lane_class = iota(shape, 1) >> 5
    core_row = jnp.where(row >= 48, 1, 0)
    row_y = (row - 48 * core_row) // 12
    row_class = ((row_y & 1) << 1) + core_row
    spots = [(row_class == r) & (lane_class == r) for r in range(RATE)]
    fars = []
    last = jnp.zeros(shape, F32)
    for section in range(3):
        rows = slice((6 + section) * SUB, (7 + section) * SUB)
        far = jnp.zeros(shape, F32)
        freed = jnp.zeros(shape, F32)
        for src in range(N_SEQ):
            piece = got[src, rows].astype(F32)
            far = far + jnp.where(lane_class == src, 0.0, piece)
            freed = freed + jnp.where(lane_class == src, piece, 0.0)
        fars.append(far)
        last = last + pltpu.roll(freed, FAR * (section + 1), 1)
    fars.append(last)
    for index, far in enumerate(fars):
        near_at = (2 + index) * SUB
        turns = [far] + [pltpu.roll(far, FAR * t, 1) for t in range(1, RATE)]
        for src in range(N_SEQ):
            total = got[src, near_at : near_at + SUB].astype(F32)
            for r in range(RATE):
                total = total + jnp.where(spots[r], turns[(r - src) & 3], 0.0)
            left[near_at : near_at + SUB, src * TOK : (src + 1) * TOK] = total.astype(BF)
    whole_ref[...] = nn(left[...], right[...])
    loss = got[0, SECTIONS * SUB :].astype(F32)
    for src in range(1, N_SEQ):
        loss = loss + got[src, SECTIONS * SUB :].astype(F32)
    loss = jnp.sum(loss, axis=0, keepdims=True)[:, 0:1]
    tail_ref[...] = split_rows(jnp.broadcast_to(loss, (YROWS, D)), (YROWS, D), 72)


def place_kernel(whole_ref, tail_ref, wait1, wait2, wait3, mine_ref, other_ref):
    core = lax.axis_index("slide") & 1
    tail = tail_ref[72:]
    for turn, ref in enumerate((mine_ref, other_ref)):
        side = ((core + turn) & 1) * 48
        blocks = [whole_ref[pl.ds(pl.multiple_of(z * SUB + side, 16), 48)] for z in range(6)]
        for y in range(NY):
            rows = [block[12 * y : 12 * (y + 1)] for block in blocks]
            ref[y * YROWS : (y + 1) * YROWS] = jnp.concatenate(rows + [tail], 0).astype(BF)


def resplit(total):
    row = iota(total.shape, 0)
    loss = jnp.sum(jnp.where(row >= 72, total, 0.0), axis=0, keepdims=True)
    pieces = split_rows(jnp.broadcast_to(loss, total.shape), total.shape, 72)
    return jnp.where(row >= 72, pieces, total), loss


def core_kernel(mine_ref, other_ref, y0, y1, y2, y3):
    y = (lax.axis_index("slide") >> 1) & 3
    for turn, ref in enumerate((y0, y1, y2, y3)):
        rows = pl.ds(pl.multiple_of(((y + turn) & 3) * YROWS, 16), YROWS)
        ref[...] = resplit(mine_ref[rows].astype(F32) + other_ref[rows].astype(F32))[0].astype(BF)


def y_kernel(y0, y1, y2, y3, o0, o1, o2, o3, order_ref, out_ref):
    total = y0[...].astype(F32) + y1[...].astype(F32) + y2[...].astype(F32) + y3[...].astype(F32)
    total, loss = resplit(total)
    out_ref[0:6] = nn(order_ref[...], total.astype(BF)).astype(BF).reshape(6, 16, D)
    out = o0[...].astype(F32) + o1[...].astype(F32) + o2[...].astype(F32) + o3[...].astype(F32)
    tail = split_rows(jnp.broadcast_to(loss, (16, D)), (16, D), 12)
    for half in range(2):
        out_ref[6 + half] = (out[16 * half : 16 * (half + 1)] + tail).astype(BF)


def out_core_kernel(mine_ref, other_ref, wait0, wait1, wait2, wait3, y0, y1, y2, y3):
    y = (lax.axis_index("slide") >> 1) & 3
    for turn, ref in enumerate((y0, y1, y2, y3)):
        rows = pl.ds(pl.multiple_of(((y + turn) & 3) * SUB, 16), SUB)
        ref[...] = (mine_ref[rows].astype(F32) + other_ref[rows].astype(F32)).astype(BF)


def out_y_kernel(y0, y1, y2, y3, order_ref, x0, x1, x2, x3):
    seq = lax.axis_index("seq")
    total = y0[...].astype(F32) + y1[...].astype(F32) + y2[...].astype(F32) + y3[...].astype(F32)
    total = total.astype(BF)
    for turn, ref in enumerate((x0, x1, x2, x3)):
        rows = pl.ds(pl.multiple_of(((seq + turn) & 3) * 32, 32), 32)
        ref[...] = nn(order_ref[rows], total).astype(BF)


def z_kernel(in_ref, out_ref, loss_ref):
    total = in_ref[0].astype(F32)
    for src in range(1, NZ):
        total = total + in_ref[src].astype(F32)
    out_ref[...] = total[0:12]
    loss_ref[...] = jnp.sum(total[12:15, 0:1], axis=0, keepdims=True)


def spread_order():
    place = np.zeros((HALF, HALF), np.float32)
    for row in range(HALF):
        j, rest = divmod(row, SUB)
        c, rest = divmod(rest, 48)
        y, r = divmod(rest, 12)
        place[row, (y * NC + c) * HD + j * 12 + r] = 1.0
    return jnp.asarray(place, BF)


def out_order():
    place = np.zeros((D, D), np.float32)
    row = 0
    for c in range(NC):
        for y in range(NY):
            for j in range(N_SEQ):
                for half in range(2):
                    for r in range(12):
                        place[row, (half * 8 + y * NC + c) * HD + j * 12 + r] = 1.0
                        row += 1
    return jnp.asarray(place, BF)


def out_pad_order():
    place = np.zeros((N_SEQ * 32, SUB), np.float32)
    for j in range(N_SEQ):
        for half in range(2):
            for r in range(12):
                place[j * 32 + half * 16 + r, j * 24 + half * 12 + r] = 1.0
    return jnp.asarray(place, BF)


def pad_order():
    place = np.zeros((SUB, YROWS), np.float32)
    for z in range(6):
        for r in range(12):
            place[z * 16 + r, z * 12 + r] = 1.0
        for r in range(3):
            place[z * 16 + 12 + r, 72 + r] = 1.0
    return jnp.asarray(place, BF)


SMEM = pl.BlockSpec(memory_space=pltpu.SMEM)
VMEM = pl.BlockSpec(memory_space=pltpu.VMEM)
HBM = pl.BlockSpec(memory_space=pltpu.HBM)
ANY = pl.BlockSpec(memory_space=pl.ANY)


def call(kernel, out_shapes, args, scratch=(), micros=1.0, specs=None, grant=24, unread=0):
    if specs is None:
        specs = [SMEM if a.dtype == jnp.int32 else VMEM for a in args]
        specs = specs[: len(specs) - unread] + [ANY] * unread
    return pl.pallas_call(
        kernel,
        out_shape=out_shapes,
        in_specs=specs,
        out_specs=[VMEM] * len(out_shapes),
        scratch_shapes=list(scratch),
        compiler_params=pltpu.CompilerParams(vmem_limit_bytes=grant * 1024 * 1024),
        cost_estimate=pl.CostEstimate(
            flops=int(micros * 1.0e9), bytes_accessed=int(micros * 1.0e6), transcendentals=0
        ),
    )(*args)


def shape(*dims, dtype=BF):
    return jax.ShapeDtypeStruct(dims, dtype)


def slide_at(z, y, c):
    return (z * NY + y) * NC + c


CORE_PAIRS = [(i, i ^ 1) for i in range(NZ * NY * NC)]
Z_GROUPS = [[slide_at(z, y, c) for z in range(NZ)] for y in range(NY) for c in range(NC)]
SEQ_TURNS = [[(k, (k + t) % N_SEQ) for k in range(N_SEQ)] for t in range(N_SEQ)]
Y_TURNS = [
    [
        (slide_at(z, y, c), slide_at(z, (y + t) % NY, c))
        for z in range(NZ)
        for y in range(NY)
        for c in range(NC)
    ]
    for t in range(NY)
]


def swap(arrays, axis, turns, order=(1, 2, 3)):
    got = {t: lax.ppermute(arrays[t], axis, turns[t]) for t in order}
    return [arrays[0], got[1], got[2], got[3]]


def per_device(embeddings, tile_counts, masked_tiles, w_in, norm_gain, w_qkv, w_out):
    inv_count = 1.0 / (lax.axis_size("slide") * masked_tiles.shape[1])
    hidden, normed, projected, dilated = call(
        prep_kernel,
        [shape(TOK, D), shape(TOK, D), shape(TOK, 3 * D), shape(FAR, 2 * D)],
        (embeddings, masked_tiles, norm_gain, w_in, w_qkv),
        [
            pltpu.VMEM((TOK, 2 * D), BF),
            pltpu.VMEM((1, TOK), jnp.int32),
            pltpu.VMEM((D,), F32),
            pltpu.VMEM((2 * D, D), BF),
            pltpu.VMEM((D, 3 * D), BF),
            pltpu.SemaphoreType.DMA((6 + 2 * D // 256,)),
        ],
        4.0,
        [HBM] * 5,
        60,
    )
    fars = swap([dilated] * N_SEQ, "seq", SEQ_TURNS, (2, 1, 3))
    norms = swap([normed] * N_SEQ, "seq", SEQ_TURNS, (1, 3, 2))
    fk, fv, pnear, pfar, attended, tiles, flag = call(
        forward_kernel,
        [
            shape(TOK, D),
            shape(TOK, D),
            shape(GROUPS, TOK, RATE * TOK, dtype=F32),
            shape(GROUPS, TOK, TOK, dtype=F32),
            shape(TOK, D),
            shape(TOK, 2 * D),
            shape(TOK, TOK, dtype=F32),
        ],
        (tile_counts.reshape(1, 1), fars[2], fars[1], fars[3], projected, embeddings, masked_tiles),
        [pltpu.VMEM((TOK, D), F32)],
        2.0,
        [VMEM] * 7,
    )
    grad_attended, loss, out_mine, out_other = call(
        functools.partial(chain_kernel, inv_count),
        [shape(TOK, D), shape(16, 128), shape(HALF, D), shape(HALF, D)],
        (attended, hidden, tiles, flag, w_in, w_out, out_order()),
        (),
        3.0,
    )
    out_other = lax.ppermute(out_other, "slide", CORE_PAIRS)
    sent = call(
        backward_kernel,
        [shape(XROWS, TOK)] * N_SEQ,
        (projected, fk, fv, pnear, pfar, grad_attended, loss, spread_order()),
        [pltpu.VMEM((TOK, D), F32)] * 5 + [pltpu.VMEM((SECTIONS, HALF, TOK), BF)],
        8.0,
    )
    got = swap(sent, "seq", SEQ_TURNS)
    out = call(out_core_kernel, [shape(SUB, D)] * NY, (out_mine, out_other, sent[0], norms[1], norms[3], norms[2]), unread=4)
    out = swap(out, "slide", Y_TURNS)
    out_sums = call(
        out_y_kernel, [shape(32, D)] * N_SEQ, (*out, out_pad_order()), (), 20.0
    )
    out = swap(out_sums, "seq", SEQ_TURNS)
    whole, tail = call(
        product_kernel,
        [shape(6 * SUB, D, dtype=F32), shape(YROWS, D, dtype=F32)],
        (*got, norms[0], norms[1], norms[3], norms[2], out_sums[0]),
        [
            pltpu.VMEM((N_SEQ, XROWS, TOK), BF),
            pltpu.VMEM((6 * SUB, N_SEQ * TOK), BF),
            pltpu.VMEM((N_SEQ * TOK, D), BF),
        ],
        15.0,
        unread=1,
    )
    mine, other = call(
        place_kernel,
        [shape(NY * YROWS, D)] * 2,
        (whole, tail, *out[1:]),
        unread=3,
    )
    other = lax.ppermute(other, "slide", CORE_PAIRS)
    by_y = call(core_kernel, [shape(YROWS, D)] * NY, (mine, other))
    by_y = swap(by_y, "slide", Y_TURNS)
    (by_z,) = call(
        y_kernel,
        [shape(NZ, 16, D)],
        (by_y[0], by_y[2], by_y[1], by_y[3], *out, pad_order()),
    )
    by_z = lax.all_to_all(by_z, "slide", 0, 0, tiled=True, axis_index_groups=Z_GROUPS)
    gradients, loss = call(z_kernel, [shape(12, D, dtype=F32), shape(1, 1, dtype=F32)], (by_z,))
    return (gradients, loss[0, 0])


def solution(mesh):
    in_specs = (P("slide", "seq", None), P("slide"), P("slide", None), P(), P(), P(), P())
    out_specs = (P(("slide", "seq"), None), P())
    return jax.shard_map(
        per_device, mesh=mesh, in_specs=in_specs, out_specs=out_specs, check_vma=False
    )
```

```python
import functools
import math

import numpy as np
import jax
import jax.numpy as jnp
from jax import lax
from jax.experimental import pallas as pl
from jax.experimental.pallas import tpu as pltpu
from jax.sharding import PartitionSpec as P

HEADS = 16
RATE = 4
HD = 48
D = 768
TOK = 128
N_SEQ = 4
GROUPS = HEADS // RATE
FAR = TOK // RATE
NORM_EPS = 1e-06
NEG_FILL = -1e30
SCALE = 1.0 / math.sqrt(HD)
BF = jnp.bfloat16
F32 = jnp.float32
HALF = 384
SUB = 96
SECTIONS = 9
YROWS = 80
XROWS = SECTIONS * SUB + 16
NZ, NY, NC = 8, 4, 2


def dot(a, b, dims):
    return lax.dot_general(a, b, (dims, ((), ())), preferred_element_type=F32)


def nn(a, b):
    return dot(a, b, ((1,), (0,)))


def nt(a, b):
    return dot(a, b, ((1,), (1,)))


def tn(a, b):
    return dot(a, b, ((0,), (0,)))


def iota(shape, dim):
    return lax.broadcasted_iota(jnp.int32, shape, dim)


def class_major(index):
    return (index & (FAR - 1)) * RATE + (index >> 5)


def split_rows(value, shape, first):
    high = value.astype(BF).astype(F32)
    rest = value - high
    mid = rest.astype(BF).astype(F32)
    low = rest - mid
    row = iota(shape, 0)
    return jnp.where(
        row == first,
        high,
        jnp.where(row == first + 1, mid, jnp.where(row == first + 2, low, 0.0)),
    )


def class_order():
    shape = (TOK, TOK)
    return (iota(shape, 1) == class_major(iota(shape, 0))).astype(F32).astype(BF)


def masked_rows(positions, masked):
    hits = jnp.where(positions == masked, 1.0, 0.0)
    return jnp.broadcast_to(jnp.max(hits, axis=1, keepdims=True), (TOK, TOK))


def prep_kernel(
    tiles_hbm, masked_hbm, gain_hbm, w_in_hbm, w_qkv_hbm,
    hidden_out, normed_out, proj_out, dilated_out,
    tiles, masked, gain, w_in, w_qkv, sems,
):
    blocks = w_in_hbm.shape[0] // 256
    loads = [
        pltpu.make_async_copy(masked_hbm, masked, sems.at[0]),
        pltpu.make_async_copy(tiles_hbm.at[0], tiles, sems.at[1]),
        pltpu.make_async_copy(gain_hbm, gain, sems.at[2]),
    ]
    chunks = [
        pltpu.make_async_copy(
            w_in_hbm.at[256 * i : 256 * (i + 1)], w_in.at[256 * i : 256 * (i + 1)], sems.at[6 + i]
        )
        for i in range(blocks)
    ]
    parts = [
        pltpu.make_async_copy(
            w_qkv_hbm.at[:, D * i : D * (i + 1)], w_qkv.at[:, D * i : D * (i + 1)], sems.at[3 + i]
        )
        for i in range(3)
    ]
    for copy in loads + chunks + parts[1:] + parts[:1]:
        copy.start()
    order = class_order()
    positions = lax.axis_index("seq") * TOK + iota((TOK, TOK), 0)
    loads[0].wait()
    flag = masked_rows(positions, masked[...])[:, 0:1] > 0.5
    loads[1].wait()
    hidden = jnp.zeros((TOK, D), F32)
    for i in range(blocks):
        cols = slice(256 * i, 256 * (i + 1))
        inputs = jnp.where(flag, jnp.zeros((), BF), tiles[:, cols])
        chunks[i].wait()
        hidden += nn(inputs, w_in[cols])
    hidden_f = nn(order, hidden.astype(BF))
    hidden_out[...] = hidden_f.astype(BF)
    scale_rows = lax.rsqrt(jnp.mean(hidden_f * hidden_f, axis=1, keepdims=True) + NORM_EPS)
    loads[2].wait()
    normed = (hidden_f * scale_rows * gain[...].reshape(1, D)).astype(BF)
    normed_out[...] = normed
    for part in (1, 2, 0):
        parts[part].wait()
        for block in range(D // 256):
            first = part * D + block * 256
            rows = nn(normed, w_qkv[:, first : first + 256]).astype(BF)
            proj_out[:, first : first + 256] = rows
            if part > 0:
                dilated_out[:, first - D : first - D + 256] = dilate(rows, block * 256)


def dilate(rows, lane0):
    lane_class = ((iota((FAR, 256), 1) + lane0) // HD) & 3
    return by_class(lane_class, [rows[FAR * r : FAR * (r + 1)] for r in range(RATE)])


def window(group):
    return (group * RATE * HD) // 128 * 128


def head_masks(group):
    lane = iota((TOK, 256), 1) + window(group)
    row_class = iota((TOK, 256), 0) >> 5
    masks = []
    for r in range(RATE):
        first = (group * RATE + r) * HD
        masks.append((lane >= first) & (lane < first + HD))
    picked = masks[0] & (row_class == 0)
    for r in range(1, RATE):
        picked = picked | (masks[r] & (row_class == r))
    return masks, picked


def keep(mask, value):
    return jnp.where(mask, value, jnp.zeros((), value.dtype))


def by_class(own_class, pieces):
    out = pieces[0]
    for r in range(1, RATE):
        out = jnp.where(own_class == r, pieces[r], out)
    return out


def forward_kernel(
    count_ref, f2, f1, f3, proj_ref, tiles_ref, masked_ref,
    fk_ref, fv_ref, pnear_ref, pfar_ref, att_ref, tiles_out, flag_ref,
    att_acc,
):
    count = count_ref[...]
    seq = lax.axis_index("seq")
    pos0 = seq * TOK
    for turn, ref in enumerate((f1, f2, f3)):
        rows = pl.ds(pl.multiple_of(((seq - turn - 1) & 3) * FAR, FAR), FAR)
        fk_ref[rows] = ref[:, 0:D]
        fv_ref[rows] = ref[:, D:]
    own_rows = pl.ds(pl.multiple_of(seq * FAR, FAR), FAR)
    for part, far_ref in enumerate((fk_ref, fv_ref)):
        for block in range(D // 256):
            first = (1 + part) * D + block * 256
            far_ref[own_rows, block * 256 : (block + 1) * 256] = dilate(
                proj_ref[:, first : first + 256], block * 256
            )
    flag_ref[...] = masked_rows(pos0 + class_major(iota((TOK, TOK), 0)), masked_ref[...])
    tiles_out[...] = nn(class_order(), tiles_ref[0]).astype(BF)

    square = (TOK, TOK)
    key_pos = pos0 + class_major(iota(square, 0))
    query_pos = pos0 + class_major(iota(square, 1))
    near_ok = (key_pos < count) | (key_pos == query_pos)
    far_row = iota(square, 0)
    far_ok = (far_row >> 5) * TOK + (far_row & (FAR - 1)) * RATE + (iota(square, 1) >> 5) < count
    own_class = iota((1, TOK), 1) >> 5

    att_acc[...] = jnp.zeros_like(att_acc)
    for g in range(GROUPS):
        lo = window(g)
        win = slice(lo, lo + 256)
        masks, picked = head_masks(g)
        q = proj_ref[:, lo : lo + 256]
        k = proj_ref[:, D + lo : D + lo + 256]
        v = proj_ref[:, 2 * D + lo : 2 * D + lo + 256]
        near = nt(k, jnp.concatenate([keep(m, q) for m in masks], 0))
        far = jnp.where(far_ok, nt(fk_ref[:, win], keep(picked, q)) * SCALE, NEG_FILL)
        far_max = jnp.max(far, axis=0, keepdims=True)
        scores = [
            jnp.where(near_ok, near[:, TOK * r : TOK * (r + 1)] * SCALE, NEG_FILL) for r in range(RATE)
        ]
        tops = []
        for r in range(RATE):
            top = jnp.max(scores[r], axis=0, keepdims=True)
            tops.append(jnp.where(own_class == r, jnp.maximum(top, far_max), top))
        exps = [jnp.exp(scores[r] - tops[r]) for r in range(RATE)]
        far_exp = jnp.exp(far - by_class(own_class, tops))
        far_sum = jnp.sum(far_exp, axis=0, keepdims=True)
        inverse = []
        for r in range(RATE):
            total = jnp.sum(exps[r], axis=0, keepdims=True)
            inverse.append(1.0 / jnp.where(own_class == r, total + far_sum, total))
        probs = [exps[r] * inverse[r] for r in range(RATE)]
        far_probs = far_exp * by_class(own_class, inverse)
        for r in range(RATE):
            pnear_ref[g, :, TOK * r : TOK * (r + 1)] = probs[r]
        pfar_ref[g] = far_probs
        att = tn(
            jnp.concatenate([p.astype(BF) for p in probs], 0),
            jnp.concatenate([keep(m, v) for m in masks], 0),
        )
        att_acc[:, win] += att + keep(picked, tn(far_probs.astype(BF), fv_ref[:, win]))
    att_ref[...] = att_acc[...].astype(BF)


def chain_kernel(
    inv_count,
    att_ref, hidden_ref, tiles_ref, flag_ref, w_in_ref, w_out_ref, order_ref,
    ga_ref, loss_ref, mine_ref, other_ref,
):
    core = lax.axis_index("slide") & 1
    attended = att_ref[...]
    mixed = (hidden_ref[...].astype(F32) + nn(attended, w_out_ref[...])).astype(BF)
    flag = flag_ref[:, 0:1] > 0.5
    error = jnp.where(flag, nt(mixed, w_in_ref[...]) - tiles_ref[...].astype(F32), 0.0)
    loss = jnp.sum(jnp.sum(error * error, axis=1, keepdims=True), axis=0, keepdims=True) * inv_count
    loss_ref[...] = split_rows(jnp.broadcast_to(loss, (16, 128)), (16, 128), 0).astype(BF)
    grad_pred = (2.0 * inv_count * error).astype(BF)
    grad_mixed = nn(grad_pred, w_in_ref[...]).astype(BF)
    ga_ref[...] = nt(grad_mixed, w_out_ref[...]).astype(BF)
    for turn, ref in enumerate((mine_ref, other_ref)):
        first = pl.multiple_of(((core + turn) & 1) * HALF, HALF)
        left = nt(order_ref[pl.ds(first, HALF)], grad_mixed).astype(BF)
        ref[...] = nn(left, attended).astype(BF)


def backward_kernel(
    proj_ref, fk_ref, fv_ref, pnear_ref, pfar_ref, ga_ref, loss_ref, spread_ref,
    x0, x1, x2, x3,
    gq, gk, gv, gkf, gvf, turned,
):
    seq = lax.axis_index("seq")
    own_class = iota((1, TOK), 1) >> 5
    for ref in (gq, gk, gv, gkf, gvf):
        ref[...] = jnp.zeros_like(ref)
    for g in range(GROUPS):
        lo = window(g)
        win = slice(lo, lo + 256)
        masks, picked = head_masks(g)
        q = proj_ref[:, lo : lo + 256]
        k = proj_ref[:, D + lo : D + lo + 256]
        v = proj_ref[:, 2 * D + lo : 2 * D + lo + 256]
        ga = ga_ref[:, win]
        fk = fk_ref[:, win]
        fv = fv_ref[:, win]
        ga_stack = jnp.concatenate([keep(m, ga) for m in masks], 0)
        ga_picked = keep(picked, ga)
        near = nt(v, ga_stack)
        far = nt(fv, ga_picked)
        probs = [pnear_ref[g, :, TOK * r : TOK * (r + 1)] for r in range(RATE)]
        far_probs = pfar_ref[g]
        far_dot = jnp.sum(far_probs * far, axis=0, keepdims=True)
        grads = [near[:, TOK * r : TOK * (r + 1)] for r in range(RATE)]
        dots = []
        for r in range(RATE):
            own = jnp.sum(probs[r] * grads[r], axis=0, keepdims=True)
            dots.append(jnp.where(own_class == r, own + far_dot, own))
        scores = [(probs[r] * (grads[r] - dots[r]) * SCALE).astype(BF) for r in range(RATE)]
        far_scores = (far_probs * (far - by_class(own_class, dots)) * SCALE).astype(BF)
        gq[:, win] += tn(
            jnp.concatenate(scores, 0), jnp.concatenate([keep(m, k) for m in masks], 0)
        ) + keep(picked, tn(far_scores, fk))
        gk[:, win] += nn(
            jnp.concatenate(scores, 1), jnp.concatenate([keep(m, q) for m in masks], 0)
        )
        gv[:, win] += nn(jnp.concatenate([p.astype(BF) for p in probs], 1), ga_stack)
        gkf[:, win] += nn(far_scores, keep(picked, q))
        gvf[:, win] += nn(far_probs.astype(BF), ga_picked)
    own = pl.ds(pl.multiple_of(seq * FAR, FAR), FAR)
    lane_class = (iota((FAR, D), 1) // HD) & 3
    for near_ref, far_ref in ((gk, gkf), (gv, gvf)):
        own_far = far_ref[own]
        for r in range(RATE):
            near_ref[FAR * r : FAR * (r + 1)] += jnp.where(lane_class == r, own_far, 0.0)
    for turn, (ref, cols) in enumerate(
        ((gkf, slice(0, HALF)), (gkf, slice(HALF, D)), (gvf, slice(0, HALF)))
    ):
        other = pl.ds(pl.multiple_of(((seq + turn + 1) & 3) * FAR, FAR), FAR)
        ref[own, cols] = gvf[other, HALF:]
    place = spread_ref[...]
    for section, value in enumerate((gq, gk, gv, gkf)):
        halves = jnp.concatenate([value[:, 0:HALF], value[:, HALF:]], 0).astype(BF)
        both = nt(place, halves).astype(BF)
        turned[2 * section] = both[:, 0:TOK]
        turned[2 * section + 1] = both[:, TOK:]
    turned[SECTIONS - 1] = nt(place, gvf[:, 0:HALF].astype(BF)).astype(BF)
    for turn, ref in enumerate((x0, x1, x2, x3)):
        first = pl.multiple_of(((seq + turn) & 3) * SUB, 16)
        for section in range(SECTIONS):
            ref[section * SUB : (section + 1) * SUB] = turned[section, pl.ds(first, SUB)]
        ref[SECTIONS * SUB :] = loss_ref[...]


def product_kernel(
    x0, x1, x2, x3, n0, n1, n3, n2, wait_ref, whole_ref, tail_ref, got, left, right
):
    seq = lax.axis_index("seq")
    for turn, (x_ref, n_ref) in enumerate(zip((x0, x1, x2, x3), (n0, n1, n2, n3))):
        src = (seq - turn) & 3
        got[src] = x_ref[...]
        right[pl.ds(pl.multiple_of(src * TOK, TOK), TOK)] = n_ref[...]
    for src in range(N_SEQ):
        left[0 : 2 * SUB, src * TOK : (src + 1) * TOK] = got[src, 0 : 2 * SUB]
    shape = (SUB, TOK)
    row = iota(shape, 0)
    lane_class = iota(shape, 1) >> 5
    core_row = jnp.where(row >= 48, 1, 0)
    row_y = (row - 48 * core_row) // 12
    row_class = ((row_y & 1) << 1) + core_row
    spots = [(row_class == r) & (lane_class == r) for r in range(RATE)]
    fars = []
    last = jnp.zeros(shape, F32)
    for section in range(3):
        rows = slice((6 + section) * SUB, (7 + section) * SUB)
        far = jnp.zeros(shape, F32)
        freed = jnp.zeros(shape, F32)
        for src in range(N_SEQ):
            piece = got[src, rows].astype(F32)
            far = far + jnp.where(lane_class == src, 0.0, piece)
            freed = freed + jnp.where(lane_class == src, piece, 0.0)
        fars.append(far)
        last = last + pltpu.roll(freed, FAR * (section + 1), 1)
    fars.append(last)
    for index, far in enumerate(fars):
        near_at = (2 + index) * SUB
        turns = [far] + [pltpu.roll(far, FAR * t, 1) for t in range(1, RATE)]
        for src in range(N_SEQ):
            total = got[src, near_at : near_at + SUB].astype(F32)
            for r in range(RATE):
                total = total + jnp.where(spots[r], turns[(r - src) & 3], 0.0)
            left[near_at : near_at + SUB, src * TOK : (src + 1) * TOK] = total.astype(BF)
    whole_ref[...] = nn(left[...], right[...])
    loss = got[0, SECTIONS * SUB :].astype(F32)
    for src in range(1, N_SEQ):
        loss = loss + got[src, SECTIONS * SUB :].astype(F32)
    loss = jnp.sum(loss, axis=0, keepdims=True)[:, 0:1]
    tail_ref[...] = split_rows(jnp.broadcast_to(loss, (YROWS, D)), (YROWS, D), 72)


def place_kernel(whole_ref, tail_ref, wait1, wait2, wait3, mine_ref, other_ref):
    core = lax.axis_index("slide") & 1
    tail = tail_ref[72:]
    for turn, ref in enumerate((mine_ref, other_ref)):
        side = ((core + turn) & 1) * 48
        blocks = [whole_ref[pl.ds(pl.multiple_of(z * SUB + side, 16), 48)] for z in range(6)]
        for y in range(NY):
            rows = [block[12 * y : 12 * (y + 1)] for block in blocks]
            ref[y * YROWS : (y + 1) * YROWS] = jnp.concatenate(rows + [tail], 0).astype(BF)


def resplit(total):
    row = iota(total.shape, 0)
    loss = jnp.sum(jnp.where(row >= 72, total, 0.0), axis=0, keepdims=True)
    pieces = split_rows(jnp.broadcast_to(loss, total.shape), total.shape, 72)
    return jnp.where(row >= 72, pieces, total), loss


def core_kernel(mine_ref, other_ref, y0, y1, y2, y3):
    y = (lax.axis_index("slide") >> 1) & 3
    for turn, ref in enumerate((y0, y1, y2, y3)):
        rows = pl.ds(pl.multiple_of(((y + turn) & 3) * YROWS, 16), YROWS)
        ref[...] = resplit(mine_ref[rows].astype(F32) + other_ref[rows].astype(F32))[0].astype(BF)


def y_kernel(y0, y1, y2, y3, o0, o1, o2, o3, order_ref, out_ref):
    total = y0[...].astype(F32) + y1[...].astype(F32) + y2[...].astype(F32) + y3[...].astype(F32)
    total, loss = resplit(total)
    out_ref[0:6] = nn(order_ref[...], total.astype(BF)).astype(BF).reshape(6, 16, D)
    out = o0[...].astype(F32) + o1[...].astype(F32) + o2[...].astype(F32) + o3[...].astype(F32)
    tail = split_rows(jnp.broadcast_to(loss, (16, D)), (16, D), 12)
    for half in range(2):
        out_ref[6 + half] = (out[16 * half : 16 * (half + 1)] + tail).astype(BF)


def out_core_kernel(mine_ref, other_ref, wait0, wait1, wait2, wait3, y0, y1, y2, y3):
    y = (lax.axis_index("slide") >> 1) & 3
    for turn, ref in enumerate((y0, y1, y2, y3)):
        rows = pl.ds(pl.multiple_of(((y + turn) & 3) * SUB, 16), SUB)
        ref[...] = (mine_ref[rows].astype(F32) + other_ref[rows].astype(F32)).astype(BF)


def out_y_kernel(y0, y1, y2, y3, order_ref, x0, x1, x2, x3):
    seq = lax.axis_index("seq")
    total = y0[...].astype(F32) + y1[...].astype(F32) + y2[...].astype(F32) + y3[...].astype(F32)
    total = total.astype(BF)
    for turn, ref in enumerate((x0, x1, x2, x3)):
        rows = pl.ds(pl.multiple_of(((seq + turn) & 3) * 32, 32), 32)
        ref[...] = nn(order_ref[rows], total).astype(BF)


def z_kernel(in_ref, out_ref, loss_ref):
    total = in_ref[0].astype(F32)
    for src in range(1, NZ):
        total = total + in_ref[src].astype(F32)
    out_ref[...] = total[0:12]
    loss_ref[...] = jnp.sum(total[12:15, 0:1], axis=0, keepdims=True)


def spread_order():
    place = np.zeros((HALF, HALF), np.float32)
    for row in range(HALF):
        j, rest = divmod(row, SUB)
        c, rest = divmod(rest, 48)
        y, r = divmod(rest, 12)
        place[row, (y * NC + c) * HD + j * 12 + r] = 1.0
    return jnp.asarray(place, BF)


def out_order():
    place = np.zeros((D, D), np.float32)
    row = 0
    for c in range(NC):
        for y in range(NY):
            for j in range(N_SEQ):
                for half in range(2):
                    for r in range(12):
                        place[row, (half * 8 + y * NC + c) * HD + j * 12 + r] = 1.0
                        row += 1
    return jnp.asarray(place, BF)


def out_pad_order():
    place = np.zeros((N_SEQ * 32, SUB), np.float32)
    for j in range(N_SEQ):
        for half in range(2):
            for r in range(12):
                place[j * 32 + half * 16 + r, j * 24 + half * 12 + r] = 1.0
    return jnp.asarray(place, BF)


def pad_order():
    place = np.zeros((SUB, YROWS), np.float32)
    for z in range(6):
        for r in range(12):
            place[z * 16 + r, z * 12 + r] = 1.0
        for r in range(3):
            place[z * 16 + 12 + r, 72 + r] = 1.0
    return jnp.asarray(place, BF)


SMEM = pl.BlockSpec(memory_space=pltpu.SMEM)
VMEM = pl.BlockSpec(memory_space=pltpu.VMEM)
HBM = pl.BlockSpec(memory_space=pltpu.HBM)
ANY = pl.BlockSpec(memory_space=pl.ANY)


def call(kernel, out_shapes, args, scratch=(), micros=1.0, specs=None, grant=24, unread=0):
    if specs is None:
        specs = [SMEM if a.dtype == jnp.int32 else VMEM for a in args]
        specs = specs[: len(specs) - unread] + [ANY] * unread
    return pl.pallas_call(
        kernel,
        out_shape=out_shapes,
        in_specs=specs,
        out_specs=[VMEM] * len(out_shapes),
        scratch_shapes=list(scratch),
        compiler_params=pltpu.CompilerParams(vmem_limit_bytes=grant * 1024 * 1024),
        cost_estimate=pl.CostEstimate(
            flops=int(micros * 1.0e9), bytes_accessed=int(micros * 1.0e6), transcendentals=0
        ),
    )(*args)


def shape(*dims, dtype=BF):
    return jax.ShapeDtypeStruct(dims, dtype)


def slide_at(z, y, c):
    return (z * NY + y) * NC + c


CORE_PAIRS = [(i, i ^ 1) for i in range(NZ * NY * NC)]
Z_GROUPS = [[slide_at(z, y, c) for z in range(NZ)] for y in range(NY) for c in range(NC)]
SEQ_TURNS = [[(k, (k + t) % N_SEQ) for k in range(N_SEQ)] for t in range(N_SEQ)]
Y_TURNS = [
    [
        (slide_at(z, y, c), slide_at(z, (y + t) % NY, c))
        for z in range(NZ)
        for y in range(NY)
        for c in range(NC)
    ]
    for t in range(NY)
]


def swap(arrays, axis, turns, order=(1, 2, 3)):
    got = {t: lax.ppermute(arrays[t], axis, turns[t]) for t in order}
    return [arrays[0], got[1], got[2], got[3]]


def per_device(embeddings, tile_counts, masked_tiles, w_in, norm_gain, w_qkv, w_out):
    inv_count = 1.0 / (lax.axis_size("slide") * masked_tiles.shape[1])
    hidden, normed, projected, dilated = call(
        prep_kernel,
        [shape(TOK, D), shape(TOK, D), shape(TOK, 3 * D), shape(FAR, 2 * D)],
        (embeddings, masked_tiles, norm_gain, w_in, w_qkv),
        [
            pltpu.VMEM((TOK, 2 * D), BF),
            pltpu.VMEM((1, TOK), jnp.int32),
            pltpu.VMEM((D,), F32),
            pltpu.VMEM((2 * D, D), BF),
            pltpu.VMEM((D, 3 * D), BF),
            pltpu.SemaphoreType.DMA((6 + 2 * D // 256,)),
        ],
        4.0,
        [HBM] * 5,
        60,
    )
    fars = swap([dilated] * N_SEQ, "seq", SEQ_TURNS, (2, 1, 3))
    norms = swap([normed] * N_SEQ, "seq", SEQ_TURNS, (1, 3, 2))
    fk, fv, pnear, pfar, attended, tiles, flag = call(
        forward_kernel,
        [
            shape(TOK, D),
            shape(TOK, D),
            shape(GROUPS, TOK, RATE * TOK, dtype=F32),
            shape(GROUPS, TOK, TOK, dtype=F32),
            shape(TOK, D),
            shape(TOK, 2 * D),
            shape(TOK, TOK, dtype=F32),
        ],
        (tile_counts.reshape(1, 1), fars[2], fars[1], fars[3], projected, embeddings, masked_tiles),
        [pltpu.VMEM((TOK, D), F32)],
        2.0,
        [VMEM] * 7,
    )
    grad_attended, loss, out_mine, out_other = call(
        functools.partial(chain_kernel, inv_count),
        [shape(TOK, D), shape(16, 128), shape(HALF, D), shape(HALF, D)],
        (attended, hidden, tiles, flag, w_in, w_out, out_order()),
        (),
        3.0,
    )
    out_other = lax.ppermute(out_other, "slide", CORE_PAIRS)
    sent = call(
        backward_kernel,
        [shape(XROWS, TOK)] * N_SEQ,
        (projected, fk, fv, pnear, pfar, grad_attended, loss, spread_order()),
        [pltpu.VMEM((TOK, D), F32)] * 5 + [pltpu.VMEM((SECTIONS, HALF, TOK), BF)],
        8.0,
    )
    got = swap(sent, "seq", SEQ_TURNS)
    out = call(out_core_kernel, [shape(SUB, D)] * NY, (out_mine, out_other, sent[0], norms[1], norms[3], norms[2]), unread=4)
    out = swap(out, "slide", Y_TURNS)
    out_sums = call(
        out_y_kernel, [shape(32, D)] * N_SEQ, (*out, out_pad_order())
    )
    out = swap(out_sums, "seq", SEQ_TURNS)
    whole, tail = call(
        product_kernel,
        [shape(6 * SUB, D, dtype=F32), shape(YROWS, D, dtype=F32)],
        (*got, norms[0], norms[1], norms[3], norms[2], out_sums[0]),
        [
            pltpu.VMEM((N_SEQ, XROWS, TOK), BF),
            pltpu.VMEM((6 * SUB, N_SEQ * TOK), BF),
            pltpu.VMEM((N_SEQ * TOK, D), BF),
        ],
        15.0,
        unread=1,
    )
    mine, other = call(
        place_kernel,
        [shape(NY * YROWS, D)] * 2,
        (whole, tail, *out[1:]),
        unread=3,
    )
    other = lax.ppermute(other, "slide", CORE_PAIRS)
    by_y = call(core_kernel, [shape(YROWS, D)] * NY, (mine, other))
    by_y = swap(by_y, "slide", Y_TURNS)
    (by_z,) = call(
        y_kernel,
        [shape(NZ, 16, D)],
        (by_y[0], by_y[2], by_y[1], by_y[3], *out, pad_order()),
    )
    by_z = lax.all_to_all(by_z, "slide", 0, 0, tiled=True, axis_index_groups=Z_GROUPS)
    gradients, loss = call(z_kernel, [shape(12, D, dtype=F32), shape(1, 1, dtype=F32)], (by_z,))
    return (gradients, loss[0, 0])


def solution(mesh):
    in_specs = (P("slide", "seq", None), P("slide"), P("slide", None), P(), P(), P(), P())
    out_specs = (P(("slide", "seq"), None), P())
    return jax.shard_map(
        per_device, mesh=mesh, in_specs=in_specs, out_specs=out_specs, check_vma=False
    )
```

```python
import functools
import math

import numpy as np
import jax
import jax.numpy as jnp
from jax import lax
from jax.experimental import pallas as pl
from jax.experimental.pallas import tpu as pltpu
from jax.sharding import PartitionSpec as P

HEADS = 16
RATE = 4
HD = 48
D = 768
TOK = 128
N_SEQ = 4
GROUPS = HEADS // RATE
FAR = TOK // RATE
NORM_EPS = 1e-06
NEG_FILL = -1e30
SCALE = 1.0 / math.sqrt(HD)
BF = jnp.bfloat16
F32 = jnp.float32
HALF = 384
SUB = 96
SECTIONS = 9
YROWS = 80
XROWS = SECTIONS * SUB + 16
NZ, NY, NC = 8, 4, 2


def dot(a, b, dims):
    return lax.dot_general(a, b, (dims, ((), ())), preferred_element_type=F32)


def nn(a, b):
    return dot(a, b, ((1,), (0,)))


def nt(a, b):
    return dot(a, b, ((1,), (1,)))


def tn(a, b):
    return dot(a, b, ((0,), (0,)))


def iota(shape, dim):
    return lax.broadcasted_iota(jnp.int32, shape, dim)


def class_major(index):
    return (index & (FAR - 1)) * RATE + (index >> 5)


def split_rows(value, shape, first):
    high = value.astype(BF).astype(F32)
    rest = value - high
    mid = rest.astype(BF).astype(F32)
    low = rest - mid
    row = iota(shape, 0)
    return jnp.where(
        row == first,
        high,
        jnp.where(row == first + 1, mid, jnp.where(row == first + 2, low, 0.0)),
    )


def class_order():
    shape = (TOK, TOK)
    return (iota(shape, 1) == class_major(iota(shape, 0))).astype(F32).astype(BF)


def masked_rows(positions, masked):
    hits = jnp.where(positions == masked, 1.0, 0.0)
    return jnp.broadcast_to(jnp.max(hits, axis=1, keepdims=True), (TOK, TOK))


def prep_kernel(
    tiles_hbm, masked_hbm, gain_hbm, w_in_hbm, w_qkv_hbm,
    hidden_out, normed_out, proj_out, dilated_out,
    tiles, masked, gain, w_in, w_qkv, sems,
):
    blocks = w_in_hbm.shape[0] // 256
    loads = [
        pltpu.make_async_copy(masked_hbm, masked, sems.at[0]),
        pltpu.make_async_copy(tiles_hbm.at[0], tiles, sems.at[1]),
        pltpu.make_async_copy(gain_hbm, gain, sems.at[2]),
    ]
    chunks = [
        pltpu.make_async_copy(
            w_in_hbm.at[256 * i : 256 * (i + 1)], w_in.at[256 * i : 256 * (i + 1)], sems.at[6 + i]
        )
        for i in range(blocks)
    ]
    parts = [
        pltpu.make_async_copy(
            w_qkv_hbm.at[:, D * i : D * (i + 1)], w_qkv.at[:, D * i : D * (i + 1)], sems.at[3 + i]
        )
        for i in range(3)
    ]
    for copy in loads + chunks + parts[1:] + parts[:1]:
        copy.start()
    order = class_order()
    positions = lax.axis_index("seq") * TOK + iota((TOK, TOK), 0)
    loads[0].wait()
    flag = masked_rows(positions, masked[...])[:, 0:1] > 0.5
    loads[1].wait()
    hidden = jnp.zeros((TOK, D), F32)
    for i in range(blocks):
        cols = slice(256 * i, 256 * (i + 1))
        inputs = jnp.where(flag, jnp.zeros((), BF), tiles[:, cols])
        chunks[i].wait()
        hidden += nn(inputs, w_in[cols])
    hidden_f = nn(order, hidden.astype(BF))
    hidden_out[...] = hidden_f.astype(BF)
    scale_rows = lax.rsqrt(jnp.mean(hidden_f * hidden_f, axis=1, keepdims=True) + NORM_EPS)
    loads[2].wait()
    normed = (hidden_f * scale_rows * gain[...].reshape(1, D)).astype(BF)
    normed_out[...] = normed
    for part in (1, 2, 0):
        parts[part].wait()
        for block in range(D // 256):
            first = part * D + block * 256
            rows = nn(normed, w_qkv[:, first : first + 256]).astype(BF)
            proj_out[:, first : first + 256] = rows
            if part > 0:
                dilated_out[:, first - D : first - D + 256] = dilate(rows, block * 256)


def dilate(rows, lane0):
    lane_class = ((iota((FAR, 256), 1) + lane0) // HD) & 3
    return by_class(lane_class, [rows[FAR * r : FAR * (r + 1)] for r in range(RATE)])


def window(group):
    return (group * RATE * HD) // 128 * 128


def head_masks(group):
    lane = iota((TOK, 256), 1) + window(group)
    row_class = iota((TOK, 256), 0) >> 5
    masks = []
    for r in range(RATE):
        first = (group * RATE + r) * HD
        masks.append((lane >= first) & (lane < first + HD))
    picked = masks[0] & (row_class == 0)
    for r in range(1, RATE):
        picked = picked | (masks[r] & (row_class == r))
    return masks, picked


def keep(mask, value):
    return jnp.where(mask, value, jnp.zeros((), value.dtype))


def by_class(own_class, pieces):
    out = pieces[0]
    for r in range(1, RATE):
        out = jnp.where(own_class == r, pieces[r], out)
    return out


def forward_kernel(
    count_ref, f2, f1, f3, proj_ref, tiles_ref, masked_ref,
    fk_ref, fv_ref, pnear_ref, pfar_ref, att_ref, tiles_out, flag_ref,
    att_acc,
):
    count = count_ref[...]
    seq = lax.axis_index("seq")
    pos0 = seq * TOK
    for turn, ref in enumerate((f1, f2, f3)):
        rows = pl.ds(pl.multiple_of(((seq - turn - 1) & 3) * FAR, FAR), FAR)
        fk_ref[rows] = ref[:, 0:D]
        fv_ref[rows] = ref[:, D:]
    own_rows = pl.ds(pl.multiple_of(seq * FAR, FAR), FAR)
    for part, far_ref in enumerate((fk_ref, fv_ref)):
        for block in range(D // 256):
            first = (1 + part) * D + block * 256
            far_ref[own_rows, block * 256 : (block + 1) * 256] = dilate(
                proj_ref[:, first : first + 256], block * 256
            )
    flag_ref[...] = masked_rows(pos0 + class_major(iota((TOK, TOK), 0)), masked_ref[...])
    tiles_out[...] = nn(class_order(), tiles_ref[0]).astype(BF)

    square = (TOK, TOK)
    key_pos = pos0 + class_major(iota(square, 0))
    query_pos = pos0 + class_major(iota(square, 1))
    near_ok = (key_pos < count) | (key_pos == query_pos)
    far_row = iota(square, 0)
    far_ok = (far_row >> 5) * TOK + (far_row & (FAR - 1)) * RATE + (iota(square, 1) >> 5) < count
    own_class = iota((1, TOK), 1) >> 5

    att_acc[...] = jnp.zeros_like(att_acc)
    for g in range(GROUPS):
        lo = window(g)
        win = slice(lo, lo + 256)
        masks, picked = head_masks(g)
        q = proj_ref[:, lo : lo + 256]
        k = proj_ref[:, D + lo : D + lo + 256]
        v = proj_ref[:, 2 * D + lo : 2 * D + lo + 256]
        near = nt(k, jnp.concatenate([keep(m, q) for m in masks], 0))
        far = jnp.where(far_ok, nt(fk_ref[:, win], keep(picked, q)) * SCALE, NEG_FILL)
        far_max = jnp.max(far, axis=0, keepdims=True)
        scores = [
            jnp.where(near_ok, near[:, TOK * r : TOK * (r + 1)] * SCALE, NEG_FILL) for r in range(RATE)
        ]
        tops = []
        for r in range(RATE):
            top = jnp.max(scores[r], axis=0, keepdims=True)
            tops.append(jnp.where(own_class == r, jnp.maximum(top, far_max), top))
        exps = [jnp.exp(scores[r] - tops[r]) for r in range(RATE)]
        far_exp = jnp.exp(far - by_class(own_class, tops))
        far_sum = jnp.sum(far_exp, axis=0, keepdims=True)
        inverse = []
        for r in range(RATE):
            total = jnp.sum(exps[r], axis=0, keepdims=True)
            inverse.append(1.0 / jnp.where(own_class == r, total + far_sum, total))
        probs = [exps[r] * inverse[r] for r in range(RATE)]
        far_probs = far_exp * by_class(own_class, inverse)
        for r in range(RATE):
            pnear_ref[g, :, TOK * r : TOK * (r + 1)] = probs[r]
        pfar_ref[g] = far_probs
        att = tn(
            jnp.concatenate([p.astype(BF) for p in probs], 0),
            jnp.concatenate([keep(m, v) for m in masks], 0),
        )
        att_acc[:, win] += att + keep(picked, tn(far_probs.astype(BF), fv_ref[:, win]))
    att_ref[...] = att_acc[...].astype(BF)


def chain_kernel(
    inv_count,
    att_ref, hidden_ref, tiles_ref, flag_ref, w_in_ref, w_out_ref, order_ref,
    ga_ref, loss_ref, mine_ref, other_ref,
):
    core = lax.axis_index("slide") & 1
    attended = att_ref[...]
    mixed = (hidden_ref[...].astype(F32) + nn(attended, w_out_ref[...])).astype(BF)
    flag = flag_ref[:, 0:1] > 0.5
    error = jnp.where(flag, nt(mixed, w_in_ref[...]) - tiles_ref[...].astype(F32), 0.0)
    loss = jnp.sum(jnp.sum(error * error, axis=1, keepdims=True), axis=0, keepdims=True) * inv_count
    loss_ref[...] = split_rows(jnp.broadcast_to(loss, (16, 128)), (16, 128), 0).astype(BF)
    grad_pred = (2.0 * inv_count * error).astype(BF)
    grad_mixed = nn(grad_pred, w_in_ref[...]).astype(BF)
    ga_ref[...] = nt(grad_mixed, w_out_ref[...]).astype(BF)
    for turn, ref in enumerate((mine_ref, other_ref)):
        first = pl.multiple_of(((core + turn) & 1) * HALF, HALF)
        left = nt(order_ref[pl.ds(first, HALF)], grad_mixed).astype(BF)
        ref[...] = nn(left, attended).astype(BF)


def backward_kernel(
    proj_ref, fk_ref, fv_ref, pnear_ref, pfar_ref, ga_ref, loss_ref, spread_ref,
    x0, x1, x2, x3,
    gq, gk, gv, gkf, gvf, turned,
):
    seq = lax.axis_index("seq")
    own_class = iota((1, TOK), 1) >> 5
    for ref in (gq, gk, gv, gkf, gvf):
        ref[...] = jnp.zeros_like(ref)
    for g in range(GROUPS):
        lo = window(g)
        win = slice(lo, lo + 256)
        masks, picked = head_masks(g)
        q = proj_ref[:, lo : lo + 256]
        k = proj_ref[:, D + lo : D + lo + 256]
        v = proj_ref[:, 2 * D + lo : 2 * D + lo + 256]
        ga = ga_ref[:, win]
        fk = fk_ref[:, win]
        fv = fv_ref[:, win]
        ga_stack = jnp.concatenate([keep(m, ga) for m in masks], 0)
        ga_picked = keep(picked, ga)
        near = nt(v, ga_stack)
        far = nt(fv, ga_picked)
        probs = [pnear_ref[g, :, TOK * r : TOK * (r + 1)] for r in range(RATE)]
        far_probs = pfar_ref[g]
        far_dot = jnp.sum(far_probs * far, axis=0, keepdims=True)
        grads = [near[:, TOK * r : TOK * (r + 1)] for r in range(RATE)]
        dots = []
        for r in range(RATE):
            own = jnp.sum(probs[r] * grads[r], axis=0, keepdims=True)
            dots.append(jnp.where(own_class == r, own + far_dot, own))
        scores = [(probs[r] * (grads[r] - dots[r]) * SCALE).astype(BF) for r in range(RATE)]
        far_scores = (far_probs * (far - by_class(own_class, dots)) * SCALE).astype(BF)
        gq[:, win] += tn(
            jnp.concatenate(scores, 0), jnp.concatenate([keep(m, k) for m in masks], 0)
        ) + keep(picked, tn(far_scores, fk))
        gk[:, win] += nn(
            jnp.concatenate(scores, 1), jnp.concatenate([keep(m, q) for m in masks], 0)
        )
        gv[:, win] += nn(jnp.concatenate([p.astype(BF) for p in probs], 1), ga_stack)
        gkf[:, win] += nn(far_scores, keep(picked, q))
        gvf[:, win] += nn(far_probs.astype(BF), ga_picked)
    own = pl.ds(pl.multiple_of(seq * FAR, FAR), FAR)
    lane_class = (iota((FAR, D), 1) // HD) & 3
    for near_ref, far_ref in ((gk, gkf), (gv, gvf)):
        own_far = far_ref[own]
        for r in range(RATE):
            near_ref[FAR * r : FAR * (r + 1)] += jnp.where(lane_class == r, own_far, 0.0)
    for turn, (ref, cols) in enumerate(
        ((gkf, slice(0, HALF)), (gkf, slice(HALF, D)), (gvf, slice(0, HALF)))
    ):
        other = pl.ds(pl.multiple_of(((seq + turn + 1) & 3) * FAR, FAR), FAR)
        ref[own, cols] = gvf[other, HALF:]
    place = spread_ref[...]
    for section, value in enumerate((gq, gk, gv, gkf)):
        halves = jnp.concatenate([value[:, 0:HALF], value[:, HALF:]], 0).astype(BF)
        both = nt(place, halves).astype(BF)
        turned[2 * section] = both[:, 0:TOK]
        turned[2 * section + 1] = both[:, TOK:]
    turned[SECTIONS - 1] = nt(place, gvf[:, 0:HALF].astype(BF)).astype(BF)
    for turn, ref in enumerate((x0, x1, x2, x3)):
        first = pl.multiple_of(((seq + turn) & 3) * SUB, 16)
        for section in range(SECTIONS):
            ref[section * SUB : (section + 1) * SUB] = turned[section, pl.ds(first, SUB)]
        ref[SECTIONS * SUB :] = loss_ref[...]


def product_kernel(
    x0, x1, x2, x3, n0, n1, n3, n2, wait_ref, whole_ref, tail_ref, got, left, right
):
    seq = lax.axis_index("seq")
    for turn, (x_ref, n_ref) in enumerate(zip((x0, x1, x2, x3), (n0, n1, n2, n3))):
        src = (seq - turn) & 3
        got[src] = x_ref[...]
        right[pl.ds(pl.multiple_of(src * TOK, TOK), TOK)] = n_ref[...]
    for src in range(N_SEQ):
        left[0 : 2 * SUB, src * TOK : (src + 1) * TOK] = got[src, 0 : 2 * SUB]
    shape = (SUB, TOK)
    row = iota(shape, 0)
    lane_class = iota(shape, 1) >> 5
    core_row = jnp.where(row >= 48, 1, 0)
    row_y = (row - 48 * core_row) // 12
    row_class = ((row_y & 1) << 1) + core_row
    spots = [(row_class == r) & (lane_class == r) for r in range(RATE)]
    fars = []
    last = jnp.zeros(shape, F32)
    for section in range(3):
        rows = slice((6 + section) * SUB, (7 + section) * SUB)
        far = jnp.zeros(shape, F32)
        freed = jnp.zeros(shape, F32)
        for src in range(N_SEQ):
            piece = got[src, rows].astype(F32)
            far = far + jnp.where(lane_class == src, 0.0, piece)
            freed = freed + jnp.where(lane_class == src, piece, 0.0)
        fars.append(far)
        last = last + pltpu.roll(freed, FAR * (section + 1), 1)
    fars.append(last)
    for index, far in enumerate(fars):
        near_at = (2 + index) * SUB
        turns = [far] + [pltpu.roll(far, FAR * t, 1) for t in range(1, RATE)]
        for src in range(N_SEQ):
            total = got[src, near_at : near_at + SUB].astype(F32)
            for r in range(RATE):
                total = total + jnp.where(spots[r], turns[(r - src) & 3], 0.0)
            left[near_at : near_at + SUB, src * TOK : (src + 1) * TOK] = total.astype(BF)
    whole_ref[...] = nn(left[...], right[...])
    loss = got[0, SECTIONS * SUB :].astype(F32)
    for src in range(1, N_SEQ):
        loss = loss + got[src, SECTIONS * SUB :].astype(F32)
    loss = jnp.sum(loss, axis=0, keepdims=True)[:, 0:1]
    tail_ref[...] = split_rows(jnp.broadcast_to(loss, (YROWS, D)), (YROWS, D), 72)


def place_kernel(whole_ref, tail_ref, wait1, wait2, wait3, mine_ref, other_ref):
    core = lax.axis_index("slide") & 1
    tail = tail_ref[72:]
    for turn, ref in enumerate((mine_ref, other_ref)):
        side = ((core + turn) & 1) * 48
        blocks = [whole_ref[pl.ds(pl.multiple_of(z * SUB + side, 16), 48)] for z in range(6)]
        for y in range(NY):
            rows = [block[12 * y : 12 * (y + 1)] for block in blocks]
            ref[y * YROWS : (y + 1) * YROWS] = jnp.concatenate(rows + [tail], 0).astype(BF)


def resplit(total):
    row = iota(total.shape, 0)
    loss = jnp.sum(jnp.where(row >= 72, total, 0.0), axis=0, keepdims=True)
    pieces = split_rows(jnp.broadcast_to(loss, total.shape), total.shape, 72)
    return jnp.where(row >= 72, pieces, total), loss


def core_kernel(mine_ref, other_ref, y0, y1, y2, y3):
    y = (lax.axis_index("slide") >> 1) & 3
    for turn, ref in enumerate((y0, y1, y2, y3)):
        rows = pl.ds(pl.multiple_of(((y + turn) & 3) * YROWS, 16), YROWS)
        ref[...] = resplit(mine_ref[rows].astype(F32) + other_ref[rows].astype(F32))[0].astype(BF)


def y_kernel(y0, y1, y2, y3, o0, o1, o2, o3, order_ref, out_ref):
    total = y0[...].astype(F32) + y1[...].astype(F32) + y2[...].astype(F32) + y3[...].astype(F32)
    total, loss = resplit(total)
    out_ref[0:6] = nn(order_ref[...], total.astype(BF)).astype(BF).reshape(6, 16, D)
    out = o0[...].astype(F32) + o1[...].astype(F32) + o2[...].astype(F32) + o3[...].astype(F32)
    tail = split_rows(jnp.broadcast_to(loss, (16, D)), (16, D), 12)
    for half in range(2):
        out_ref[6 + half] = (out[16 * half : 16 * (half + 1)] + tail).astype(BF)


def out_core_kernel(mine_ref, other_ref, wait0, wait1, wait2, wait3, y0, y1, y2, y3):
    y = (lax.axis_index("slide") >> 1) & 3
    for turn, ref in enumerate((y0, y1, y2, y3)):
        rows = pl.ds(pl.multiple_of(((y + turn) & 3) * SUB, 16), SUB)
        ref[...] = (mine_ref[rows].astype(F32) + other_ref[rows].astype(F32)).astype(BF)


def out_y_kernel(y0, y1, y2, y3, order_ref, x0, x1, x2, x3):
    seq = lax.axis_index("seq")
    total = y0[...].astype(F32) + y1[...].astype(F32) + y2[...].astype(F32) + y3[...].astype(F32)
    total = total.astype(BF)
    for turn, ref in enumerate((x0, x1, x2, x3)):
        rows = pl.ds(pl.multiple_of(((seq + turn) & 3) * 32, 32), 32)
        ref[...] = nn(order_ref[rows], total).astype(BF)


def z_kernel(in_ref, out_ref, loss_ref):
    total = in_ref[0].astype(F32)
    for src in range(1, NZ):
        total = total + in_ref[src].astype(F32)
    out_ref[...] = total[0:12]
    loss_ref[...] = jnp.sum(total[12:15, 0:1], axis=0, keepdims=True)


def spread_order():
    place = np.zeros((HALF, HALF), np.float32)
    for row in range(HALF):
        j, rest = divmod(row, SUB)
        c, rest = divmod(rest, 48)
        y, r = divmod(rest, 12)
        place[row, (y * NC + c) * HD + j * 12 + r] = 1.0
    return jnp.asarray(place, BF)


def out_order():
    place = np.zeros((D, D), np.float32)
    row = 0
    for c in range(NC):
        for y in range(NY):
            for j in range(N_SEQ):
                for half in range(2):
                    for r in range(12):
                        place[row, (half * 8 + y * NC + c) * HD + j * 12 + r] = 1.0
                        row += 1
    return jnp.asarray(place, BF)


def out_pad_order():
    place = np.zeros((N_SEQ * 32, SUB), np.float32)
    for j in range(N_SEQ):
        for half in range(2):
            for r in range(12):
                place[j * 32 + half * 16 + r, j * 24 + half * 12 + r] = 1.0
    return jnp.asarray(place, BF)


def pad_order():
    place = np.zeros((SUB, YROWS), np.float32)
    for z in range(6):
        for r in range(12):
            place[z * 16 + r, z * 12 + r] = 1.0
        for r in range(3):
            place[z * 16 + 12 + r, 72 + r] = 1.0
    return jnp.asarray(place, BF)


SMEM = pl.BlockSpec(memory_space=pltpu.SMEM)
VMEM = pl.BlockSpec(memory_space=pltpu.VMEM)
HBM = pl.BlockSpec(memory_space=pltpu.HBM)
ANY = pl.BlockSpec(memory_space=pl.ANY)


def call(kernel, out_shapes, args, scratch=(), micros=1.0, specs=None, grant=24, unread=0):
    if specs is None:
        specs = [SMEM if a.dtype == jnp.int32 else VMEM for a in args]
        specs = specs[: len(specs) - unread] + [ANY] * unread
    return pl.pallas_call(
        kernel,
        out_shape=out_shapes,
        in_specs=specs,
        out_specs=[VMEM] * len(out_shapes),
        scratch_shapes=list(scratch),
        compiler_params=pltpu.CompilerParams(vmem_limit_bytes=grant * 1024 * 1024),
        cost_estimate=pl.CostEstimate(
            flops=int(micros * 1.0e9), bytes_accessed=int(micros * 1.0e6), transcendentals=0
        ),
    )(*args)


def shape(*dims, dtype=BF):
    return jax.ShapeDtypeStruct(dims, dtype)


def slide_at(z, y, c):
    return (z * NY + y) * NC + c


CORE_PAIRS = [(i, i ^ 1) for i in range(NZ * NY * NC)]
Z_GROUPS = [[slide_at(z, y, c) for z in range(NZ)] for y in range(NY) for c in range(NC)]
SEQ_TURNS = [[(k, (k + t) % N_SEQ) for k in range(N_SEQ)] for t in range(N_SEQ)]
Y_TURNS = [
    [
        (slide_at(z, y, c), slide_at(z, (y + t) % NY, c))
        for z in range(NZ)
        for y in range(NY)
        for c in range(NC)
    ]
    for t in range(NY)
]


def swap(arrays, axis, turns, order=(1, 2, 3)):
    got = {t: lax.ppermute(arrays[t], axis, turns[t]) for t in order}
    return [arrays[0], got[1], got[2], got[3]]


def per_device(embeddings, tile_counts, masked_tiles, w_in, norm_gain, w_qkv, w_out):
    inv_count = 1.0 / (lax.axis_size("slide") * masked_tiles.shape[1])
    hidden, normed, projected, dilated = call(
        prep_kernel,
        [shape(TOK, D), shape(TOK, D), shape(TOK, 3 * D), shape(FAR, 2 * D)],
        (embeddings, masked_tiles, norm_gain, w_in, w_qkv),
        [
            pltpu.VMEM((TOK, 2 * D), BF),
            pltpu.VMEM((1, TOK), jnp.int32),
            pltpu.VMEM((D,), F32),
            pltpu.VMEM((2 * D, D), BF),
            pltpu.VMEM((D, 3 * D), BF),
            pltpu.SemaphoreType.DMA((6 + 2 * D // 256,)),
        ],
        4.0,
        [HBM] * 5,
        60,
    )
    fars = swap([dilated] * N_SEQ, "seq", SEQ_TURNS, (2, 1, 3))
    norms = swap([normed] * N_SEQ, "seq", SEQ_TURNS, (1, 3, 2))
    fk, fv, pnear, pfar, attended, tiles, flag = call(
        forward_kernel,
        [
            shape(TOK, D),
            shape(TOK, D),
            shape(GROUPS, TOK, RATE * TOK, dtype=F32),
            shape(GROUPS, TOK, TOK, dtype=F32),
            shape(TOK, D),
            shape(TOK, 2 * D),
            shape(TOK, TOK, dtype=F32),
        ],
        (tile_counts.reshape(1, 1), fars[2], fars[1], fars[3], projected, embeddings, masked_tiles),
        [pltpu.VMEM((TOK, D), F32)],
        2.0,
        [VMEM] * 7,
    )
    grad_attended, loss, out_mine, out_other = call(
        functools.partial(chain_kernel, inv_count),
        [shape(TOK, D), shape(16, 128), shape(HALF, D), shape(HALF, D)],
        (attended, hidden, tiles, flag, w_in, w_out, out_order()),
        (),
        3.0,
    )
    out_other = lax.ppermute(out_other, "slide", CORE_PAIRS)
    sent = call(
        backward_kernel,
        [shape(XROWS, TOK)] * N_SEQ,
        (projected, fk, fv, pnear, pfar, grad_attended, loss, spread_order()),
        [pltpu.VMEM((TOK, D), F32)] * 5 + [pltpu.VMEM((SECTIONS, HALF, TOK), BF)],
        8.0,
    )
    got = swap(sent, "seq", SEQ_TURNS)
    out = call(out_core_kernel, [shape(SUB, D)] * NY, (out_mine, out_other, sent[0], norms[1], norms[3], norms[2]), unread=4, micros=0.01)
    out = swap(out, "slide", Y_TURNS)
    out_sums = call(
        out_y_kernel, [shape(32, D)] * N_SEQ, (*out, out_pad_order()), (), 0.01
    )
    out = swap(out_sums, "seq", SEQ_TURNS)
    whole, tail = call(
        product_kernel,
        [shape(6 * SUB, D, dtype=F32), shape(YROWS, D, dtype=F32)],
        (*got, norms[0], norms[1], norms[3], norms[2], out_sums[0]),
        [
            pltpu.VMEM((N_SEQ, XROWS, TOK), BF),
            pltpu.VMEM((6 * SUB, N_SEQ * TOK), BF),
            pltpu.VMEM((N_SEQ * TOK, D), BF),
        ],
        15.0,
        unread=1,
    )
    mine, other = call(
        place_kernel,
        [shape(NY * YROWS, D)] * 2,
        (whole, tail, *out[1:]),
        unread=3,
    )
    other = lax.ppermute(other, "slide", CORE_PAIRS)
    by_y = call(core_kernel, [shape(YROWS, D)] * NY, (mine, other))
    by_y = swap(by_y, "slide", Y_TURNS)
    (by_z,) = call(
        y_kernel,
        [shape(NZ, 16, D)],
        (by_y[0], by_y[2], by_y[1], by_y[3], *out, pad_order()),
    )
    by_z = lax.all_to_all(by_z, "slide", 0, 0, tiled=True, axis_index_groups=Z_GROUPS)
    gradients, loss = call(z_kernel, [shape(12, D, dtype=F32), shape(1, 1, dtype=F32)], (by_z,))
    return (gradients, loss[0, 0])


def solution(mesh):
    in_specs = (P("slide", "seq", None), P("slide"), P("slide", None), P(), P(), P(), P())
    out_specs = (P(("slide", "seq"), None), P())
    return jax.shard_map(
        per_device, mesh=mesh, in_specs=in_specs, out_specs=out_specs, check_vma=False
    )
```

```python
import functools
import math

import numpy as np
import jax
import jax.numpy as jnp
from jax import lax
from jax.experimental import pallas as pl
from jax.experimental.pallas import tpu as pltpu
from jax.sharding import PartitionSpec as P

HEADS = 16
RATE = 4
HD = 48
D = 768
TOK = 128
N_SEQ = 4
GROUPS = HEADS // RATE
FAR = TOK // RATE
NORM_EPS = 1e-06
NEG_FILL = -1e30
SCALE = 1.0 / math.sqrt(HD)
BF = jnp.bfloat16
F32 = jnp.float32
HALF = 384
SUB = 96
SECTIONS = 9
YROWS = 80
XROWS = SECTIONS * SUB + 16
NZ, NY, NC = 8, 4, 2


def dot(a, b, dims):
    return lax.dot_general(a, b, (dims, ((), ())), preferred_element_type=F32)


def nn(a, b):
    return dot(a, b, ((1,), (0,)))


def nt(a, b):
    return dot(a, b, ((1,), (1,)))


def tn(a, b):
    return dot(a, b, ((0,), (0,)))


def iota(shape, dim):
    return lax.broadcasted_iota(jnp.int32, shape, dim)


def class_major(index):
    return (index & (FAR - 1)) * RATE + (index >> 5)


def split_rows(value, shape, first):
    high = value.astype(BF).astype(F32)
    rest = value - high
    mid = rest.astype(BF).astype(F32)
    low = rest - mid
    row = iota(shape, 0)
    return jnp.where(
        row == first,
        high,
        jnp.where(row == first + 1, mid, jnp.where(row == first + 2, low, 0.0)),
    )


def class_order():
    shape = (TOK, TOK)
    return (iota(shape, 1) == class_major(iota(shape, 0))).astype(F32).astype(BF)


def masked_rows(positions, masked):
    hits = jnp.where(positions == masked, 1.0, 0.0)
    return jnp.broadcast_to(jnp.max(hits, axis=1, keepdims=True), (TOK, TOK))


def prep_kernel(
    tiles_hbm, masked_hbm, gain_hbm, w_in_hbm, w_qkv_hbm,
    hidden_out, normed_out, proj_out, dilated_out,
    tiles, masked, gain, w_in, w_qkv, sems,
):
    blocks = w_in_hbm.shape[0] // 256
    loads = [
        pltpu.make_async_copy(masked_hbm, masked, sems.at[0]),
        pltpu.make_async_copy(tiles_hbm.at[0], tiles, sems.at[1]),
        pltpu.make_async_copy(gain_hbm, gain, sems.at[2]),
    ]
    chunks = [
        pltpu.make_async_copy(
            w_in_hbm.at[256 * i : 256 * (i + 1)], w_in.at[256 * i : 256 * (i + 1)], sems.at[6 + i]
        )
        for i in range(blocks)
    ]
    parts = [
        pltpu.make_async_copy(
            w_qkv_hbm.at[:, D * i : D * (i + 1)], w_qkv.at[:, D * i : D * (i + 1)], sems.at[3 + i]
        )
        for i in range(3)
    ]
    for copy in loads + chunks + parts[1:] + parts[:1]:
        copy.start()
    order = class_order()
    positions = lax.axis_index("seq") * TOK + iota((TOK, TOK), 0)
    loads[0].wait()
    flag = masked_rows(positions, masked[...])[:, 0:1] > 0.5
    loads[1].wait()
    hidden = jnp.zeros((TOK, D), F32)
    for i in range(blocks):
        cols = slice(256 * i, 256 * (i + 1))
        inputs = jnp.where(flag, jnp.zeros((), BF), tiles[:, cols])
        chunks[i].wait()
        hidden += nn(inputs, w_in[cols])
    hidden_f = nn(order, hidden.astype(BF))
    hidden_out[...] = hidden_f.astype(BF)
    scale_rows = lax.rsqrt(jnp.mean(hidden_f * hidden_f, axis=1, keepdims=True) + NORM_EPS)
    loads[2].wait()
    normed = (hidden_f * scale_rows * gain[...].reshape(1, D)).astype(BF)
    normed_out[...] = normed
    for part in (1, 2, 0):
        parts[part].wait()
        for block in range(D // 256):
            first = part * D + block * 256
            rows = nn(normed, w_qkv[:, first : first + 256]).astype(BF)
            proj_out[:, first : first + 256] = rows
            if part > 0:
                dilated_out[:, first - D : first - D + 256] = dilate(rows, block * 256)


def dilate(rows, lane0):
    lane_class = ((iota((FAR, 256), 1) + lane0) // HD) & 3
    return by_class(lane_class, [rows[FAR * r : FAR * (r + 1)] for r in range(RATE)])


def window(group):
    return (group * RATE * HD) // 128 * 128


def head_masks(group):
    lane = iota((TOK, 256), 1) + window(group)
    row_class = iota((TOK, 256), 0) >> 5
    masks = []
    for r in range(RATE):
        first = (group * RATE + r) * HD
        masks.append((lane >= first) & (lane < first + HD))
    picked = masks[0] & (row_class == 0)
    for r in range(1, RATE):
        picked = picked | (masks[r] & (row_class == r))
    return masks, picked


def keep(mask, value):
    return jnp.where(mask, value, jnp.zeros((), value.dtype))


def by_class(own_class, pieces):
    out = pieces[0]
    for r in range(1, RATE):
        out = jnp.where(own_class == r, pieces[r], out)
    return out


def forward_kernel(
    count_ref, f2, f1, f3, proj_ref, tiles_ref, masked_ref,
    fk_ref, fv_ref, pnear_ref, pfar_ref, att_ref, tiles_out, flag_ref,
    att_acc,
):
    count = count_ref[...]
    seq = lax.axis_index("seq")
    pos0 = seq * TOK
    for turn, ref in enumerate((f1, f2, f3)):
        rows = pl.ds(pl.multiple_of(((seq - turn - 1) & 3) * FAR, FAR), FAR)
        fk_ref[rows] = ref[:, 0:D]
        fv_ref[rows] = ref[:, D:]
    own_rows = pl.ds(pl.multiple_of(seq * FAR, FAR), FAR)
    for part, far_ref in enumerate((fk_ref, fv_ref)):
        for block in range(D // 256):
            first = (1 + part) * D + block * 256
            far_ref[own_rows, block * 256 : (block + 1) * 256] = dilate(
                proj_ref[:, first : first + 256], block * 256
            )
    flag_ref[...] = masked_rows(pos0 + class_major(iota((TOK, TOK), 0)), masked_ref[...])
    tiles_out[...] = nn(class_order(), tiles_ref[0]).astype(BF)

    square = (TOK, TOK)
    key_pos = pos0 + class_major(iota(square, 0))
    query_pos = pos0 + class_major(iota(square, 1))
    near_ok = (key_pos < count) | (key_pos == query_pos)
    far_row = iota(square, 0)
    far_ok = (far_row >> 5) * TOK + (far_row & (FAR - 1)) * RATE + (iota(square, 1) >> 5) < count
    own_class = iota((1, TOK), 1) >> 5

    att_acc[...] = jnp.zeros_like(att_acc)
    for g in range(GROUPS):
        lo = window(g)
        win = slice(lo, lo + 256)
        masks, picked = head_masks(g)
        q = proj_ref[:, lo : lo + 256]
        k = proj_ref[:, D + lo : D + lo + 256]
        v = proj_ref[:, 2 * D + lo : 2 * D + lo + 256]
        near = nt(k, jnp.concatenate([keep(m, q) for m in masks], 0))
        far = jnp.where(far_ok, nt(fk_ref[:, win], keep(picked, q)) * SCALE, NEG_FILL)
        far_max = jnp.max(far, axis=0, keepdims=True)
        scores = [
            jnp.where(near_ok, near[:, TOK * r : TOK * (r + 1)] * SCALE, NEG_FILL) for r in range(RATE)
        ]
        tops = []
        for r in range(RATE):
            top = jnp.max(scores[r], axis=0, keepdims=True)
            tops.append(jnp.where(own_class == r, jnp.maximum(top, far_max), top))
        exps = [jnp.exp(scores[r] - tops[r]) for r in range(RATE)]
        far_exp = jnp.exp(far - by_class(own_class, tops))
        far_sum = jnp.sum(far_exp, axis=0, keepdims=True)
        inverse = []
        for r in range(RATE):
            total = jnp.sum(exps[r], axis=0, keepdims=True)
            inverse.append(1.0 / jnp.where(own_class == r, total + far_sum, total))
        probs = [exps[r] * inverse[r] for r in range(RATE)]
        far_probs = far_exp * by_class(own_class, inverse)
        for r in range(RATE):
            pnear_ref[g, :, TOK * r : TOK * (r + 1)] = probs[r]
        pfar_ref[g] = far_probs
        att = tn(
            jnp.concatenate([p.astype(BF) for p in probs], 0),
            jnp.concatenate([keep(m, v) for m in masks], 0),
        )
        att_acc[:, win] += att + keep(picked, tn(far_probs.astype(BF), fv_ref[:, win]))
    att_ref[...] = att_acc[...].astype(BF)


def chain_kernel(
    inv_count,
    att_ref, hidden_ref, tiles_ref, flag_ref, w_in_ref, w_out_ref, order_ref,
    ga_ref, loss_ref, mine_ref, other_ref,
):
    core = lax.axis_index("slide") & 1
    attended = att_ref[...]
    mixed = (hidden_ref[...].astype(F32) + nn(attended, w_out_ref[...])).astype(BF)
    flag = flag_ref[:, 0:1] > 0.5
    error = jnp.where(flag, nt(mixed, w_in_ref[...]) - tiles_ref[...].astype(F32), 0.0)
    loss = jnp.sum(jnp.sum(error * error, axis=1, keepdims=True), axis=0, keepdims=True) * inv_count
    loss_ref[...] = split_rows(jnp.broadcast_to(loss, (16, 128)), (16, 128), 0).astype(BF)
    grad_pred = (2.0 * inv_count * error).astype(BF)
    grad_mixed = nn(grad_pred, w_in_ref[...]).astype(BF)
    ga_ref[...] = nt(grad_mixed, w_out_ref[...]).astype(BF)
    for turn, ref in enumerate((mine_ref, other_ref)):
        first = pl.multiple_of(((core + turn) & 1) * HALF, HALF)
        left = nt(order_ref[pl.ds(first, HALF)], grad_mixed).astype(BF)
        ref[...] = nn(left, attended).astype(BF)


def backward_kernel(
    proj_ref, fk_ref, fv_ref, pnear_ref, pfar_ref, ga_ref, loss_ref, spread_ref,
    x0, x1, x2, x3,
    gq, gk, gv, gkf, gvf, turned,
):
    seq = lax.axis_index("seq")
    own_class = iota((1, TOK), 1) >> 5
    for ref in (gq, gk, gv, gkf, gvf):
        ref[...] = jnp.zeros_like(ref)
    for g in range(GROUPS):
        lo = window(g)
        win = slice(lo, lo + 256)
        masks, picked = head_masks(g)
        q = proj_ref[:, lo : lo + 256]
        k = proj_ref[:, D + lo : D + lo + 256]
        v = proj_ref[:, 2 * D + lo : 2 * D + lo + 256]
        ga = ga_ref[:, win]
        fk = fk_ref[:, win]
        fv = fv_ref[:, win]
        ga_stack = jnp.concatenate([keep(m, ga) for m in masks], 0)
        ga_picked = keep(picked, ga)
        near = nt(v, ga_stack)
        far = nt(fv, ga_picked)
        probs = [pnear_ref[g, :, TOK * r : TOK * (r + 1)] for r in range(RATE)]
        far_probs = pfar_ref[g]
        far_dot = jnp.sum(far_probs * far, axis=0, keepdims=True)
        grads = [near[:, TOK * r : TOK * (r + 1)] for r in range(RATE)]
        dots = []
        for r in range(RATE):
            own = jnp.sum(probs[r] * grads[r], axis=0, keepdims=True)
            dots.append(jnp.where(own_class == r, own + far_dot, own))
        scores = [(probs[r] * (grads[r] - dots[r]) * SCALE).astype(BF) for r in range(RATE)]
        far_scores = (far_probs * (far - by_class(own_class, dots)) * SCALE).astype(BF)
        gq[:, win] += tn(
            jnp.concatenate(scores, 0), jnp.concatenate([keep(m, k) for m in masks], 0)
        ) + keep(picked, tn(far_scores, fk))
        gk[:, win] += nn(
            jnp.concatenate(scores, 1), jnp.concatenate([keep(m, q) for m in masks], 0)
        )
        gv[:, win] += nn(jnp.concatenate([p.astype(BF) for p in probs], 1), ga_stack)
        gkf[:, win] += nn(far_scores, keep(picked, q))
        gvf[:, win] += nn(far_probs.astype(BF), ga_picked)
    own = pl.ds(pl.multiple_of(seq * FAR, FAR), FAR)
    lane_class = (iota((FAR, D), 1) // HD) & 3
    for near_ref, far_ref in ((gk, gkf), (gv, gvf)):
        own_far = far_ref[own]
        for r in range(RATE):
            near_ref[FAR * r : FAR * (r + 1)] += jnp.where(lane_class == r, own_far, 0.0)
    for turn, (ref, cols) in enumerate(
        ((gkf, slice(0, HALF)), (gkf, slice(HALF, D)), (gvf, slice(0, HALF)))
    ):
        other = pl.ds(pl.multiple_of(((seq + turn + 1) & 3) * FAR, FAR), FAR)
        ref[own, cols] = gvf[other, HALF:]
    place = spread_ref[...]
    for section, value in enumerate((gq, gk, gv, gkf)):
        halves = jnp.concatenate([value[:, 0:HALF], value[:, HALF:]], 0).astype(BF)
        both = nt(place, halves).astype(BF)
        turned[2 * section] = both[:, 0:TOK]
        turned[2 * section + 1] = both[:, TOK:]
    turned[SECTIONS - 1] = nt(place, gvf[:, 0:HALF].astype(BF)).astype(BF)
    for turn, ref in enumerate((x0, x1, x2, x3)):
        first = pl.multiple_of(((seq + turn) & 3) * SUB, 16)
        for section in range(SECTIONS):
            ref[section * SUB : (section + 1) * SUB] = turned[section, pl.ds(first, SUB)]
        ref[SECTIONS * SUB :] = loss_ref[...]


def product_kernel(
    x0, x1, x2, x3, n0, n1, n3, n2, wait_ref, whole_ref, tail_ref, got, left, right
):
    seq = lax.axis_index("seq")
    for turn, (x_ref, n_ref) in enumerate(zip((x0, x1, x2, x3), (n0, n1, n2, n3))):
        src = (seq - turn) & 3
        got[src] = x_ref[...]
        right[pl.ds(pl.multiple_of(src * TOK, TOK), TOK)] = n_ref[...]
    for src in range(N_SEQ):
        left[0 : 2 * SUB, src * TOK : (src + 1) * TOK] = got[src, 0 : 2 * SUB]
    shape = (SUB, TOK)
    row = iota(shape, 0)
    lane_class = iota(shape, 1) >> 5
    core_row = jnp.where(row >= 48, 1, 0)
    row_y = (row - 48 * core_row) // 12
    row_class = ((row_y & 1) << 1) + core_row
    spots = [(row_class == r) & (lane_class == r) for r in range(RATE)]
    fars = []
    last = jnp.zeros(shape, F32)
    for section in range(3):
        rows = slice((6 + section) * SUB, (7 + section) * SUB)
        far = jnp.zeros(shape, F32)
        freed = jnp.zeros(shape, F32)
        for src in range(N_SEQ):
            piece = got[src, rows].astype(F32)
            far = far + jnp.where(lane_class == src, 0.0, piece)
            freed = freed + jnp.where(lane_class == src, piece, 0.0)
        fars.append(far)
        last = last + pltpu.roll(freed, FAR * (section + 1), 1)
    fars.append(last)
    for index, far in enumerate(fars):
        near_at = (2 + index) * SUB
        turns = [far] + [pltpu.roll(far, FAR * t, 1) for t in range(1, RATE)]
        for src in range(N_SEQ):
            total = got[src, near_at : near_at + SUB].astype(F32)
            for r in range(RATE):
                total = total + jnp.where(spots[r], turns[(r - src) & 3], 0.0)
            left[near_at : near_at + SUB, src * TOK : (src + 1) * TOK] = total.astype(BF)
    whole_ref[...] = nn(left[...], right[...])
    loss = got[0, SECTIONS * SUB :].astype(F32)
    for src in range(1, N_SEQ):
        loss = loss + got[src, SECTIONS * SUB :].astype(F32)
    loss = jnp.sum(loss, axis=0, keepdims=True)[:, 0:1]
    tail_ref[...] = split_rows(jnp.broadcast_to(loss, (YROWS, D)), (YROWS, D), 72)


def place_kernel(whole_ref, tail_ref, wait1, wait2, wait3, mine_ref, other_ref):
    core = lax.axis_index("slide") & 1
    tail = tail_ref[72:]
    for turn, ref in enumerate((mine_ref, other_ref)):
        side = ((core + turn) & 1) * 48
        blocks = [whole_ref[pl.ds(pl.multiple_of(z * SUB + side, 16), 48)] for z in range(6)]
        for y in range(NY):
            rows = [block[12 * y : 12 * (y + 1)] for block in blocks]
            ref[y * YROWS : (y + 1) * YROWS] = jnp.concatenate(rows + [tail], 0).astype(BF)


def resplit(total):
    row = iota(total.shape, 0)
    loss = jnp.sum(jnp.where(row >= 72, total, 0.0), axis=0, keepdims=True)
    pieces = split_rows(jnp.broadcast_to(loss, total.shape), total.shape, 72)
    return jnp.where(row >= 72, pieces, total), loss


def core_kernel(mine_ref, other_ref, y0, y1, y2, y3):
    y = (lax.axis_index("slide") >> 1) & 3
    for turn, ref in enumerate((y0, y1, y2, y3)):
        rows = pl.ds(pl.multiple_of(((y + turn) & 3) * YROWS, 16), YROWS)
        ref[...] = resplit(mine_ref[rows].astype(F32) + other_ref[rows].astype(F32))[0].astype(BF)


def y_kernel(y0, y2, y1, y3, o0, o1, o2, o3, out_ref):
    total = y0[...].astype(F32) + y1[...].astype(F32) + y2[...].astype(F32) + y3[...].astype(F32)
    total, _ = resplit(total)
    out = o0[...].astype(F32) + o1[...].astype(F32) + o2[...].astype(F32) + o3[...].astype(F32)
    tail = total[72:, 0:128]
    for z in range(NZ):
        rows = total[12 * z : 12 * (z + 1)] if z < 6 else out[16 * (z - 6) : 16 * (z - 6) + 12]
        pieces = [rows[:, 128 * block : 128 * (block + 1)] for block in range(6)]
        out_ref[z] = jnp.concatenate(pieces + [tail], 0).astype(BF)


def out_core_kernel(mine_ref, other_ref, wait0, wait1, wait2, wait3, y0, y1, y2, y3):
    y = (lax.axis_index("slide") >> 1) & 3
    for turn, ref in enumerate((y0, y1, y2, y3)):
        rows = pl.ds(pl.multiple_of(((y + turn) & 3) * SUB, 16), SUB)
        ref[...] = (mine_ref[rows].astype(F32) + other_ref[rows].astype(F32)).astype(BF)


def out_y_kernel(y0, y1, y2, y3, order_ref, x0, x1, x2, x3):
    seq = lax.axis_index("seq")
    total = y0[...].astype(F32) + y1[...].astype(F32) + y2[...].astype(F32) + y3[...].astype(F32)
    total = total.astype(BF)
    for turn, ref in enumerate((x0, x1, x2, x3)):
        rows = pl.ds(pl.multiple_of(((seq + turn) & 3) * 32, 32), 32)
        ref[...] = nn(order_ref[rows], total).astype(BF)


def z_kernel(in_ref, out_ref, loss_ref):
    total = in_ref[0].astype(F32)
    for src in range(1, NZ):
        total = total + in_ref[src].astype(F32)
    for block in range(6):
        out_ref[:, 128 * block : 128 * (block + 1)] = total[12 * block : 12 * (block + 1)]
    loss_ref[...] = jnp.sum(total[72:75, 0:1], axis=0, keepdims=True)


def spread_order():
    place = np.zeros((HALF, HALF), np.float32)
    for row in range(HALF):
        j, rest = divmod(row, SUB)
        c, rest = divmod(rest, 48)
        y, r = divmod(rest, 12)
        place[row, (y * NC + c) * HD + j * 12 + r] = 1.0
    return jnp.asarray(place, BF)


def out_order():
    place = np.zeros((D, D), np.float32)
    row = 0
    for c in range(NC):
        for y in range(NY):
            for j in range(N_SEQ):
                for half in range(2):
                    for r in range(12):
                        place[row, (half * 8 + y * NC + c) * HD + j * 12 + r] = 1.0
                        row += 1
    return jnp.asarray(place, BF)


def out_pad_order():
    place = np.zeros((N_SEQ * 32, SUB), np.float32)
    for j in range(N_SEQ):
        for half in range(2):
            for r in range(12):
                place[j * 32 + half * 16 + r, j * 24 + half * 12 + r] = 1.0
    return jnp.asarray(place, BF)


SMEM = pl.BlockSpec(memory_space=pltpu.SMEM)
VMEM = pl.BlockSpec(memory_space=pltpu.VMEM)
HBM = pl.BlockSpec(memory_space=pltpu.HBM)
ANY = pl.BlockSpec(memory_space=pl.ANY)


def call(kernel, out_shapes, args, scratch=(), micros=1.0, specs=None, grant=24, unread=0):
    if specs is None:
        specs = [SMEM if a.dtype == jnp.int32 else VMEM for a in args]
        specs = specs[: len(specs) - unread] + [ANY] * unread
    return pl.pallas_call(
        kernel,
        out_shape=out_shapes,
        in_specs=specs,
        out_specs=[VMEM] * len(out_shapes),
        scratch_shapes=list(scratch),
        compiler_params=pltpu.CompilerParams(vmem_limit_bytes=grant * 1024 * 1024),
        cost_estimate=pl.CostEstimate(
            flops=int(micros * 1.0e9), bytes_accessed=int(micros * 1.0e6), transcendentals=0
        ),
    )(*args)


def shape(*dims, dtype=BF):
    return jax.ShapeDtypeStruct(dims, dtype)


def slide_at(z, y, c):
    return (z * NY + y) * NC + c


CORE_PAIRS = [(i, i ^ 1) for i in range(NZ * NY * NC)]
Z_GROUPS = [[slide_at(z, y, c) for z in range(NZ)] for y in range(NY) for c in range(NC)]
SEQ_TURNS = [[(k, (k + t) % N_SEQ) for k in range(N_SEQ)] for t in range(N_SEQ)]
Y_TURNS = [
    [
        (slide_at(z, y, c), slide_at(z, (y + t) % NY, c))
        for z in range(NZ)
        for y in range(NY)
        for c in range(NC)
    ]
    for t in range(NY)
]


def swap(arrays, axis, turns, order=(1, 2, 3)):
    got = {t: lax.ppermute(arrays[t], axis, turns[t]) for t in order}
    return [arrays[0], got[1], got[2], got[3]]


def per_device(embeddings, tile_counts, masked_tiles, w_in, norm_gain, w_qkv, w_out):
    inv_count = 1.0 / (lax.axis_size("slide") * masked_tiles.shape[1])
    hidden, normed, projected, dilated = call(
        prep_kernel,
        [shape(TOK, D), shape(TOK, D), shape(TOK, 3 * D), shape(FAR, 2 * D)],
        (embeddings, masked_tiles, norm_gain, w_in, w_qkv),
        [
            pltpu.VMEM((TOK, 2 * D), BF),
            pltpu.VMEM((1, TOK), jnp.int32),
            pltpu.VMEM((D,), F32),
            pltpu.VMEM((2 * D, D), BF),
            pltpu.VMEM((D, 3 * D), BF),
            pltpu.SemaphoreType.DMA((6 + 2 * D // 256,)),
        ],
        4.0,
        [HBM] * 5,
        60,
    )
    fars = swap([dilated] * N_SEQ, "seq", SEQ_TURNS, (2, 1, 3))
    norms = swap([normed] * N_SEQ, "seq", SEQ_TURNS, (1, 3, 2))
    fk, fv, pnear, pfar, attended, tiles, flag = call(
        forward_kernel,
        [
            shape(TOK, D),
            shape(TOK, D),
            shape(GROUPS, TOK, RATE * TOK, dtype=F32),
            shape(GROUPS, TOK, TOK, dtype=F32),
            shape(TOK, D),
            shape(TOK, 2 * D),
            shape(TOK, TOK, dtype=F32),
        ],
        (tile_counts.reshape(1, 1), fars[2], fars[1], fars[3], projected, embeddings, masked_tiles),
        [pltpu.VMEM((TOK, D), F32)],
        2.0,
        [VMEM] * 7,
    )
    grad_attended, loss, out_mine, out_other = call(
        functools.partial(chain_kernel, inv_count),
        [shape(TOK, D), shape(16, 128), shape(HALF, D), shape(HALF, D)],
        (attended, hidden, tiles, flag, w_in, w_out, out_order()),
        (),
        3.0,
    )
    out_other = lax.ppermute(out_other, "slide", CORE_PAIRS)
    sent = call(
        backward_kernel,
        [shape(XROWS, TOK)] * N_SEQ,
        (projected, fk, fv, pnear, pfar, grad_attended, loss, spread_order()),
        [pltpu.VMEM((TOK, D), F32)] * 5 + [pltpu.VMEM((SECTIONS, HALF, TOK), BF)],
        8.0,
    )
    got = swap(sent, "seq", SEQ_TURNS)
    out = call(out_core_kernel, [shape(SUB, D)] * NY, (out_mine, out_other, sent[0], norms[1], norms[3], norms[2]), unread=4)
    out = swap(out, "slide", Y_TURNS)
    out_sums = call(
        out_y_kernel, [shape(32, D)] * N_SEQ, (*out, out_pad_order())
    )
    out = swap(out_sums, "seq", SEQ_TURNS)
    whole, tail = call(
        product_kernel,
        [shape(6 * SUB, D, dtype=F32), shape(YROWS, D, dtype=F32)],
        (*got, norms[0], norms[1], norms[3], norms[2], out_sums[0]),
        [
            pltpu.VMEM((N_SEQ, XROWS, TOK), BF),
            pltpu.VMEM((6 * SUB, N_SEQ * TOK), BF),
            pltpu.VMEM((N_SEQ * TOK, D), BF),
        ],
        15.0,
        unread=1,
    )
    mine, other = call(
        place_kernel,
        [shape(NY * YROWS, D)] * 2,
        (whole, tail, *out[1:]),
        unread=3,
    )
    other = lax.ppermute(other, "slide", CORE_PAIRS)
    by_y = call(core_kernel, [shape(YROWS, D)] * NY, (mine, other))
    by_y = swap(by_y, "slide", Y_TURNS)
    (by_z,) = call(
        y_kernel,
        [shape(NZ, 80, 128)],
        (by_y[0], by_y[2], by_y[1], by_y[3], *out),
    )
    by_z = lax.all_to_all(by_z, "slide", 0, 0, tiled=True, axis_index_groups=Z_GROUPS)
    gradients, loss = call(z_kernel, [shape(12, D, dtype=F32), shape(1, 1, dtype=F32)], (by_z,))
    return (gradients, loss[0, 0])


def solution(mesh):
    in_specs = (P("slide", "seq", None), P("slide"), P("slide", None), P(), P(), P(), P())
    out_specs = (P(("slide", "seq"), None), P())
    return jax.shard_map(
        per_device, mesh=mesh, in_specs=in_specs, out_specs=out_specs, check_vma=False
    )
```
